32 devices in a mesh: dp: 8 (over y, x, core), mp: 4 (over z).
Axes of the slice: x: 2, y: 2, z: 4, core: 2. Of those that a mesh axis runs over, the one named last changes fastest.
Arguments:
- residual_in: float32 [8192, 1024], P(('dp', 'mp')), may hold values from -60 to 60
- cotangent: float32 [8192, 1024], P(('dp', 'mp')), may hold values from -6 to 6
- expert_ids: int32 [8192, 8], P(('dp', 'mp')), may hold values from 0 to 31, all different within a row; in each aligned block of 256 rows (0 to 255, 256 to 511, ...) at most 80 rows name the same one
- attn_gain: float32 [1024], P(('dp', 'mp')), may hold values from 0.5 to 1.5
- query_w: float32 [1024, 1024], P('dp', 'mp'), may hold values from -0.1875 to 0.1875
- key_value_weight: float32 [1024, 1024], P('dp', 'mp'), may hold values from -0.1875 to 0.1875
- output_w: float32 [1024, 1024], P('mp', 'dp'), may hold values from -3 to 3
- moe_gain: float32 [1024], P(('dp', 'mp')), may hold values from 0.5 to 1.5
- router_w: float32 [1024, 32], P(('dp', 'mp')), may hold values from -0.09375 to 0.09375
- gateup_w: float32 [32, 2, 512, 1024], P('dp', None, 'mp'), may hold values from -0.1875 to 0.1875
- down_w: float32 [32, 512, 1024], P('dp', 'mp'), may hold values from -2 to 2
- attn_gain_mean: float32 [1024], P(('dp', 'mp')), may hold values from -384 to 384
- attn_gain_var: float32 [1024], P(('dp', 'mp')), may hold values from 491.52 to 49152
- query_mean: float32 [1024, 1024], P('dp', 'mp'), may hold values from -320 to 320
- query_var: float32 [1024, 1024], P('dp', 'mp'), may hold values from 327.68 to 32768
- key_value_first_moment: float32 [1024, 1024], P('dp', 'mp'), may hold values from -320 to 320
- key_value_second_moment: float32 [1024, 1024], P('dp', 'mp'), may hold values from 327.68 to 32768
- output_mean: float32 [1024, 1024], P('mp', 'dp'), may hold values from -64 to 64
- output_var: float32 [1024, 1024], P('mp', 'dp'), may hold values from 13.1072 to 1310.72
- moe_gain_mean: float32 [1024], P(('dp', 'mp')), may hold values from -256 to 256
- moe_gain_var: float32 [1024], P(('dp', 'mp')), may hold values from 163.84 to 16384
- router_mean: float32 [1024, 32], P(('dp', 'mp')), may hold values from -640 to 640
- router_var: float32 [1024, 32], P(('dp', 'mp')), may hold values from 1310.72 to 131072
- gateup_mean: float32 [32, 2, 512, 1024], P('dp', None, 'mp'), may hold values from -16 to 16
- gateup_var: float32 [32, 2, 512, 1024], P('dp', None, 'mp'), may hold values from 0.8192 to 81.92
- down_mean: float32 [32, 512, 1024], P('dp', 'mp'), may hold values from -1 to 1
- down_var: float32 [32, 512, 1024], P('dp', 'mp'), may hold values from 0.00458752 to 0.458752
Outputs:
- block_out: float32 [8192, 1024], P(('dp', 'mp'))
- input_grad: float32 [8192, 1024], P(('dp', 'mp'))
- attn_gain_grad: float32 [1024], P(('dp', 'mp'))
- attn_gain_new: float32 [1024], P(('dp', 'mp'))
- attn_gain_mean_new: float32 [1024], P(('dp', 'mp'))
- attn_gain_var_new: float32 [1024], P(('dp', 'mp'))
- query_grad: float32 [1024, 1024], P('dp', 'mp')
- query_new: float32 [1024, 1024], P('dp', 'mp')
- query_mean_new: float32 [1024, 1024], P('dp', 'mp')
- query_var_new: float32 [1024, 1024], P('dp', 'mp')
- keyval_grad: float32 [1024, 1024], P('dp', 'mp')
- keyval_new: float32 [1024, 1024], P('dp', 'mp')
- keyval_mean_new: float32 [1024, 1024], P('dp', 'mp')
- keyval_var_new: float32 [1024, 1024], P('dp', 'mp')
- output_grad: float32 [1024, 1024], P('mp', 'dp')
- output_new: float32 [1024, 1024], P('mp', 'dp')
- output_mean_new: float32 [1024, 1024], P('mp', 'dp')
- output_var_new: float32 [1024, 1024], P('mp', 'dp')
- moe_gain_grad: float32 [1024], P(('dp', 'mp'))
- moe_gain_new: float32 [1024], P(('dp', 'mp'))
- moe_gain_mean_new: float32 [1024], P(('dp', 'mp'))
- moe_gain_var_new: float32 [1024], P(('dp', 'mp'))
- router_grad: float32 [1024, 32], P(('dp', 'mp'))
- router_new: float32 [1024, 32], P(('dp', 'mp'))
- router_mean_new: float32 [1024, 32], P(('dp', 'mp'))
- router_var_new: float32 [1024, 32], P(('dp', 'mp'))
- gateup_grad: float32 [32, 2, 512, 1024], P('dp', None, 'mp')
- gateup_new: float32 [32, 2, 512, 1024], P('dp', None, 'mp')
- gateup_mean_new: float32 [32, 2, 512, 1024], P('dp', None, 'mp')
- gateup_var_new: float32 [32, 2, 512, 1024], P('dp', None, 'mp')
- down_grad: float32 [32, 512, 1024], P('dp', 'mp')
- down_new: float32 [32, 512, 1024], P('dp', 'mp')
- down_mean_new: float32 [32, 512, 1024], P('dp', 'mp')
- down_var_new: float32 [32, 512, 1024], P('dp', 'mp')
The draws below stay inside these ranges and needn't reach their ends.
Inputs may be any that keep to these rules, and one draw needn't show every extreme that they name: `expert_ids`: the 8 experts of a row differ. Among the 256 rows of one device (aligned blocks of rows) no expert is named more than 80 times, a bound that some block reaches.
All inputs are finite; a program needn't handle non-finite values.
Results may differ from the reference program's by a relative error of at most 0.02.
Values may be sent and summed in bfloat16 or wider, within the bound.
A program may use at most 256 MiB of HBM per device.

```python
import math
import jax
import jax.numpy as jnp
import numpy as np
from jax import lax

MODEL_WIDTH = 1024
QUERY_HEADS = 16
KEY_VALUE_HEADS = 8
HEAD_SIZE = 64
EXPERTS = 32
TOPK = 8
FF = 512
SEQUENCE_TOKENS = 512
TOK_DEV = 256
STEP = 3
TOKEN_TOTAL = 8192
CAP = 80
N_DP = 8
N_MP = 4


def draw_residual_in(key, part):
    key_rows, key_cols, key_base = jax.random.split(key, 3)
    full_shape = (TOKEN_TOTAL, MODEL_WIDTH)
    row_scale = jnp.exp(jax.random.uniform(key_rows, (TOKEN_TOTAL, 1), jnp.float32, math.log(0.4), math.log(4.0)))
    col_scale = jnp.exp(jax.random.uniform(key_cols, (1, MODEL_WIDTH), jnp.float32, math.log(0.4), math.log(4.0)))
    values = jax.random.normal(key_base, full_shape, jnp.float32)
    return jnp.clip(values * row_scale * col_scale, -60.0, 60.0)


def steps_of(key, dims, cuts, least, high):
    def one(axis_at, blocks):
        heights = jax.random.uniform(jax.random.fold_in(jax.random.fold_in(key, 6), axis_at), (blocks,), jnp.float32, least / len(cuts), high / len(cuts))
        return jnp.repeat(jnp.exp(heights), dims[axis_at] // blocks).reshape((-1,) + (1,) * (len(dims) - axis_at - 1))

    level = one(*cuts[0])
    for cut in cuts[1:]:
        level = level * one(*cut)
    return level


def routed_block(rng, own, number, rows, amount, top, bound, slope):
    ranking = jax.random.permutation(rng, amount)
    heavy_load, ordinary = shares(amount, rows * top, bound, slope, True), shares(amount, rows * top, bound, slope, False)
    places = jnp.arange(amount)

    def named(tallies, turn):
        used = int((tallies > 0).sum())
        fixed = max(1, used // 4)
        passed = fixed + (places - fixed + turn * (used - fixed)) % max(1, amount - fixed)
        return jnp.zeros((amount,), jnp.int32).at[ranking[jnp.where(places < fixed, places, passed)]].set(jnp.asarray(tallies, jnp.int32))

    tallies = jnp.where(number % 4 == 0, named(heavy_load, number // 4), named(ordinary, number - number // 4 - 1))
    mixed = jax.random.permutation(jax.random.fold_in(own, 3), amount)
    giver, sink = mixed[0:amount // 2 * 2:2], mixed[1:amount // 2 * 2:2]
    slack = jnp.minimum(tallies[giver] - 1, bound - tallies[sink]) // 2
    slack = jnp.where((giver == ranking[0]) | (sink == ranking[0]) | (tallies[sink] == 0), 0, jnp.maximum(slack, 0))
    passed = jax.random.randint(jax.random.fold_in(own, 4), (amount // 2,), 0, 1 << 20) % (slack + 1)
    tallies = tallies.at[giver].add(-passed).at[sink].add(passed)
    labels = jnp.searchsorted(jnp.cumsum(tallies), jnp.arange(rows * top), side="right").astype(jnp.int32)
    table = labels.reshape(top, rows).T
    table = table[jax.random.permutation(jax.random.fold_in(own, 1), rows)]
    turn = jax.random.randint(jax.random.fold_in(own, 2), (rows, 1), 0, top)
    return jnp.take_along_axis(table, (jnp.arange(top)[None, :] + turn) % top, axis=1)


def shares(amount, total, limit, skew, full):
    loads = [(1 << 20) // math.isqrt(standing ** skew) + 1 for standing in range(1, amount + 1)]
    largest = limit if full else min(limit, max(-(-total // amount), total * loads[0] // sum(loads)))
    least = 1 if total - largest >= amount - 1 else 0
    counts, surplus = [largest] + [least] * (amount - 1), total - largest - least * (amount - 1)
    while surplus > 0:
        movable = [i for i in range(1, amount) if counts[i] < largest] or [i for i in range(1, amount) if counts[i] < limit]
        whole, remaining = sum([loads[i] for i in movable]), surplus
        for i in movable:
            extra = min(limit - counts[i], max(1, remaining * loads[i] // whole), surplus)
            counts[i] = counts[i] + extra
            surplus = surplus - extra
    return np.array(counts)


def noise(rng, extent, deviation, most, cuts=(), kind=jnp.bfloat16):
    drawn = jax.random.normal(rng, extent, jnp.float32) * deviation
    if len(cuts) > 0:
        drawn = steps_of(rng, extent, cuts, -0.22, 0.18) * drawn
    return jnp.clip(drawn, min=-most, max=most).astype(kind)


def setup_inputs(seed: int = 0) -> dict:
    streams_of = jax.random.split(jax.random.key(seed), 28)
    residual_in = draw_residual_in(jax.random.fold_in(streams_of[27], 71), 0)
    cotangent = noise(streams_of[1], (TOKEN_TOTAL, MODEL_WIDTH), 1.0, 6.0, ((0, 32),), jnp.float32)
    expert_ids_keys = jax.random.split(jax.random.fold_in(streams_of[2], 1), TOKEN_TOTAL // TOK_DEV)
    expert_ids_turns = jax.random.permutation(jax.random.fold_in(streams_of[2], 3), TOKEN_TOTAL // TOK_DEV)
    expert_ids = jax.vmap(lambda own, number: routed_block(jax.random.fold_in(streams_of[2], 2), own, number, TOK_DEV, EXPERTS, TOPK, CAP, 2))(expert_ids_keys, expert_ids_turns).reshape((TOKEN_TOTAL, TOPK))
    attn_gain = jnp.clip(1.0 + 0.1 * jax.random.normal(streams_of[3], (MODEL_WIDTH,), jnp.float32), 0.5, 1.5)
    query_w = noise(streams_of[4], (MODEL_WIDTH, QUERY_HEADS * HEAD_SIZE), MODEL_WIDTH ** -0.5, 0.1875, ((0, 8), (1, 4)), jnp.float32)
    key_value_weight = noise(streams_of[5], (MODEL_WIDTH, 2 * KEY_VALUE_HEADS * HEAD_SIZE), MODEL_WIDTH ** -0.5, 0.1875, ((0, 8), (1, 4)), jnp.float32)
    output_w = noise(streams_of[6], (QUERY_HEADS * HEAD_SIZE, MODEL_WIDTH), 4 ** -0.5, 3.0, ((0, 4), (1, 8)), jnp.float32)
    moe_gain = jnp.clip(1.0 + 0.1 * jax.random.normal(streams_of[7], (MODEL_WIDTH,), jnp.float32), 0.5, 1.5)
    router_w = noise(streams_of[8], (MODEL_WIDTH, EXPERTS), (4 * MODEL_WIDTH) ** -0.5, 0.09375, ((0, 32),), jnp.float32)
    gateup_w = noise(streams_of[9], (EXPERTS, 2, FF, MODEL_WIDTH), MODEL_WIDTH ** -0.5, 0.1875, ((0, 8), (2, 4)), jnp.float32)
    down_w = noise(streams_of[10], (EXPERTS, FF, MODEL_WIDTH), 8 ** -0.5, 2.0, ((0, 8), (1, 4)), jnp.float32)
    attn_gain_mean = noise(streams_of[11], (MODEL_WIDTH,), (0.7 * TOKEN_TOTAL ** 0.5), 384.0, ((0, 32),), jnp.float32)
    attn_gain_var = jnp.clip(jnp.exp(math.log(49152.0) - 4.6051702 * jax.random.uniform(streams_of[12], (MODEL_WIDTH,), jnp.float32) ** steps_of(streams_of[12], (MODEL_WIDTH,), ((0, 32),), -0.2, 0.2)), 491.52, 49152.0)
    query_mean = noise(streams_of[13], (MODEL_WIDTH, QUERY_HEADS * HEAD_SIZE), (0.6 * TOKEN_TOTAL ** 0.5), 320.0, ((0, 8), (1, 4)), jnp.float32)
    query_var = jnp.clip(jnp.exp(math.log(32768.0) - 4.6051702 * jax.random.uniform(streams_of[14], (MODEL_WIDTH, QUERY_HEADS * HEAD_SIZE), jnp.float32) ** steps_of(streams_of[14], (MODEL_WIDTH, QUERY_HEADS * HEAD_SIZE), ((0, 8), (1, 4)), -0.2, 0.2)), 327.68, 32768.0)
    key_value_first_moment = noise(streams_of[15], (MODEL_WIDTH, 2 * KEY_VALUE_HEADS * HEAD_SIZE), (0.6 * TOKEN_TOTAL ** 0.5), 320.0, ((0, 8), (1, 4)), jnp.float32)
    key_value_second_moment = jnp.clip(jnp.exp(math.log(32768.0) - 4.6051702 * jax.random.uniform(streams_of[16], (MODEL_WIDTH, 2 * KEY_VALUE_HEADS * HEAD_SIZE), jnp.float32) ** steps_of(streams_of[16], (MODEL_WIDTH, 2 * KEY_VALUE_HEADS * HEAD_SIZE), ((0, 8), (1, 4)), -0.2, 0.2)), 327.68, 32768.0)
    output_mean = noise(streams_of[17], (QUERY_HEADS * HEAD_SIZE, MODEL_WIDTH), (0.12 * TOKEN_TOTAL ** 0.5), 64.0, ((0, 4), (1, 8)), jnp.float32)
    output_var = jnp.clip(jnp.exp(math.log(1310.72) - 4.6051702 * jax.random.uniform(streams_of[18], (QUERY_HEADS * HEAD_SIZE, MODEL_WIDTH), jnp.float32) ** steps_of(streams_of[18], (QUERY_HEADS * HEAD_SIZE, MODEL_WIDTH), ((0, 4), (1, 8)), -0.2, 0.2)), 13.1072, 1310.72)
    moe_gain_mean = noise(streams_of[19], (MODEL_WIDTH,), (0.45 * TOKEN_TOTAL ** 0.5), 256.0, ((0, 32),), jnp.float32)
    moe_gain_var = jnp.clip(jnp.exp(math.log(16384.0) - 4.6051702 * jax.random.uniform(streams_of[20], (MODEL_WIDTH,), jnp.float32) ** steps_of(streams_of[20], (MODEL_WIDTH,), ((0, 32),), -0.2, 0.2)), 163.84, 16384.0)
    router_mean = noise(streams_of[21], (MODEL_WIDTH, EXPERTS), (1.2 * TOKEN_TOTAL ** 0.5), 640.0, ((0, 32),), jnp.float32)
    router_var = jnp.clip(jnp.exp(math.log(131072.0) - 4.6051702 * jax.random.uniform(streams_of[22], (MODEL_WIDTH, EXPERTS), jnp.float32) ** steps_of(streams_of[22], (MODEL_WIDTH, EXPERTS), ((0, 32),), -0.2, 0.2)), 1310.72, 131072.0)
    gateup_mean = noise(streams_of[23], (EXPERTS, 2, FF, MODEL_WIDTH), (0.03 * TOKEN_TOTAL ** 0.5), 16.0, ((0, 8), (2, 4)), jnp.float32)
    gateup_var = jnp.clip(jnp.exp(math.log(81.92) - 4.6051702 * jax.random.uniform(streams_of[24], (EXPERTS, 2, FF, MODEL_WIDTH), jnp.float32) ** steps_of(streams_of[24], (EXPERTS, 2, FF, MODEL_WIDTH), ((0, 8), (2, 4)), -0.2, 0.2)), 0.8192, 81.92)
    down_mean = noise(streams_of[25], (EXPERTS, FF, MODEL_WIDTH), (0.002 * TOKEN_TOTAL ** 0.5), 1.0, ((0, 8), (1, 4)), jnp.float32)
    down_var = jnp.clip(jnp.exp(math.log(0.458752) - 4.6051702 * jax.random.uniform(streams_of[26], (EXPERTS, FF, MODEL_WIDTH), jnp.float32) ** steps_of(streams_of[26], (EXPERTS, FF, MODEL_WIDTH), ((0, 8), (1, 4)), -0.2, 0.2)), 0.00458752, 0.458752)
    return {"residual_in": residual_in, "cotangent": cotangent, "expert_ids": expert_ids, "attn_gain": attn_gain, "query_w": query_w, "key_value_weight": key_value_weight, "output_w": output_w, "moe_gain": moe_gain, "router_w": router_w, "gateup_w": gateup_w, "down_w": down_w, "attn_gain_mean": attn_gain_mean, "attn_gain_var": attn_gain_var, "query_mean": query_mean, "query_var": query_var, "key_value_first_moment": key_value_first_moment, "key_value_second_moment": key_value_second_moment, "output_mean": output_mean, "output_var": output_var, "moe_gain_mean": moe_gain_mean, "moe_gain_var": moe_gain_var, "router_mean": router_mean, "router_var": router_var, "gateup_mean": gateup_mean, "gateup_var": gateup_var, "down_mean": down_mean, "down_var": down_var}


NORM_EPS = 1e-06

@jax.custom_vjp
def to_bfloat(v):
    return lax.optimization_barrier(v.astype(jnp.bfloat16)).astype(jnp.float32)

@jax.custom_vjp
def to_bfloat_pullback(v):
    return v

def low_keep(v):
    return (to_bfloat(v), None)

def low_pass(kept, grad):
    return (grad,)

def back_keep(v):
    return (v, None)

def back_low(kept, grad):
    return (to_bfloat(grad),)
to_bfloat.defvjp(low_keep, low_pass)
to_bfloat_pullback.defvjp(back_keep, back_low)

def matrix_product(formula, left_arg, right_arg):
    return jnp.einsum(formula, left_arg, right_arg, precision=lax.Precision.HIGHEST)

def apply_rotary_embedding(value, direction):
    length = value.shape[1]
    width = value.shape[-1]
    half_width = width // 2
    position = jnp.arange(length, dtype=jnp.float32)
    frequency = jnp.exp(-math.log(10000.0) * jnp.arange(half_width, dtype=jnp.float32) * 2.0 / width)
    angles = position[:, None] * frequency[None, :]
    cosine = jnp.cos(angles)[:, None, :]
    sine_val = direction * jnp.sin(angles)[:, None, :]
    front = value[..., :half_width]
    rear = value[..., half_width:]
    return jnp.concatenate([front * cosine - rear * sine_val, rear * cosine + front * sine_val], -1)

def causal_mask(length):
    index = jnp.arange(length, dtype=jnp.int32)
    return index[:, None] >= index[None, :]

def block_forward(params, resid, ids):
    attn_gain, query_w, key_value_weight, output_w, moe_gain, router_w, gateup_w, down_w = params
    row_count = resid.shape[0]
    sequence_count = row_count // SEQUENCE_TOKENS
    queries_per_group = QUERY_HEADS // KEY_VALUE_HEADS
    inv_one = lax.rsqrt(lax.optimization_barrier(jnp.mean(resid * resid, -1, keepdims=True)) + NORM_EPS)
    first_normed_input = to_bfloat(resid * inv_one * attn_gain)
    query_linear = to_bfloat_pullback(matrix_product('gk,ki->gi', first_normed_input, to_bfloat(query_w)))
    key_value_linear = to_bfloat_pullback(matrix_product('gk,ki->gi', first_normed_input, to_bfloat(key_value_weight))).reshape(sequence_count, SEQUENCE_TOKENS, KEY_VALUE_HEADS, 2, HEAD_SIZE)
    query_rows = to_bfloat(apply_rotary_embedding(query_linear.reshape(sequence_count, SEQUENCE_TOKENS, QUERY_HEADS, HEAD_SIZE), 1.0)).reshape(sequence_count, SEQUENCE_TOKENS, KEY_VALUE_HEADS, queries_per_group, HEAD_SIZE)
    keys_rot = to_bfloat(apply_rotary_embedding(key_value_linear[:, :, :, 0], 1.0))
    values = to_bfloat(key_value_linear[:, :, :, 1])
    causal = causal_mask(SEQUENCE_TOKENS)
    raw_scores = to_bfloat_pullback(matrix_product('nqkgd,nskd->nkgqs', query_rows, keys_rot) / math.sqrt(HEAD_SIZE))
    exp_scores = jnp.where(causal, jnp.exp(jnp.where(causal, raw_scores, 0.0)), 0.0)
    attn_probs = to_bfloat(exp_scores / lax.optimization_barrier(jnp.sum(exp_scores, -1, keepdims=True)))
    context = matrix_product('nkgqs,nskd->nqkgd', attn_probs, values)
    context = to_bfloat(to_bfloat_pullback(context)).reshape(row_count, QUERY_HEADS * HEAD_SIZE)
    attn_out = to_bfloat_pullback(matrix_product('tc,cd->td', context, to_bfloat(output_w)))
    hidden = resid + attn_out
    inv_two = lax.rsqrt(lax.optimization_barrier(jnp.mean(hidden * hidden, -1, keepdims=True)) + NORM_EPS)
    normed_two = to_bfloat(hidden * inv_two * moe_gain)
    logits = to_bfloat_pullback(matrix_product('td,de->te', normed_two, to_bfloat(router_w)))
    exp_logits = jnp.exp(logits)
    router_probs = exp_logits / lax.optimization_barrier(jnp.sum(exp_logits, -1, keepdims=True))
    picked = jnp.take_along_axis(router_probs, ids, axis=1)
    onehot = (ids[:, :, None] == jnp.arange(EXPERTS, dtype=jnp.int32)[None, None, :]).astype(jnp.int32)
    chosen = lax.optimization_barrier(jnp.sum(onehot, 1)).reshape(N_MP, TOK_DEV, EXPERTS)
    before = (jnp.cumsum(chosen, 1) - chosen).reshape(row_count, EXPERTS)
    slot_index = lax.optimization_barrier(jnp.sum(onehot * before[:, None, :], -1))
    device_index = (jnp.arange(row_count, dtype=jnp.int32) // TOK_DEV)[:, None]
    flat_slot = (ids * (N_MP * CAP) + device_index * CAP + slot_index).reshape(-1).astype(jnp.int32)
    token_index = jnp.repeat(jnp.arange(row_count, dtype=jnp.int32), TOPK)
    source = jnp.full((EXPERTS * N_MP * CAP,), row_count, jnp.int32).at[flat_slot].set(token_index)
    padded = jnp.concatenate([normed_two, jnp.zeros((1, MODEL_WIDTH), normed_two.dtype)], 0)
    dispatch = to_bfloat_pullback(padded[source]).reshape(EXPERTS, N_MP * CAP, MODEL_WIDTH)
    gate_up = to_bfloat_pullback(matrix_product('erd,ecfd->ercf', dispatch, to_bfloat(gateup_w)))
    activation = to_bfloat(jax.nn.silu(gate_up[:, :, 0]) * gate_up[:, :, 1])
    expert_out = to_bfloat(to_bfloat_pullback(matrix_product('erf,efd->erd', activation, to_bfloat(down_w)))).reshape(EXPERTS * N_MP * CAP, MODEL_WIDTH)
    picked_rows = expert_out[flat_slot].reshape(row_count, TOPK, MODEL_WIDTH)
    mixture = lax.optimization_barrier(jnp.sum(picked[:, :, None] * picked_rows, 1))
    return hidden + mixture

def adamw(weight, gradient, moment_one, moment_two, rate_val, decay_val):
    first_new = 0.9 * moment_one + 0.1 * gradient
    second_new = 0.95 * moment_two + 0.05 * gradient * gradient
    first_hat = first_new / (1.0 - 0.9 ** STEP)
    second_hat = second_new / (1.0 - 0.95 ** STEP)
    weight_new = weight - rate_val * (first_hat / (jnp.sqrt(second_hat) + 1e-08) + decay_val * weight)
    return (gradient, weight_new, first_new, second_new)

def reference(residual_in, cotangent, expert_ids, attn_gain, query_w, key_value_weight, output_w, moe_gain, router_w, gateup_w, down_w, attn_gain_mean, attn_gain_var, query_mean, query_var, key_value_first_moment, key_value_second_moment, output_mean, output_var, moe_gain_mean, moe_gain_var, router_mean, router_var, gateup_mean, gateup_var, down_mean, down_var):
    params = (attn_gain, query_w, key_value_weight, output_w, moe_gain, router_w, gateup_w, down_w)
    row_count = TOK_DEV * N_MP

    def group_step(totals, inputs):
        resid_block, cot_block, ids_block = inputs
        block_out, pullback = jax.vjp(lambda params_in, resid_in: block_forward(params_in, resid_in, ids_block), params, resid_block)
        group_grads, resid_grad = pullback(cot_block)
        totals = jax.tree.map(lambda left_val, right_val: left_val + right_val, totals, group_grads)
        return (totals, (block_out, resid_grad))
    zero_grads = jax.tree.map(jnp.zeros_like, params)
    blocks = (residual_in.reshape(N_DP, row_count, MODEL_WIDTH), cotangent.reshape(N_DP, row_count, MODEL_WIDTH), expert_ids.reshape(N_DP, row_count, TOPK))
    totals, (outputs, resid_grads) = lax.scan(group_step, zero_grads, blocks)
    block_out = outputs.reshape(TOKEN_TOTAL, MODEL_WIDTH)
    input_grad = resid_grads.reshape(TOKEN_TOTAL, MODEL_WIDTH)
    matrix_rate = 0.2 / math.sqrt(MODEL_WIDTH)
    gain_one = adamw(attn_gain, totals[0], attn_gain_mean, attn_gain_var, 0.1, 0.0)
    query_all = adamw(query_w, totals[1], query_mean, query_var, matrix_rate, 0.1)
    keyval_all = adamw(key_value_weight, totals[2], key_value_first_moment, key_value_second_moment, matrix_rate, 0.1)
    output_all = adamw(output_w, totals[3], output_mean, output_var, 0.1, 0.1)
    gain_two = adamw(moe_gain, totals[4], moe_gain_mean, moe_gain_var, 0.1, 0.0)
    router_all = adamw(router_w, totals[5], router_mean, router_var, matrix_rate, 0.1)
    gateup_all = adamw(gateup_w, totals[6], gateup_mean, gateup_var, matrix_rate, 0.1)
    down_all = adamw(down_w, totals[7], down_mean, down_var, 0.07, 0.1)
    return (block_out, input_grad, gain_one[0], gain_one[1], gain_one[2], gain_one[3], query_all[0], query_all[1], query_all[2], query_all[3], keyval_all[0], keyval_all[1], keyval_all[2], keyval_all[3], output_all[0], output_all[1], output_all[2], output_all[3], gain_two[0], gain_two[1], gain_two[2], gain_two[3], router_all[0], router_all[1], router_all[2], router_all[3], gateup_all[0], gateup_all[1], gateup_all[2], gateup_all[3], down_all[0], down_all[1], down_all[2], down_all[3])
```

```python
import functools
import math

import jax
import jax.numpy as jnp
from jax import lax
from jax.experimental import pallas as pl
from jax.experimental.pallas import tpu as pltpu
from jax.sharding import PartitionSpec as P

MODEL_WIDTH = 1024
QUERY_HEADS = 16
KEY_VALUE_HEADS = 8
HEAD_SIZE = 64
EXPERTS = 32
TOPK = 8
SEQUENCE_TOKENS = 512
STEP = 3
CAP = 80

NORM_EPS = 1e-06
MESH = pl.DeviceIdType.MESH
BF16 = jnp.bfloat16
F32 = jnp.float32


def flip(index, mask):
    return index + mask * (1 - 2 * lax.rem(lax.div(index, mask), 2))


def flip_all(index, masks):
    bit = 1
    while bit <= masks:
        if masks & bit:
            index = flip(index, bit)
        bit *= 2
    return index


def bits_of(size):
    return [1 << i for i in range(size.bit_length() - 1)]


def orders_of(n_dp):
    bits = bits_of(n_dp)
    return bits[1:] + bits[:1], bits[1:][::-1] + bits[:1]


def place_of(order, j):
    place = -1
    for at, mask in enumerate(order):
        if j & mask:
            place = at
    return place


def greet(partners):
    barrier = pltpu.get_barrier_semaphore()
    for partner in partners:
        pl.semaphore_signal(barrier, inc=1, device_id=partner, device_id_type=MESH)
    pl.semaphore_wait(barrier, len(partners))


class Copies:
    def __init__(self, send_sems, recv_sems):
        self.send_sems, self.recv_sems = send_sems, recv_sems
        self.used = 0
        self.sent = []

    def slot(self):
        self.used += 1
        return self.used - 1

    def make(self, source, target, device, slot):
        return pltpu.make_async_remote_copy(
            src_ref=source,
            dst_ref=target,
            send_sem=self.send_sems.at[slot],
            recv_sem=self.recv_sems.at[slot],
            device_id=device,
            device_id_type=MESH,
        )

    def start(self, source, target, device, slot):
        copy = self.make(source, target, device, slot)
        copy.start()
        self.sent.append(copy)

    def wait(self, target, device, slot):
        self.make(target, target, device, slot).wait_recv()

    def finish(self):
        for copy in self.sent:
            copy.wait_send()


class TreeGather:
    def __init__(self, copies, order, n_dp, me, source, target):
        self.copies, self.order, self.n_dp, self.me = copies, order, n_dp, me
        self.source, self.target = source, target
        self.slots = {j: copies.slot() for j in range(1, n_dp)}

    def level(self, j):
        return bin(j).count("1")

    def send(self, j):
        dp, mp = self.me
        for mask in self.order[place_of(self.order, j) + 1 :]:
            self.copies.start(
                self.source(j), self.target(j, mask), (flip(dp, mask), mp), self.slots[j ^ mask]
            )

    def receive(self, j):
        self.copies.wait(self.source(j), self.me, self.slots[j])

    def steps(self):
        return sorted(range(1, self.n_dp), key=lambda j: (self.level(j), place_of(self.order, j)))


def run_gathers(trees):
    n_dp = trees[0].n_dp
    for level in range(1, n_dp.bit_length()):
        for tree in trees:
            for j in tree.steps():
                if tree.level(j) == level:
                    tree.receive(j)
                    tree.send(j)


class TreeReduce:
    def __init__(self, copies, order, n_dp, me, block, room, add):
        self.copies, self.order, self.n_dp, self.me = copies, order, n_dp, me
        self.block, self.room, self.add = block, room, add
        self.keys = [
            (j, q) for j in range(n_dp) for q in range(len(order) - 1, place_of(order, j), -1)
        ]
        self.slots = {key: copies.slot() for key in self.keys}

    def number(self, key):
        return self.keys.index(key)

    def send(self, j):
        dp, mp = self.me
        p = place_of(self.order, j)
        last = len(self.order) - 1
        source = self.block(j) if p == last else self.room(self.number((j, last)))
        mask = self.order[p]
        key = (j ^ mask, p)
        self.copies.start(source, self.room(self.number(key)), (flip(dp, mask), mp), self.slots[key])

    def collect(self, j):
        last = len(self.order) - 1
        for q in range(last, place_of(self.order, j), -1):
            here = self.room(self.number((j, q)))
            self.copies.wait(here, self.me, self.slots[(j, q)])
            if q == last:
                self.add(here, self.block(j))
            else:
                self.add(self.room(self.number((j, last))), here)

    def total(self):
        return self.room(self.number((0, len(self.order) - 1)))


def run_reduces(trees):
    n_dp = trees[0].n_dp
    last = len(trees[0].order) - 1
    for tree in trees:
        for j in range(1, n_dp):
            if place_of(tree.order, j) == last:
                tree.send(j)
    for p in range(last - 1, -1, -1):
        for tree in trees:
            for j in range(1, n_dp):
                if place_of(tree.order, j) == p:
                    tree.collect(j)
                    tree.send(j)
    for tree in trees:
        tree.collect(0)


def add_rows(step=16):
    def add(here, other):
        def body(i, carry):
            rows = pl.ds(pl.multiple_of(i * step, step), step)
            total = here[..., rows, :].astype(F32) + other[..., rows, :].astype(F32)
            here[..., rows, :] = total.astype(here.dtype)
            return carry

        lax.fori_loop(0, here.shape[-2] // step, body, 0)

    return add


def hbm():
    return pl.BlockSpec(memory_space=pl.ANY)


def vmem():
    return pl.BlockSpec(memory_space=pltpu.VMEM)


def params(identity, limit=None):
    return pltpu.CompilerParams(
        collective_id=identity, has_side_effects=True, vmem_limit_bytes=limit
    )


def gather_weights(n_dp, n_mp, small, shards):
    half = n_mp // 2
    kinds, rows, cols = shards.shape
    order_a, order_b = orders_of(n_dp)
    n_copies = 2 * (n_mp - 1) + 6 * (n_dp - 1)

    def kernel(small_ref, shard_ref, small_all, full, send_sems, recv_sems, local_sems):
        dp, mp = lax.axis_index("dp"), lax.axis_index("mp")
        me = (dp, mp)
        copies = Copies(send_sems, recv_sems)
        own_small = small_all.at[dp, mp]
        column = pl.multiple_of(mp * cols, cols)
        own_rows = pl.ds(pl.multiple_of(dp * rows, rows), rows)
        own_full = full.at[:, own_rows, pl.ds(column, cols)]
        keep = [
            pltpu.make_async_copy(small_ref, own_small, local_sems.at[0]),
            pltpu.make_async_copy(shard_ref, own_full, local_sems.at[1]),
        ]
        for copy in keep:
            copy.start()
        greet(
            [(flip_all(dp, mask), mp) for mask in bits_of(n_dp)]
            + [(dp, flip_all(mp, k)) for k in range(1, n_mp)]
        )
        near = lax.div(mp, half)
        line = {}
        for k in range(1, n_mp):
            device = (dp, flip_all(mp, k))
            line[k] = (copies.slot(), copies.slot())
            copies.start(small_ref, own_small, device, line[k][0])
            copies.start(shard_ref, own_full, device, line[k][1])

        def small_tree(chunk):
            first = pl.multiple_of(chunk * half, half)

            def ref(j, mask=0):
                return small_all.at[flip_all(dp, j), pl.ds(first, half)]

            return TreeGather(copies, order_a, n_dp, me, ref, ref)

        def tree(chunk, part, order):
            first = pl.multiple_of(chunk * half * cols, half * cols)
            part_rows = rows // 2

            def ref(j, mask=0):
                start = flip_all(dp, j) * rows + part * part_rows
                return full.at[
                    :,
                    pl.ds(pl.multiple_of(start, part_rows), part_rows),
                    pl.ds(first, half * cols),
                ]

            return TreeGather(copies, order, n_dp, me, ref, ref)

        groups = []
        for chunk in (near, 1 - near):
            groups.append(
                [small_tree(chunk), tree(chunk, 0, order_a), tree(chunk, 1, order_b)]
            )
        for copy in keep:
            copy.wait()
        for number, group in enumerate(groups):
            for k in range(1, n_mp) if number else range(1, half):
                if number == 0 or k >= half:
                    other = flip_all(mp, k)
                    copies.wait(small_all.at[dp, other], me, line[k][0])
                    theirs = pl.ds(pl.multiple_of(other * cols, cols), cols)
                    copies.wait(full.at[:, own_rows, theirs], me, line[k][1])
            for one in group:
                one.send(0)
        for level in range(1, n_dp.bit_length()):
            for group in groups:
                for one in group:
                    for j in one.steps():
                        if one.level(j) == level:
                            one.receive(j)
                            one.send(j)
        copies.finish()

    return pl.pallas_call(
        kernel,
        out_shape=(
            jax.ShapeDtypeStruct((n_dp, n_mp) + small.shape, small.dtype),
            jax.ShapeDtypeStruct((kinds, n_dp * rows, n_mp * cols), shards.dtype),
        ),
        in_specs=[hbm(), hbm()],
        out_specs=(hbm(), hbm()),
        scratch_shapes=[
            pltpu.SemaphoreType.DMA((n_copies,)),
            pltpu.SemaphoreType.DMA((n_copies,)),
            pltpu.SemaphoreType.DMA((2,)),
        ],
        compiler_params=params(0),
        name="gather_weights",
    )(small, shards)


def gather_tokens(n_dp, n_mp, identity, rows, table):
    half = n_mp // 2
    tokens = rows.shape[0]
    order_a, order_b = orders_of(n_dp)
    n_copies = 2 + 6 * (n_dp - 1)

    def kernel(rows_ref, table_ref, rows_all, table_all, send_sems, recv_sems, local_sems):
        dp, mp = lax.axis_index("dp"), lax.axis_index("mp")
        me = (dp, mp)
        partner = (dp, flip_all(mp, half))
        copies = Copies(send_sems, recv_sems)
        keep = [
            pltpu.make_async_copy(rows_ref, rows_all.at[0, 0], local_sems.at[0]),
            pltpu.make_async_copy(table_ref, table_all.at[0, 0], local_sems.at[1]),
        ]
        for copy in keep:
            copy.start()
        greet([(flip_all(dp, mask), mp) for mask in bits_of(n_dp)] + [partner])
        across = (copies.slot(), copies.slot())
        copies.start(rows_ref, rows_all.at[1, 0], partner, across[0])
        copies.start(table_ref, table_all.at[1, 0], partner, across[1])

        def row_tree(group, part, order):
            cut = pl.ds(part * (tokens // 2), tokens // 2)
            return TreeGather(
                copies,
                order,
                n_dp,
                me,
                lambda j: rows_all.at[group, j, cut],
                lambda j, mask: rows_all.at[group, j ^ mask, cut],
            )

        def table_tree(group, order):
            return TreeGather(
                copies,
                order,
                n_dp,
                me,
                lambda j: table_all.at[group, j],
                lambda j, mask: table_all.at[group, j ^ mask],
            )

        groups = [
            [row_tree(group, 0, order_a), row_tree(group, 1, order_b), table_tree(group, order_a)]
            for group in range(2)
        ]
        for copy in keep:
            copy.wait()
        for one in groups[0]:
            one.send(0)
        run_gathers(groups[0])
        copies.wait(rows_all.at[1, 0], me, across[0])
        copies.wait(table_all.at[1, 0], me, across[1])
        for one in groups[1]:
            one.send(0)
        run_gathers(groups[1])
        copies.finish()

    return pl.pallas_call(
        kernel,
        out_shape=(
            jax.ShapeDtypeStruct((2, n_dp) + rows.shape, rows.dtype),
            jax.ShapeDtypeStruct((2, n_dp) + table.shape, table.dtype),
        ),
        in_specs=[hbm(), hbm()],
        out_specs=(hbm(), hbm()),
        scratch_shapes=[
            pltpu.SemaphoreType.DMA((n_copies,)),
            pltpu.SemaphoreType.DMA((n_copies,)),
            pltpu.SemaphoreType.DMA((2,)),
        ],
        compiler_params=params(identity),
        name="gather_tokens",
    )(rows, table)


def reduce_tokens(n_dp, n_mp, identity, terms, table=None):
    half = n_mp // 2
    tokens, width = terms.shape[2:]
    order_a, order_b = orders_of(n_dp)
    n_copies = 4 * (n_dp - 1) + 1 + (2 * n_dp - 1 if table is not None else 0)

    def kernel(*refs):
        if table is not None:
            terms_ref, table_ref, out_ref, parts_ref, *refs = refs
        else:
            terms_ref, out_ref, *refs = refs
        rooms, across, send_sems, recv_sems, local_sems = refs
        dp, mp = lax.axis_index("dp"), lax.axis_index("mp")
        me = (dp, mp)
        other = flip_all(mp, half)
        partner = (dp, other)
        copies = Copies(send_sems, recv_sems)
        if table is not None:
            greet(
                [
                    (flip_all(dp, j), other if group else mp)
                    for group in range(2)
                    for j in range(n_dp)
                    if group + j
                ]
            )
        else:
            greet([(flip_all(dp, mask), mp) for mask in bits_of(n_dp)] + [partner])
        kind = lax.div(mp, half)
        parts = {}
        if table is not None:
            keep = pltpu.make_async_copy(
                table_ref.at[0, 0], parts_ref.at[dp, kind], local_sems.at[0]
            )
            keep.start()
            for group in range(2):
                for j in range(n_dp):
                    if group + j:
                        device = (flip_all(dp, j), other if group else mp)
                        parts[group, j] = copies.slot()
                        copies.start(
                            table_ref.at[group, j], parts_ref.at[dp, kind], device, parts[group, j]
                        )

        def tree(group, part, order):
            cut = pl.ds(part * (tokens // 2), tokens // 2)
            return TreeReduce(
                copies,
                order,
                n_dp,
                me,
                lambda j: terms_ref.at[group, j, cut],
                lambda number: rooms.at[group, part, number],
                add_rows(),
            )

        groups = [[tree(group, 0, order_a), tree(group, 1, order_b)] for group in (1, 0)]
        run_reduces(groups[0] + groups[1])
        last = copies.slot()
        mine = [rooms.at[1, part, groups[0][part].number((0, len(order_a) - 1))] for part in (0, 1)]
        own = [rooms.at[0, part, groups[1][part].number((0, len(order_a) - 1))] for part in (0, 1)]
        for part in (0, 1):
            out_ref[pl.ds(part * (tokens // 2), tokens // 2), :] = mine[part][...].astype(F32)
        for part in (0, 1):
            across[0, pl.ds(part * (tokens // 2), tokens // 2), :] = mine[part][...]
        copies.start(across.at[0], across.at[1], partner, last)
        copies.wait(across.at[1], me, last)
        for part in (0, 1):
            cut = pl.ds(part * (tokens // 2), tokens // 2)
            out_ref[cut, :] = own[part][...].astype(F32) + across[1, cut, :].astype(F32)
        if table is not None:
            keep.wait()
            for group in range(2):
                for j in range(n_dp):
                    if group + j:
                        theirs = 1 - kind if group else kind
                        copies.wait(
                            parts_ref.at[flip_all(dp, j), theirs], me, parts[group, j]
                        )
        copies.finish()

    out_shape = [jax.ShapeDtypeStruct((tokens, width), F32)]
    if table is not None:
        out_shape.append(jax.ShapeDtypeStruct((n_dp, 2) + table.shape[2:], table.dtype))
    return pl.pallas_call(
        kernel,
        out_shape=tuple(out_shape),
        in_specs=[vmem()] * (2 if table is not None else 1),
        out_specs=tuple([vmem()] * len(out_shape)),
        scratch_shapes=[
            pltpu.VMEM((2, 2, n_dp - 1, tokens // 2, width), terms.dtype),
            pltpu.VMEM((2, tokens, width), terms.dtype),
            pltpu.SemaphoreType.DMA((n_copies,)),
            pltpu.SemaphoreType.DMA((n_copies,)),
            pltpu.SemaphoreType.DMA((1,)),
        ],
        compiler_params=params(identity, 48 << 20),
        name="reduce_tokens",
    )(*([terms, table] if table is not None else [terms]))


def reduce_weights(n_dp, n_mp, identity, grads, small):
    kinds, rows_all, cols_all = grads.shape
    rows, cols = rows_all // n_dp, cols_all // n_mp
    order_a, order_b = orders_of(n_dp)
    n_copies = 3 * (n_dp - 1) + 2 * (n_mp - 1)
    part_rows = rows // 2

    def kernel(grads_ref, small_ref, out_ref, small_out, rooms, small_rooms, line, small_line, send_sems, recv_sems):
        dp, mp = lax.axis_index("dp"), lax.axis_index("mp")
        me = (dp, mp)
        copies = Copies(send_sems, recv_sems)
        greet(
            [(flip_all(dp, mask), mp) for mask in bits_of(n_dp)]
            + [(dp, flip_all(mp, k)) for k in range(1, n_mp)]
        )

        def tree(part, order):
            def block(j):
                start = flip_all(dp, j) * rows + part * part_rows
                return grads_ref.at[:, pl.ds(pl.multiple_of(start, part_rows), part_rows), :]

            return TreeReduce(
                copies, order, n_dp, me, block, lambda number: rooms.at[part, number], add_rows()
            )

        def add_whole(here, other):
            here[...] = here[...] + other[...]

        trees = [
            TreeReduce(
                copies,
                order_a,
                n_dp,
                me,
                lambda j: small_ref.at[flip_all(dp, j)],
                lambda number: small_rooms.at[number],
                add_whole,
            ),
            tree(0, order_a),
            tree(1, order_b),
        ]
        run_reduces(trees)
        slots = {k: (copies.slot(), copies.slot()) for k in range(1, n_mp)}
        totals = [one.total() for one in trees]

        def columns(who):
            return pl.ds(pl.multiple_of(who * cols, cols), cols)

        for part in (0, 1):
            for k in range(n_mp):
                line[0, k, :, pl.ds(part * part_rows, part_rows), :] = totals[1 + part][
                    :, :, columns(flip_all(mp, k))
                ]
        for k in range(1, n_mp):
            device = (dp, flip_all(mp, k))
            copies.start(totals[0].at[device[1]], small_line.at[k], device, slots[k][0])
            copies.start(line.at[0, k], line.at[1, k], device, slots[k][1])
        small_out[...] = totals[0][mp]
        out_ref[...] = line[0, 0].astype(F32)
        for k in range(1, n_mp):
            copies.wait(small_line.at[k], me, slots[k][0])
            small_out[...] += small_line[k]
            copies.wait(line.at[1, k], me, slots[k][1])
            out_ref[...] += line[1, k].astype(F32)
        copies.finish()

    return pl.pallas_call(
        kernel,
        out_shape=(
            jax.ShapeDtypeStruct((kinds, rows, cols), F32),
            jax.ShapeDtypeStruct(small.shape[2:], F32),
        ),
        in_specs=[vmem(), vmem()],
        out_specs=(vmem(), vmem()),
        scratch_shapes=[
            pltpu.VMEM((2, n_dp - 1, kinds, part_rows, cols_all), grads.dtype),
            pltpu.VMEM((n_dp - 1,) + small.shape[1:], small.dtype),
            pltpu.VMEM((2, n_mp, kinds, rows, cols), grads.dtype),
            pltpu.VMEM((n_mp,) + small.shape[2:], small.dtype),
            pltpu.SemaphoreType.DMA((n_copies,)),
            pltpu.SemaphoreType.DMA((n_copies,)),
        ],
        compiler_params=params(identity, 48 << 20),
        name="reduce_weights",
    )(grads, small)


def rotary_tables(positions):
    half_width = HEAD_SIZE // 2
    frequency = jnp.exp(
        -math.log(10000.0) * jnp.arange(half_width, dtype=F32) * 2.0 / HEAD_SIZE
    )
    angles = positions.astype(F32)[:, None] * frequency[None, :]
    return jnp.cos(angles)[:, None, :], jnp.sin(angles)[:, None, :]


def rotate(value, cosine, sine):
    half_width = value.shape[-1] // 2
    front = value[..., :half_width]
    rear = value[..., half_width:]
    return jnp.concatenate([front * cosine - rear * sine, rear * cosine + front * sine], -1)


def adamw(weight, gradient, moment_one, moment_two, rate_val, decay_val):
    first_new = 0.9 * moment_one + 0.1 * gradient
    second_new = 0.95 * moment_two + 0.05 * gradient * gradient
    first_hat = first_new / (1.0 - 0.9**STEP)
    second_hat = second_new / (1.0 - 0.95**STEP)
    weight_new = weight - rate_val * (
        first_hat / (jnp.sqrt(second_hat) + 1e-08) + decay_val * weight
    )
    return (gradient, weight_new, first_new, second_new)


def local(
    n_dp,
    n_mp,
    residual_in,
    cotangent,
    expert_ids,
    attn_gain,
    query_w,
    key_value_weight,
    output_w,
    moe_gain,
    router_w,
    gateup_w,
    down_w,
    attn_gain_mean,
    attn_gain_var,
    query_mean,
    query_var,
    key_value_first_moment,
    key_value_second_moment,
    output_mean,
    output_var,
    moe_gain_mean,
    moe_gain_var,
    router_mean,
    router_var,
    gateup_mean,
    gateup_var,
    down_mean,
    down_var,
):
    dp, mp = lax.axis_index("dp"), lax.axis_index("mp")
    half = n_mp // 2
    kind = mp // half
    tokens = residual_in.shape[0]
    owned = gateup_w.shape[0]
    shared = owned // 2
    hidden_units = down_w.shape[1]
    flips = [[(i, i ^ k) for i in range(n_mp)] for k in range(n_mp)]

    packed = jnp.concatenate([gateup_w, down_w[:, None]], 1).astype(BF16)
    mine = jnp.where(kind == 0, packed[:shared], packed[shared:])
    theirs = jnp.where(kind == 0, packed[shared:], packed[:shared])
    expert_parts = [mine] + [
        lax.ppermute(mine if k < half else theirs, "mp", flips[k]) for k in range(1, n_mp)
    ]

    expert_range = jnp.arange(EXPERTS, dtype=jnp.int32)
    onehot = (expert_ids[:, :, None] == expert_range[None, None, :]).astype(jnp.int32)
    onehot_float = onehot.astype(F32)
    chosen = jnp.sum(onehot, 1)
    before = jnp.cumsum(chosen, 0) - chosen
    place = jnp.where(chosen > 0, before, -1).T

    own_gain, own_router = attn_gain.shape[0], router_w.shape[0]
    lanes = 128
    small = jnp.zeros((8 + own_router, lanes), F32)
    small = small.at[0, :own_gain].set(attn_gain).at[1, :own_gain].set(moe_gain)
    small = small.at[8:, :EXPERTS].set(router_w)
    shards = jnp.stack([query_w, key_value_weight, output_w.T]).astype(BF16)
    small_all, projections = gather_weights(n_dp, n_mp, small, shards)
    gain_one = small_all[:, :, 0, :own_gain].reshape(-1)
    gain_two = small_all[:, :, 1, :own_gain].reshape(-1)
    router_low = small_all[:, :, 8:, :EXPERTS].reshape(MODEL_WIDTH, EXPERTS).astype(BF16)
    query_full, keyval_full, output_turned = projections[0], projections[1], projections[2]
    cot_low = cotangent.astype(BF16)
    cot_all, place_all = gather_tokens(n_dp, n_mp, 1, cot_low, place)

    inv_one = lax.rsqrt(jnp.mean(residual_in * residual_in, -1, keepdims=True) + NORM_EPS)
    normed_one = (residual_in * inv_one * gain_one).astype(BF16)
    normed_other = lax.ppermute(normed_one, "mp", flips[1])
    per_sequence = SEQUENCE_TOKENS // tokens
    own_positions = (mp % per_sequence) * tokens + jnp.arange(tokens, dtype=jnp.int32)
    other_positions = (flip(mp, 1) % per_sequence) * tokens + jnp.arange(tokens, dtype=jnp.int32)
    key_positions = jnp.concatenate([other_positions, own_positions])
    queries_per_group = QUERY_HEADS // KEY_VALUE_HEADS
    score_scale = 1.0 / math.sqrt(HEAD_SIZE)
    causal = own_positions[:, None] >= key_positions[None, :]
    query_cos, query_sin = rotary_tables(own_positions)
    key_cos, key_sin = rotary_tables(key_positions)
    query_linear = jnp.dot(normed_one, query_full, preferred_element_type=F32)
    keyval_linear = jnp.dot(
        jnp.concatenate([normed_other, normed_one]), keyval_full, preferred_element_type=F32
    ).reshape(2 * tokens, KEY_VALUE_HEADS, 2, HEAD_SIZE)
    query_rows = (
        rotate(query_linear.reshape(tokens, QUERY_HEADS, HEAD_SIZE), query_cos, query_sin)
        .astype(BF16)
        .reshape(tokens, KEY_VALUE_HEADS, queries_per_group, HEAD_SIZE)
    )
    keys_rot = rotate(keyval_linear[:, :, 0], key_cos, key_sin).astype(BF16)
    values = keyval_linear[:, :, 1].astype(BF16)
    raw_scores = (
        jnp.einsum("qkgd,skd->kgqs", query_rows, keys_rot, preferred_element_type=F32) * score_scale
    )
    exp_scores = jnp.where(causal, jnp.exp(jnp.where(causal, raw_scores, 0.0)), 0.0)
    row_total = jnp.sum(exp_scores, -1, keepdims=True)
    log_total = jnp.log(row_total)
    attn_probs = (exp_scores / row_total).astype(BF16)
    context = (
        jnp.einsum("kgqs,skd->qkgd", attn_probs, values, preferred_element_type=F32)
        .astype(BF16)
        .reshape(tokens, -1)
    )
    attn_out = jnp.einsum("tc,dc->td", context, output_turned, preferred_element_type=F32)
    hidden = residual_in + attn_out
    inv_two = lax.rsqrt(jnp.mean(hidden * hidden, -1, keepdims=True) + NORM_EPS)
    normed_two = (hidden * inv_two * gain_two).astype(BF16)
    logits = jnp.dot(normed_two, router_low, preferred_element_type=F32)
    exp_logits = jnp.exp(logits)
    router_probs = exp_logits / jnp.sum(exp_logits, -1, keepdims=True)

    token_all, probs_all = gather_tokens(n_dp, n_mp, 2, normed_two, router_probs.T)
    blocks = 2 * n_dp
    first_expert = dp * owned + kind * shared
    token_all = token_all.reshape(blocks, tokens, MODEL_WIDTH)
    cot_all = cot_all.reshape(blocks, tokens, MODEL_WIDTH)
    own_place = lax.dynamic_slice_in_dim(
        place_all.reshape(blocks, EXPERTS, tokens), first_expert, shared, 1
    )
    own_probs = lax.dynamic_slice_in_dim(
        probs_all.reshape(blocks, EXPERTS, tokens), first_expert, shared, 1
    )
    hit = own_place[:, :, None, :] == jnp.arange(CAP, dtype=jnp.int32)[None, None, :, None]
    pick = hit.astype(BF16)
    weight = jnp.sum(jnp.where(hit, own_probs[:, :, None, :], 0.0), -1)
    weight = weight.transpose(1, 0, 2).reshape(shared, blocks * CAP, 1)

    def slots_of(rows):
        found = jnp.einsum("best,btd->ebsd", pick, rows, preferred_element_type=F32)
        return found.astype(BF16).reshape(shared, blocks * CAP, MODEL_WIDTH)

    def sums_of(slots):
        per_block = slots.reshape(shared, blocks, CAP, MODEL_WIDTH)
        found = jnp.einsum("best,ebsd->btd", pick, per_block, preferred_element_type=F32)
        return found.astype(BF16).reshape(2, n_dp, tokens, MODEL_WIDTH)

    received = slots_of(token_all)
    cot_slots = slots_of(cot_all)
    experts = jnp.stack(expert_parts, 2)
    gateup_full = experts[:, :2].reshape(shared, 2, n_mp * hidden_units, MODEL_WIDTH)
    down_full = experts[:, 2].reshape(shared, n_mp * hidden_units, MODEL_WIDTH)
    gate_up = jnp.einsum("erd,ecfd->ercf", received, gateup_full, preferred_element_type=F32)
    gate_val, up_val = gate_up[:, :, 0], gate_up[:, :, 1]
    sigmoid_val = jax.nn.sigmoid(gate_val)
    silu_val = gate_val * sigmoid_val
    activation = (silu_val * up_val).astype(BF16)
    expert_out = jnp.einsum("erf,efd->erd", activation, down_full, preferred_element_type=F32)
    gate_dot_slots = jnp.sum(cot_slots.astype(F32) * expert_out, -1)
    gate_dot_slots = gate_dot_slots.reshape(shared, blocks, CAP).transpose(1, 0, 2)
    gate_dots = jnp.sum(jnp.where(hit, gate_dot_slots[..., None], 0.0), 2)
    gate_dots = jnp.pad(gate_dots, ((0, 0), (0, 8 - shared), (0, 0)))
    gate_dots = gate_dots.reshape(2, n_dp, 8, tokens)
    mixture_terms = sums_of((weight * expert_out).astype(BF16))
    mixture, gate_parts = reduce_tokens(n_dp, n_mp, 3, mixture_terms, gate_dots)
    block_out = hidden + mixture
    grad_probs = gate_parts[:, :, :shared].reshape(EXPERTS, tokens).T
    grad_rows = (weight * cot_slots.astype(F32)).astype(BF16)
    grad_act = jnp.einsum("erd,efd->erf", grad_rows, down_full, preferred_element_type=F32)
    grad_down = jnp.einsum("erf,erd->efd", activation, grad_rows, preferred_element_type=F32)
    grad_gate = grad_act * up_val * sigmoid_val * (1.0 + gate_val * (1.0 - sigmoid_val))
    grad_up = grad_act * silu_val
    grad_pair = jnp.stack([grad_gate, grad_up], 2).astype(BF16)
    grad_slots = jnp.einsum(
        "ercf,ecfd->erd", grad_pair, gateup_full, preferred_element_type=F32
    ).astype(BF16)
    grad_gateup = jnp.einsum("ercf,erd->ecfd", grad_pair, received, preferred_element_type=F32)
    (grad_normed_two,) = reduce_tokens(n_dp, n_mp, 4, sums_of(grad_slots))

    grad_experts = jnp.concatenate(
        [
            grad_gateup.reshape(shared, 2, n_mp, hidden_units, MODEL_WIDTH),
            grad_down.reshape(shared, 1, n_mp, hidden_units, MODEL_WIDTH),
        ],
        1,
    ).astype(BF16)
    arrived = [grad_experts[:, :, 0]] + [
        lax.ppermute(grad_experts[:, :, k], "mp", flips[k]) for k in range(1, n_mp)
    ]
    near_sum = sum(part.astype(F32) for part in arrived[:half])
    far_sum = sum(part.astype(F32) for part in arrived[half:])
    expert_grad = jnp.where(
        kind == 0,
        jnp.concatenate([near_sum, far_sum], 0),
        jnp.concatenate([far_sum, near_sum], 0),
    )
    gateup_grad, down_grad = expert_grad[:, :2], expert_grad[:, 2]

    grad_probs = jnp.where(chosen > 0, grad_probs, 0.0)
    grad_logits = (
        router_probs * (grad_probs - jnp.sum(router_probs * grad_probs, -1, keepdims=True))
    ).astype(BF16)
    grad_normed_two = grad_normed_two + jnp.einsum(
        "te,de->td", grad_logits, router_low, preferred_element_type=F32
    )
    grad_router = jnp.einsum("td,te->de", normed_two, grad_logits, preferred_element_type=F32)
    scaled_two = gain_two * grad_normed_two
    grad_hidden = (
        cotangent
        + inv_two * scaled_two
        - hidden * inv_two**3 * jnp.mean(scaled_two * hidden, -1, keepdims=True)
    )
    grad_gain_two = jnp.sum(grad_normed_two * hidden * inv_two, 0)

    grad_attn = grad_hidden.astype(BF16)
    grad_ctx = jnp.dot(grad_attn, output_turned, preferred_element_type=F32).astype(BF16)
    grad_output = jnp.einsum("td,tc->dc", grad_attn, context, preferred_element_type=F32)
    grad_ctx = grad_ctx.reshape(tokens, KEY_VALUE_HEADS, queries_per_group, HEAD_SIZE)
    probs_float = jnp.where(causal, jnp.exp(jnp.where(causal, raw_scores - log_total, 0.0)), 0.0)
    grad_p = jnp.einsum("qkgd,skd->kgqs", grad_ctx, values, preferred_element_type=F32)
    delta_sum = jnp.sum(probs_float * grad_p, -1, keepdims=True)
    grad_s = (probs_float * (grad_p - delta_sum)).astype(BF16)
    grad_q = (
        jnp.einsum("kgqs,skd->qkgd", grad_s, keys_rot, preferred_element_type=F32) * score_scale
    )
    grad_k = (
        jnp.einsum("kgqs,qkgd->skd", grad_s, query_rows, preferred_element_type=F32) * score_scale
    )
    grad_v = jnp.einsum("kgqs,qkgd->skd", attn_probs, grad_ctx, preferred_element_type=F32)
    grad_q_lin = (
        rotate(grad_q.reshape(tokens, QUERY_HEADS, HEAD_SIZE), query_cos, -query_sin)
        .astype(BF16)
        .reshape(tokens, -1)
    )
    grad_kv = jnp.stack([rotate(grad_k, key_cos, -key_sin), grad_v], 2).reshape(2 * tokens, -1)
    grad_kv_other = lax.ppermute(grad_kv[:tokens].astype(BF16), "mp", flips[1])
    grad_kv_lin = (grad_kv[tokens:] + grad_kv_other.astype(F32)).astype(BF16)
    grad_normed_one = jnp.einsum(
        "tc,dc->td", grad_q_lin, query_full, preferred_element_type=F32
    ) + jnp.einsum("tc,dc->td", grad_kv_lin, keyval_full, preferred_element_type=F32)
    grad_query = jnp.einsum("td,tc->dc", normed_one, grad_q_lin, preferred_element_type=F32)
    grad_keyval = jnp.einsum("td,tc->dc", normed_one, grad_kv_lin, preferred_element_type=F32)
    scaled_one = gain_one * grad_normed_one
    input_grad = (
        grad_hidden
        + inv_one * scaled_one
        - residual_in * inv_one**3 * jnp.mean(scaled_one * residual_in, -1, keepdims=True)
    )
    grad_gain_one = jnp.sum(grad_normed_one * residual_in * inv_one, 0)

    grads = jnp.stack([grad_query, grad_keyval, grad_output]).astype(BF16)
    small_grads = jnp.zeros((n_dp, n_mp, 8 + own_router, lanes), F32)
    small_grads = small_grads.at[:, :, 0, :own_gain].set(grad_gain_one.reshape(n_dp, n_mp, -1))
    small_grads = small_grads.at[:, :, 1, :own_gain].set(grad_gain_two.reshape(n_dp, n_mp, -1))
    small_grads = small_grads.at[:, :, 8:, :EXPERTS].set(
        grad_router.reshape(n_dp, n_mp, own_router, EXPERTS)
    )
    grads, small_grads = reduce_weights(n_dp, n_mp, 5, grads, small_grads)
    query_grad, keyval_grad, output_grad = grads[0], grads[1], grads[2].T
    gain_one_grad, gain_two_grad = small_grads[0, :own_gain], small_grads[1, :own_gain]
    router_grad = small_grads[8:, :EXPERTS]
    matrix_rate = 0.2 / math.sqrt(MODEL_WIDTH)
    gain_one_all = adamw(attn_gain, gain_one_grad, attn_gain_mean, attn_gain_var, 0.1, 0.0)
    query_all = adamw(query_w, query_grad, query_mean, query_var, matrix_rate, 0.1)
    keyval_all = adamw(
        key_value_weight,
        keyval_grad,
        key_value_first_moment,
        key_value_second_moment,
        matrix_rate,
        0.1,
    )
    output_all = adamw(output_w, output_grad, output_mean, output_var, 0.1, 0.1)
    gain_two_all = adamw(moe_gain, gain_two_grad, moe_gain_mean, moe_gain_var, 0.1, 0.0)
    router_all = adamw(router_w, router_grad, router_mean, router_var, matrix_rate, 0.1)
    gateup_all = adamw(gateup_w, gateup_grad, gateup_mean, gateup_var, matrix_rate, 0.1)
    down_all = adamw(down_w, down_grad, down_mean, down_var, 0.07, 0.1)
    return (
        block_out,
        input_grad,
        gain_one_all[0],
        gain_one_all[1],
        gain_one_all[2],
        gain_one_all[3],
        query_all[0],
        query_all[1],
        query_all[2],
        query_all[3],
        keyval_all[0],
        keyval_all[1],
        keyval_all[2],
        keyval_all[3],
        output_all[0],
        output_all[1],
        output_all[2],
        output_all[3],
        gain_two_all[0],
        gain_two_all[1],
        gain_two_all[2],
        gain_two_all[3],
        router_all[0],
        router_all[1],
        router_all[2],
        router_all[3],
        gateup_all[0],
        gateup_all[1],
        gateup_all[2],
        gateup_all[3],
        down_all[0],
        down_all[1],
        down_all[2],
        down_all[3],
    )


def solution(mesh):
    in_specs = (
        P(("dp", "mp"), None),
        P(("dp", "mp"), None),
        P(("dp", "mp"), None),
        P(("dp", "mp")),
        P("dp", "mp"),
        P("dp", "mp"),
        P("mp", "dp"),
        P(("dp", "mp")),
        P(("dp", "mp"), None),
        P("dp", None, "mp", None),
        P("dp", "mp", None),
        P(("dp", "mp")),
        P(("dp", "mp")),
        P("dp", "mp"),
        P("dp", "mp"),
        P("dp", "mp"),
        P("dp", "mp"),
        P("mp", "dp"),
        P("mp", "dp"),
        P(("dp", "mp")),
        P(("dp", "mp")),
        P(("dp", "mp"), None),
        P(("dp", "mp"), None),
        P("dp", None, "mp", None),
        P("dp", None, "mp", None),
        P("dp", "mp", None),
        P("dp", "mp", None),
    )
    out_specs = (
        P(("dp", "mp"), None),
        P(("dp", "mp"), None),
        P(("dp", "mp")),
        P(("dp", "mp")),
        P(("dp", "mp")),
        P(("dp", "mp")),
        P("dp", "mp"),
        P("dp", "mp"),
        P("dp", "mp"),
        P("dp", "mp"),
        P("dp", "mp"),
        P("dp", "mp"),
        P("dp", "mp"),
        P("dp", "mp"),
        P("mp", "dp"),
        P("mp", "dp"),
        P("mp", "dp"),
        P("mp", "dp"),
        P(("dp", "mp")),
        P(("dp", "mp")),
        P(("dp", "mp")),
        P(("dp", "mp")),
        P(("dp", "mp"), None),
        P(("dp", "mp"), None),
        P(("dp", "mp"), None),
        P(("dp", "mp"), None),
        P("dp", None, "mp", None),
        P("dp", None, "mp", None),
        P("dp", None, "mp", None),
        P("dp", None, "mp", None),
        P("dp", "mp", None),
        P("dp", "mp", None),
        P("dp", "mp", None),
        P("dp", "mp", None),
    )
    step = functools.partial(local, mesh.shape["dp"], mesh.shape["mp"])
    return jax.shard_map(step, mesh=mesh, in_specs=in_specs, out_specs=out_specs, check_vma=False)
```

```python
import functools
import math

import jax
import jax.numpy as jnp
from jax import lax
from jax.experimental import pallas as pl
from jax.experimental.pallas import tpu as pltpu
from jax.sharding import PartitionSpec as P

MODEL_WIDTH = 1024
QUERY_HEADS = 16
KEY_VALUE_HEADS = 8
HEAD_SIZE = 64
EXPERTS = 32
TOPK = 8
SEQUENCE_TOKENS = 512
STEP = 3
CAP = 80

NORM_EPS = 1e-06
MESH = pl.DeviceIdType.MESH
BF16 = jnp.bfloat16
F32 = jnp.float32


def flip(index, mask):
    return index + mask * (1 - 2 * lax.rem(lax.div(index, mask), 2))


def flip_all(index, masks):
    bit = 1
    while bit <= masks:
        if masks & bit:
            index = flip(index, bit)
        bit *= 2
    return index


def bits_of(size):
    return [1 << i for i in range(size.bit_length() - 1)]


def orders_of(n_dp):
    bits = bits_of(n_dp)
    return bits[1:] + bits[:1], bits[1:][::-1] + bits[:1]


def place_of(order, j):
    place = -1
    for at, mask in enumerate(order):
        if j & mask:
            place = at
    return place


def greet(partners):
    barrier = pltpu.get_barrier_semaphore()
    for partner in partners:
        pl.semaphore_signal(barrier, inc=1, device_id=partner, device_id_type=MESH)
    pl.semaphore_wait(barrier, len(partners))


class Copies:
    def __init__(self, send_sems, recv_sems):
        self.send_sems, self.recv_sems = send_sems, recv_sems
        self.used = 0
        self.sent = []

    def slot(self):
        self.used += 1
        return self.used - 1

    def make(self, source, target, device, slot):
        return pltpu.make_async_remote_copy(
            src_ref=source,
            dst_ref=target,
            send_sem=self.send_sems.at[slot],
            recv_sem=self.recv_sems.at[slot],
            device_id=device,
            device_id_type=MESH,
        )

    def start(self, source, target, device, slot):
        copy = self.make(source, target, device, slot)
        copy.start()
        self.sent.append(copy)

    def wait(self, target, device, slot):
        self.make(target, target, device, slot).wait_recv()

    def finish(self):
        for copy in self.sent:
            copy.wait_send()


class TreeGather:
    def __init__(self, copies, order, n_dp, me, source, target):
        self.copies, self.order, self.n_dp, self.me = copies, order, n_dp, me
        self.source, self.target = source, target
        self.slots = {j: copies.slot() for j in range(1, n_dp)}

    def level(self, j):
        return bin(j).count("1")

    def send(self, j):
        dp, mp = self.me
        for mask in self.order[place_of(self.order, j) + 1 :]:
            self.copies.start(
                self.source(j), self.target(j, mask), (flip(dp, mask), mp), self.slots[j ^ mask]
            )

    def receive(self, j):
        self.copies.wait(self.source(j), self.me, self.slots[j])

    def steps(self):
        return sorted(range(1, self.n_dp), key=lambda j: (self.level(j), place_of(self.order, j)))


def run_gathers(trees):
    n_dp = trees[0].n_dp
    for level in range(1, n_dp.bit_length()):
        for tree in trees:
            for j in tree.steps():
                if tree.level(j) == level:
                    tree.receive(j)
                    tree.send(j)


class TreeReduce:
    def __init__(self, copies, order, n_dp, me, block, room, add):
        self.copies, self.order, self.n_dp, self.me = copies, order, n_dp, me
        self.block, self.room, self.add = block, room, add
        self.keys = [
            (j, q) for j in range(n_dp) for q in range(len(order) - 1, place_of(order, j), -1)
        ]
        self.slots = {key: copies.slot() for key in self.keys}

    def number(self, key):
        return self.keys.index(key)

    def send(self, j):
        dp, mp = self.me
        p = place_of(self.order, j)
        last = len(self.order) - 1
        source = self.block(j) if p == last else self.room(self.number((j, last)))
        mask = self.order[p]
        key = (j ^ mask, p)
        self.copies.start(source, self.room(self.number(key)), (flip(dp, mask), mp), self.slots[key])

    def collect(self, j):
        last = len(self.order) - 1
        for q in range(last, place_of(self.order, j), -1):
            here = self.room(self.number((j, q)))
            self.copies.wait(here, self.me, self.slots[(j, q)])
            if q == last:
                self.add(here, self.block(j))
            else:
                self.add(self.room(self.number((j, last))), here)

    def total(self):
        return self.room(self.number((0, len(self.order) - 1)))


def run_reduces(trees):
    n_dp = trees[0].n_dp
    last = len(trees[0].order) - 1
    for tree in trees:
        for j in range(1, n_dp):
            if place_of(tree.order, j) == last:
                tree.send(j)
    for p in range(last - 1, -1, -1):
        for tree in trees:
            for j in range(1, n_dp):
                if place_of(tree.order, j) == p:
                    tree.collect(j)
                    tree.send(j)
    for tree in trees:
        tree.collect(0)


def add_rows(step=16):
    def add(here, other):
        def body(i, carry):
            rows = pl.ds(pl.multiple_of(i * step, step), step)
            total = here[..., rows, :].astype(F32) + other[..., rows, :].astype(F32)
            here[..., rows, :] = total.astype(here.dtype)
            return carry

        lax.fori_loop(0, here.shape[-2] // step, body, 0)

    return add


def hbm():
    return pl.BlockSpec(memory_space=pl.ANY)


def vmem():
    return pl.BlockSpec(memory_space=pltpu.VMEM)


def params(identity, limit=None):
    return pltpu.CompilerParams(
        collective_id=identity, has_side_effects=True, vmem_limit_bytes=limit
    )


def gather_weights(n_dp, n_mp, small, shards):
    half = n_mp // 2
    kinds, rows, cols = shards.shape
    order_a, order_b = orders_of(n_dp)
    n_copies = 2 * (n_mp - 1) + 6 * (n_dp - 1)

    def kernel(small_ref, shard_ref, small_all, full, send_sems, recv_sems, local_sems):
        dp, mp = lax.axis_index("dp"), lax.axis_index("mp")
        me = (dp, mp)
        copies = Copies(send_sems, recv_sems)
        own_small = small_all.at[dp, mp]
        column = pl.multiple_of(mp * cols, cols)
        own_rows = pl.ds(pl.multiple_of(dp * rows, rows), rows)
        own_full = full.at[:, own_rows, pl.ds(column, cols)]
        keep = [
            pltpu.make_async_copy(small_ref, own_small, local_sems.at[0]),
            pltpu.make_async_copy(shard_ref, own_full, local_sems.at[1]),
        ]
        for copy in keep:
            copy.start()
        greet(
            [(flip_all(dp, mask), mp) for mask in bits_of(n_dp)]
            + [(dp, flip_all(mp, k)) for k in range(1, n_mp)]
        )
        near = lax.div(mp, half)
        line = {}
        for k in range(1, n_mp):
            device = (dp, flip_all(mp, k))
            line[k] = (copies.slot(), copies.slot())
            copies.start(small_ref, own_small, device, line[k][0])
            copies.start(shard_ref, own_full, device, line[k][1])

        def small_tree(chunk):
            first = pl.multiple_of(chunk * half, half)

            def ref(j, mask=0):
                return small_all.at[flip_all(dp, j), pl.ds(first, half)]

            return TreeGather(copies, order_a, n_dp, me, ref, ref)

        def tree(chunk, part, order):
            first = pl.multiple_of(chunk * half * cols, half * cols)
            part_rows = rows // 2

            def ref(j, mask=0):
                start = flip_all(dp, j) * rows + part * part_rows
                return full.at[
                    :,
                    pl.ds(pl.multiple_of(start, part_rows), part_rows),
                    pl.ds(first, half * cols),
                ]

            return TreeGather(copies, order, n_dp, me, ref, ref)

        groups = []
        for chunk in (near, 1 - near):
            groups.append(
                [small_tree(chunk), tree(chunk, 0, order_a), tree(chunk, 1, order_b)]
            )
        for copy in keep:
            copy.wait()
        for number, group in enumerate(groups):
            for k in range(1, n_mp) if number else range(1, half):
                if number == 0 or k >= half:
                    other = flip_all(mp, k)
                    copies.wait(small_all.at[dp, other], me, line[k][0])
                    theirs = pl.ds(pl.multiple_of(other * cols, cols), cols)
                    copies.wait(full.at[:, own_rows, theirs], me, line[k][1])
            for one in group:
                one.send(0)
        for level in range(1, n_dp.bit_length()):
            for group in groups:
                for one in group:
                    for j in one.steps():
                        if one.level(j) == level:
                            one.receive(j)
                            one.send(j)
        copies.finish()

    return pl.pallas_call(
        kernel,
        out_shape=(
            jax.ShapeDtypeStruct((n_dp, n_mp) + small.shape, small.dtype),
            jax.ShapeDtypeStruct((kinds, n_dp * rows, n_mp * cols), shards.dtype),
        ),
        in_specs=[hbm(), hbm()],
        out_specs=(hbm(), hbm()),
        scratch_shapes=[
            pltpu.SemaphoreType.DMA((n_copies,)),
            pltpu.SemaphoreType.DMA((n_copies,)),
            pltpu.SemaphoreType.DMA((2,)),
        ],
        compiler_params=params(0),
        name="gather_weights",
    )(small, shards)


def gather_tokens(n_dp, groups, identity, rows):
    n_copies = groups - 1 + 2 * groups * (n_dp - 1)

    def kernel(rows_ref, rows_all, send_sems, recv_sems, local_sem):
        dp, mp = lax.axis_index("dp"), lax.axis_index("mp")
        me = (dp, mp)
        partner = (dp, flip(mp, 1))
        copies = Copies(send_sems, recv_sems)
        keep = pltpu.make_async_copy(rows_ref, rows_all.at[0, 0], local_sem.at[0])
        keep.start()
        greet([(flip_all(dp, mask), mp) for mask in bits_of(n_dp)] + [partner] * (groups - 1))
        if groups > 1:
            across = copies.slot()
            copies.start(rows_ref, rows_all.at[1, 0], partner, across)
        trees = [row_trees(copies, n_dp, me, rows_all, group) for group in range(groups)]
        keep.wait()
        for one in trees[0]:
            one.send(0)
        if groups > 1:
            copies.wait(rows_all.at[1, 0], me, across)
            for one in trees[1]:
                one.send(0)
        run_gathers(sum(trees, []))
        copies.finish()

    return pl.pallas_call(
        kernel,
        out_shape=jax.ShapeDtypeStruct((groups, n_dp) + rows.shape, rows.dtype),
        in_specs=[hbm()],
        out_specs=hbm(),
        scratch_shapes=[
            pltpu.SemaphoreType.DMA((n_copies,)),
            pltpu.SemaphoreType.DMA((n_copies,)),
            pltpu.SemaphoreType.DMA((1,)),
        ],
        compiler_params=params(identity),
        name="gather_tokens",
    )(rows)


def row_trees(copies, n_dp, me, rows_all, group):
    tokens = rows_all.shape[2]

    def tree(part, order):
        cut = pl.ds(part * (tokens // 2), tokens // 2)
        return TreeGather(
            copies,
            order,
            n_dp,
            me,
            lambda j: rows_all.at[group, j, cut],
            lambda j, mask: rows_all.at[group, j ^ mask, cut],
        )

    return [tree(part, order) for part, order in enumerate(orders_of(n_dp))]


class TokenReduce:
    def __init__(self, copies, n_dp, me, terms, rooms, across):
        dp, mp = me
        self.copies, self.me, self.across = copies, me, across
        self.partner = (dp, flip(mp, 1))
        self.tokens = terms.shape[2]
        self.n_dp = n_dp
        self.last = n_dp.bit_length() - 2
        self.groups = terms.shape[0]
        self.slot = copies.slot()

        def tree(group, part, order):
            cut = pl.ds(part * (self.tokens // 2), self.tokens // 2)
            return TreeReduce(
                copies,
                order,
                n_dp,
                me,
                lambda j: terms.at[group, j, cut],
                lambda number: rooms.at[group, part, number],
                add_rows(),
            )

        self.trees = [
            [tree(group, part, order) for part, order in enumerate(orders_of(n_dp))]
            for group in range(self.groups)
        ]

    def first(self, group, j):
        for tree in self.trees[group]:
            tree.send(j)

    def level(self, group, p):
        if group == self.groups:
            return
        for j in range(1, self.n_dp):
            for tree in self.trees[group]:
                if place_of(tree.order, j) == p:
                    tree.collect(j)
                    tree.send(j)

    def pass_on(self):
        if self.groups == 1:
            return
        for part, tree in enumerate(self.trees[1]):
            tree.collect(0)
            cut = pl.ds(part * (self.tokens // 2), self.tokens // 2)
            self.across[0, cut, :] = tree.total()[...]
        self.copies.start(self.across.at[0], self.across.at[1], self.partner, self.slot)

    def end(self, out_ref):
        for tree in self.trees[0]:
            tree.collect(0)
        if self.groups > 1:
            self.copies.wait(self.across.at[1], self.me, self.slot)
        for part, tree in enumerate(self.trees[0]):
            cut = pl.ds(part * (self.tokens // 2), self.tokens // 2)
            total = tree.total()[...].astype(F32)
            if self.groups > 1:
                total = total + self.across[1, cut, :].astype(F32)
            out_ref[cut, :] = total


def reduce_rooms(groups, n_dp, tokens, width, dtype):
    return [
        pltpu.VMEM((groups, 2, n_dp - 1, tokens // 2, width), dtype),
        pltpu.VMEM((2, tokens, width), dtype),
    ]


def reduce_tokens(identity, terms):
    groups, n_dp, tokens, width = terms.shape
    n_copies = 2 * groups * (n_dp - 1) + 1

    def kernel(terms_ref, out_ref, rooms, across, send_sems, recv_sems):
        dp, mp = lax.axis_index("dp"), lax.axis_index("mp")
        me = (dp, mp)
        copies = Copies(send_sems, recv_sems)
        greet(
            [(flip_all(dp, mask), mp) for mask in bits_of(n_dp)]
            + [(dp, flip(mp, 1))] * (groups - 1)
        )
        reduce = TokenReduce(copies, n_dp, me, terms_ref, rooms, across)
        for group in range(groups)[::-1]:
            for j in range(1, n_dp, 2):
                reduce.first(group, j)
        for p in range(reduce.last - 1, -1, -1):
            reduce.level(1, p)
        reduce.pass_on()
        for p in range(reduce.last - 1, -1, -1):
            reduce.level(0, p)
        reduce.end(out_ref)
        copies.finish()

    return pl.pallas_call(
        kernel,
        out_shape=jax.ShapeDtypeStruct((tokens, width), F32),
        in_specs=[vmem()],
        out_specs=vmem(),
        scratch_shapes=reduce_rooms(groups, n_dp, tokens, width, terms.dtype)
        + [
            pltpu.SemaphoreType.DMA((n_copies,)),
            pltpu.SemaphoreType.DMA((n_copies,)),
        ],
        compiler_params=params(identity, 48 << 20),
        name="reduce_tokens",
    )(terms)


def dot(a, b, contract):
    return lax.dot_general(a, b, ((contract[:1], contract[1:]), ((), ())), preferred_element_type=F32)


NN, NT, TN = (1, 0), (1, 1), (0, 0)


def run_expert(n_dp, n_mp, groups, identity, index, shared, parts, inputs):
    first, last = index == 0, index == shared - 1
    hidden, width = parts[0].shape[1:]
    units = n_mp * hidden
    blocks = groups * n_dp
    slots = blocks * CAP
    tokens = inputs["rows"].shape[0] if first else inputs["tokens"]
    per_tile = 4
    tile = per_tile * CAP
    low = lambda *shape: jax.ShapeDtypeStruct(shape, BF16)
    single = lambda *shape: jax.ShapeDtypeStruct(shape, F32)

    arrays, places = {}, {}

    def give(name, value, spec):
        arrays[name], places[name] = value, spec

    for k in range(n_mp):
        give(f"part{k}", parts[k], hbm())
    if first:
        give("rows", inputs["rows"], hbm())
        give("own_table", inputs["table"], hbm())
        give("cots", inputs["cots"], hbm())
    else:
        give("tables_in", inputs["tables"], vmem())
        give("gates_in", inputs["gates"], vmem())
        give("x_in", inputs["x"][index], vmem())
        give("c_in", inputs["c"][index], vmem())
    if last:
        for i in range(index):
            give(f"y{i}", inputs["y"][i], vmem())
            give(f"d{i}", inputs["d"][i], vmem())
    outs, out_places = {}, {}

    def get(name, shape, spec):
        outs[name], out_places[name] = shape, spec

    for k in range(n_mp):
        get(f"grad{k}", low(3, hidden, width), vmem())
    if first and not last:
        get("tables", single(blocks, 8, tokens), vmem())
        for i in range(1, shared):
            get(f"x{i}", low(slots, width), vmem())
            get(f"c{i}", low(slots, width), vmem())
    if not last:
        get("gates", single(blocks, 8, tokens), vmem())
        get("y", low(slots, width), vmem())
        get("d", low(slots, width), vmem())
    else:
        get("terms", low(groups, n_dp, tokens, width), hbm())
        get("gate_parts", single(n_dp, groups, 8, tokens), hbm())
        get("total", single(tokens, width), vmem())
    scratch = {
        "weights": pltpu.VMEM((3, units, width), BF16),
        "act": pltpu.VMEM((slots, units), BF16),
        "pair": pltpu.VMEM((slots, 2 * units), BF16),
        "grad_rows": pltpu.VMEM((slots, width), BF16),
        "part_sems": pltpu.SemaphoreType.DMA((3 * n_mp,)),
    }
    n_copies = 0
    if first:
        n_copies += blocks + 2 * groups * (n_dp - 1)
        scratch["tokens_all"] = pltpu.VMEM((groups, n_dp, tokens, width), BF16)
        scratch["x_own"] = pltpu.VMEM((slots, width), BF16)
        scratch["c_own"] = pltpu.VMEM((slots, width), BF16)
        scratch["cot"] = pltpu.VMEM((2, tokens, width), BF16)
        scratch["cot_sems"] = pltpu.SemaphoreType.DMA((2,))
        scratch["keep_sems"] = pltpu.SemaphoreType.DMA((2,))
        if last:
            scratch["tables"] = pltpu.VMEM((blocks, 8, tokens), F32)
    if last:
        n_copies += 2 * groups * (n_dp - 1) + blocks
        scratch["gates"] = pltpu.VMEM((blocks, 8, tokens), F32)
        scratch["y"] = pltpu.VMEM((slots, width), BF16)
        scratch["d"] = pltpu.VMEM((slots, width), BF16)
        scratch["grads_all"] = pltpu.VMEM((groups, n_dp, tokens, width), BF16)
        scratch["sums"] = pltpu.VMEM((2, tokens, width), BF16)
        scratch["sum_sems"] = pltpu.SemaphoreType.DMA((2,))
        scratch["gate_sem"] = pltpu.SemaphoreType.DMA((1,))
        scratch["rooms"], scratch["across"] = reduce_rooms(groups, n_dp, tokens, width, BF16)
    scratch["send_sems"] = pltpu.SemaphoreType.DMA((n_copies,))
    scratch["recv_sems"] = pltpu.SemaphoreType.DMA((n_copies,))
    names = list(arrays) + list(outs) + list(scratch)

    def kernel(*refs):
        r = dict(zip(names, refs, strict=True))
        dp, mp = lax.axis_index("dp"), lax.axis_index("mp")
        me = (dp, mp)
        other = flip(mp, 1)
        kind = lax.rem(mp, groups)
        copies = Copies(r["send_sems"], r["recv_sems"])
        peers = {
            (group, j): (flip_all(dp, j), other if group else mp)
            for group in range(groups)
            for j in range(n_dp)
            if group + j
        }
        weights, act, pair, grad_rows = r["weights"], r["act"], r["pair"], r["grad_rows"]
        loads = [
            pltpu.make_async_copy(
                r[f"part{k}"].at[c],
                weights.at[c, pl.ds(k * hidden, hidden)],
                r["part_sems"].at[3 * k + c],
            )
            for k in range(n_mp)
            for c in range(3)
        ]
        for copy in loads:
            copy.start()
        tables = r["tables"] if first else r["tables_in"]
        x_refs = {index: r["x_own"] if first else r["x_in"]}
        c_refs = {index: r["c_own"] if first else r["c_in"]}
        if first:
            x_refs |= {i: r[f"x{i}"] for i in range(1, shared)}
            c_refs |= {i: r[f"c{i}"] for i in range(1, shared)}

        def hits(block, experts):
            slot = lax.broadcasted_iota(jnp.int32, (CAP, tokens), 0).astype(F32)
            found = [slot == tables[block, pl.ds(i, 1), :] for i in experts]
            return found[0] if len(found) == 1 else jnp.concatenate(found, 0)

        def rows_of(block):
            return pl.ds(pl.multiple_of(block * CAP, 16), CAP)

        if first:
            rows_all, cots = r["tokens_all"], r["cots"]
            keep = [
                pltpu.make_async_copy(r["rows"], rows_all.at[0, 0], r["keep_sems"].at[0]),
                pltpu.make_async_copy(
                    r["own_table"].at[dp, kind], tables.at[0], r["keep_sems"].at[1]
                ),
            ]
            for copy in keep:
                copy.start()
            order = [(group, 0) for group in range(groups)]
            for level in range(1, n_dp.bit_length()):
                for group in range(groups):
                    order += [(group, j) for j in range(n_dp) if bin(j).count("1") == level]

            def cot_copy(number):
                group, j = order[number]
                return pltpu.make_async_copy(
                    cots.at[group, j], r["cot"].at[number % 2], r["cot_sems"].at[number % 2]
                )

            cot_copy(0).start()
            greet(list(peers.values()))
            across = copies.slot()
            if groups > 1:
                copies.start(r["rows"], rows_all.at[1, 0], peers[1, 0], across)
            sent = {}
            for key, device in peers.items():
                sent[key] = copies.slot()
                group, j = key
                copies.start(
                    r["own_table"].at[device[0], lax.rem(device[1], groups)],
                    tables.at[group * n_dp + j],
                    device,
                    sent[key],
                )
            trees = [row_trees(copies, n_dp, me, rows_all, group) for group in range(groups)]
            keep[0].wait()
            for tree in trees[0]:
                tree.send(0)
            keep[1].wait()

            def fill(number):
                group, j = order[number]
                block = group * n_dp + j
                if number:
                    copies.wait(tables.at[block], me, sent[group, j])
                if number + 1 < blocks:
                    cot_copy(number + 1).start()
                pick = hits(block, range(shared)).astype(BF16)
                found = dot(pick, rows_all[group, j], NN).astype(BF16)
                for i in range(shared):
                    x_refs[i][block * CAP : (block + 1) * CAP, :] = found[i * CAP : (i + 1) * CAP]
                cot_copy(number).wait()
                found = dot(pick, r["cot"][number % 2], NN).astype(BF16)
                for i in range(shared):
                    c_refs[i][block * CAP : (block + 1) * CAP, :] = found[i * CAP : (i + 1) * CAP]

            for number, (group, j) in enumerate(order):
                if j:
                    for tree in sorted(trees[group], key=lambda tree: place_of(tree.order, j)):
                        tree.receive(j)
                        tree.send(j)
                elif group:
                    copies.wait(rows_all.at[1, 0], me, across)
                    for tree in trees[1]:
                        tree.send(0)
                fill(number)
        else:
            greet(list(peers.values()))
        if last:
            gates = r["gates"]
            if index:
                gates[...] = r["gates_in"][...]
        else:
            gates = r["gates"]
        for copy in loads:
            copy.wait()
        x_all, c_all = x_refs[index], c_refs[index]
        y_all, d_all = r["y"], r["d"]

        def work(step, carry):
            rows = pl.ds(pl.multiple_of(step * tile, 16), tile)
            x = x_all[rows, :]
            gate = dot(x, weights[0], NT)
            up = dot(x, weights[1], NT)
            sigmoid = 1.0 / (1.0 + jnp.exp(-gate))
            silu = gate * sigmoid
            activation = (silu * up).astype(BF16)
            act[rows, :] = activation
            made = dot(activation, weights[2], NN)
            cot = c_all[rows, :].astype(F32)
            chosen, scores = [], []
            dots = jnp.sum(cot * made, -1, keepdims=True)
            for b in range(per_tile):
                block = step * per_tile + b
                hit = hits(block, (index,))
                chance = tables[block, pl.ds(4 + index, 1), :]
                chosen.append(jnp.sum(jnp.where(hit, chance, 0.0), -1, keepdims=True))
                here = dots[b * CAP : (b + 1) * CAP]
                gates[block, pl.ds(index, 1), :] = jnp.sum(
                    jnp.where(hit, here, 0.0), 0, keepdims=True
                )
            share = jnp.concatenate(chosen, 0)
            y_all[rows, :] = (share * made).astype(BF16)
            back = (share * cot).astype(BF16)
            grad_rows[rows, :] = back
            grad_act = dot(back, weights[2], NT)
            grad_gate = grad_act * up * sigmoid * (1.0 + gate * (1.0 - sigmoid))
            grad_gate = grad_gate.astype(BF16)
            grad_up = (grad_act * silu).astype(BF16)
            pair[rows, pl.ds(0, units)] = grad_gate
            pair[rows, pl.ds(units, units)] = grad_up
            d_all[rows, :] = (dot(grad_gate, weights[0], NN) + dot(grad_up, weights[1], NN)).astype(
                BF16
            )
            return carry

        lax.fori_loop(0, blocks // per_tile, work, 0)

        def weight_grad(k):
            x, back = x_all[...], grad_rows[...]
            for c, source in enumerate((pair, pair, act)):
                columns = pl.ds(k * hidden + (units if c == 1 else 0), hidden)
                rhs = back if c == 2 else x
                r[f"grad{k}"][c] = dot(source[:, columns], rhs, TN).astype(BF16)

        if not last:
            for k in range(n_mp):
                weight_grad(k)
        else:
            y_refs = [r[f"y{i}"] for i in range(index)] + [y_all]
            d_refs = [r[f"d{i}"] for i in range(index)] + [d_all]
            reduce = TokenReduce(copies, n_dp, me, r["grads_all"], r["rooms"], r["across"])
            back = range(groups)[::-1]
            order = [(g, j) for g in back for j in range(1, n_dp, 2)]
            order += [(g, j) for g in back for j in range(0, n_dp, 2)]

            def sum_copy(number):
                group, j = order[number]
                return pltpu.make_async_copy(
                    r["sums"].at[number % 2], r["terms"].at[group, j], r["sum_sems"].at[number % 2]
                )

            sent = {}
            own_gates = pltpu.make_async_copy(
                gates.at[0], r["gate_parts"].at[dp, kind], r["gate_sem"].at[0]
            )
            own_gates.start()
            for number, (group, j) in enumerate(order):
                block = group * n_dp + j
                if group + j:
                    sent[group, j] = copies.slot()
                    copies.start(
                        gates.at[block],
                        r["gate_parts"].at[dp, kind],
                        peers[group, j],
                        sent[group, j],
                    )
                pick = hits(block, range(shared)).astype(BF16)
                there = rows_of(block)
                found = jnp.concatenate([ref[there, :] for ref in d_refs], 0)
                r["grads_all"][group, j] = dot(pick, found, TN).astype(BF16)
                if j % 2:
                    reduce.first(group, j)
                found = jnp.concatenate([ref[there, :] for ref in y_refs], 0)
                if number > 1:
                    sum_copy(number - 2).wait()
                r["sums"][number % 2] = dot(pick, found, TN).astype(BF16)
                sum_copy(number).start()
            left = list(range(n_mp))

            def some(count):
                for _ in range(count):
                    if left:
                        weight_grad(left.pop(0))

            for p in range(reduce.last - 1, -1, -1):
                reduce.level(1, p)
                some(1)
            reduce.pass_on()
            for p in range(reduce.last - 1, -1, -1):
                reduce.level(0, p)
                some(1)
            some(n_mp)
            reduce.end(r["total"])
            for number in (blocks - 2, blocks - 1):
                sum_copy(number).wait()
            own_gates.wait()
            for (group, j), device in peers.items():
                theirs = 1 - kind if group else kind
                copies.wait(r["gate_parts"].at[device[0], theirs], me, sent[group, j])
        copies.finish()

    results = pl.pallas_call(
        kernel,
        out_shape=tuple(outs.values()),
        in_specs=list(places.values()),
        out_specs=tuple(out_places.values()),
        scratch_shapes=list(scratch.values()),
        compiler_params=params(identity, 60 << 20),
        name=f"expert{index}",
    )(*arrays.values())
    return dict(zip(outs, results, strict=True))


def reduce_weights(n_dp, n_mp, identity, grads, small):
    kinds, rows_all, cols_all = grads.shape
    rows, cols = rows_all // n_dp, cols_all // n_mp
    order_a, order_b = orders_of(n_dp)
    n_copies = 3 * (n_dp - 1) + 2 * (n_mp - 1)
    part_rows = rows // 2

    def kernel(grads_ref, small_ref, out_ref, small_out, rooms, small_rooms, line, small_line, send_sems, recv_sems):
        dp, mp = lax.axis_index("dp"), lax.axis_index("mp")
        me = (dp, mp)
        copies = Copies(send_sems, recv_sems)
        greet(
            [(flip_all(dp, mask), mp) for mask in bits_of(n_dp)]
            + [(dp, flip_all(mp, k)) for k in range(1, n_mp)]
        )

        def tree(part, order):
            def block(j):
                start = flip_all(dp, j) * rows + part * part_rows
                return grads_ref.at[:, pl.ds(pl.multiple_of(start, part_rows), part_rows), :]

            return TreeReduce(
                copies, order, n_dp, me, block, lambda number: rooms.at[part, number], add_rows()
            )

        def add_whole(here, other):
            here[...] = here[...] + other[...]

        trees = [
            TreeReduce(
                copies,
                order_a,
                n_dp,
                me,
                lambda j: small_ref.at[flip_all(dp, j)],
                lambda number: small_rooms.at[number],
                add_whole,
            ),
            tree(0, order_a),
            tree(1, order_b),
        ]
        run_reduces(trees)
        slots = {k: (copies.slot(), copies.slot()) for k in range(1, n_mp)}
        totals = [one.total() for one in trees]

        def columns(who):
            return pl.ds(pl.multiple_of(who * cols, cols), cols)

        for part in (0, 1):
            for k in range(n_mp):
                line[0, k, :, pl.ds(part * part_rows, part_rows), :] = totals[1 + part][
                    :, :, columns(flip_all(mp, k))
                ]
        for k in range(1, n_mp):
            device = (dp, flip_all(mp, k))
            copies.start(totals[0].at[device[1]], small_line.at[k], device, slots[k][0])
            copies.start(line.at[0, k], line.at[1, k], device, slots[k][1])
        small_out[...] = totals[0][mp]
        out_ref[...] = line[0, 0].astype(F32)
        for k in range(1, n_mp):
            copies.wait(small_line.at[k], me, slots[k][0])
            small_out[...] += small_line[k]
            copies.wait(line.at[1, k], me, slots[k][1])
            out_ref[...] += line[1, k].astype(F32)
        copies.finish()

    return pl.pallas_call(
        kernel,
        out_shape=(
            jax.ShapeDtypeStruct((kinds, rows, cols), F32),
            jax.ShapeDtypeStruct(small.shape[2:], F32),
        ),
        in_specs=[vmem(), vmem()],
        out_specs=(vmem(), vmem()),
        scratch_shapes=[
            pltpu.VMEM((2, n_dp - 1, kinds, part_rows, cols_all), grads.dtype),
            pltpu.VMEM((n_dp - 1,) + small.shape[1:], small.dtype),
            pltpu.VMEM((2, n_mp, kinds, rows, cols), grads.dtype),
            pltpu.VMEM((n_mp,) + small.shape[2:], small.dtype),
            pltpu.SemaphoreType.DMA((n_copies,)),
            pltpu.SemaphoreType.DMA((n_copies,)),
        ],
        compiler_params=params(identity, 48 << 20),
        name="reduce_weights",
    )(grads, small)


def rotary_tables(positions):
    half_width = HEAD_SIZE // 2
    frequency = jnp.exp(
        -math.log(10000.0) * jnp.arange(half_width, dtype=F32) * 2.0 / HEAD_SIZE
    )
    angles = positions.astype(F32)[:, None] * frequency[None, :]
    return jnp.cos(angles)[:, None, :], jnp.sin(angles)[:, None, :]


def rotate(value, cosine, sine):
    half_width = value.shape[-1] // 2
    front = value[..., :half_width]
    rear = value[..., half_width:]
    return jnp.concatenate([front * cosine - rear * sine, rear * cosine + front * sine], -1)


def adamw(weight, gradient, moment_one, moment_two, rate_val, decay_val):
    first_new = 0.9 * moment_one + 0.1 * gradient
    second_new = 0.95 * moment_two + 0.05 * gradient * gradient
    first_hat = first_new / (1.0 - 0.9**STEP)
    second_hat = second_new / (1.0 - 0.95**STEP)
    weight_new = weight - rate_val * (
        first_hat / (jnp.sqrt(second_hat) + 1e-08) + decay_val * weight
    )
    return (gradient, weight_new, first_new, second_new)


def local(
    n_dp,
    n_mp,
    residual_in,
    cotangent,
    expert_ids,
    attn_gain,
    query_w,
    key_value_weight,
    output_w,
    moe_gain,
    router_w,
    gateup_w,
    down_w,
    attn_gain_mean,
    attn_gain_var,
    query_mean,
    query_var,
    key_value_first_moment,
    key_value_second_moment,
    output_mean,
    output_var,
    moe_gain_mean,
    moe_gain_var,
    router_mean,
    router_var,
    gateup_mean,
    gateup_var,
    down_mean,
    down_var,
):
    dp, mp = lax.axis_index("dp"), lax.axis_index("mp")
    groups = 2 if 2 * n_dp <= 16 else 1
    kind = mp % groups
    tokens = residual_in.shape[0]
    owned = gateup_w.shape[0]
    shared = owned // groups
    hidden_units = down_w.shape[1]
    flips = [[(i, i ^ k) for i in range(n_mp)] for k in range(n_mp)]

    expert_range = jnp.arange(EXPERTS, dtype=jnp.int32)
    onehot = (expert_ids[:, :, None] == expert_range[None, None, :]).astype(jnp.int32)
    onehot_float = onehot.astype(F32)
    chosen = jnp.sum(onehot, 1)
    before = jnp.cumsum(chosen, 0) - chosen
    place = jnp.where(chosen > 0, before, -1)

    own_gain, own_router = attn_gain.shape[0], router_w.shape[0]
    lanes = 128
    small = jnp.zeros((8 + own_router, lanes), F32)
    small = small.at[0, :own_gain].set(attn_gain).at[1, :own_gain].set(moe_gain)
    small = small.at[8:, :EXPERTS].set(router_w)
    shards = jnp.stack([query_w, key_value_weight, output_w.T]).astype(BF16)
    small_all, projections = gather_weights(n_dp, n_mp, small, shards)
    gain_one = small_all[:, :, 0, :own_gain].reshape(-1)
    gain_two = small_all[:, :, 1, :own_gain].reshape(-1)
    router_low = small_all[:, :, 8:, :EXPERTS].reshape(MODEL_WIDTH, EXPERTS).astype(BF16)
    query_full, keyval_full, output_turned = projections[0], projections[1], projections[2]
    packed = jnp.concatenate([gateup_w, down_w[:, None]], 1)
    packed, projections = lax.optimization_barrier((packed, projections))
    packed = packed.astype(BF16)
    expert_parts = []
    for i in range(shared):
        mine = theirs = packed[groups * i]
        if groups > 1:
            mine = jnp.where(kind == 0, packed[2 * i], packed[2 * i + 1])
            theirs = jnp.where(kind == 0, packed[2 * i + 1], packed[2 * i])
        expert_parts.append(
            [mine]
            + [lax.ppermute(theirs if k % 2 else mine, "mp", flips[k]) for k in range(1, n_mp)]
        )
    cot_all = gather_tokens(n_dp, groups, 1, cotangent.astype(BF16))

    inv_one = lax.rsqrt(jnp.mean(residual_in * residual_in, -1, keepdims=True) + NORM_EPS)
    normed_one = (residual_in * inv_one * gain_one).astype(BF16)
    normed_other = lax.ppermute(normed_one, "mp", flips[1])
    per_sequence = SEQUENCE_TOKENS // tokens
    own_positions = (mp % per_sequence) * tokens + jnp.arange(tokens, dtype=jnp.int32)
    other_positions = (flip(mp, 1) % per_sequence) * tokens + jnp.arange(tokens, dtype=jnp.int32)
    key_positions = jnp.concatenate([other_positions, own_positions])
    queries_per_group = QUERY_HEADS // KEY_VALUE_HEADS
    score_scale = 1.0 / math.sqrt(HEAD_SIZE)
    causal = own_positions[:, None] >= key_positions[None, :]
    query_cos, query_sin = rotary_tables(own_positions)
    key_cos, key_sin = rotary_tables(key_positions)
    query_linear = jnp.dot(normed_one, query_full, preferred_element_type=F32)
    keyval_linear = jnp.dot(
        jnp.concatenate([normed_other, normed_one]), keyval_full, preferred_element_type=F32
    ).reshape(2 * tokens, KEY_VALUE_HEADS, 2, HEAD_SIZE)
    query_rows = (
        rotate(query_linear.reshape(tokens, QUERY_HEADS, HEAD_SIZE), query_cos, query_sin)
        .astype(BF16)
        .reshape(tokens, KEY_VALUE_HEADS, queries_per_group, HEAD_SIZE)
    )
    keys_rot = rotate(keyval_linear[:, :, 0], key_cos, key_sin).astype(BF16)
    values = keyval_linear[:, :, 1].astype(BF16)
    raw_scores = (
        jnp.einsum("qkgd,skd->kgqs", query_rows, keys_rot, preferred_element_type=F32) * score_scale
    )
    exp_scores = jnp.where(causal, jnp.exp(jnp.where(causal, raw_scores, 0.0)), 0.0)
    row_total = jnp.sum(exp_scores, -1, keepdims=True)
    log_total = jnp.log(row_total)
    attn_probs = (exp_scores / row_total).astype(BF16)
    context = (
        jnp.einsum("kgqs,skd->qkgd", attn_probs, values, preferred_element_type=F32)
        .astype(BF16)
        .reshape(tokens, -1)
    )
    attn_out = jnp.einsum("tc,dc->td", context, output_turned, preferred_element_type=F32)
    hidden = residual_in + attn_out
    inv_two = lax.rsqrt(jnp.mean(hidden * hidden, -1, keepdims=True) + NORM_EPS)
    normed_two = (hidden * inv_two * gain_two).astype(BF16)
    logits = jnp.dot(normed_two, router_low, preferred_element_type=F32)
    exp_logits = jnp.exp(logits)
    router_probs = exp_logits / jnp.sum(exp_logits, -1, keepdims=True)

    table = jnp.zeros((n_dp, groups, 8, tokens), F32)
    by_owner = place.astype(F32).T.reshape(n_dp, shared, groups, tokens).transpose(0, 2, 1, 3)
    table = table.at[:, :, :shared].set(by_owner)
    by_owner = router_probs.T.reshape(n_dp, shared, groups, tokens).transpose(0, 2, 1, 3)
    table = table.at[:, :, 4 : 4 + shared].set(by_owner)
    made = {"rows": normed_two, "table": table, "cots": cot_all, "tokens": tokens}
    made |= {"x": {}, "c": {}, "y": {}, "d": {}}
    expert_grads = []
    for i in range(shared):
        found = run_expert(n_dp, n_mp, groups, 2 + i, i, shared, expert_parts[i], made)
        for name, value in found.items():
            if name[0] in "xc" and name[1:].isdigit():
                made[name[0]][int(name[1:])] = value
            elif name in ("y", "d"):
                made[name][i] = value
            elif name in ("tables", "gates"):
                made[name] = value
        sent = [found[f"grad{k}"] for k in range(n_mp)]
        expert_grads.append(
            sent[:1] + [lax.ppermute(sent[k], "mp", flips[k]) for k in range(1, n_mp)]
        )
    grad_normed_two, gate_parts = found["total"], found["gate_parts"]
    mixture = reduce_tokens(2 + shared, found["terms"])
    block_out = hidden + mixture
    grad_probs = gate_parts[:, :, :shared].transpose(0, 2, 1, 3).reshape(EXPERTS, tokens).T
    pairs = []
    for i in range(shared):
        if groups == 1:
            pairs.append(sum(part.astype(F32) for part in expert_grads[i]))
            continue
        same = sum(part.astype(F32) for part in expert_grads[i][0::2])
        turned = sum(part.astype(F32) for part in expert_grads[i][1::2])
        pairs.append(jnp.where(kind == 0, same, turned))
        pairs.append(jnp.where(kind == 0, turned, same))
    expert_grad = jnp.stack(pairs)
    gateup_grad, down_grad = expert_grad[:, :2], expert_grad[:, 2]

    grad_logits = (
        router_probs * (grad_probs - jnp.sum(router_probs * grad_probs, -1, keepdims=True))
    ).astype(BF16)
    grad_normed_two = grad_normed_two + jnp.einsum(
        "te,de->td", grad_logits, router_low, preferred_element_type=F32
    )
    grad_router = jnp.einsum("td,te->de", normed_two, grad_logits, preferred_element_type=F32)
    scaled_two = gain_two * grad_normed_two
    grad_hidden = (
        cotangent
        + inv_two * scaled_two
        - hidden * inv_two**3 * jnp.mean(scaled_two * hidden, -1, keepdims=True)
    )
    grad_gain_two = jnp.sum(grad_normed_two * hidden * inv_two, 0)

    grad_attn = grad_hidden.astype(BF16)
    grad_ctx = jnp.dot(grad_attn, output_turned, preferred_element_type=F32).astype(BF16)
    grad_output = jnp.einsum("td,tc->dc", grad_attn, context, preferred_element_type=F32)
    grad_ctx = grad_ctx.reshape(tokens, KEY_VALUE_HEADS, queries_per_group, HEAD_SIZE)
    probs_float = jnp.where(causal, jnp.exp(jnp.where(causal, raw_scores - log_total, 0.0)), 0.0)
    grad_p = jnp.einsum("qkgd,skd->kgqs", grad_ctx, values, preferred_element_type=F32)
    delta_sum = jnp.sum(probs_float * grad_p, -1, keepdims=True)
    grad_s = (probs_float * (grad_p - delta_sum)).astype(BF16)
    grad_q = (
        jnp.einsum("kgqs,skd->qkgd", grad_s, keys_rot, preferred_element_type=F32) * score_scale
    )
    grad_k = (
        jnp.einsum("kgqs,qkgd->skd", grad_s, query_rows, preferred_element_type=F32) * score_scale
    )
    grad_v = jnp.einsum("kgqs,qkgd->skd", attn_probs, grad_ctx, preferred_element_type=F32)
    grad_q_lin = (
        rotate(grad_q.reshape(tokens, QUERY_HEADS, HEAD_SIZE), query_cos, -query_sin)
        .astype(BF16)
        .reshape(tokens, -1)
    )
    grad_kv = jnp.stack([rotate(grad_k, key_cos, -key_sin), grad_v], 2).reshape(2 * tokens, -1)
    grad_kv_other = lax.ppermute(grad_kv[:tokens].astype(BF16), "mp", flips[1])
    grad_kv_lin = (grad_kv[tokens:] + grad_kv_other.astype(F32)).astype(BF16)
    grad_normed_one = jnp.einsum(
        "tc,dc->td", grad_q_lin, query_full, preferred_element_type=F32
    ) + jnp.einsum("tc,dc->td", grad_kv_lin, keyval_full, preferred_element_type=F32)
    grad_query = jnp.einsum("td,tc->dc", normed_one, grad_q_lin, preferred_element_type=F32)
    grad_keyval = jnp.einsum("td,tc->dc", normed_one, grad_kv_lin, preferred_element_type=F32)
    scaled_one = gain_one * grad_normed_one
    input_grad = (
        grad_hidden
        + inv_one * scaled_one
        - residual_in * inv_one**3 * jnp.mean(scaled_one * residual_in, -1, keepdims=True)
    )
    grad_gain_one = jnp.sum(grad_normed_one * residual_in * inv_one, 0)

    grads = jnp.stack([grad_query, grad_keyval, grad_output]).astype(BF16)
    small_grads = jnp.zeros((n_dp, n_mp, 8 + own_router, lanes), F32)
    small_grads = small_grads.at[:, :, 0, :own_gain].set(grad_gain_one.reshape(n_dp, n_mp, -1))
    small_grads = small_grads.at[:, :, 1, :own_gain].set(grad_gain_two.reshape(n_dp, n_mp, -1))
    small_grads = small_grads.at[:, :, 8:, :EXPERTS].set(
        grad_router.reshape(n_dp, n_mp, own_router, EXPERTS)
    )
    grads, small_grads = reduce_weights(n_dp, n_mp, 3 + shared, grads, small_grads)
    query_grad, keyval_grad, output_grad = grads[0], grads[1], grads[2].T
    gain_one_grad, gain_two_grad = small_grads[0, :own_gain], small_grads[1, :own_gain]
    router_grad = small_grads[8:, :EXPERTS]
    matrix_rate = 0.2 / math.sqrt(MODEL_WIDTH)
    gain_one_all = adamw(attn_gain, gain_one_grad, attn_gain_mean, attn_gain_var, 0.1, 0.0)
    query_all = adamw(query_w, query_grad, query_mean, query_var, matrix_rate, 0.1)
    keyval_all = adamw(
        key_value_weight,
        keyval_grad,
        key_value_first_moment,
        key_value_second_moment,
        matrix_rate,
        0.1,
    )
    output_all = adamw(output_w, output_grad, output_mean, output_var, 0.1, 0.1)
    gain_two_all = adamw(moe_gain, gain_two_grad, moe_gain_mean, moe_gain_var, 0.1, 0.0)
    router_all = adamw(router_w, router_grad, router_mean, router_var, matrix_rate, 0.1)
    gateup_all = adamw(gateup_w, gateup_grad, gateup_mean, gateup_var, matrix_rate, 0.1)
    down_all = adamw(down_w, down_grad, down_mean, down_var, 0.07, 0.1)
    return (
        block_out,
        input_grad,
        gain_one_all[0],
        gain_one_all[1],
        gain_one_all[2],
        gain_one_all[3],
        query_all[0],
        query_all[1],
        query_all[2],
        query_all[3],
        keyval_all[0],
        keyval_all[1],
        keyval_all[2],
        keyval_all[3],
        output_all[0],
        output_all[1],
        output_all[2],
        output_all[3],
        gain_two_all[0],
        gain_two_all[1],
        gain_two_all[2],
        gain_two_all[3],
        router_all[0],
        router_all[1],
        router_all[2],
        router_all[3],
        gateup_all[0],
        gateup_all[1],
        gateup_all[2],
        gateup_all[3],
        down_all[0],
        down_all[1],
        down_all[2],
        down_all[3],
    )


def solution(mesh):
    in_specs = (
        P(("dp", "mp"), None),
        P(("dp", "mp"), None),
        P(("dp", "mp"), None),
        P(("dp", "mp")),
        P("dp", "mp"),
        P("dp", "mp"),
        P("mp", "dp"),
        P(("dp", "mp")),
        P(("dp", "mp"), None),
        P("dp", None, "mp", None),
        P("dp", "mp", None),
        P(("dp", "mp")),
        P(("dp", "mp")),
        P("dp", "mp"),
        P("dp", "mp"),
        P("dp", "mp"),
        P("dp", "mp"),
        P("mp", "dp"),
        P("mp", "dp"),
        P(("dp", "mp")),
        P(("dp", "mp")),
        P(("dp", "mp"), None),
        P(("dp", "mp"), None),
        P("dp", None, "mp", None),
        P("dp", None, "mp", None),
        P("dp", "mp", None),
        P("dp", "mp", None),
    )
    out_specs = (
        P(("dp", "mp"), None),
        P(("dp", "mp"), None),
        P(("dp", "mp")),
        P(("dp", "mp")),
        P(("dp", "mp")),
        P(("dp", "mp")),
        P("dp", "mp"),
        P("dp", "mp"),
        P("dp", "mp"),
        P("dp", "mp"),
        P("dp", "mp"),
        P("dp", "mp"),
        P("dp", "mp"),
        P("dp", "mp"),
        P("mp", "dp"),
        P("mp", "dp"),
        P("mp", "dp"),
        P("mp", "dp"),
        P(("dp", "mp")),
        P(("dp", "mp")),
        P(("dp", "mp")),
        P(("dp", "mp")),
        P(("dp", "mp"), None),
        P(("dp", "mp"), None),
        P(("dp", "mp"), None),
        P(("dp", "mp"), None),
        P("dp", None, "mp", None),
        P("dp", None, "mp", None),
        P("dp", None, "mp", None),
        P("dp", None, "mp", None),
        P("dp", "mp", None),
        P("dp", "mp", None),
        P("dp", "mp", None),
        P("dp", "mp", None),
    )
    step = functools.partial(local, mesh.shape["dp"], mesh.shape["mp"])
    return jax.shard_map(step, mesh=mesh, in_specs=in_specs, out_specs=out_specs, check_vma=False)
```

```python
import functools
import math
import types

import jax
import jax.numpy as jnp
import numpy as np
from jax import lax
from jax.experimental import pallas as pl
from jax.experimental.pallas import tpu as pltpu
from jax.sharding import PartitionSpec as P

MODEL_WIDTH = 1024
QUERY_HEADS = 16
KEY_VALUE_HEADS = 8
HEAD_SIZE = 64
EXPERTS = 32
TOPK = 8
SEQUENCE_TOKENS = 512
STEP = 3
CAP = 80

NORM_EPS = 1e-06
MESH = pl.DeviceIdType.MESH
BF16 = jnp.bfloat16
F32 = jnp.float32


def flip(index, mask):
    return index + mask * (1 - 2 * lax.rem(lax.div(index, mask), 2))


def flip_all(index, masks):
    bit = 1
    while bit <= masks:
        if masks & bit:
            index = flip(index, bit)
        bit *= 2
    return index


def bits_of(size):
    return [1 << i for i in range(size.bit_length() - 1)]


def orders_of(n_dp):
    bits = bits_of(n_dp)
    return bits[1:] + bits[:1], bits[1:][::-1] + bits[:1]


def place_of(order, j):
    place = -1
    for at, mask in enumerate(order):
        if j & mask:
            place = at
    return place


def greet(partners):
    barrier = pltpu.get_barrier_semaphore()
    for partner in partners:
        pl.semaphore_signal(barrier, inc=1, device_id=partner, device_id_type=MESH)
    pl.semaphore_wait(barrier, len(partners))


class Copies:
    def __init__(self, send_sems, recv_sems):
        self.send_sems, self.recv_sems = send_sems, recv_sems
        self.used = 0
        self.sent = []

    def slot(self):
        self.used += 1
        return self.used - 1

    def make(self, source, target, device, slot):
        return pltpu.make_async_remote_copy(
            src_ref=source,
            dst_ref=target,
            send_sem=self.send_sems.at[slot],
            recv_sem=self.recv_sems.at[slot],
            device_id=device,
            device_id_type=MESH,
        )

    def start(self, source, target, device, slot):
        copy = self.make(source, target, device, slot)
        copy.start()
        self.sent.append(copy)

    def wait(self, target, device, slot):
        self.make(target, target, device, slot).wait_recv()

    def finish(self):
        for copy in self.sent:
            copy.wait_send()


class TreeGather:
    def __init__(self, copies, order, n_dp, me, source, target):
        self.copies, self.order, self.n_dp, self.me = copies, order, n_dp, me
        self.source, self.target = source, target
        self.slots = {j: copies.slot() for j in range(1, n_dp)}

    def level(self, j):
        return bin(j).count("1")

    def send(self, j):
        dp, mp = self.me
        for mask in self.order[place_of(self.order, j) + 1 :]:
            self.copies.start(
                self.source(j), self.target(j, mask), (flip(dp, mask), mp), self.slots[j ^ mask]
            )

    def receive(self, j):
        self.copies.wait(self.source(j), self.me, self.slots[j])

    def steps(self):
        return sorted(range(1, self.n_dp), key=lambda j: (self.level(j), place_of(self.order, j)))


def run_gathers(trees):
    n_dp = trees[0].n_dp
    for level in range(1, n_dp.bit_length()):
        for tree in trees:
            for j in tree.steps():
                if tree.level(j) == level:
                    tree.receive(j)
                    tree.send(j)


class TreeReduce:
    def __init__(self, copies, order, n_dp, me, block, room, add):
        self.copies, self.order, self.n_dp, self.me = copies, order, n_dp, me
        self.block, self.room, self.add = block, room, add
        self.keys = [
            (j, q) for j in range(n_dp) for q in range(len(order) - 1, place_of(order, j), -1)
        ]
        self.slots = {key: copies.slot() for key in self.keys}

    def number(self, key):
        return self.keys.index(key)

    def send(self, j):
        dp, mp = self.me
        p = place_of(self.order, j)
        last = len(self.order) - 1
        source = self.block(j) if p == last else self.room(self.number((j, last)))
        mask = self.order[p]
        key = (j ^ mask, p)
        self.copies.start(source, self.room(self.number(key)), (flip(dp, mask), mp), self.slots[key])

    def collect(self, j):
        last = len(self.order) - 1
        for q in range(last, place_of(self.order, j), -1):
            here = self.room(self.number((j, q)))
            self.copies.wait(here, self.me, self.slots[(j, q)])
            if q == last:
                self.add(here, self.block(j))
            else:
                self.add(self.room(self.number((j, last))), here)

    def total(self):
        return self.room(self.number((0, len(self.order) - 1)))


def add_rows(step=16):
    def add(here, other):
        def body(i, carry):
            rows = pl.ds(pl.multiple_of(i * step, step), step)
            total = here[..., rows, :].astype(F32) + other[..., rows, :].astype(F32)
            here[..., rows, :] = total.astype(here.dtype)
            return carry

        lax.fori_loop(0, here.shape[-2] // step, body, 0)

    return add


def hbm():
    return pl.BlockSpec(memory_space=pl.ANY)


def vmem():
    return pl.BlockSpec(memory_space=pltpu.VMEM)


def params(identity, limit=None):
    return pltpu.CompilerParams(
        collective_id=identity, has_side_effects=True, vmem_limit_bytes=limit
    )


def launch(kernel, identity, ins, outs, scratch, n_copies, limit=None):
    def flat(entries):
        names, leaves, specs = [], [], []
        for name, (value, spec) in entries.items():
            several = isinstance(value, list)
            new = value if several else [value]
            names.append((name, len(new) if several else None))
            leaves += new
            specs += [spec] * len(new)
        return names, leaves, specs

    def unflat(names, leaves):
        leaves, found = list(leaves), {}
        for name, count in names:
            found[name] = leaves[0] if count is None else leaves[:count]
            leaves = leaves[1 if count is None else count :]
        return found

    scratch = scratch | dict(
        send_sems=pltpu.SemaphoreType.DMA((n_copies,)),
        recv_sems=pltpu.SemaphoreType.DMA((n_copies,)),
    )
    in_names, values, in_specs = flat(ins)
    out_names, shapes, out_specs = flat(outs)
    scratch_names = [(name, None) for name in scratch]

    def body(*refs):
        named = unflat(in_names + out_names + scratch_names, refs)
        kernel(types.SimpleNamespace(**named))

    results = pl.pallas_call(
        body,
        out_shape=tuple(shapes),
        in_specs=in_specs,
        out_specs=tuple(out_specs),
        scratch_shapes=list(scratch.values()),
        compiler_params=params(identity, limit),
        cost_estimate=pl.CostEstimate(flops=1, bytes_accessed=1, transcendentals=0),
        name=kernel.__name__,
    )(*values)
    return types.SimpleNamespace(**unflat(out_names, results))


def low(*shape):
    return jax.ShapeDtypeStruct(shape, BF16)


def single(*shape):
    return jax.ShapeDtypeStruct(shape, F32)


def dot(a, b, contract):
    return lax.dot_general(a, b, ((contract[:1], contract[1:]), ((), ())), preferred_element_type=F32)


NN, NT, TN = (1, 0), (1, 1), (0, 0)


def gain_rows(small_all, row):
    n_devices = math.prod(small_all.shape[:2])
    n_tiles = MODEL_WIDTH // 128
    per_tile = n_devices // n_tiles
    n_mp = small_all.shape[1]
    tiles = []
    for tile in range(n_tiles):
        total = None
        for device in range(tile * per_tile, (tile + 1) * per_tile):
            part = small_all[device // n_mp, device % n_mp, row : row + 1, :]
            total = part if total is None else total + part
        tiles.append(total)
    return tiles


def prologue(n_dp, n_mp, groups, identity, small, shards, cot, residual):
    half = n_mp // 2
    kinds, rows, cols = shards.shape
    tokens, width = cot.shape
    order_a, order_b = orders_of(n_dp)
    n_copies = 2 * (n_mp - 1) + 4 * (n_dp - 1) + 1

    def gather_line(r):
        dp, mp = lax.axis_index("dp"), lax.axis_index("mp")
        me = (dp, mp)
        neighbour = (dp, flip(mp, 1))
        copies = Copies(r.send_sems, r.recv_sems)
        own_small = r.small_all.at[dp, mp]
        own_cols = pl.ds(pl.multiple_of(mp * cols, cols), cols)
        own_part = r.row_block.at[:, :, own_cols]
        r.small_all[dp, mp] = r.small[...]
        r.row_block[:, :, own_cols] = r.shards[...]
        r.cots[0] = r.cot[...]
        greet(
            [(flip_all(dp, mask), mp) for mask in bits_of(n_dp)]
            + [(dp, flip_all(mp, k)) for k in range(1, n_mp)]
        )
        near = lax.div(mp, half)
        line = {}
        for k in range(1, n_mp):
            line[k] = (copies.slot(), copies.slot())
            copies.start(r.small, own_small, (dp, flip_all(mp, k)), line[k][0])
        for k in range(1, n_mp):
            copies.start(r.shards, own_part, (dp, flip_all(mp, k)), line[k][1])
        across = copies.slot()

        def small_tree(chunk):
            first = pl.multiple_of(chunk * half, half)

            def ref(j, mask=0):
                return r.small_all.at[flip_all(dp, j), pl.ds(first, half)]

            return TreeGather(copies, order_a, n_dp, me, ref, ref)

        small_trees = [small_tree(chunk) for chunk in (near, 1 - near)]
        cot_trees = row_trees(copies, n_dp, me, r.cots)
        for chunk in (0, 1):
            for k in range(1, half) if chunk == 0 else range(half, n_mp):
                copies.wait(r.small_all.at[dp, flip_all(mp, k)], me, line[k][0])
            small_trees[chunk].send(0)
        for one in cot_trees:
            one.send(0)
        top = n_dp.bit_length() - 1
        for level in range(1, top + 1):
            run_level(small_trees, level)
            if level < top:
                run_level(cot_trees, level)
        residual_rows = r.residual[...]
        inverse = lax.rsqrt(jnp.mean(residual_rows * residual_rows, -1, keepdims=True) + NORM_EPS)
        for number, gain in enumerate(gain_rows(r.small_all, 0)):
            lanes = slice(number * 128, (number + 1) * 128)
            r.normed[0, :, lanes] = (residual_rows[:, lanes] * inverse * gain).astype(BF16)
        copies.start(r.normed.at[0], r.normed.at[1], neighbour, across)
        run_level(cot_trees, top)
        for k in range(1, n_mp):
            other = pl.multiple_of(flip_all(mp, k) * cols, cols)
            copies.wait(r.row_block.at[:, :, pl.ds(other, cols)], me, line[k][1])
        copies.wait(r.normed.at[1], me, across)
        copies.finish()

    return launch(
        gather_line,
        identity,
        dict(
            small=(small, vmem()), shards=(shards, vmem()), cot=(cot, vmem()), residual=(residual, vmem())
        ),
        dict(
            small_all=(single(n_dp, n_mp, *small.shape), vmem()),
            row_block=(low(kinds, rows, n_mp * cols), vmem()),
            cots=(low(n_dp, tokens, width), vmem()),
            normed=(low(2, tokens, width), vmem()),
        ),
        {},
        n_copies,
        32 << 20,
    )


def run_level(trees, level):
    for one in trees:
        for j in one.steps():
            if one.level(j) == level:
                one.receive(j)
                one.send(j)


def gather_rows(n_dp, groups, identity, row_block, cot):
    kinds, rows, width = row_block.shape
    part_rows = rows // 2

    def gather_weights(r):
        dp, mp = lax.axis_index("dp"), lax.axis_index("mp")
        me = (dp, mp)
        copies = Copies(r.send_sems, r.recv_sems)
        neighbour = (dp, flip(mp, 1))
        r.full[:, pl.ds(pl.multiple_of(dp * rows, rows), rows), :] = r.row_block[...]
        greet([(flip_all(dp, mask), mp) for mask in bits_of(n_dp)] + [neighbour] * (groups - 1))
        across = copies.slot()
        if groups > 1:
            copies.start(r.cot, r.cot_other, neighbour, across)

        def tree(part, order):
            def ref(j, mask=0):
                start = flip_all(dp, j) * rows + part * part_rows
                return r.full.at[:, pl.ds(pl.multiple_of(start, part_rows), part_rows), :]

            return TreeGather(copies, order, n_dp, me, ref, ref)

        trees = [tree(part, order) for part, order in enumerate(orders_of(n_dp))]
        for one in trees:
            one.send(0)
        run_gathers(trees)
        if groups > 1:
            copies.wait(r.cot_other, me, across)
        copies.finish()

    return launch(
        gather_weights,
        identity,
        dict(row_block=(row_block, vmem()), cot=(cot, vmem())),
        dict(full=(low(kinds, n_dp * rows, width), vmem()), cot_other=(low(*cot.shape), vmem())),
        {},
        2 * (n_dp - 1) + 1,
        32 << 20,
    )


def row_trees(copies, n_dp, me, rows_all):
    tokens = rows_all.shape[1]

    def tree(part, order):
        cut = pl.ds(part * (tokens // 2), tokens // 2)
        return TreeGather(
            copies,
            order,
            n_dp,
            me,
            lambda j: rows_all.at[j, cut],
            lambda j, mask: rows_all.at[j ^ mask, cut],
        )

    return [tree(part, order) for part, order in enumerate(orders_of(n_dp))]


def rotary_constants():
    half_width = HEAD_SIZE // 2
    frequency = np.exp(
        np.float32(-math.log(10000.0)) * np.arange(half_width, dtype=np.float32) * np.float32(2.0)
        / np.float32(HEAD_SIZE)
    ).astype(np.float32)
    angles = np.arange(SEQUENCE_TOKENS, dtype=np.float32)[:, None] * frequency[None, :]
    cosine, sine = np.cos(angles), np.sin(angles)
    cosine = np.concatenate([cosine, cosine], 1)
    sine = np.concatenate([-sine, sine], 1)
    queries = np.stack([np.tile(cosine, (1, 2)), np.tile(sine, (1, 2))])
    keys = np.stack(
        [
            np.concatenate([cosine, np.ones_like(cosine)], 1),
            np.concatenate([sine, np.zeros_like(sine)], 1),
        ]
    )
    return queries.astype(np.float32), keys.astype(np.float32)


def rotate(value, cosine, sine):
    lane = lax.broadcasted_iota(jnp.int32, value.shape, 1)
    rolled = jnp.where(
        lane % HEAD_SIZE < HEAD_SIZE // 2,
        pltpu.roll(value, 128 - HEAD_SIZE // 2, 1),
        pltpu.roll(value, HEAD_SIZE // 2, 1),
    )
    return value * cosine + rolled * sine


def group_operands(queries, keyval):
    lane = lax.broadcasted_iota(jnp.int32, queries.shape, 1)
    both = jnp.concatenate(
        [jnp.where(lane < HEAD_SIZE, queries, 0.0), jnp.where(lane < HEAD_SIZE, 0.0, queries)], 0
    ).astype(BF16)
    lane = lax.broadcasted_iota(jnp.int32, keyval.shape, 1)
    turned = pltpu.roll(keyval, HEAD_SIZE, 1)
    keys = jnp.where(lane < HEAD_SIZE, keyval, turned).astype(BF16)
    values = jnp.where(lane < HEAD_SIZE, turned, keyval).astype(BF16)
    return both, keys, values


def merge_heads(both):
    tokens = both.shape[0] // 2
    lane = lax.broadcasted_iota(jnp.int32, (tokens, 128), 1)
    return jnp.where(lane < HEAD_SIZE, both[:tokens], both[tokens:])


def seen(tokens, mp):
    shape = (2 * tokens, 2 * tokens)
    row = lax.broadcasted_iota(jnp.int32, shape, 0) % tokens
    key = lax.broadcasted_iota(jnp.int32, shape, 1)
    shift = tokens - 2 * tokens * lax.rem(mp, 2)
    key = jnp.where(key < tokens, key, key - tokens + shift)
    return key <= row


def softmax_of(both, keys, mask):
    scores = dot(both, keys, NT) * (1.0 / math.sqrt(HEAD_SIZE))
    raised = jnp.exp(jnp.where(mask, scores, -1e30))
    return raised / jnp.sum(raised, -1, keepdims=True)


def attention_forward(
    n_dp, groups, shared, identity, residual, normed, full, gain_two, router, places, cot_other, rotary
):
    tokens, width = residual.shape
    query_rotary, own_rotary, other_rotary = rotary
    n_heads = width // 128
    n_copies = 2 * (n_dp - 1)

    def attention(r):
        dp, mp = lax.axis_index("dp"), lax.axis_index("mp")
        me = (dp, mp)
        copies = Copies(r.send_sems, r.recv_sems)
        loads = [
            pltpu.make_async_copy(r.full.at[c], r.weights.at[c], r.local_sems.at[c])
            for c in range(3)
        ]
        for copy in loads:
            copy.start()
        r.cots[0] = r.cot_other[...]
        greet([(flip_all(dp, mask), mp) for mask in bits_of(n_dp)])
        trees = row_trees(copies, n_dp, me, r.cots) if groups > 1 else []
        for one in trees:
            one.send(0)
        top = n_dp.bit_length() - 1
        loads[0].wait()
        r.q[...] = dot(r.normed[0], r.weights[0], NN)
        loads[1].wait()
        for part in (0, 1):
            r.kv[part] = dot(r.normed[part], r.weights[1], NN)
        run_level(trees, 1)
        mask = seen(tokens, mp)

        def head(k, carry):
            lanes = pl.ds(pl.multiple_of(k * 128, 128), 128)
            queries = rotate(r.q[:, lanes], r.query_rotary[0], r.query_rotary[1])
            r.queries[:, lanes] = queries.astype(BF16)
            parts = []
            for part, table in enumerate((r.own_rotary, r.other_rotary)):
                parts.append(rotate(r.kv[part, :, lanes], table[0], table[1]))
                r.keyval[part, :, lanes] = parts[part].astype(BF16)
            both, keys, values = group_operands(queries, jnp.concatenate(parts, 0))
            chance = softmax_of(both, keys, mask).astype(BF16)
            r.context[:, lanes] = merge_heads(dot(chance, values, NN)).astype(BF16)
            return carry

        for level in range(2, top + 1):
            first, end = [(level - 2 + i) * n_heads // (top - 1) for i in (0, 1)]
            lax.fori_loop(first, end, head, 0)
            run_level(trees, level)
        loads[2].wait()
        hidden = r.residual[...] + dot(r.context[...], r.weights[2], NT)
        r.hidden[...] = hidden
        inverse = lax.rsqrt(jnp.mean(hidden * hidden, -1, keepdims=True) + NORM_EPS)
        normed = (hidden * inverse * r.gain_two[...]).astype(BF16)
        r.normed_two[...] = normed
        logits = dot(normed, r.router[...], NN)
        lane = lax.broadcasted_iota(jnp.int32, logits.shape, 1)
        raised = jnp.where(lane < EXPERTS, jnp.exp(logits), 0.0)
        probs = raised / jnp.sum(raised, -1, keepdims=True)
        r.probs[...] = probs
        turned = probs.T
        r.table[...] = r.places[...]
        for expert in range(EXPERTS):
            owner, which = divmod(expert, groups * shared)
            r.table[owner, which % groups, 4 + which // groups, :] = turned[expert]
        copies.finish()

    return launch(
        attention,
        identity,
        dict(
            residual=(residual, vmem()),
            normed=(normed, vmem()),
            full=(full, hbm()),
            gain_two=(gain_two, vmem()),
            router=(router, vmem()),
            places=(places, vmem()),
            cot_other=(cot_other, vmem()),
            query_rotary=(query_rotary, vmem()),
            own_rotary=(own_rotary, vmem()),
            other_rotary=(other_rotary, vmem()),
        ),
        dict(
            cots=(low(n_dp, tokens, width), vmem()),
            queries=(low(tokens, width), vmem()),
            keyval=(low(2, tokens, width), vmem()),
            context=(low(tokens, width), vmem()),
            hidden=(single(tokens, width), vmem()),
            normed_two=(low(tokens, width), vmem()),
            probs=(single(tokens, 128), vmem()),
            table=(single(*places.shape), vmem()),
        ),
        dict(
            weights=pltpu.VMEM((3, width, width), BF16),
            q=pltpu.VMEM((tokens, width), F32),
            kv=pltpu.VMEM((2, tokens, width), F32),
            local_sems=pltpu.SemaphoreType.DMA((3,)),
        ),
        n_copies,
        48 << 20,
    )


def attention_backward(n_dp, n_mp, groups, shared, identity, given, first_row):
    tokens, width = given.residual.shape
    n_heads = width // 128
    n_devices = n_dp * n_mp
    own_router = width // n_devices
    per_tile = n_devices // n_heads
    rows, cols = width // n_dp, width // n_mp
    part_rows = rows // 2
    orders = orders_of(n_dp)
    n_copies = (2 * groups + 7) * (n_dp - 1) + 1 + 5 * (n_mp - 1) + 1

    rooms, across_room = reduce_rooms(groups, n_dp, tokens, width, BF16)

    def attention_back(r):
        dp, mp = lax.axis_index("dp"), lax.axis_index("mp")
        me = (dp, mp)
        neighbour = (dp, flip(mp, 1))
        copies = Copies(r.send_sems, r.recv_sems)
        loads = [
            pltpu.make_async_copy(r.full.at[c], r.weights.at[c], r.local_sems.at[c])
            for c in (2, 0, 1)
        ]
        for copy in loads:
            copy.start()
        greet(
            [(flip_all(dp, mask), mp) for mask in bits_of(n_dp)]
            + [(dp, flip_all(mp, k)) for k in range(1, n_mp)]
        )
        mixture = TokenReduce(copies, n_dp, me, r.terms, r.rooms, r.across)
        for group in range(groups)[::-1]:
            for j in range(1, n_dp, 2):
                mixture.first(group, j)
        last = mixture.last
        travels = {k: copies.slot() for k in range(1, n_mp)}

        def send_expert(k):
            copies.start(
                r.expert_grads[k - 1], r.arrived[k - 1], (dp, flip_all(mp, k)), travels[k]
            )

        for k in range(2, n_mp):
            send_expert(k)
        r.turned[...] = jnp.zeros_like(r.turned)
        for expert in range(EXPERTS):
            owner, which = divmod(expert, groups * shared)
            r.turned[expert, :] = r.gate_parts[owner, which % groups, which // groups, :]
        grad_probs = r.turned[...].T
        probs = r.probs[...]
        grad_logits = (
            probs * (grad_probs - jnp.sum(probs * grad_probs, -1, keepdims=True))
        ).astype(BF16)
        grad_normed_two = r.total[...] + dot(grad_logits, r.router[...], NT)
        r.grad_router[...] = dot(r.normed_two[...], grad_logits, TN)
        hidden = r.hidden[...]
        inverse = lax.rsqrt(jnp.mean(hidden * hidden, -1, keepdims=True) + NORM_EPS)
        scaled = r.gain_two[...] * grad_normed_two
        grad_hidden = (
            r.cotangent[...]
            + inverse * scaled
            - hidden * (inverse * inverse * inverse) * jnp.mean(scaled * hidden, -1, keepdims=True)
        )
        r.grad_hidden[...] = grad_hidden
        gain_two = jnp.sum(grad_normed_two * hidden * inverse, 0, keepdims=True)
        grad_attn = grad_hidden.astype(BF16)
        r.grad_attn[...] = grad_attn
        def weight_tree(c, part):
            def block(j):
                start = flip_all(dp, j) * rows + part * part_rows
                return r.grads.at[c, pl.ds(pl.multiple_of(start, part_rows), part_rows), :]

            return TreeReduce(
                copies,
                orders[part],
                n_dp,
                me,
                block,
                lambda number: r.weight_rooms.at[c, part, number],
                add_rows(),
            )

        weight_trees = [[weight_tree(c, part) for part in (0, 1)] for c in range(3)]

        def weight_level(c, p):
            for j in range(1, n_dp):
                for one in weight_trees[c]:
                    if place_of(one.order, j) == p:
                        if p < last:
                            one.collect(j)
                        one.send(j)

        r.grads[2] = dot(grad_attn, r.context[...], TN).astype(BF16)
        weight_level(2, last)
        mixture.level(1, last - 1)
        loads[0].wait()
        r.grad_context[...] = dot(r.grad_attn[...], r.weights[2], NN).astype(BF16)
        mask = seen(tokens, mp)

        def head(k, carry):
            lanes = pl.ds(pl.multiple_of(k * 128, 128), 128)
            keyval = jnp.concatenate([r.keyval[0, :, lanes], r.keyval[1, :, lanes]], 0)
            both, keys, values = group_operands(r.queries[:, lanes].astype(F32), keyval.astype(F32))
            grad_both = group_operands(r.grad_context[:, lanes].astype(F32), keyval.astype(F32))[0]
            chance = softmax_of(both, keys, mask)
            grad_p = dot(grad_both, values, NT)
            delta = jnp.sum(chance * grad_p, -1, keepdims=True)
            grad_s = (chance * (grad_p - delta)).astype(BF16)
            scale = 1.0 / math.sqrt(HEAD_SIZE)
            grad_q = merge_heads(dot(grad_s, keys, NN)) * scale
            r.grad_q[:, lanes] = rotate(grad_q, r.query_rotary[0], -r.query_rotary[1]).astype(BF16)
            grad_k = dot(grad_s, both, TN) * scale
            grad_v = dot(chance.astype(BF16), grad_both, TN)
            lane = lax.broadcasted_iota(jnp.int32, grad_k.shape, 1)
            grad_kv = jnp.where(
                lane < HEAD_SIZE,
                grad_k + pltpu.roll(grad_k, HEAD_SIZE, 1),
                grad_v + pltpu.roll(grad_v, HEAD_SIZE, 1),
            )
            r.grad_kv[:, lanes] = grad_kv[:tokens]
            r.swap[0, :, lanes] = grad_kv[tokens:].astype(BF16)
            return carry

        sent = {}

        def line_out(c):
            for part, one in enumerate(weight_trees[c]):
                one.collect(0)
                total = one.total()
                for k in range(n_mp):
                    there = pl.ds(pl.multiple_of(flip_all(mp, k) * cols, cols), cols)
                    r.line[0, c, k, pl.ds(part * part_rows, part_rows), :] = total[:, there]
            for k in range(1, n_mp):
                sent[c, k] = copies.slot()
                copies.start(
                    r.line.at[0, c, k], r.line.at[1, c, k], (dp, flip_all(mp, k)), sent[c, k]
                )

        stages = []
        for p in range(last - 2, -1, -1):
            stages.append([lambda p=p: mixture.level(1, p)])
        stages.append([lambda: weight_level(2, last - 1), mixture.pass_on])
        for p in range(last - 1, -1, -1):
            stages.append([lambda p=p: mixture.level(0, p)])
            if p < last - 1:
                stages[-1].append(lambda p=p: weight_level(2, p))
        loops = min(len(stages), n_heads)
        for step in range(loops):
            lax.fori_loop(step * n_heads // loops, (step + 1) * n_heads // loops, head, 0)
            if step == loops - 1:
                across = copies.slot()
                copies.start(r.swap.at[0], r.swap.at[1], neighbour, across)
                send_expert(1)
            for stage in stages.pop(0):
                stage()
        for stage in sum(stages, []):
            stage()
        r.grads[0] = dot(r.normed[0], r.grad_q[...], TN).astype(BF16)
        weight_level(0, last)
        loads[1].wait()
        r.grad_normed[...] = dot(r.grad_q[...], r.weights[0], NT)
        weight_level(0, last - 1)
        line_out(2)
        copies.wait(r.swap.at[1], me, across)

        def turn_back(k, carry):
            lanes = pl.ds(pl.multiple_of(k * 128, 128), 128)
            total = r.grad_kv[:, lanes] + r.swap[1, :, lanes].astype(F32)
            total = rotate(total, r.own_rotary[0], -r.own_rotary[1])
            r.grad_kv_low[:, lanes] = total.astype(BF16)
            return carry

        lax.fori_loop(0, n_heads, turn_back, 0)
        loads[2].wait()
        r.grads[1] = dot(r.normed[0], r.grad_kv_low[...], TN).astype(BF16)
        weight_level(1, last)
        grad_normed = r.grad_normed[...] + dot(r.grad_kv_low[...], r.weights[1], NT)
        residual = r.residual[...]
        inverse = lax.rsqrt(jnp.mean(residual * residual, -1, keepdims=True) + NORM_EPS)
        scaled = r.gain_one[...] * grad_normed
        r.input_grad[...] = (
            r.grad_hidden[...]
            + inverse * scaled
            - residual * (inverse * inverse * inverse) * jnp.mean(scaled * residual, -1, keepdims=True)
        )
        gain_one = jnp.sum(grad_normed * residual * inverse, 0, keepdims=True)
        r.small[...] = jnp.zeros_like(r.small)
        for device in range(n_devices):
            tile = device // per_tile
            owner = r.small.at[device // n_mp, device % n_mp]
            owner[0:1, :] = gain_one[:, tile * 128 : (tile + 1) * 128]
            owner[1:2, :] = gain_two[:, tile * 128 : (tile + 1) * 128]
            owner[first_row : first_row + own_router, :] = r.grad_router[
                device * own_router : (device + 1) * own_router, :
            ]

        def add_whole(here, other):
            here[...] = here[...] + other[...]

        small_tree = TreeReduce(
            copies,
            orders[0],
            n_dp,
            me,
            lambda j: r.small.at[flip_all(dp, j)],
            lambda number: r.small_rooms.at[number],
            add_whole,
        )
        for j in range(1, n_dp):
            if place_of(orders[0], j) == last:
                small_tree.send(j)
        for p in range(last - 1, -1, -1):
            if p < last - 1:
                weight_level(0, p)
            weight_level(1, p)
            for j in range(1, n_dp):
                if place_of(orders[0], j) == p:
                    small_tree.collect(j)
                    small_tree.send(j)
        for c in (0, 1):
            line_out(c)
        small_tree.collect(0)
        small_total = small_tree.total()
        for k in range(1, n_mp):
            device = (dp, flip_all(mp, k))
            sent[k] = copies.slot()
            copies.start(small_total.at[device[1]], r.small_line.at[k], device, sent[k])
        mixture.end(r.block_out)
        r.block_out[...] += r.hidden[...]
        for c in (2, 0, 1):
            r.shards[c] = r.line[0, c, 0].astype(F32)
            for k in range(1, n_mp):
                copies.wait(r.line.at[1, c, k], me, sent[c, k])
                r.shards[c] += r.line[1, c, k].astype(F32)
        r.small_shard[...] = small_total[mp]
        for k in range(1, n_mp):
            copies.wait(r.small_line.at[k], me, sent[k])
            r.small_shard[...] += r.small_line[k]
        for k in range(1, n_mp):
            copies.wait(r.arrived[k - 1], me, travels[k])
        copies.finish()

    return launch(
        attention_back,
        identity,
        dict(
            full=(given.full, hbm()),
            expert_grads=(given.expert_grads, hbm()),
            residual=(given.residual, vmem()),
            hidden=(given.hidden, vmem()),
            cotangent=(given.cotangent, vmem()),
            total=(given.total, vmem()),
            gate_parts=(given.gate_parts, vmem()),
            terms=(given.terms, vmem()),
            probs=(given.probs, vmem()),
            normed=(given.normed, vmem()),
            normed_two=(given.normed_two, vmem()),
            queries=(given.queries, vmem()),
            keyval=(given.keyval, vmem()),
            context=(given.context, vmem()),
            gain_one=(given.gain_one, vmem()),
            gain_two=(given.gain_two, vmem()),
            router=(given.router, vmem()),
            query_rotary=(given.rotary[0], vmem()),
            own_rotary=(given.rotary[1], vmem()),
        ),
        dict(
            input_grad=(single(tokens, width), vmem()),
            block_out=(single(tokens, width), vmem()),
            arrived=([low(*grad.shape) for grad in given.expert_grads], hbm()),
            shards=(single(3, rows, cols), vmem()),
            small_shard=(single(first_row + own_router, 128), vmem()),
        ),
        dict(
            grads=pltpu.VMEM((3, width, width), BF16),
            small=pltpu.VMEM((n_dp, n_mp, first_row + own_router, 128), F32),
            small_rooms=pltpu.VMEM((n_dp - 1, n_mp, first_row + own_router, 128), F32),
            small_line=pltpu.VMEM((n_mp, first_row + own_router, 128), F32),
            weight_rooms=pltpu.VMEM((3, 2, n_dp - 1, part_rows, width), BF16),
            line=pltpu.VMEM((2, 3, n_mp, rows, cols), BF16),
            rooms=rooms,
            across=across_room,
            weights=pltpu.VMEM((3, width, width), BF16),
            turned=pltpu.VMEM((128, tokens), F32),
            grad_router=pltpu.VMEM((width, 128), F32),
            grad_hidden=pltpu.VMEM((tokens, width), F32),
            grad_attn=pltpu.VMEM((tokens, width), BF16),
            grad_context=pltpu.VMEM((tokens, width), BF16),
            grad_q=pltpu.VMEM((tokens, width), BF16),
            grad_kv=pltpu.VMEM((tokens, width), F32),
            grad_kv_low=pltpu.VMEM((tokens, width), BF16),
            grad_normed=pltpu.VMEM((tokens, width), F32),
            swap=pltpu.VMEM((2, tokens, width), BF16),
            local_sems=pltpu.SemaphoreType.DMA((3,)),
        ),
        n_copies,
        62 << 20,
    )


class TokenReduce:
    def __init__(self, copies, n_dp, me, terms, rooms, across):
        dp, mp = me
        self.copies, self.me, self.across = copies, me, across
        self.partner = (dp, flip(mp, 1))
        self.tokens = terms.shape[2]
        self.n_dp = n_dp
        self.last = n_dp.bit_length() - 2
        self.groups = terms.shape[0]
        self.slot = copies.slot()

        def tree(group, part, order):
            cut = pl.ds(part * (self.tokens // 2), self.tokens // 2)
            return TreeReduce(
                copies,
                order,
                n_dp,
                me,
                lambda j: terms.at[group, j, cut],
                lambda number: rooms.at[group, part, number],
                add_rows(),
            )

        self.trees = [
            [tree(group, part, order) for part, order in enumerate(orders_of(n_dp))]
            for group in range(self.groups)
        ]

    def first(self, group, j):
        for tree in self.trees[group]:
            tree.send(j)

    def level(self, group, p):
        if group == self.groups:
            return
        for j in range(1, self.n_dp):
            for tree in self.trees[group]:
                if place_of(tree.order, j) == p:
                    tree.collect(j)
                    tree.send(j)

    def pass_on(self):
        if self.groups == 1:
            return
        for part, tree in enumerate(self.trees[1]):
            tree.collect(0)
            cut = pl.ds(part * (self.tokens // 2), self.tokens // 2)
            self.across[0, cut, :] = tree.total()[...]
        self.copies.start(self.across.at[0], self.across.at[1], self.partner, self.slot)

    def end(self, out_ref):
        for tree in self.trees[0]:
            tree.collect(0)
        if self.groups > 1:
            self.copies.wait(self.across.at[1], self.me, self.slot)
        for part, tree in enumerate(self.trees[0]):
            cut = pl.ds(part * (self.tokens // 2), self.tokens // 2)
            total = tree.total()[...].astype(F32)
            if self.groups > 1:
                total = total + self.across[1, cut, :].astype(F32)
            out_ref[cut, :] = total


def reduce_rooms(groups, n_dp, tokens, width, dtype):
    return [
        pltpu.VMEM((groups, 2, n_dp - 1, tokens // 2, width), dtype),
        pltpu.VMEM((2, tokens, width), dtype),
    ]


def run_expert(n_dp, n_mp, groups, identity, index, shared, parts, inputs):
    first, last = index == 0, index == shared - 1
    hidden, width = parts[0].shape[1:]
    units = n_mp * hidden
    blocks = groups * n_dp
    slots = blocks * CAP
    tokens = inputs.rows.shape[0]
    per_tile = 4
    tile = per_tile * CAP
    ins = dict(part=(parts, hbm()))
    outs = dict(grad=([low(3, hidden, width) for _ in range(n_mp)], vmem()))
    scratch = dict(
        weights=pltpu.VMEM((3, units, width), BF16),
        act=pltpu.VMEM((slots, units), BF16),
        pair=pltpu.VMEM((slots, 2 * units), BF16),
        grad_rows=pltpu.VMEM((slots, width), BF16),
        part_sems=pltpu.SemaphoreType.DMA((3 * n_mp,)),
    )
    n_copies = 1
    slot_rows = pltpu.VMEM((slots, width), BF16)
    if first:
        n_copies += blocks + 2 * groups * (n_dp - 1)
        ins |= dict(
            rows=(inputs.rows, hbm()), own_table=(inputs.table, hbm()), cots=(inputs.cots, hbm())
        )
        scratch |= dict(
            tokens_all=pltpu.VMEM((groups, n_dp, tokens, width), BF16),
            x_own=slot_rows,
            c_own=slot_rows,
            cot=pltpu.VMEM((2, tokens, width), BF16),
            cot_sems=pltpu.SemaphoreType.DMA((2,)),
            keep_sems=pltpu.SemaphoreType.DMA((2,)),
        )
    else:
        ins |= dict(
            tables_in=(inputs.tables, vmem()),
            gates_in=(inputs.gates, vmem()),
            x_in=(inputs.x[index], vmem()),
            c_in=(inputs.c[index], vmem()),
        )
    if first and last:
        scratch |= dict(tables=pltpu.VMEM((blocks, 8, tokens), F32))
    elif first:
        rest = [low(slots, width) for _ in range(1, shared)]
        outs |= dict(tables=(single(blocks, 8, tokens), vmem()))
        outs |= dict(x=(rest, vmem()), c=(rest, vmem()))
    if last:
        n_copies += 2 * groups * (n_dp - 1) + blocks
        ins |= dict(y_before=(inputs.y, vmem()), d_before=(inputs.d, vmem()))
        outs |= dict(
            terms=(low(groups, n_dp, tokens, width), hbm()),
            gate_parts=(single(n_dp, groups, 8, tokens), hbm()),
            total=(single(tokens, width), vmem()),
        )
        rooms, across_room = reduce_rooms(groups, n_dp, tokens, width, BF16)
        scratch |= dict(
            gates=pltpu.VMEM((blocks, 8, tokens), F32),
            y=slot_rows,
            d=slot_rows,
            grads_all=pltpu.VMEM((groups, n_dp, tokens, width), BF16),
            sums=pltpu.VMEM((2, tokens, width), BF16),
            sum_sems=pltpu.SemaphoreType.DMA((2,)),
            gate_sem=pltpu.SemaphoreType.DMA((1,)),
            rooms=rooms,
            across=across_room,
        )
    else:
        outs |= dict(
            gates=(single(blocks, 8, tokens), vmem()),
            y=(low(slots, width), vmem()),
            d=(low(slots, width), vmem()),
        )

    def expert(r):
        dp, mp = lax.axis_index("dp"), lax.axis_index("mp")
        me = (dp, mp)
        other = flip(mp, 1)
        kind = lax.rem(mp, groups)
        copies = Copies(r.send_sems, r.recv_sems)
        peers = {
            (group, j): (flip_all(dp, j), other if group else mp)
            for group in range(groups)
            for j in range(n_dp)
            if group + j
        }
        weights, act, pair, grad_rows = r.weights, r.act, r.pair, r.grad_rows
        loads = [
            pltpu.make_async_copy(
                r.part[k].at[c],
                weights.at[c, pl.ds(k * hidden, hidden)],
                r.part_sems.at[3 * k + c],
            )
            for k in range(n_mp)
            for c in range(3)
        ]
        for copy in loads:
            copy.start()
        tables = r.tables if first else r.tables_in
        x_refs = {index: r.x_own if first else r.x_in}
        c_refs = {index: r.c_own if first else r.c_in}
        if first:
            x_refs |= {i + 1: ref for i, ref in enumerate(r.x if shared > 1 else [])}
            c_refs |= {i + 1: ref for i, ref in enumerate(r.c if shared > 1 else [])}

        def hits(block, experts):
            slot = lax.broadcasted_iota(jnp.int32, (CAP, tokens), 0).astype(F32)
            found = [slot == tables[block, pl.ds(i, 1), :] for i in experts]
            return found[0] if len(found) == 1 else jnp.concatenate(found, 0)

        def rows_of(block):
            return pl.ds(pl.multiple_of(block * CAP, 16), CAP)

        if first:
            rows_all, cots = r.tokens_all, r.cots
            keep = [
                pltpu.make_async_copy(r.rows, rows_all.at[0, 0], r.keep_sems.at[0]),
                pltpu.make_async_copy(
                    r.own_table.at[dp, kind], tables.at[0], r.keep_sems.at[1]
                ),
            ]
            for copy in keep:
                copy.start()
            order = [(group, 0) for group in range(groups)]
            for level in range(1, n_dp.bit_length()):
                for group in range(groups):
                    order += [(group, j) for j in range(n_dp) if bin(j).count("1") == level]

            def cot_copy(number):
                group, j = order[number]
                return pltpu.make_async_copy(
                    cots[group].at[j], r.cot.at[number % 2], r.cot_sems.at[number % 2]
                )

            cot_copy(0).start()
            greet(list(peers.values()))
            across = copies.slot()
            if groups > 1:
                copies.start(r.rows, rows_all.at[1, 0], peers[1, 0], across)
            sent = {}
            for key, device in peers.items():
                sent[key] = copies.slot()
                group, j = key
                copies.start(
                    r.own_table.at[device[0], lax.rem(device[1], groups)],
                    tables.at[group * n_dp + j],
                    device,
                    sent[key],
                )
            trees = [row_trees(copies, n_dp, me, rows_all.at[group]) for group in range(groups)]
            keep[0].wait()
            for tree in trees[0]:
                tree.send(0)
            keep[1].wait()

            def fill(number):
                group, j = order[number]
                block = group * n_dp + j
                if number:
                    copies.wait(tables.at[block], me, sent[group, j])
                if number + 1 < blocks:
                    cot_copy(number + 1).start()
                pick = hits(block, range(shared)).astype(BF16)
                found = dot(pick, rows_all[group, j], NN).astype(BF16)
                for i in range(shared):
                    x_refs[i][block * CAP : (block + 1) * CAP, :] = found[i * CAP : (i + 1) * CAP]
                cot_copy(number).wait()
                found = dot(pick, r.cot[number % 2], NN).astype(BF16)
                for i in range(shared):
                    c_refs[i][block * CAP : (block + 1) * CAP, :] = found[i * CAP : (i + 1) * CAP]

            for number, (group, j) in enumerate(order):
                if j:
                    for tree in sorted(trees[group], key=lambda tree: place_of(tree.order, j)):
                        tree.receive(j)
                        tree.send(j)
                elif group:
                    copies.wait(rows_all.at[1, 0], me, across)
                    for tree in trees[1]:
                        tree.send(0)
                fill(number)
        else:
            greet(list(peers.values()))
        if last:
            gates = r.gates
            if index:
                gates[...] = r.gates_in[...]
        else:
            gates = r.gates
        for copy in loads:
            copy.wait()
        x_all, c_all = x_refs[index], c_refs[index]
        y_all, d_all = r.y, r.d

        def work(step, carry):
            rows = pl.ds(pl.multiple_of(step * tile, 16), tile)
            x = x_all[rows, :]
            gate = dot(x, weights[0], NT)
            up = dot(x, weights[1], NT)
            sigmoid = 1.0 / (1.0 + jnp.exp(-gate))
            silu = gate * sigmoid
            activation = (silu * up).astype(BF16)
            act[rows, :] = activation
            made = dot(activation, weights[2], NN)
            cot = c_all[rows, :].astype(F32)
            chosen, scores = [], []
            dots = jnp.sum(cot * made, -1, keepdims=True)
            for b in range(per_tile):
                block = step * per_tile + b
                hit = hits(block, (index,))
                chance = tables[block, pl.ds(4 + index, 1), :]
                chosen.append(jnp.sum(jnp.where(hit, chance, 0.0), -1, keepdims=True))
                here = dots[b * CAP : (b + 1) * CAP]
                gates[block, pl.ds(index, 1), :] = jnp.sum(
                    jnp.where(hit, here, 0.0), 0, keepdims=True
                )
            share = jnp.concatenate(chosen, 0)
            y_all[rows, :] = (share * made).astype(BF16)
            back = (share * cot).astype(BF16)
            grad_rows[rows, :] = back
            grad_act = dot(back, weights[2], NT)
            grad_gate = grad_act * up * sigmoid * (1.0 + gate * (1.0 - sigmoid))
            grad_gate = grad_gate.astype(BF16)
            grad_up = (grad_act * silu).astype(BF16)
            pair[rows, pl.ds(0, units)] = grad_gate
            pair[rows, pl.ds(units, units)] = grad_up
            d_all[rows, :] = (dot(grad_gate, weights[0], NN) + dot(grad_up, weights[1], NN)).astype(
                BF16
            )
            return carry

        lax.fori_loop(0, blocks // per_tile, work, 0)

        def weight_grad(k):
            x, back = x_all[...], grad_rows[...]
            for c, source in enumerate((pair, pair, act)):
                columns = pl.ds(k * hidden + (units if c == 1 else 0), hidden)
                rhs = back if c == 2 else x
                r.grad[k][c] = dot(source[:, columns], rhs, TN).astype(BF16)

        if not last:
            for k in range(n_mp):
                weight_grad(k)
        else:
            y_refs = r.y_before + [y_all]
            d_refs = r.d_before + [d_all]
            reduce = TokenReduce(copies, n_dp, me, r.grads_all, r.rooms, r.across)
            back = range(groups)[::-1]
            order = [(g, j) for g in back for j in range(1, n_dp, 2)]
            order += [(g, j) for g in back for j in range(0, n_dp, 2)]

            def sum_copy(number):
                group, j = order[number]
                return pltpu.make_async_copy(
                    r.sums.at[number % 2], r.terms.at[group, j], r.sum_sems.at[number % 2]
                )

            sent = {}
            own_gates = pltpu.make_async_copy(
                gates.at[0], r.gate_parts.at[dp, kind], r.gate_sem.at[0]
            )
            own_gates.start()
            for number, (group, j) in enumerate(order):
                block = group * n_dp + j
                if group + j:
                    sent[group, j] = copies.slot()
                    copies.start(
                        gates.at[block],
                        r.gate_parts.at[dp, kind],
                        peers[group, j],
                        sent[group, j],
                    )
                pick = hits(block, range(shared)).astype(BF16)
                there = rows_of(block)
                found = jnp.concatenate([ref[there, :] for ref in d_refs], 0)
                r.grads_all[group, j] = dot(pick, found, TN).astype(BF16)
                if j % 2:
                    reduce.first(group, j)
                found = jnp.concatenate([ref[there, :] for ref in y_refs], 0)
                if number > 1:
                    sum_copy(number - 2).wait()
                r.sums[number % 2] = dot(pick, found, TN).astype(BF16)
                sum_copy(number).start()
            left = list(range(n_mp))

            def some(count):
                for _ in range(count):
                    if left:
                        weight_grad(left.pop(0))

            for p in range(reduce.last - 1, -1, -1):
                reduce.level(1, p)
                some(1)
            reduce.pass_on()
            for p in range(reduce.last - 1, -1, -1):
                reduce.level(0, p)
                some(1)
            some(n_mp)
            reduce.end(r.total)
            for number in (blocks - 2, blocks - 1):
                sum_copy(number).wait()
            own_gates.wait()
            for (group, j), device in peers.items():
                theirs = 1 - kind if group else kind
                copies.wait(r.gate_parts.at[device[0], theirs], me, sent[group, j])
        copies.finish()

    return launch(expert, identity, ins, outs, scratch, n_copies, 60 << 20)


def adamw(weight, gradient, moment_one, moment_two, rate_val, decay_val):
    first_new = 0.9 * moment_one + 0.1 * gradient
    second_new = 0.95 * moment_two + 0.05 * gradient * gradient
    first_hat = first_new / (1.0 - 0.9**STEP)
    second_hat = second_new / (1.0 - 0.95**STEP)
    weight_new = weight - rate_val * (
        first_hat / (jnp.sqrt(second_hat) + 1e-08) + decay_val * weight
    )
    return (gradient, weight_new, first_new, second_new)


def local(
    n_dp,
    n_mp,
    residual_in,
    cotangent,
    expert_ids,
    attn_gain,
    query_w,
    key_value_weight,
    output_w,
    moe_gain,
    router_w,
    gateup_w,
    down_w,
    attn_gain_mean,
    attn_gain_var,
    query_mean,
    query_var,
    key_value_first_moment,
    key_value_second_moment,
    output_mean,
    output_var,
    moe_gain_mean,
    moe_gain_var,
    router_mean,
    router_var,
    gateup_mean,
    gateup_var,
    down_mean,
    down_var,
):
    mp = lax.axis_index("mp")
    place_in_all = lax.axis_index("dp") * n_mp + mp
    groups = 2 if 2 * n_dp <= 16 else 1
    kind = mp % groups
    tokens = residual_in.shape[0]
    owned = gateup_w.shape[0]
    shared = owned // groups
    hidden_units = down_w.shape[1]
    flips = [[(i, i ^ k) for i in range(n_mp)] for k in range(n_mp)]
    own_gain, own_router = attn_gain.shape[0], router_w.shape[0]
    first_row, lanes = 8, 128
    per_tile = lanes // own_gain

    def spread(gain):
        return jnp.where(jnp.arange(lanes) // own_gain == place_in_all % per_tile, jnp.tile(gain, per_tile), 0.0)

    small = jnp.concatenate(
        [
            spread(attn_gain)[None],
            spread(moe_gain)[None],
            jnp.zeros((first_row - 2, lanes), F32),
            jnp.pad(router_w, ((0, 0), (0, lanes - EXPERTS))),
        ]
    )
    shards = jnp.stack([query_w, key_value_weight, output_w.T]).astype(BF16)
    cot_low = cotangent.astype(BF16)
    start = prologue(n_dp, n_mp, groups, 0, small, shards, cot_low, residual_in)
    small_all = start.small_all
    gains = [
        jnp.sum(small_all[:, :, row].reshape(-1, per_tile, lanes), 1).reshape(1, -1) for row in (0, 1)
    ]
    router_low = small_all[:, :, first_row:].reshape(MODEL_WIDTH, lanes).astype(BF16)

    expert_range = jnp.arange(EXPERTS, dtype=jnp.int32)
    onehot = (expert_ids[:, :, None] == expert_range[None, None, :]).astype(jnp.int32)
    chosen = jnp.sum(onehot, 1)
    before = jnp.cumsum(chosen, 0) - chosen
    place = jnp.where(chosen > 0, before, -1)
    by_owner = place.astype(F32).T.reshape(n_dp, shared, groups, tokens).transpose(0, 2, 1, 3)
    places = jnp.pad(by_owner, ((0, 0), (0, 0), (0, 8 - shared), (0, 0)))

    packed = jnp.concatenate([gateup_w, down_w[:, None]], 1).astype(BF16)

    def send_weights(i, after):
        mine = theirs = packed[groups * i]
        if groups > 1:
            mine = jnp.where(kind == 0, packed[2 * i], packed[2 * i + 1])
            theirs = jnp.where(kind == 0, packed[2 * i + 1], packed[2 * i])
        mine, theirs, after = lax.optimization_barrier((mine, theirs, after))
        parts = [mine] + [
            lax.ppermute(theirs if k % 2 else mine, "mp", flips[k]) for k in range(1, n_mp)
        ]
        return parts, after

    expert_parts = [None] * shared
    expert_parts[0], row_block = send_weights(0, start.row_block)
    whole = gather_rows(n_dp, groups, 1, row_block, cot_low)
    full = whole.full

    query_table, key_table = (jnp.asarray(table) for table in rotary_constants())
    part = mp % 2
    rotary = [
        lax.dynamic_slice_in_dim(table, which * tokens, tokens, 1)
        for table, which in ((query_table, part), (key_table, part), (key_table, 1 - part))
    ]
    front = attention_forward(
        n_dp,
        groups,
        shared,
        2,
        residual_in,
        start.normed,
        full,
        gains[1],
        router_low,
        places,
        whole.cot_other,
        rotary,
    )

    rows = front.normed_two
    for i in range(1, shared):
        expert_parts[i], (rows, expert_parts[i - 1]) = send_weights(i, (rows, expert_parts[i - 1]))
    made = types.SimpleNamespace(
        rows=rows, table=front.table, cots=[start.cots, front.cots][:groups], y=[], d=[]
    )
    expert_grads = []
    for i in range(shared):
        found = run_expert(n_dp, n_mp, groups, 3 + i, i, shared, expert_parts[i], made)
        if i < shared - 1:
            made.gates = found.gates
            made.y, made.d = made.y + [found.y], made.d + [found.d]
            if i == 0:
                made.tables, made.x, made.c = found.tables, [None] + found.x, [None] + found.c
        if i < shared - 1:
            expert_grads.append(
                found.grad[:1]
                + [lax.ppermute(found.grad[k], "mp", flips[k]) for k in range(1, n_mp)]
            )
    total, expert_grads = lax.optimization_barrier((found.total, expert_grads))
    given = types.SimpleNamespace(
        full=full,
        residual=residual_in,
        hidden=front.hidden,
        cotangent=cotangent,
        total=total,
        expert_grads=found.grad[1:],
        gate_parts=found.gate_parts,
        terms=found.terms,
        probs=front.probs,
        normed=start.normed,
        normed_two=front.normed_two,
        queries=front.queries,
        keyval=front.keyval,
        context=front.context,
        gain_one=gains[0],
        gain_two=gains[1],
        router=router_low,
        rotary=rotary,
    )
    back = attention_backward(n_dp, n_mp, groups, shared, 3 + shared, given, first_row)
    input_grad, block_out = back.input_grad, back.block_out
    expert_grads = expert_grads + [found.grad[:1] + back.arrived]
    pairs = []
    for i in range(shared):
        if groups == 1:
            pairs.append(sum(part.astype(F32) for part in expert_grads[i]))
            continue
        same = sum(part.astype(F32) for part in expert_grads[i][0::2])
        turned = sum(part.astype(F32) for part in expert_grads[i][1::2])
        pairs.append(jnp.where(kind == 0, same, turned))
        pairs.append(jnp.where(kind == 0, turned, same))
    expert_grad = jnp.stack(pairs)
    gateup_grad, down_grad = expert_grad[:, :2], expert_grad[:, 2]

    grads, small_grads = back.shards, back.small_shard
    query_grad, keyval_grad, output_grad = grads[0], grads[1], grads[2].T
    first_lane = (place_in_all % per_tile) * own_gain
    gain_one_grad, gain_two_grad = (
        lax.dynamic_slice_in_dim(small_grads[row], first_lane, own_gain) for row in (0, 1)
    )
    router_grad = small_grads[first_row:, :EXPERTS]
    matrix_rate = 0.2 / math.sqrt(MODEL_WIDTH)
    gain_one_all = adamw(attn_gain, gain_one_grad, attn_gain_mean, attn_gain_var, 0.1, 0.0)
    query_all = adamw(query_w, query_grad, query_mean, query_var, matrix_rate, 0.1)
    keyval_all = adamw(
        key_value_weight,
        keyval_grad,
        key_value_first_moment,
        key_value_second_moment,
        matrix_rate,
        0.1,
    )
    output_all = adamw(output_w, output_grad, output_mean, output_var, 0.1, 0.1)
    gain_two_all = adamw(moe_gain, gain_two_grad, moe_gain_mean, moe_gain_var, 0.1, 0.0)
    router_all = adamw(router_w, router_grad, router_mean, router_var, matrix_rate, 0.1)
    gateup_all = adamw(gateup_w, gateup_grad, gateup_mean, gateup_var, matrix_rate, 0.1)
    down_all = adamw(down_w, down_grad, down_mean, down_var, 0.07, 0.1)
    return (
        block_out,
        input_grad,
        gain_one_all[0],
        gain_one_all[1],
        gain_one_all[2],
        gain_one_all[3],
        query_all[0],
        query_all[1],
        query_all[2],
        query_all[3],
        keyval_all[0],
        keyval_all[1],
        keyval_all[2],
        keyval_all[3],
        output_all[0],
        output_all[1],
        output_all[2],
        output_all[3],
        gain_two_all[0],
        gain_two_all[1],
        gain_two_all[2],
        gain_two_all[3],
        router_all[0],
        router_all[1],
        router_all[2],
        router_all[3],
        gateup_all[0],
        gateup_all[1],
        gateup_all[2],
        gateup_all[3],
        down_all[0],
        down_all[1],
        down_all[2],
        down_all[3],
    )


def solution(mesh):
    in_specs = (
        P(("dp", "mp"), None),
        P(("dp", "mp"), None),
        P(("dp", "mp"), None),
        P(("dp", "mp")),
        P("dp", "mp"),
        P("dp", "mp"),
        P("mp", "dp"),
        P(("dp", "mp")),
        P(("dp", "mp"), None),
        P("dp", None, "mp", None),
        P("dp", "mp", None),
        P(("dp", "mp")),
        P(("dp", "mp")),
        P("dp", "mp"),
        P("dp", "mp"),
        P("dp", "mp"),
        P("dp", "mp"),
        P("mp", "dp"),
        P("mp", "dp"),
        P(("dp", "mp")),
        P(("dp", "mp")),
        P(("dp", "mp"), None),
        P(("dp", "mp"), None),
        P("dp", None, "mp", None),
        P("dp", None, "mp", None),
        P("dp", "mp", None),
        P("dp", "mp", None),
    )
    out_specs = (
        P(("dp", "mp"), None),
        P(("dp", "mp"), None),
        P(("dp", "mp")),
        P(("dp", "mp")),
        P(("dp", "mp")),
        P(("dp", "mp")),
        P("dp", "mp"),
        P("dp", "mp"),
        P("dp", "mp"),
        P("dp", "mp"),
        P("dp", "mp"),
        P("dp", "mp"),
        P("dp", "mp"),
        P("dp", "mp"),
        P("mp", "dp"),
        P("mp", "dp"),
        P("mp", "dp"),
        P("mp", "dp"),
        P(("dp", "mp")),
        P(("dp", "mp")),
        P(("dp", "mp")),
        P(("dp", "mp")),
        P(("dp", "mp"), None),
        P(("dp", "mp"), None),
        P(("dp", "mp"), None),
        P(("dp", "mp"), None),
        P("dp", None, "mp", None),
        P("dp", None, "mp", None),
        P("dp", None, "mp", None),
        P("dp", None, "mp", None),
        P("dp", "mp", None),
        P("dp", "mp", None),
        P("dp", "mp", None),
        P("dp", "mp", None),
    )
    step = functools.partial(local, mesh.shape["dp"], mesh.shape["mp"])
    return jax.shard_map(step, mesh=mesh, in_specs=in_specs, out_specs=out_specs, check_vma=False)
```

```python
import functools
import math
import types

import jax
import jax.numpy as jnp
import numpy as np
from jax import lax
from jax.experimental import pallas as pl
from jax.experimental.pallas import tpu as pltpu
from jax.sharding import PartitionSpec as P

MODEL_WIDTH = 1024
QUERY_HEADS = 16
KEY_VALUE_HEADS = 8
HEAD_SIZE = 64
EXPERTS = 32
TOPK = 8
SEQUENCE_TOKENS = 512
STEP = 3
CAP = 80

NORM_EPS = 1e-06
MESH = pl.DeviceIdType.MESH
BF16 = jnp.bfloat16
F32 = jnp.float32


def flip(index, mask):
    return index + mask * (1 - 2 * lax.rem(lax.div(index, mask), 2))


def flip_all(index, masks):
    bit = 1
    while bit <= masks:
        if masks & bit:
            index = flip(index, bit)
        bit *= 2
    return index


def bits_of(size):
    return [1 << i for i in range(size.bit_length() - 1)]


def orders_of(n_dp):
    bits = bits_of(n_dp)
    return bits[1:] + bits[:1], bits[1:][::-1] + bits[:1]


def place_of(order, j):
    place = -1
    for at, mask in enumerate(order):
        if j & mask:
            place = at
    return place


def greet(partners):
    barrier = pltpu.get_barrier_semaphore()
    for partner in partners:
        pl.semaphore_signal(barrier, inc=1, device_id=partner, device_id_type=MESH)
    pl.semaphore_wait(barrier, len(partners))


class Copies:
    def __init__(self, send_sems, recv_sems):
        self.send_sems, self.recv_sems = send_sems, recv_sems
        self.used = 0
        self.sent = []

    def slot(self):
        self.used += 1
        return self.used - 1

    def make(self, source, target, device, slot):
        return pltpu.make_async_remote_copy(
            src_ref=source,
            dst_ref=target,
            send_sem=self.send_sems.at[slot],
            recv_sem=self.recv_sems.at[slot],
            device_id=device,
            device_id_type=MESH,
        )

    def start(self, source, target, device, slot):
        copy = self.make(source, target, device, slot)
        copy.start()
        self.sent.append(copy)

    def wait(self, target, device, slot):
        self.make(target, target, device, slot).wait_recv()

    def finish(self):
        for copy in self.sent:
            copy.wait_send()
        self.sent = []


class TreeGather:
    def __init__(self, copies, order, n_dp, me, source, target):
        self.copies, self.order, self.n_dp, self.me = copies, order, n_dp, me
        self.source, self.target = source, target
        self.slots = {j: copies.slot() for j in range(1, n_dp)}

    def level(self, j):
        return bin(j).count("1")

    def send(self, j):
        dp, mp = self.me
        for mask in self.order[place_of(self.order, j) + 1 :]:
            self.copies.start(
                self.source(j), self.target(j, mask), (flip(dp, mask), mp), self.slots[j ^ mask]
            )

    def receive(self, j):
        self.copies.wait(self.source(j), self.me, self.slots[j])

    def steps(self):
        return sorted(range(1, self.n_dp), key=lambda j: (self.level(j), place_of(self.order, j)))


def run_gathers(trees):
    n_dp = trees[0].n_dp
    for level in range(1, n_dp.bit_length()):
        for tree in trees:
            for j in tree.steps():
                if tree.level(j) == level:
                    tree.receive(j)
                    tree.send(j)


class TreeReduce:
    def __init__(self, copies, order, n_dp, me, block, room, add):
        self.copies, self.order, self.n_dp, self.me = copies, order, n_dp, me
        self.block, self.room, self.add = block, room, add
        self.keys = [
            (j, q) for j in range(n_dp) for q in range(len(order) - 1, place_of(order, j), -1)
        ]
        self.slots = {key: copies.slot() for key in self.keys}

    def number(self, key):
        return self.keys.index(key)

    def send(self, j):
        dp, mp = self.me
        p = place_of(self.order, j)
        last = len(self.order) - 1
        source = self.block(j) if p == last else self.room(self.number((j, last)))
        mask = self.order[p]
        key = (j ^ mask, p)
        self.copies.start(source, self.room(self.number(key)), (flip(dp, mask), mp), self.slots[key])

    def collect(self, j):
        last = len(self.order) - 1
        for q in range(last, place_of(self.order, j), -1):
            here = self.room(self.number((j, q)))
            self.copies.wait(here, self.me, self.slots[(j, q)])
            if q == last:
                self.add(here, self.block(j))
            else:
                self.add(self.room(self.number((j, last))), here)

    def total(self):
        return self.room(self.number((0, len(self.order) - 1)))


def add_rows(step=16):
    def add(here, other):
        def body(i, carry):
            rows = pl.ds(pl.multiple_of(i * step, step), step)
            total = here[..., rows, :].astype(F32) + other[..., rows, :].astype(F32)
            here[..., rows, :] = total.astype(here.dtype)
            return carry

        lax.fori_loop(0, here.shape[-2] // step, body, 0)

    return add


def hbm():
    return pl.BlockSpec(memory_space=pl.ANY)


def vmem():
    return pl.BlockSpec(memory_space=pltpu.VMEM)


def params(identity, limit=None):
    return pltpu.CompilerParams(
        collective_id=identity, has_side_effects=True, vmem_limit_bytes=limit
    )


def launch(kernel, identity, ins, outs, scratch, n_copies, limit=None):
    def flat(entries):
        names, leaves, specs = [], [], []
        for name, (value, spec) in entries.items():
            several = isinstance(value, list)
            new = value if several else [value]
            names.append((name, len(new) if several else None))
            leaves += new
            specs += [spec] * len(new)
        return names, leaves, specs

    def unflat(names, leaves):
        leaves, found = list(leaves), {}
        for name, count in names:
            found[name] = leaves[0] if count is None else leaves[:count]
            leaves = leaves[1 if count is None else count :]
        return found

    scratch = scratch | dict(
        send_sems=pltpu.SemaphoreType.DMA((n_copies,)),
        recv_sems=pltpu.SemaphoreType.DMA((n_copies,)),
    )
    in_names, values, in_specs = flat(ins)
    out_names, shapes, out_specs = flat(outs)
    scratch_names = [(name, None) for name in scratch]

    def body(*refs):
        named = unflat(in_names + out_names + scratch_names, refs)
        kernel(types.SimpleNamespace(**named))

    results = pl.pallas_call(
        body,
        out_shape=tuple(shapes),
        in_specs=in_specs,
        out_specs=tuple(out_specs),
        scratch_shapes=list(scratch.values()),
        compiler_params=params(identity, limit),
        cost_estimate=pl.CostEstimate(flops=1, bytes_accessed=1, transcendentals=0),
        name=kernel.__name__,
    )(*values)
    return types.SimpleNamespace(**unflat(out_names, results))


def low(*shape):
    return jax.ShapeDtypeStruct(shape, BF16)


def single(*shape):
    return jax.ShapeDtypeStruct(shape, F32)


def dot(a, b, contract):
    return lax.dot_general(a, b, ((contract[:1], contract[1:]), ((), ())), preferred_element_type=F32)


NN, NT, TN = (1, 0), (1, 1), (0, 0)


def prologue(n_dp, n_mp, groups, identity, small, shards, cot, residual):
    half = n_mp // 2
    kinds, rows, cols = shards.shape
    tokens, width = cot.shape
    order_a, _ = orders_of(n_dp)
    n_copies = 2 * (n_mp - 1) + 4 * (n_dp - 1) + 1

    def gather_line(r):
        dp, mp = lax.axis_index("dp"), lax.axis_index("mp")
        me = (dp, mp)
        neighbour = (dp, flip(mp, 1))
        copies = Copies(r.send_sems, r.recv_sems)
        own_small = r.small_all.at[dp, mp]
        own_cols = pl.ds(pl.multiple_of(mp * cols, cols), cols)
        own_part = r.row_block.at[:, :, own_cols]
        r.small_all[dp, mp] = r.small[...]
        residual_rows = r.residual[...]
        inverse = lax.rsqrt(jnp.mean(residual_rows * residual_rows, -1, keepdims=True) + NORM_EPS)
        r.scaled[0] = (residual_rows * inverse).astype(BF16)
        r.row_block[:, :, own_cols] = r.shards[...]
        r.cots[0] = r.cot[...]
        greet(
            [(flip_all(dp, mask), mp) for mask in bits_of(n_dp)]
            + [(dp, flip_all(mp, k)) for k in range(1, n_mp)]
        )
        near = lax.div(mp, half)
        line = {}
        for k in range(1, n_mp):
            line[k] = (copies.slot(), copies.slot())
            copies.start(r.small, own_small, (dp, flip_all(mp, k)), line[k][0])
        across = copies.slot()
        copies.start(r.scaled.at[0], r.scaled.at[1], neighbour, across)
        for k in range(1, n_mp):
            copies.start(r.shards, own_part, (dp, flip_all(mp, k)), line[k][1])

        def small_tree(chunk):
            first = pl.multiple_of(chunk * half, half)

            def ref(j, mask=0):
                return r.small_all.at[flip_all(dp, j), pl.ds(first, half)]

            return TreeGather(copies, order_a, n_dp, me, ref, ref)

        small_trees = [small_tree(chunk) for chunk in (near, 1 - near)]
        cot_trees = row_trees(copies, n_dp, me, r.cots)
        for chunk in (0, 1):
            for k in range(1, half) if chunk == 0 else range(half, n_mp):
                copies.wait(r.small_all.at[dp, flip_all(mp, k)], me, line[k][0])
            small_trees[chunk].send(0)
        for one in cot_trees:
            one.send(0)
        top = n_dp.bit_length() - 1
        for level in range(1, top + 1):
            run_level(small_trees, level)
            run_level(cot_trees, level)
        for k in range(1, n_mp):
            other = pl.multiple_of(flip_all(mp, k) * cols, cols)
            copies.wait(r.row_block.at[:, :, pl.ds(other, cols)], me, line[k][1])
        copies.wait(r.scaled.at[1], me, across)
        copies.finish()

    return launch(
        gather_line,
        identity,
        dict(
            small=(small, vmem()), shards=(shards, vmem()), cot=(cot, vmem()), residual=(residual, vmem())
        ),
        dict(
            small_all=(single(n_dp, n_mp, *small.shape), vmem()),
            row_block=(low(kinds, rows, n_mp * cols), vmem()),
            cots=(low(n_dp, tokens, width), vmem()),
            scaled=(low(2, tokens, width), vmem()),
        ),
        {},
        n_copies,
        32 << 20,
    )


def run_level(trees, level):
    for one in trees:
        for j in one.steps():
            if one.level(j) == level:
                one.receive(j)
                one.send(j)


def send_experts(copies, me, span, packed, near, experts):
    dp, mp = me
    slots = {}
    for i, expert in enumerate(experts):
        for k in range(1, span):
            slots[i, k] = copies.slot()
            copies.start(
                packed.at[expert], near[k - 1].at[i], (dp, flip_all(mp, k)), slots[i, k]
            )
    return slots


def wait_experts(copies, me, near, slots):
    for (i, k), slot in slots.items():
        copies.wait(near[k - 1].at[i], me, slot)


def gather_rows(n_dp, n_mp, groups, identity, row_block, cot, packed, experts):
    span = n_mp // groups
    n_experts = len(experts)
    kinds, rows, width = row_block.shape
    part_rows = rows // 2

    def gather_weights(r):
        dp, mp = lax.axis_index("dp"), lax.axis_index("mp")
        me = (dp, mp)
        copies = Copies(r.send_sems, r.recv_sems)
        partner = (dp, flip_all(mp, span))
        r.full[:, pl.ds(pl.multiple_of(dp * rows, rows), rows), :] = r.row_block[...]
        greet(
            [(flip_all(dp, mask), mp) for mask in bits_of(n_dp)]
            + [partner] * (groups - 1)
            + [(dp, flip_all(mp, k)) for k in range(1, span)]
        )
        across = copies.slot()
        if groups > 1:
            copies.start(r.cot, r.cot_other, partner, across)
        sent = send_experts(copies, me, span, r.packed, r.near, experts)

        def tree(part, order):
            def ref(j, mask=0):
                start = flip_all(dp, j) * rows + part * part_rows
                return r.full.at[:, pl.ds(pl.multiple_of(start, part_rows), part_rows), :]

            return TreeGather(copies, order, n_dp, me, ref, ref)

        trees = [tree(part, order) for part, order in enumerate(orders_of(n_dp))]
        for one in trees:
            one.send(0)
        run_gathers(trees)
        if groups > 1:
            copies.wait(r.cot_other, me, across)
        wait_experts(copies, me, r.near, sent)
        copies.finish()

    return launch(
        gather_weights,
        identity,
        dict(row_block=(row_block, vmem()), cot=(cot, vmem()), packed=(packed, hbm())),
        dict(
            full=(low(kinds, n_dp * rows, width), vmem()),
            cot_other=(low(*cot.shape), vmem()),
            near=([low(n_experts, *packed.shape[1:]) for _ in range(1, span)], hbm()),
        ),
        {},
        2 * (n_dp - 1) + 1 + n_experts * (span - 1),
        32 << 20,
    )


def row_trees(copies, n_dp, me, rows_all):
    tokens = rows_all.shape[1]

    def tree(part, order):
        cut = pl.ds(part * (tokens // 2), tokens // 2)
        return TreeGather(
            copies,
            order,
            n_dp,
            me,
            lambda j: rows_all.at[j, cut],
            lambda j, mask: rows_all.at[j ^ mask, cut],
        )

    return [tree(part, order) for part, order in enumerate(orders_of(n_dp))]


def rotary_constants():
    half_width = HEAD_SIZE // 2
    frequency = np.exp(
        np.float32(-math.log(10000.0)) * np.arange(half_width, dtype=np.float32) * np.float32(2.0)
        / np.float32(HEAD_SIZE)
    ).astype(np.float32)
    angles = np.arange(SEQUENCE_TOKENS, dtype=np.float32)[:, None] * frequency[None, :]
    cosine, sine = np.cos(angles), np.sin(angles)
    cosine = np.concatenate([cosine, cosine], 1)
    sine = np.concatenate([-sine, sine], 1)
    queries = np.stack([np.tile(cosine, (1, 2)), np.tile(sine, (1, 2))])
    keys = np.stack(
        [
            np.concatenate([cosine, np.ones_like(cosine)], 1),
            np.concatenate([sine, np.zeros_like(sine)], 1),
        ]
    )
    return queries.astype(np.float32), keys.astype(np.float32)


def rotate(value, cosine, sine):
    lane = lax.broadcasted_iota(jnp.int32, value.shape, 1)
    rolled = jnp.where(
        lane % HEAD_SIZE < HEAD_SIZE // 2,
        pltpu.roll(value, 128 - HEAD_SIZE // 2, 1),
        pltpu.roll(value, HEAD_SIZE // 2, 1),
    )
    return value * cosine + rolled * sine


def group_operands(queries, keyval):
    lane = lax.broadcasted_iota(jnp.int32, queries.shape, 1)
    both = jnp.concatenate(
        [jnp.where(lane < HEAD_SIZE, queries, 0.0), jnp.where(lane < HEAD_SIZE, 0.0, queries)], 0
    ).astype(BF16)
    lane = lax.broadcasted_iota(jnp.int32, keyval.shape, 1)
    turned = pltpu.roll(keyval, HEAD_SIZE, 1)
    keys = jnp.where(lane < HEAD_SIZE, keyval, turned).astype(BF16)
    values = jnp.where(lane < HEAD_SIZE, turned, keyval).astype(BF16)
    return both, keys, values


def merge_heads(both):
    tokens = both.shape[0] // 2
    lane = lax.broadcasted_iota(jnp.int32, (tokens, 128), 1)
    return jnp.where(lane < HEAD_SIZE, both[:tokens], both[tokens:])


def seen(tokens, mp):
    shape = (2 * tokens, 2 * tokens)
    row = lax.broadcasted_iota(jnp.int32, shape, 0) % tokens
    key = lax.broadcasted_iota(jnp.int32, shape, 1)
    shift = tokens - 2 * tokens * lax.rem(mp, 2)
    key = jnp.where(key < tokens, key, key - tokens + shift)
    return key <= row


def softmax_of(both, keys, mask):
    scores = dot(both, keys, NT) * (1.0 / math.sqrt(HEAD_SIZE))
    raised = jnp.exp(jnp.where(mask, scores, -1e30))
    return raised / jnp.sum(raised, -1, keepdims=True)


def attention_forward(
    n_dp, n_mp, groups, identity, residual, scaled, full, gains, router, places, cot_other, rotary, packed, experts
):
    tokens, width = residual.shape
    query_rotary, own_rotary, other_rotary = rotary
    n_heads = width // 128
    span = n_mp // groups
    owned = EXPERTS // n_dp
    n_experts = len(experts)
    n_copies = 2 * (n_dp - 1) + n_experts * (span - 1)

    def attention(r):
        dp, mp = lax.axis_index("dp"), lax.axis_index("mp")
        me = (dp, mp)
        copies = Copies(r.send_sems, r.recv_sems)
        loads = [
            pltpu.make_async_copy(r.full.at[c], r.weights.at[c], r.local_sems.at[c])
            for c in range(3)
        ]
        for copy in loads:
            copy.start()
        r.cots[0] = r.cot_other[...]
        greet(
            [(flip_all(dp, mask), mp) for mask in bits_of(n_dp)]
            + [(dp, flip_all(mp, k)) for k in range(1, span)]
        )
        sent = send_experts(copies, me, span, r.packed, r.near, experts)
        trees = row_trees(copies, n_dp, me, r.cots) if groups > 1 else []
        for one in trees:
            one.send(0)
        top = n_dp.bit_length() - 1
        residual = r.residual[...]
        inverse = lax.rsqrt(jnp.mean(residual * residual, -1, keepdims=True) + NORM_EPS)
        gain_one = r.gains[0:1, :]
        r.normed[0] = (residual * inverse * gain_one).astype(BF16)
        r.normed[1] = (r.scaled[1].astype(F32) * gain_one).astype(BF16)
        loads[0].wait()
        r.q[...] = dot(r.normed[0], r.weights[0], NN)
        loads[1].wait()
        for part in (0, 1):
            r.kv[part] = dot(r.normed[part], r.weights[1], NN)
        run_level(trees, 1)
        mask = seen(tokens, mp)

        def head(k, carry):
            lanes = pl.ds(pl.multiple_of(k * 128, 128), 128)
            queries = rotate(r.q[:, lanes], r.query_rotary[0], r.query_rotary[1])
            r.queries[:, lanes] = queries.astype(BF16)
            parts = []
            for part, table in enumerate((r.own_rotary, r.other_rotary)):
                parts.append(rotate(r.kv[part, :, lanes], table[0], table[1]))
                r.keyval[part, :, lanes] = parts[part].astype(BF16)
            both, keys, values = group_operands(queries, jnp.concatenate(parts, 0))
            chance = softmax_of(both, keys, mask).astype(BF16)
            r.context[:, lanes] = merge_heads(dot(chance, values, NN)).astype(BF16)
            return carry

        for level in range(2, top + 1):
            first, end = [(level - 2 + i) * n_heads // (top - 1) for i in (0, 1)]
            lax.fori_loop(first, end, head, 0)
            run_level(trees, level)
        loads[2].wait()
        hidden = r.residual[...] + dot(r.context[...], r.weights[2], NT)
        r.hidden[...] = hidden
        inverse = lax.rsqrt(jnp.mean(hidden * hidden, -1, keepdims=True) + NORM_EPS)
        normed = (hidden * inverse * r.gains[1:2, :]).astype(BF16)
        r.normed_two[...] = normed
        logits = dot(normed, r.router[...], NN)
        lane = lax.broadcasted_iota(jnp.int32, logits.shape, 1)
        raised = jnp.where(lane < EXPERTS, jnp.exp(logits), 0.0)
        probs = raised / jnp.sum(raised, -1, keepdims=True)
        r.probs[...] = probs
        turned = probs.T
        r.table[...] = r.places[...]
        for expert in range(EXPERTS):
            owner, which = divmod(expert, owned)
            r.table[owner, 4 + which, :] = turned[expert]
        wait_experts(copies, me, r.near, sent)
        copies.finish()

    return launch(
        attention,
        identity,
        dict(
            residual=(residual, vmem()),
            scaled=(scaled, vmem()),
            full=(full, hbm()),
            gains=(gains, vmem()),
            packed=(packed, hbm()),
            router=(router, vmem()),
            places=(places, vmem()),
            cot_other=(cot_other, vmem()),
            query_rotary=(query_rotary, vmem()),
            own_rotary=(own_rotary, vmem()),
            other_rotary=(other_rotary, vmem()),
        ),
        dict(
            cots=(low(n_dp, tokens, width), vmem()),
            near=([low(n_experts, *packed.shape[1:]) for _ in range(1, span)], hbm()),
            normed=(low(2, tokens, width), vmem()),
            queries=(low(tokens, width), vmem()),
            keyval=(low(2, tokens, width), vmem()),
            context=(low(tokens, width), vmem()),
            hidden=(single(tokens, width), vmem()),
            normed_two=(low(tokens, width), vmem()),
            probs=(single(tokens, 128), vmem()),
            table=(single(*places.shape), vmem()),
        ),
        dict(
            weights=pltpu.VMEM((3, width, width), BF16),
            q=pltpu.VMEM((tokens, width), F32),
            kv=pltpu.VMEM((2, tokens, width), F32),
            local_sems=pltpu.SemaphoreType.DMA((3,)),
        ),
        n_copies,
        48 << 20,
    )


def attention_backward(n_dp, n_mp, groups, identity, given, first_row):
    tokens, width = given.residual.shape
    n_heads = width // 128
    n_devices = n_dp * n_mp
    own_router = width // n_devices
    per_tile = n_devices // n_heads
    rows, cols = width // n_dp, width // n_mp
    part_rows = rows // 2
    orders = orders_of(n_dp)
    span = n_mp // groups
    owned = EXPERTS // n_dp
    n_late = given.late[0].shape[0] if given.late else 0
    n_copies = (2 * groups + 7) * (n_dp - 1) + 1 + 4 * (n_mp - 1) + 1 + n_late * (span - 1)

    rooms, across_room = reduce_rooms(groups, n_dp, tokens, width, BF16)

    def attention_back(r):
        dp, mp = lax.axis_index("dp"), lax.axis_index("mp")
        me = (dp, mp)
        neighbour = (dp, flip(mp, 1))
        copies = Copies(r.send_sems, r.recv_sems)
        loads = [
            pltpu.make_async_copy(r.full.at[c], r.weights.at[c], r.local_sems.at[c])
            for c in (2, 0, 1)
        ]
        for copy in loads:
            copy.start()
        greet(
            [(flip_all(dp, mask), mp) for mask in bits_of(n_dp)]
            + [(dp, flip_all(mp, k)) for k in range(1, n_mp)]
        )
        partner = (dp, flip_all(mp, span))
        mixture = TokenReduce(copies, n_dp, me, partner, r.terms, r.rooms, r.across)
        for group in range(groups)[::-1]:
            for j in range(1, n_dp, 2):
                mixture.first(group, j)
        last = mixture.last
        travels = {}

        def send_late(i):
            if i < n_late:
                for k in range(1, span):
                    travels[i, k] = copies.slot()
                    copies.start(
                        r.late[k - 1].at[i],
                        r.arrived[k - 1].at[i],
                        (dp, flip_all(mp, k)),
                        travels[i, k],
                    )

        send_late(0)
        r.turned[...] = jnp.zeros_like(r.turned)
        for expert in range(EXPERTS):
            owner, which = divmod(expert, owned)
            parts = r.gate_parts[owner, 0, which, :]
            for group in range(1, groups):
                parts = parts + r.gate_parts[owner, group, which, :]
            r.turned[expert, :] = parts
        grad_probs = r.turned[...].T
        probs = r.probs[...]
        grad_logits = (
            probs * (grad_probs - jnp.sum(probs * grad_probs, -1, keepdims=True))
        ).astype(BF16)
        grad_normed_two = r.total[...] + dot(grad_logits, r.router[...], NT)
        r.grad_router[...] = dot(r.normed_two[...], grad_logits, TN)
        hidden = r.hidden[...]
        inverse = lax.rsqrt(jnp.mean(hidden * hidden, -1, keepdims=True) + NORM_EPS)
        scaled = r.gains[1:2, :] * grad_normed_two
        grad_hidden = (
            r.cotangent[...]
            + inverse * scaled
            - hidden * (inverse * inverse * inverse) * jnp.mean(scaled * hidden, -1, keepdims=True)
        )
        r.grad_hidden[...] = grad_hidden
        gain_two = jnp.sum(grad_normed_two * hidden * inverse, 0, keepdims=True)
        grad_attn = grad_hidden.astype(BF16)
        r.grad_attn[...] = grad_attn
        def weight_tree(c, part):
            def block(j):
                start = flip_all(dp, j) * rows + part * part_rows
                return r.grads.at[c, pl.ds(pl.multiple_of(start, part_rows), part_rows), :]

            return TreeReduce(
                copies,
                orders[part],
                n_dp,
                me,
                block,
                lambda number: r.weight_rooms.at[c, part, number],
                add_rows(),
            )

        weight_trees = [[weight_tree(c, part) for part in (0, 1)] for c in range(3)]

        def weight_level(c, p):
            for j in range(1, n_dp):
                for one in weight_trees[c]:
                    if place_of(one.order, j) == p:
                        if p < last:
                            one.collect(j)
                        one.send(j)

        r.grads[2] = dot(grad_attn, r.context[...], TN).astype(BF16)
        weight_level(2, last)
        mixture.level(1, last - 1)
        loads[0].wait()
        r.grad_context[...] = dot(r.grad_attn[...], r.weights[2], NN).astype(BF16)
        mask = seen(tokens, mp)

        def head(k, carry):
            lanes = pl.ds(pl.multiple_of(k * 128, 128), 128)
            keyval = jnp.concatenate([r.keyval[0, :, lanes], r.keyval[1, :, lanes]], 0)
            both, keys, values = group_operands(r.queries[:, lanes].astype(F32), keyval.astype(F32))
            grad_both = group_operands(r.grad_context[:, lanes].astype(F32), keyval.astype(F32))[0]
            chance = softmax_of(both, keys, mask)
            grad_p = dot(grad_both, values, NT)
            delta = jnp.sum(chance * grad_p, -1, keepdims=True)
            grad_s = (chance * (grad_p - delta)).astype(BF16)
            scale = 1.0 / math.sqrt(HEAD_SIZE)
            grad_q = merge_heads(dot(grad_s, keys, NN)) * scale
            r.grad_q[:, lanes] = rotate(grad_q, r.query_rotary[0], -r.query_rotary[1]).astype(BF16)
            grad_k = dot(grad_s, both, TN) * scale
            grad_v = dot(chance.astype(BF16), grad_both, TN)
            lane = lax.broadcasted_iota(jnp.int32, grad_k.shape, 1)
            grad_kv = jnp.where(
                lane < HEAD_SIZE,
                grad_k + pltpu.roll(grad_k, HEAD_SIZE, 1),
                grad_v + pltpu.roll(grad_v, HEAD_SIZE, 1),
            )
            r.grad_kv[:, lanes] = grad_kv[:tokens]
            r.swap[0, :, lanes] = grad_kv[tokens:].astype(BF16)
            return carry

        sent = {}

        def line_out(c):
            for part, one in enumerate(weight_trees[c]):
                one.collect(0)
                total = one.total()
                for k in range(n_mp):
                    there = pl.ds(pl.multiple_of(flip_all(mp, k) * cols, cols), cols)
                    r.line[0, c, k, pl.ds(part * part_rows, part_rows), :] = total[:, there]
            for k in range(1, n_mp):
                sent[c, k] = copies.slot()
                copies.start(
                    r.line.at[0, c, k], r.line.at[1, c, k], (dp, flip_all(mp, k)), sent[c, k]
                )

        stages = []
        for p in range(last - 2, -1, -1):
            stages.append([lambda p=p: mixture.level(1, p)])
        stages.append([lambda: weight_level(2, last - 1), mixture.pass_on])
        for p in range(last - 1, -1, -1):
            stages.append([lambda p=p: mixture.level(0, p)])
            if p < last - 1:
                stages[-1].append(lambda p=p: weight_level(2, p))
        loops = min(len(stages), n_heads)
        for step in range(loops):
            lax.fori_loop(step * n_heads // loops, (step + 1) * n_heads // loops, head, 0)
            if step == loops - 1:
                across = copies.slot()
                copies.start(r.swap.at[0], r.swap.at[1], neighbour, across)
                for i in range(1, n_late):
                    send_late(i)
            for stage in stages.pop(0):
                stage()
        for stage in sum(stages, []):
            stage()
        r.grads[0] = dot(r.normed[0], r.grad_q[...], TN).astype(BF16)
        weight_level(0, last)
        loads[1].wait()
        r.grad_normed[...] = dot(r.grad_q[...], r.weights[0], NT)
        weight_level(0, last - 1)
        line_out(2)
        copies.wait(r.swap.at[1], me, across)

        def turn_back(k, carry):
            lanes = pl.ds(pl.multiple_of(k * 128, 128), 128)
            total = r.grad_kv[:, lanes] + r.swap[1, :, lanes].astype(F32)
            total = rotate(total, r.own_rotary[0], -r.own_rotary[1])
            r.grad_kv_low[:, lanes] = total.astype(BF16)
            return carry

        lax.fori_loop(0, n_heads, turn_back, 0)
        loads[2].wait()
        r.grads[1] = dot(r.normed[0], r.grad_kv_low[...], TN).astype(BF16)
        weight_level(1, last)
        grad_normed = r.grad_normed[...] + dot(r.grad_kv_low[...], r.weights[1], NT)
        residual = r.residual[...]
        inverse = lax.rsqrt(jnp.mean(residual * residual, -1, keepdims=True) + NORM_EPS)
        scaled = r.gains[0:1, :] * grad_normed
        r.input_grad[...] = (
            r.grad_hidden[...]
            + inverse * scaled
            - residual * (inverse * inverse * inverse) * jnp.mean(scaled * residual, -1, keepdims=True)
        )
        gain_one = jnp.sum(grad_normed * residual * inverse, 0, keepdims=True)
        r.small[...] = jnp.zeros_like(r.small)
        for device in range(n_devices):
            tile = device // per_tile
            owner = r.small.at[device // n_mp, device % n_mp]
            owner[0:1, :] = gain_one[:, tile * 128 : (tile + 1) * 128]
            owner[1:2, :] = gain_two[:, tile * 128 : (tile + 1) * 128]
            owner[first_row : first_row + own_router, :] = r.grad_router[
                device * own_router : (device + 1) * own_router, :
            ]

        def add_whole(here, other):
            here[...] = here[...] + other[...]

        small_tree = TreeReduce(
            copies,
            orders[0],
            n_dp,
            me,
            lambda j: r.small.at[flip_all(dp, j)],
            lambda number: r.small_rooms.at[number],
            add_whole,
        )
        for j in range(1, n_dp):
            if place_of(orders[0], j) == last:
                small_tree.send(j)
        for p in range(last - 1, -1, -1):
            if p < last - 1:
                weight_level(0, p)
            weight_level(1, p)
            for j in range(1, n_dp):
                if place_of(orders[0], j) == p:
                    small_tree.collect(j)
                    small_tree.send(j)
        for c in (0, 1):
            line_out(c)
        small_tree.collect(0)
        small_total = small_tree.total()
        for k in range(1, n_mp):
            device = (dp, flip_all(mp, k))
            sent[k] = copies.slot()
            copies.start(small_total.at[device[1]], r.small_line.at[k], device, sent[k])
        mixture.end(r.block_out)
        r.block_out[...] += r.hidden[...]
        for c in (2, 0, 1):
            r.shards[c] = r.line[0, c, 0].astype(F32)
            for k in range(1, n_mp):
                copies.wait(r.line.at[1, c, k], me, sent[c, k])
                r.shards[c] += r.line[1, c, k].astype(F32)
        r.small_shard[...] = small_total[mp]
        for k in range(1, n_mp):
            copies.wait(r.small_line.at[k], me, sent[k])
            r.small_shard[...] += r.small_line[k]
        wait_experts(copies, me, r.arrived, travels)
        copies.finish()

    return launch(
        attention_back,
        identity,
        dict(
            full=(given.full, hbm()),
            late=(given.late, hbm()),
            residual=(given.residual, vmem()),
            hidden=(given.hidden, vmem()),
            cotangent=(given.cotangent, vmem()),
            total=(given.total, vmem()),
            gate_parts=(given.gate_parts, vmem()),
            terms=(given.terms, vmem()),
            probs=(given.probs, vmem()),
            normed=(given.normed, vmem()),
            normed_two=(given.normed_two, vmem()),
            queries=(given.queries, vmem()),
            keyval=(given.keyval, vmem()),
            context=(given.context, vmem()),
            gains=(given.gains, vmem()),
            router=(given.router, vmem()),
            query_rotary=(given.rotary[0], vmem()),
            own_rotary=(given.rotary[1], vmem()),
        ),
        dict(
            input_grad=(single(tokens, width), vmem()),
            block_out=(single(tokens, width), vmem()),
            arrived=([low(*grad.shape) for grad in given.late], hbm()),
            shards=(single(3, rows, cols), vmem()),
            small_shard=(single(first_row + own_router, 128), vmem()),
        ),
        dict(
            grads=pltpu.VMEM((3, width, width), BF16),
            small=pltpu.VMEM((n_dp, n_mp, first_row + own_router, 128), F32),
            small_rooms=pltpu.VMEM((n_dp - 1, n_mp, first_row + own_router, 128), F32),
            small_line=pltpu.VMEM((n_mp, first_row + own_router, 128), F32),
            weight_rooms=pltpu.VMEM((3, 2, n_dp - 1, part_rows, width), BF16),
            line=pltpu.VMEM((2, 3, n_mp, rows, cols), BF16),
            rooms=rooms,
            across=across_room,
            weights=pltpu.VMEM((3, width, width), BF16),
            turned=pltpu.VMEM((128, tokens), F32),
            grad_router=pltpu.VMEM((width, 128), F32),
            grad_hidden=pltpu.VMEM((tokens, width), F32),
            grad_attn=pltpu.VMEM((tokens, width), BF16),
            grad_context=pltpu.VMEM((tokens, width), BF16),
            grad_q=pltpu.VMEM((tokens, width), BF16),
            grad_kv=pltpu.VMEM((tokens, width), F32),
            grad_kv_low=pltpu.VMEM((tokens, width), BF16),
            grad_normed=pltpu.VMEM((tokens, width), F32),
            swap=pltpu.VMEM((2, tokens, width), BF16),
            local_sems=pltpu.SemaphoreType.DMA((3,)),
        ),
        n_copies,
        62 << 20,
    )


class TokenReduce:
    def __init__(self, copies, n_dp, me, partner, terms, rooms, across):
        self.copies, self.me, self.across = copies, me, across
        self.partner = partner
        self.tokens = terms.shape[2]
        self.n_dp = n_dp
        self.last = n_dp.bit_length() - 2
        self.groups = terms.shape[0]
        self.slot = copies.slot()

        def tree(group, part, order):
            cut = pl.ds(part * (self.tokens // 2), self.tokens // 2)
            return TreeReduce(
                copies,
                order,
                n_dp,
                me,
                lambda j: terms.at[group, j, cut],
                lambda number: rooms.at[group, part, number],
                add_rows(),
            )

        self.trees = [
            [tree(group, part, order) for part, order in enumerate(orders_of(n_dp))]
            for group in range(self.groups)
        ]

    def first(self, group, j):
        for tree in self.trees[group]:
            tree.send(j)

    def level(self, group, p):
        if group == self.groups:
            return
        for j in range(1, self.n_dp):
            for tree in self.trees[group]:
                if place_of(tree.order, j) == p:
                    tree.collect(j)
                    tree.send(j)

    def pass_on(self):
        if self.groups == 1:
            return
        for part, tree in enumerate(self.trees[1]):
            tree.collect(0)
            cut = pl.ds(part * (self.tokens // 2), self.tokens // 2)
            self.across[0, cut, :] = tree.total()[...]
        self.copies.start(self.across.at[0], self.across.at[1], self.partner, self.slot)

    def end(self, out_ref):
        for tree in self.trees[0]:
            tree.collect(0)
        if self.groups > 1:
            self.copies.wait(self.across.at[1], self.me, self.slot)
        for part, tree in enumerate(self.trees[0]):
            cut = pl.ds(part * (self.tokens // 2), self.tokens // 2)
            total = tree.total()[...].astype(F32)
            if self.groups > 1:
                total = total + self.across[1, cut, :].astype(F32)
            out_ref[cut, :] = total


def reduce_rooms(groups, n_dp, tokens, width, dtype):
    return [
        pltpu.VMEM((groups, 2, n_dp - 1, tokens // 2, width), dtype),
        pltpu.VMEM((2, tokens, width), dtype),
    ]


def run_experts(n_dp, n_mp, groups, identity, rows, table, cots, packed, near):
    owned, _, hidden, width = packed.shape
    span = n_mp // groups
    units = span * hidden
    blocks = groups * n_dp
    slots = blocks * CAP
    tokens = rows.shape[0]
    per_tile = 4
    tile = per_tile * CAP
    n_tiles = blocks // per_tile
    here = [expert for experts, _ in near for expert in experts]
    coming = [expert for expert in range(owned) if expert not in here]
    n_sent = min(owned, 2)
    n_late = owned - n_sent
    n_copies = groups + 2 * (blocks - 1) + 4 * groups * (n_dp - 1)
    n_copies += (len(coming) + n_sent) * (span - 1)
    order = []
    for group in range(groups):
        for level in range(n_dp.bit_length()):
            order += [(group, j) for j in range(n_dp) if bin(j).count("1") == level]

    def experts(r):
        dp, mp = lax.axis_index("dp"), lax.axis_index("mp")
        me = (dp, mp)
        other = flip_all(mp, span)
        copies = Copies(r.send_sems, r.recv_sems)
        peers = {
            (group, j): (flip_all(dp, j), other if group else mp)
            for group in range(groups)
            for j in range(n_dp)
            if group + j
        }
        local = iter(range(n_loads))

        def load(source, target):
            copy = pltpu.make_async_copy(source, target, r.load_sems.at[next(local)])
            copy.start()
            return copy

        def units_of(k):
            return pl.ds(k * hidden, hidden)

        own_table = load(r.own_table.at[dp], r.tables.at[0])
        own_rows = load(r.rows, r.rows_all.at[0, 0])
        loads = [
            [load(r.packed.at[e], r.weights.at[e, :, units_of(0)])] for e in range(owned)
        ]
        for number, (some, _) in enumerate(near):
            for i, e in enumerate(some):
                for k in range(1, span):
                    source = r.near[number * (span - 1) + k - 1].at[i]
                    loads[e].append(load(source, r.weights.at[e, :, units_of(k)]))

        def cot_copy(number):
            group, j = order[number]
            return pltpu.make_async_copy(
                r.cots[group].at[j], r.cot.at[number % 2], r.cot_sems.at[number % 2]
            )

        cot_copy(0).start()
        greet(list(peers.values()) + [(dp, flip_all(mp, k)) for k in range(1, span)])
        if groups > 1:
            across = copies.slot()
            copies.start(r.rows, r.rows_all.at[1, 0], peers[1, 0], across)
        sent = {}
        for (group, j), device in peers.items():
            sent[group, j] = copies.slot()
            copies.start(
                r.own_table.at[device[0]],
                r.tables.at[order.index((group, j))],
                device,
                sent[group, j],
            )
        trees = [row_trees(copies, n_dp, me, r.rows_all.at[group]) for group in range(groups)]
        own_rows.wait()
        for tree in trees[0]:
            tree.send(0)
        own_table.wait()

        def hits(number, some):
            slot = lax.broadcasted_iota(jnp.int32, (CAP, tokens), 0).astype(F32)
            found = [slot == r.tables[number, pl.ds(i, 1), :] for i in some]
            return found[0] if len(found) == 1 else jnp.concatenate(found, 0)

        def fill(number):
            group, j = order[number]
            if number:
                copies.wait(r.tables.at[number], me, sent[group, j])
            if number + 1 < blocks:
                cot_copy(number + 1).start()
            pick = hits(number, range(owned)).astype(BF16)
            there = slice(number * CAP, (number + 1) * CAP)
            found = dot(pick, r.rows_all[group, j], NN).astype(BF16)
            for i in range(owned):
                r.x[i + 1, there, :] = found[i * CAP : (i + 1) * CAP]
            cot_copy(number).wait()
            found = dot(pick, r.cot[number % 2], NN).astype(BF16)
            for i in range(owned):
                r.y[i, there, :] = found[i * CAP : (i + 1) * CAP]

        def work(e, step):
            rows = pl.ds(pl.multiple_of(step * tile, 16), tile)
            x = r.x[e + 1, rows, :]
            gate = dot(x, r.weights[e, 0], NT)
            up = dot(x, r.weights[e, 1], NT)
            sigmoid = 1.0 / (1.0 + jnp.exp(-gate))
            silu = gate * sigmoid
            activation = (silu * up).astype(BF16)
            r.act[rows, :] = activation
            made = dot(activation, r.weights[e, 2], NN)
            cot = r.y[e, rows, :].astype(F32)
            chosen = []
            dots = jnp.sum(cot * made, -1, keepdims=True)
            for b in range(per_tile):
                number = step * per_tile + b
                hit = hits(number, (e,))
                chance = r.tables[number, pl.ds(4 + e, 1), :]
                chosen.append(jnp.sum(jnp.where(hit, chance, 0.0), -1, keepdims=True))
                mine = dots[b * CAP : (b + 1) * CAP]
                r.gates[number, pl.ds(e, 1), :] = jnp.sum(
                    jnp.where(hit, mine, 0.0), 0, keepdims=True
                )
            share = jnp.concatenate(chosen, 0)
            r.y[e, rows, :] = (share * made).astype(BF16)
            back = (share * cot).astype(BF16)
            r.back[rows, :] = back
            grad_act = dot(back, r.weights[e, 2], NT)
            grad_gate = grad_act * up * sigmoid * (1.0 + gate * (1.0 - sigmoid))
            grad_gate = grad_gate.astype(BF16)
            grad_up = (grad_act * silu).astype(BF16)
            r.pair[rows, pl.ds(0, units)] = grad_gate
            r.pair[rows, pl.ds(units, units)] = grad_up
            found = dot(grad_gate, r.weights[e, 0], NN) + dot(grad_up, r.weights[e, 1], NN)
            r.x[e, rows, :] = found.astype(BF16)

        def ready(e):
            for copy in loads[e]:
                copy.wait()
            if e in coming:
                for k in range(1, span):
                    copies.wait(r.weights.at[e, :, units_of(k)], me, weights_sent[e, k])

        stores = []

        def weight_grad(e):
            for c in range(3):
                source = r.act[...] if c == 2 else r.pair[:, pl.ds(c * units, units)]
                rhs = r.back[...] if c == 2 else r.x[e + 1]
                r.weights[e, c] = dot(source, rhs, TN).astype(BF16)
            stores.append(load(r.weights.at[e, :, units_of(0)], r.grad_own.at[e]))
            for k in range(1, span):
                source = r.weights.at[e, :, units_of(k)]
                if e < n_sent:
                    grads_sent[e, k] = copies.slot()
                    copies.start(
                        source, r.arrived[k - 1].at[e], (dp, flip_all(mp, k)), grads_sent[e, k]
                    )
                else:
                    stores.append(load(source, r.late[k - 1].at[e - n_sent]))

        weights_sent, grads_sent = {}, {}
        ready(0)
        done = 0
        for number, (group, j) in enumerate(order):
            if j:
                for tree in sorted(trees[group], key=lambda tree: place_of(tree.order, j)):
                    tree.receive(j)
                    tree.send(j)
            elif group:
                copies.wait(r.rows_all.at[1, 0], me, across)
                for tree in trees[1]:
                    tree.send(0)
            if group == groups - 1 and j == 0:
                for e in coming:
                    for k in range(1, span):
                        weights_sent[e, k] = copies.slot()
                        copies.start(
                            r.packed.at[e],
                            r.weights.at[e, :, units_of(k)],
                            (dp, flip_all(mp, k)),
                            weights_sent[e, k],
                        )
            fill(number)
            if number % per_tile == per_tile - 1 and number < blocks - 1:
                work(0, done)
                done += 1
        work(0, done)
        weight_grad(0)

        def tiles(e, first, end):
            def step(at, carry):
                work(e, at)
                return carry

            lax.fori_loop(first, end, step, 0)

        for e in range(1, owned - 1):
            ready(e)
            tiles(e, 0, n_tiles)
            weight_grad(e)
        copies.finish()
        partner = (dp, other)
        reduce = TokenReduce(copies, n_dp, me, partner, r.rows_all, r.rooms, r.across)
        last = owned - 1
        if last:
            ready(last)
        scattered = []

        def sum_copy(at):
            group, j = scattered[at]
            return pltpu.make_async_copy(
                r.sums.at[at % 2], r.terms.at[group, j], r.sum_sems.at[at % 2]
            )

        own_gates = pltpu.make_async_copy(r.gates.at[0], r.gate_parts.at[dp, 0], r.gate_sem.at[0])
        gates_sent = {}

        def scatter(group, j):
            number = order.index((group, j))
            if number:
                gates_sent[group, j] = copies.slot()
                copies.start(
                    r.gates.at[number],
                    r.gate_parts.at[dp, group],
                    peers[group, j],
                    gates_sent[group, j],
                )
            else:
                own_gates.start()
            there = slice(number * CAP, (number + 1) * CAP)
            pick = hits(number, range(owned)).astype(BF16)
            found = jnp.concatenate([r.x[e, there, :] for e in range(owned)], 0)
            r.rows_all[group, j] = dot(pick, found, TN).astype(BF16)
            if j % 2:
                reduce.first(group, j)
            found = jnp.concatenate([r.y[e, there, :] for e in range(owned)], 0)
            at = len(scattered)
            scattered.append((group, j))
            if at > 1:
                sum_copy(at - 2).wait()
            r.sums[at % 2] = dot(pick, found, TN).astype(BF16)
            sum_copy(at).start()

        halves = [
            (n_tiles * group // groups, n_tiles * (group + 1) // groups) for group in range(groups)
        ]
        levels = list(range(reduce.last - 1, -1, -1))
        for group in range(groups)[::-1]:
            first, end = halves[group]
            if last == 0:
                pass
            elif group == groups - 1:
                tiles(last, first, end)
            else:
                for at in range(first, end):
                    tiles(last, at, at + 1)
                    if levels:
                        reduce.level(1, levels.pop(0))
            for j in [j for j in range(n_dp) if j % 2] + [j for j in range(n_dp) if j % 2 == 0]:
                scatter(group, j)
        if groups > 1:
            for p in levels:
                reduce.level(1, p)
        reduce.pass_on()
        for p in range(reduce.last - 1, -1, -1):
            reduce.level(0, p)
            if p == reduce.last - 1 and last:
                weight_grad(last)
        reduce.end(r.total)
        for at in (blocks - 2, blocks - 1):
            sum_copy(at).wait()
        own_gates.wait()
        for (group, j), device in peers.items():
            copies.wait(r.gate_parts.at[device[0], group], me, gates_sent[group, j])
        for (e, k), slot in grads_sent.items():
            copies.wait(r.arrived[k - 1].at[e], me, slot)
        for copy in stores:
            copy.wait()
        copies.finish()

    n_loads = 2 + owned * span + owned * span
    near_refs = [part for _, parts in near for part in parts]
    weights = packed.shape[1:]
    rooms, across_room = reduce_rooms(groups, n_dp, tokens, width, BF16)
    return launch(
        experts,
        identity,
        dict(
            rows=(rows, hbm()),
            own_table=(table, hbm()),
            cots=(cots, hbm()),
            packed=(packed, hbm()),
            near=(near_refs, hbm()),
        ),
        dict(
            terms=(low(groups, n_dp, tokens, width), hbm()),
            gate_parts=(single(n_dp, groups, 8, tokens), hbm()),
            total=(single(tokens, width), vmem()),
            grad_own=(low(owned, *weights), hbm()),
            arrived=([low(n_sent, *weights) for _ in range(1, span)], hbm()),
            late=([low(n_late, *weights) for _ in range(1, span) if n_late], hbm()),
        ),
        dict(
            weights=pltpu.VMEM((owned, 3, units, width), BF16),
            rows_all=pltpu.VMEM((groups, n_dp, tokens, width), BF16),
            x=pltpu.VMEM((owned + 1, slots, width), BF16),
            y=pltpu.VMEM((owned, slots, width), BF16),
            act=pltpu.VMEM((slots, units), BF16),
            pair=pltpu.VMEM((slots, 2 * units), BF16),
            back=pltpu.VMEM((slots, width), BF16),
            tables=pltpu.VMEM((blocks, 8, tokens), F32),
            gates=pltpu.VMEM((blocks, 8, tokens), F32),
            cot=pltpu.VMEM((2, tokens, width), BF16),
            sums=pltpu.VMEM((2, tokens, width), BF16),
            rooms=rooms,
            across=across_room,
            load_sems=pltpu.SemaphoreType.DMA((n_loads,)),
            cot_sems=pltpu.SemaphoreType.DMA((2,)),
            sum_sems=pltpu.SemaphoreType.DMA((2,)),
            gate_sem=pltpu.SemaphoreType.DMA((1,)),
        ),
        n_copies,
        63 << 20,
    )


def adamw(weight, gradient, moment_one, moment_two, rate_val, decay_val):
    first_new = 0.9 * moment_one + 0.1 * gradient
    second_new = 0.95 * moment_two + 0.05 * gradient * gradient
    first_hat = first_new / (1.0 - 0.9**STEP)
    second_hat = second_new / (1.0 - 0.95**STEP)
    weight_new = weight - rate_val * (
        first_hat / (jnp.sqrt(second_hat) + 1e-08) + decay_val * weight
    )
    return (gradient, weight_new, first_new, second_new)


def local(
    n_dp,
    n_mp,
    residual_in,
    cotangent,
    expert_ids,
    attn_gain,
    query_w,
    key_value_weight,
    output_w,
    moe_gain,
    router_w,
    gateup_w,
    down_w,
    attn_gain_mean,
    attn_gain_var,
    query_mean,
    query_var,
    key_value_first_moment,
    key_value_second_moment,
    output_mean,
    output_var,
    moe_gain_mean,
    moe_gain_var,
    router_mean,
    router_var,
    gateup_mean,
    gateup_var,
    down_mean,
    down_var,
):
    mp = lax.axis_index("mp")
    place_in_all = lax.axis_index("dp") * n_mp + mp
    groups = 2 if 2 * n_dp <= 16 else 1
    tokens = residual_in.shape[0]
    owned = gateup_w.shape[0]
    span = n_mp // groups
    own_gain, own_router = attn_gain.shape[0], router_w.shape[0]
    first_row, lanes = 8, 128
    per_tile = lanes // own_gain

    def spread(gain):
        return jnp.where(jnp.arange(lanes) // own_gain == place_in_all % per_tile, jnp.tile(gain, per_tile), 0.0)

    small = jnp.concatenate(
        [
            spread(attn_gain)[None],
            spread(moe_gain)[None],
            jnp.zeros((first_row - 2, lanes), F32),
            jnp.pad(router_w, ((0, 0), (0, lanes - EXPERTS))),
        ]
    )
    shards = jnp.stack([query_w, key_value_weight, output_w.T]).astype(BF16)
    cot_low = cotangent.astype(BF16)
    start = prologue(n_dp, n_mp, groups, 0, small, shards, cot_low, residual_in)
    small_all = start.small_all
    gains = jnp.concatenate(
        [
            jnp.sum(small_all[:, :, row].reshape(-1, per_tile, lanes), 1).reshape(1, -1)
            for row in (0, 1)
        ]
    )
    router_low = small_all[:, :, first_row:].reshape(MODEL_WIDTH, lanes).astype(BF16)

    expert_range = jnp.arange(EXPERTS, dtype=jnp.int32)
    onehot = (expert_ids[:, :, None] == expert_range[None, None, :]).astype(jnp.int32)
    chosen = jnp.sum(onehot, 1)
    before = jnp.cumsum(chosen, 0) - chosen
    place = jnp.where(chosen > 0, before, -1)
    places = jnp.pad(
        place.astype(F32).T.reshape(n_dp, owned, tokens), ((0, 0), (0, 8 - owned), (0, 0))
    )

    packed = jnp.concatenate([gateup_w, down_w[:, None]], 1).astype(BF16)
    early = [list(range(owned))[:1], list(range(owned))[1:3]]
    whole = gather_rows(n_dp, n_mp, groups, 1, start.row_block, cot_low, packed, early[0])
    full = whole.full

    query_table, key_table = (jnp.asarray(table) for table in rotary_constants())
    part = mp % 2
    rotary = [
        lax.dynamic_slice_in_dim(table, which * tokens, tokens, 1)
        for table, which in ((query_table, part), (key_table, part), (key_table, 1 - part))
    ]
    front = attention_forward(
        n_dp,
        n_mp,
        groups,
        2,
        residual_in,
        start.scaled,
        full,
        gains,
        router_low,
        places,
        whole.cot_other,
        rotary,
        packed,
        early[1],
    )

    found = run_experts(
        n_dp,
        n_mp,
        groups,
        3,
        front.normed_two,
        front.table,
        [start.cots, front.cots][:groups],
        packed,
        [(early[0], whole.near), (early[1], front.near)],
    )

    given = types.SimpleNamespace(
        full=full,
        residual=residual_in,
        hidden=front.hidden,
        cotangent=cotangent,
        total=found.total,
        late=found.late,
        gate_parts=found.gate_parts,
        terms=found.terms,
        probs=front.probs,
        normed=front.normed,
        normed_two=front.normed_two,
        queries=front.queries,
        keyval=front.keyval,
        context=front.context,
        gains=gains,
        router=router_low,
        rotary=rotary,
    )
    back = attention_backward(n_dp, n_mp, groups, 4, given, first_row)
    input_grad, block_out = back.input_grad, back.block_out
    expert_grad = found.grad_own.astype(F32)
    for k in range(1, span):
        parts = [found.arrived[k - 1]] + ([back.arrived[k - 1]] if back.arrived else [])
        expert_grad += jnp.concatenate(parts).astype(F32)
    gateup_grad, down_grad = expert_grad[:, :2], expert_grad[:, 2]
    grads, small_grads = back.shards, back.small_shard
    query_grad, keyval_grad, output_grad = grads[0], grads[1], grads[2].T
    first_lane = (place_in_all % per_tile) * own_gain
    gain_one_grad, gain_two_grad = (
        lax.dynamic_slice_in_dim(small_grads[row], first_lane, own_gain) for row in (0, 1)
    )
    router_grad = small_grads[first_row:, :EXPERTS]
    matrix_rate = 0.2 / math.sqrt(MODEL_WIDTH)
    gain_one_all = adamw(attn_gain, gain_one_grad, attn_gain_mean, attn_gain_var, 0.1, 0.0)
    query_all = adamw(query_w, query_grad, query_mean, query_var, matrix_rate, 0.1)
    keyval_all = adamw(
        key_value_weight,
        keyval_grad,
        key_value_first_moment,
        key_value_second_moment,
        matrix_rate,
        0.1,
    )
    output_all = adamw(output_w, output_grad, output_mean, output_var, 0.1, 0.1)
    gain_two_all = adamw(moe_gain, gain_two_grad, moe_gain_mean, moe_gain_var, 0.1, 0.0)
    router_all = adamw(router_w, router_grad, router_mean, router_var, matrix_rate, 0.1)
    gateup_all = adamw(gateup_w, gateup_grad, gateup_mean, gateup_var, matrix_rate, 0.1)
    down_all = adamw(down_w, down_grad, down_mean, down_var, 0.07, 0.1)
    return (
        block_out,
        input_grad,
        gain_one_all[0],
        gain_one_all[1],
        gain_one_all[2],
        gain_one_all[3],
        query_all[0],
        query_all[1],
        query_all[2],
        query_all[3],
        keyval_all[0],
        keyval_all[1],
        keyval_all[2],
        keyval_all[3],
        output_all[0],
        output_all[1],
        output_all[2],
        output_all[3],
        gain_two_all[0],
        gain_two_all[1],
        gain_two_all[2],
        gain_two_all[3],
        router_all[0],
        router_all[1],
        router_all[2],
        router_all[3],
        gateup_all[0],
        gateup_all[1],
        gateup_all[2],
        gateup_all[3],
        down_all[0],
        down_all[1],
        down_all[2],
        down_all[3],
    )


def solution(mesh):
    in_specs = (
        P(("dp", "mp"), None),
        P(("dp", "mp"), None),
        P(("dp", "mp"), None),
        P(("dp", "mp")),
        P("dp", "mp"),
        P("dp", "mp"),
        P("mp", "dp"),
        P(("dp", "mp")),
        P(("dp", "mp"), None),
        P("dp", None, "mp", None),
        P("dp", "mp", None),
        P(("dp", "mp")),
        P(("dp", "mp")),
        P("dp", "mp"),
        P("dp", "mp"),
        P("dp", "mp"),
        P("dp", "mp"),
        P("mp", "dp"),
        P("mp", "dp"),
        P(("dp", "mp")),
        P(("dp", "mp")),
        P(("dp", "mp"), None),
        P(("dp", "mp"), None),
        P("dp", None, "mp", None),
        P("dp", None, "mp", None),
        P("dp", "mp", None),
        P("dp", "mp", None),
    )
    out_specs = (
        P(("dp", "mp"), None),
        P(("dp", "mp"), None),
        P(("dp", "mp")),
        P(("dp", "mp")),
        P(("dp", "mp")),
        P(("dp", "mp")),
        P("dp", "mp"),
        P("dp", "mp"),
        P("dp", "mp"),
        P("dp", "mp"),
        P("dp", "mp"),
        P("dp", "mp"),
        P("dp", "mp"),
        P("dp", "mp"),
        P("mp", "dp"),
        P("mp", "dp"),
        P("mp", "dp"),
        P("mp", "dp"),
        P(("dp", "mp")),
        P(("dp", "mp")),
        P(("dp", "mp")),
        P(("dp", "mp")),
        P(("dp", "mp"), None),
        P(("dp", "mp"), None),
        P(("dp", "mp"), None),
        P(("dp", "mp"), None),
        P("dp", None, "mp", None),
        P("dp", None, "mp", None),
        P("dp", None, "mp", None),
        P("dp", None, "mp", None),
        P("dp", "mp", None),
        P("dp", "mp", None),
        P("dp", "mp", None),
        P("dp", "mp", None),
    )
    step = functools.partial(local, mesh.shape["dp"], mesh.shape["mp"])
    return jax.shard_map(step, mesh=mesh, in_specs=in_specs, out_specs=out_specs, check_vma=False)
```

```python
import functools
import math
import types

import jax
import jax.numpy as jnp
import numpy as np
from jax import lax
from jax.experimental import pallas as pl
from jax.experimental.pallas import tpu as pltpu
from jax.sharding import PartitionSpec as P

MODEL_WIDTH = 1024
QUERY_HEADS = 16
KEY_VALUE_HEADS = 8
HEAD_SIZE = 64
EXPERTS = 32
TOPK = 8
SEQUENCE_TOKENS = 512
STEP = 3
CAP = 80

NORM_EPS = 1e-06
MESH = pl.DeviceIdType.MESH
BF16 = jnp.bfloat16
F32 = jnp.float32


def flip(index, mask):
    return index + mask * (1 - 2 * lax.rem(lax.div(index, mask), 2))


def flip_all(index, masks):
    bit = 1
    while bit <= masks:
        if masks & bit:
            index = flip(index, bit)
        bit *= 2
    return index


def bits_of(size):
    return [1 << i for i in range(size.bit_length() - 1)]


def orders_of(n_dp):
    bits = bits_of(n_dp)
    return bits[1:] + bits[:1], bits[1:][::-1] + bits[:1]


def place_of(order, j):
    place = -1
    for at, mask in enumerate(order):
        if j & mask:
            place = at
    return place


def greet(partners):
    barrier = pltpu.get_barrier_semaphore()
    for partner in partners:
        pl.semaphore_signal(barrier, inc=1, device_id=partner, device_id_type=MESH)
    pl.semaphore_wait(barrier, len(partners))


class Copies:
    def __init__(self, send_sems, recv_sems):
        self.send_sems, self.recv_sems = send_sems, recv_sems
        self.used = 0
        self.sent = []

    def slot(self):
        self.used += 1
        return self.used - 1

    def make(self, source, target, device, slot):
        return pltpu.make_async_remote_copy(
            src_ref=source,
            dst_ref=target,
            send_sem=self.send_sems.at[slot],
            recv_sem=self.recv_sems.at[slot],
            device_id=device,
            device_id_type=MESH,
        )

    def start(self, source, target, device, slot):
        copy = self.make(source, target, device, slot)
        copy.start()
        self.sent.append(copy)

    def wait(self, target, device, slot):
        self.make(target, target, device, slot).wait_recv()

    def split(self):
        before, self.sent = self.sent, []
        return before

    def finish(self, some=None):
        for copy in self.sent if some is None else some:
            copy.wait_send()


class TreeGather:
    def __init__(self, copies, order, n_dp, me, source, target):
        self.copies, self.order, self.n_dp, self.me = copies, order, n_dp, me
        self.source, self.target = source, target
        self.slots = {j: copies.slot() for j in range(1, n_dp)}

    def level(self, j):
        return bin(j).count("1")

    def send(self, j):
        dp, mp = self.me
        for mask in self.order[place_of(self.order, j) + 1 :]:
            self.copies.start(
                self.source(j), self.target(j, mask), (flip(dp, mask), mp), self.slots[j ^ mask]
            )

    def receive(self, j):
        self.copies.wait(self.source(j), self.me, self.slots[j])

    def steps(self):
        return sorted(range(1, self.n_dp), key=lambda j: (self.level(j), place_of(self.order, j)))


def run_gathers(trees):
    n_dp = trees[0].n_dp
    for level in range(1, n_dp.bit_length()):
        for tree in trees:
            for j in tree.steps():
                if tree.level(j) == level:
                    tree.receive(j)
                    tree.send(j)


class TreeReduce:
    def __init__(self, copies, order, n_dp, me, block, room, add):
        self.copies, self.order, self.n_dp, self.me = copies, order, n_dp, me
        self.block, self.room, self.add = block, room, add
        self.keys = [
            (j, q) for j in range(n_dp) for q in range(len(order) - 1, place_of(order, j), -1)
        ]
        self.slots = {key: copies.slot() for key in self.keys}

    def number(self, key):
        return self.keys.index(key)

    def send(self, j):
        dp, mp = self.me
        p = place_of(self.order, j)
        last = len(self.order) - 1
        source = self.block(j) if p == last else self.room(self.number((j, last)))
        mask = self.order[p]
        key = (j ^ mask, p)
        self.copies.start(source, self.room(self.number(key)), (flip(dp, mask), mp), self.slots[key])

    def collect(self, j):
        last = len(self.order) - 1
        for q in range(last, place_of(self.order, j), -1):
            here = self.room(self.number((j, q)))
            self.copies.wait(here, self.me, self.slots[(j, q)])
            if q == last:
                self.add(here, self.block(j))
            else:
                self.add(self.room(self.number((j, last))), here)

    def total(self):
        return self.room(self.number((0, len(self.order) - 1)))


def add_rows(step=16):
    def add(here, other):
        def body(i, carry):
            rows = pl.ds(pl.multiple_of(i * step, step), step)
            total = here[..., rows, :].astype(F32) + other[..., rows, :].astype(F32)
            here[..., rows, :] = total.astype(here.dtype)
            return carry

        lax.fori_loop(0, here.shape[-2] // step, body, 0)

    return add


def hbm():
    return pl.BlockSpec(memory_space=pl.ANY)


def vmem():
    return pl.BlockSpec(memory_space=pltpu.VMEM)


def params(identity, limit=None):
    return pltpu.CompilerParams(
        collective_id=identity, has_side_effects=True, vmem_limit_bytes=limit
    )


def launch(kernel, identity, ins, outs, scratch, n_copies, limit=None, kept=None):
    def flat(entries):
        names, leaves, specs = [], [], []
        for name, (value, spec) in entries.items():
            several = isinstance(value, list)
            new = value if several else [value]
            names.append((name, len(new) if several else None))
            leaves += new
            specs += [spec] * len(new)
        return names, leaves, specs

    def unflat(names, leaves):
        leaves, found = list(leaves), {}
        for name, count in names:
            found[name] = leaves[0] if count is None else leaves[:count]
            leaves = leaves[1 if count is None else count :]
        return found

    scratch = scratch | dict(
        send_sems=pltpu.SemaphoreType.DMA((n_copies,)),
        recv_sems=pltpu.SemaphoreType.DMA((n_copies,)),
    )
    in_names, values, in_specs = flat(ins)
    out_names, shapes, out_specs = flat(outs)

    def numbers(names, wanted):
        at = 0
        for name, count in names:
            size = 1 if count is None else count
            if name == wanted:
                return range(at, at + size)
            at += size

    aliases = {}
    for output, source in (kept or {}).items():
        aliases |= dict(zip(numbers(in_names, source), numbers(out_names, output)))
    scratch_names = [(name, None) for name in scratch]

    def body(*refs):
        named = unflat(in_names + out_names + scratch_names, refs)
        kernel(types.SimpleNamespace(**named))

    results = pl.pallas_call(
        body,
        out_shape=tuple(shapes),
        in_specs=in_specs,
        out_specs=tuple(out_specs),
        scratch_shapes=list(scratch.values()),
        input_output_aliases=aliases,
        compiler_params=params(identity, limit),
        cost_estimate=pl.CostEstimate(flops=1, bytes_accessed=1, transcendentals=0),
        name=kernel.__name__,
    )(*values)
    return types.SimpleNamespace(**unflat(out_names, results))


def low(*shape):
    return jax.ShapeDtypeStruct(shape, BF16)


def single(*shape):
    return jax.ShapeDtypeStruct(shape, F32)


def dot(a, b, contract):
    return lax.dot_general(a, b, ((contract[:1], contract[1:]), ((), ())), preferred_element_type=F32)


NN, NT, TN = (1, 0), (1, 1), (0, 0)


def prologue(n_dp, n_mp, identity, first_row, small, shards, cot, residual, gateup, down):
    half = n_mp // 2
    kinds, rows, cols = shards.shape
    tokens, width = cot.shape
    order_a, _ = orders_of(n_dp)
    owned, _, hidden, _ = gateup.shape
    n_devices = n_dp * n_mp
    own_router = small.shape[0] - first_row
    n_copies = 2 * (n_mp - 1) + 4 * (n_dp - 1) + 1

    def gather_line(r):
        dp, mp = lax.axis_index("dp"), lax.axis_index("mp")
        me = (dp, mp)
        neighbour = (dp, flip(mp, 1))
        copies = Copies(r.send_sems, r.recv_sems)
        loads = [
            pltpu.make_async_copy(r.gateup, r.wide.at[:, pl.ds(0, 2)], r.local_sems.at[0]),
            pltpu.make_async_copy(r.down, r.wide.at[:, 2], r.local_sems.at[1]),
        ]
        for copy in loads:
            copy.start()
        own_small = r.small_all.at[dp, mp]
        own_cols = pl.ds(pl.multiple_of(mp * cols, cols), cols)
        own_part = r.row_block.at[:, :, own_cols]
        r.small_all[dp, mp] = r.small[...]
        residual_rows = r.residual[...]
        inverse = lax.rsqrt(jnp.mean(residual_rows * residual_rows, -1, keepdims=True) + NORM_EPS)
        r.scaled[0] = (residual_rows * inverse).astype(BF16)
        r.row_block[:, :, own_cols] = r.shards[...]
        r.cots[0] = r.cot[...]
        greet(
            [(flip_all(dp, mask), mp) for mask in bits_of(n_dp)]
            + [(dp, flip_all(mp, k)) for k in range(1, n_mp)]
        )
        near = lax.div(mp, half)
        line = {}
        for k in range(1, n_mp):
            line[k] = (copies.slot(), copies.slot())
            copies.start(r.small, own_small, (dp, flip_all(mp, k)), line[k][0])
        across = copies.slot()
        copies.start(r.scaled.at[0], r.scaled.at[1], neighbour, across)
        for k in range(1, n_mp):
            copies.start(r.shards, own_part, (dp, flip_all(mp, k)), line[k][1])

        def small_tree(chunk):
            first = pl.multiple_of(chunk * half, half)

            def ref(j, mask=0):
                return r.small_all.at[flip_all(dp, j), pl.ds(first, half)]

            return TreeGather(copies, order_a, n_dp, me, ref, ref)

        small_trees = [small_tree(chunk) for chunk in (near, 1 - near)]
        cot_trees = row_trees(copies, n_dp, me, r.cots)
        for chunk in (0, 1):
            for k in range(1, half) if chunk == 0 else range(half, n_mp):
                copies.wait(r.small_all.at[dp, flip_all(mp, k)], me, line[k][0])
            small_trees[chunk].send(0)
        for one in cot_trees:
            one.send(0)
        for copy in loads:
            copy.wait()
        for e in range(owned):
            r.narrow[e] = r.wide[e].astype(BF16)
        store = pltpu.make_async_copy(r.narrow, r.packed, r.local_sems.at[2])
        store.start()
        top = n_dp.bit_length() - 1
        for level in range(1, top + 1):
            run_level(small_trees, level)
            run_level(cot_trees, level)
        n_tiles = width // 128
        for row in (0, 1):
            for tile in range(n_tiles):
                total = None
                for at in range(tile * n_devices // n_tiles, (tile + 1) * n_devices // n_tiles):
                    part = r.small_all[at // n_mp, at % n_mp, row : row + 1, :]
                    total = part if total is None else total + part
                r.gains[row : row + 1, tile * 128 : (tile + 1) * 128] = total
        for at in range(n_devices):
            r.router_wide[at * own_router : (at + 1) * own_router, :] = r.small_all[
                at // n_mp, at % n_mp, first_row:, :
            ]
        r.router[...] = r.router_wide[...].astype(BF16)
        for k in range(1, n_mp):
            other = pl.multiple_of(flip_all(mp, k) * cols, cols)
            copies.wait(r.row_block.at[:, :, pl.ds(other, cols)], me, line[k][1])
        copies.wait(r.scaled.at[1], me, across)
        store.wait()
        copies.finish()

    return launch(
        gather_line,
        identity,
        dict(
            small=(small, vmem()),
            shards=(shards, vmem()),
            cot=(cot, vmem()),
            residual=(residual, vmem()),
            gateup=(gateup, hbm()),
            down=(down, hbm()),
        ),
        dict(
            gains=(single(2, width), vmem()),
            router=(low(width, 128), vmem()),
            packed=(low(owned, 3, hidden, width), hbm()),
            row_block=(low(kinds, rows, n_mp * cols), vmem()),
            cots=(low(n_dp, tokens, width), vmem()),
            scaled=(low(2, tokens, width), vmem()),
        ),
        dict(
            small_all=pltpu.VMEM((n_dp, n_mp) + small.shape, F32),
            router_wide=pltpu.VMEM((width, 128), F32),
            wide=pltpu.VMEM((owned, 3, hidden, width), F32),
            narrow=pltpu.VMEM((owned, 3, hidden, width), BF16),
            local_sems=pltpu.SemaphoreType.DMA((3,)),
        ),
        n_copies,
        32 << 20,
    )


def run_level(trees, level):
    for one in trees:
        for j in one.steps():
            if one.level(j) == level:
                one.receive(j)
                one.send(j)


def send_experts(copies, me, span, packed, near, experts):
    dp, mp = me
    slots = {}
    for i, expert in enumerate(experts):
        for k in range(1, span):
            slots[i, k] = copies.slot()
            copies.start(
                packed.at[expert], near[k - 1].at[i], (dp, flip_all(mp, k)), slots[i, k]
            )
    return slots


def wait_experts(copies, me, near, slots):
    for (i, k), slot in slots.items():
        copies.wait(near[k - 1].at[i], me, slot)


def row_trees(copies, n_dp, me, rows_all):
    tokens = rows_all.shape[1]

    def tree(part, order):
        cut = pl.ds(part * (tokens // 2), tokens // 2)
        return TreeGather(
            copies,
            order,
            n_dp,
            me,
            lambda j: rows_all.at[j, cut],
            lambda j, mask: rows_all.at[j ^ mask, cut],
        )

    return [tree(part, order) for part, order in enumerate(orders_of(n_dp))]


def rotary_constants():
    half_width = HEAD_SIZE // 2
    frequency = np.exp(
        np.float32(-math.log(10000.0)) * np.arange(half_width, dtype=np.float32) * np.float32(2.0)
        / np.float32(HEAD_SIZE)
    ).astype(np.float32)
    angles = np.arange(SEQUENCE_TOKENS, dtype=np.float32)[:, None] * frequency[None, :]
    cosine, sine = np.cos(angles), np.sin(angles)
    cosine = np.concatenate([cosine, cosine], 1)
    sine = np.concatenate([-sine, sine], 1)
    queries = np.stack([np.tile(cosine, (1, 2)), np.tile(sine, (1, 2))])
    keys = np.stack(
        [
            np.concatenate([cosine, np.ones_like(cosine)], 1),
            np.concatenate([sine, np.zeros_like(sine)], 1),
        ]
    )
    return queries.astype(np.float32), keys.astype(np.float32)


def rotate(value, cosine, sine):
    lane = lax.broadcasted_iota(jnp.int32, value.shape, 1)
    rolled = jnp.where(
        lane % HEAD_SIZE < HEAD_SIZE // 2,
        pltpu.roll(value, 128 - HEAD_SIZE // 2, 1),
        pltpu.roll(value, HEAD_SIZE // 2, 1),
    )
    return value * cosine + rolled * sine


def group_operands(queries, keyval):
    lane = lax.broadcasted_iota(jnp.int32, queries.shape, 1)
    both = jnp.concatenate(
        [jnp.where(lane < HEAD_SIZE, queries, 0.0), jnp.where(lane < HEAD_SIZE, 0.0, queries)], 0
    ).astype(BF16)
    lane = lax.broadcasted_iota(jnp.int32, keyval.shape, 1)
    turned = pltpu.roll(keyval, HEAD_SIZE, 1)
    keys = jnp.where(lane < HEAD_SIZE, keyval, turned).astype(BF16)
    values = jnp.where(lane < HEAD_SIZE, turned, keyval).astype(BF16)
    return both, keys, values


def merge_heads(both):
    tokens = both.shape[0] // 2
    lane = lax.broadcasted_iota(jnp.int32, (tokens, 128), 1)
    return jnp.where(lane < HEAD_SIZE, both[:tokens], both[tokens:])


def seen(tokens, mp):
    shape = (2 * tokens, 2 * tokens)
    row = lax.broadcasted_iota(jnp.int32, shape, 0) % tokens
    key = lax.broadcasted_iota(jnp.int32, shape, 1)
    shift = tokens - 2 * tokens * lax.rem(mp, 2)
    key = jnp.where(key < tokens, key, key - tokens + shift)
    return key <= row


def softmax_of(both, keys, mask):
    scores = dot(both, keys, NT) * (1.0 / math.sqrt(HEAD_SIZE))
    raised = jnp.exp(jnp.where(mask, scores, -1e30))
    return raised / jnp.sum(raised, -1, keepdims=True)


def attention_forward(
    n_dp, n_mp, groups, identity, residual, ids, start, cot, tables, experts
):
    tokens, width = residual.shape
    kinds, rows, _ = start.row_block.shape
    part_rows = rows // 2
    n_heads = width // 128
    span = n_mp // groups
    owned = EXPERTS // n_dp
    n_experts = len(experts)
    n_copies = 4 * (n_dp - 1) + n_experts * (span - 1) + 1

    def attention(r):
        dp, mp = lax.axis_index("dp"), lax.axis_index("mp")
        me = (dp, mp)
        partner = (dp, flip_all(mp, span))
        copies = Copies(r.send_sems, r.recv_sems)
        r.full[:, pl.ds(pl.multiple_of(dp * rows, rows), rows), :] = r.row_block[...]
        greet(
            [(flip_all(dp, mask), mp) for mask in bits_of(n_dp)]
            + [partner] * (groups - 1)
            + [(dp, flip_all(mp, k)) for k in range(1, span)]
        )
        across = copies.slot()
        if groups > 1:
            copies.start(r.cot, r.cots.at[0], partner, across)

        def tree(part, order):
            def ref(j, mask=0):
                start = flip_all(dp, j) * rows + part * part_rows
                return r.full.at[:, pl.ds(pl.multiple_of(start, part_rows), part_rows), :]

            return TreeGather(copies, order, n_dp, me, ref, ref)

        weight_trees = [tree(part, order) for part, order in enumerate(orders_of(n_dp))]
        cot_trees = row_trees(copies, n_dp, me, r.cots) if groups > 1 else []
        for one in weight_trees:
            one.send(0)
        sent = send_experts(copies, me, span, r.packed, r.near, experts)
        named = lax.broadcasted_iota(jnp.int32, (EXPERTS, tokens), 0)
        chosen = jnp.zeros((EXPERTS, tokens), F32)
        for k in range(TOPK):
            chosen += jnp.where(named == r.ids[k : k + 1, :], 1.0, 0.0)
        shape = (tokens, tokens)
        earlier = lax.broadcasted_iota(jnp.int32, shape, 0) < lax.broadcasted_iota(jnp.int32, shape, 1)
        before = dot(chosen.astype(BF16), jnp.where(earlier, 1.0, 0.0).astype(BF16), NN)
        place = jnp.where(chosen > 0.0, before, -1.0)
        r.table[...] = jnp.zeros_like(r.table)
        for expert in range(EXPERTS):
            owner, which = divmod(expert, owned)
            r.table[owner, which, :] = place[expert]
        residual = r.residual[...]
        inverse = lax.rsqrt(jnp.mean(residual * residual, -1, keepdims=True) + NORM_EPS)
        gain_one = r.gains[0:1, :]
        r.normed[0] = (residual * inverse * gain_one).astype(BF16)
        r.normed[1] = (r.scaled[1].astype(F32) * gain_one).astype(BF16)
        mask = seen(tokens, mp)
        top = n_dp.bit_length() - 1
        for level in range(1, top + 1):
            if level == top and groups > 1:
                copies.wait(r.cots.at[0], me, across)
                for one in cot_trees:
                    one.send(0)
            run_level(weight_trees, level)
        r.q[...] = dot(r.normed[0], r.full[0], NN)
        for part in (0, 1):
            r.kv[part] = dot(r.normed[part], r.full[1], NN)
        run_level(cot_trees, 1)
        which = lax.rem(mp, 2)

        def table(ref, at):
            there = pl.ds(pl.multiple_of(at * tokens, tokens), tokens)
            return ref[0, there, :], ref[1, there, :]

        def head(k, carry):
            lanes = pl.ds(pl.multiple_of(k * 128, 128), 128)
            queries = rotate(r.q[:, lanes], *table(r.query_table, which))
            r.queries[:, lanes] = queries.astype(BF16)
            parts = []
            for part, at in enumerate((which, 1 - which)):
                parts.append(rotate(r.kv[part, :, lanes], *table(r.key_table, at)))
                r.keyval[part, :, lanes] = parts[part].astype(BF16)
            both, keys, values = group_operands(queries, jnp.concatenate(parts, 0))
            chance = softmax_of(both, keys, mask).astype(BF16)
            r.context[:, lanes] = merge_heads(dot(chance, values, NN)).astype(BF16)
            return carry

        for level in range(2, top + 1):
            first, end = [(level - 2 + i) * n_heads // (top - 1) for i in (0, 1)]
            lax.fori_loop(first, end, head, 0)
            run_level(cot_trees, level)
        hidden = r.residual[...] + dot(r.context[...], r.full[2], NT)
        r.hidden[...] = hidden
        inverse = lax.rsqrt(jnp.mean(hidden * hidden, -1, keepdims=True) + NORM_EPS)
        normed = (hidden * inverse * r.gains[1:2, :]).astype(BF16)
        r.normed_two[...] = normed
        logits = dot(normed, r.router[...], NN)
        lane = lax.broadcasted_iota(jnp.int32, logits.shape, 1)
        raised = jnp.where(lane < EXPERTS, jnp.exp(logits), 0.0)
        probs = raised / jnp.sum(raised, -1, keepdims=True)
        r.probs[...] = probs
        turned = probs.T
        for expert in range(EXPERTS):
            owner, which = divmod(expert, owned)
            r.table[owner, 4 + which, :] = turned[expert]
        wait_experts(copies, me, r.near, sent)
        copies.finish()

    return launch(
        attention,
        identity,
        dict(
            residual=(residual, vmem()),
            ids=(ids, vmem()),
            scaled=(start.scaled, vmem()),
            row_block=(start.row_block, vmem()),
            cot=(cot, vmem()),
            gains=(start.gains, vmem()),
            router=(start.router, vmem()),
            packed=(start.packed, hbm()),
            query_table=(tables[0], vmem()),
            key_table=(tables[1], vmem()),
        ),
        dict(
            full=(low(kinds, n_dp * rows, width), vmem()),
            cots=(low(n_dp, tokens, width), vmem()),
            near=([low(n_experts, *start.packed.shape[1:]) for _ in range(1, span)], hbm()),
            normed=(low(2, tokens, width), vmem()),
            queries=(low(tokens, width), vmem()),
            keyval=(low(2, tokens, width), vmem()),
            context=(low(tokens, width), vmem()),
            hidden=(single(tokens, width), vmem()),
            normed_two=(low(tokens, width), vmem()),
            probs=(single(tokens, 128), vmem()),
            table=(single(n_dp, 8, tokens), vmem()),
        ),
        dict(
            q=pltpu.VMEM((tokens, width), F32),
            kv=pltpu.VMEM((2, tokens, width), F32),
        ),
        n_copies,
        48 << 20,
    )


def attention_backward(n_dp, n_mp, groups, identity, given, first_row):
    tokens, width = given.residual.shape
    n_heads = width // 128
    n_devices = n_dp * n_mp
    own_router = width // n_devices
    per_tile = n_devices // n_heads
    rows, cols = width // n_dp, width // n_mp
    part_rows = rows // 2
    orders = orders_of(n_dp)
    span = n_mp // groups
    owned = EXPERTS // n_dp
    n_late = given.late[0].shape[0] if given.late else 0
    n_copies = (2 * groups + 7) * (n_dp - 1) + 2 + 4 * (n_mp - 1) + 2 + n_late * (span - 1)

    rooms, across_room = reduce_rooms(groups, n_dp, tokens, width, BF16)

    def attention_back(r):
        dp, mp = lax.axis_index("dp"), lax.axis_index("mp")
        me = (dp, mp)
        neighbour = (dp, flip(mp, 1))
        copies = Copies(r.send_sems, r.recv_sems)
        loads = [
            pltpu.make_async_copy(r.full.at[c], r.weights.at[c], r.local_sems.at[c])
            for c in (2, 0, 1)
        ]
        for copy in loads:
            copy.start()
        even_loads = [
            pltpu.make_async_copy(
                r.terms.at[g, j], r.terms_even.at[g, j // 2], r.term_sems.at[g, j // 2]
            )
            for g in range(groups)
            for j in range(0, n_dp, 2)
        ]
        for copy in even_loads:
            copy.start()
        greet(
            [(flip_all(dp, mask), mp) for mask in bits_of(n_dp)]
            + [(dp, flip_all(mp, k)) for k in range(1, n_mp)]
        )
        partner = (dp, flip_all(mp, span))
        mixture = TokenReduce(
            copies,
            n_dp,
            me,
            partner,
            groups,
            lambda g, j: r.terms.at[g, j] if j % 2 else r.terms_even.at[g, j // 2],
            r.rooms,
            r.across,
        )
        for group in range(groups)[::-1]:
            for j in range(1, n_dp, 2):
                mixture.first(group, j)
        last = mixture.last
        for copy in even_loads:
            copy.wait()
        mixture.level(1, last - 1)
        travels = {}

        def send_late(i):
            if i < n_late:
                for k in range(1, span):
                    travels[i, k] = copies.slot()
                    copies.start(
                        r.late[k - 1].at[i],
                        r.arrived[k - 1].at[owned - n_late + i],
                        (dp, flip_all(mp, k)),
                        travels[i, k],
                    )

        send_late(0)
        r.turned[...] = jnp.zeros_like(r.turned)
        for expert in range(EXPERTS):
            owner, which = divmod(expert, owned)
            parts = r.gate_parts[owner, 0, which, :]
            for group in range(1, groups):
                parts = parts + r.gate_parts[owner, group, which, :]
            r.turned[expert, :] = parts
        grad_probs = r.turned[...].T
        probs = r.probs[...]
        grad_logits = (
            probs * (grad_probs - jnp.sum(probs * grad_probs, -1, keepdims=True))
        ).astype(BF16)
        grad_normed_two = r.total[...] + dot(grad_logits, r.router[...], NT)
        r.grad_router[...] = dot(r.normed_two[...], grad_logits, TN)
        mixture.level(0, last - 1)
        hidden = r.hidden[...]
        inverse = lax.rsqrt(jnp.mean(hidden * hidden, -1, keepdims=True) + NORM_EPS)
        scaled = r.gains[1:2, :] * grad_normed_two
        grad_hidden = (
            r.cotangent[...]
            + inverse * scaled
            - hidden * (inverse * inverse * inverse) * jnp.mean(scaled * hidden, -1, keepdims=True)
        )
        r.grad_hidden[...] = grad_hidden
        gain_two = jnp.sum(grad_normed_two * hidden * inverse, 0, keepdims=True)
        grad_attn = grad_hidden.astype(BF16)
        r.grad_attn[...] = grad_attn
        def weight_tree(c, part):
            def block(j):
                start = flip_all(dp, j) * rows + part * part_rows
                return r.grads.at[c, pl.ds(pl.multiple_of(start, part_rows), part_rows), :]

            return TreeReduce(
                copies,
                orders[part],
                n_dp,
                me,
                block,
                lambda number: r.weight_rooms.at[c, part, number],
                add_rows(),
            )

        weight_trees = [[weight_tree(c, part) for part in (0, 1)] for c in range(3)]

        def weight_level(c, p):
            for j in range(1, n_dp):
                for one in weight_trees[c]:
                    if place_of(one.order, j) == p:
                        if p < last:
                            one.collect(j)
                        one.send(j)

        r.grads[2] = dot(grad_attn, r.context[...], TN).astype(BF16)
        weight_level(2, last)
        loads[0].wait()
        r.grad_context[...] = dot(r.grad_attn[...], r.weights[2], NN).astype(BF16)
        mask = seen(tokens, mp)

        def table(ref):
            there = pl.ds(pl.multiple_of(lax.rem(mp, 2) * tokens, tokens), tokens)
            return ref[0, there, :], ref[1, there, :]

        def head(k, carry):
            lanes = pl.ds(pl.multiple_of(k * 128, 128), 128)
            keyval = jnp.concatenate([r.keyval[0, :, lanes], r.keyval[1, :, lanes]], 0)
            both, keys, values = group_operands(r.queries[:, lanes].astype(F32), keyval.astype(F32))
            grad_both = group_operands(r.grad_context[:, lanes].astype(F32), keyval.astype(F32))[0]
            chance = softmax_of(both, keys, mask)
            grad_p = dot(grad_both, values, NT)
            delta = jnp.sum(chance * grad_p, -1, keepdims=True)
            grad_s = (chance * (grad_p - delta)).astype(BF16)
            scale = 1.0 / math.sqrt(HEAD_SIZE)
            grad_q = merge_heads(dot(grad_s, keys, NN)) * scale
            cosine, sine = table(r.query_table)
            r.grad_q[:, lanes] = rotate(grad_q, cosine, -sine).astype(BF16)
            grad_k = dot(grad_s, both, TN) * scale
            grad_v = dot(chance.astype(BF16), grad_both, TN)
            lane = lax.broadcasted_iota(jnp.int32, grad_k.shape, 1)
            grad_kv = jnp.where(
                lane < HEAD_SIZE,
                grad_k + pltpu.roll(grad_k, HEAD_SIZE, 1),
                grad_v + pltpu.roll(grad_v, HEAD_SIZE, 1),
            )
            r.grad_kv[:, lanes] = grad_kv[:tokens]
            r.swap[0, :, lanes] = grad_kv[tokens:].astype(BF16)
            return carry

        sent = {}

        def line_out(c):
            for part, one in enumerate(weight_trees[c]):
                one.collect(0)
                total = one.total()
                for k in range(n_mp):
                    there = pl.ds(pl.multiple_of(flip_all(mp, k) * cols, cols), cols)
                    r.line[0, c, k, pl.ds(part * part_rows, part_rows), :] = total[:, there]
            for k in range(1, n_mp):
                sent[c, k] = copies.slot()
                copies.start(
                    r.line.at[0, c, k], r.line.at[1, c, k], (dp, flip_all(mp, k)), sent[c, k]
                )

        across = [copies.slot() for _ in range(2)]
        swaps = [pl.ds(half * (width // 2), width // 2) for half in range(2)]

        def heads(first, end):
            lax.fori_loop(first * n_heads // 4, end * n_heads // 4, head, 0)

        def swap(half):
            copies.start(
                r.swap.at[0, :, swaps[half]],
                r.swap.at[1, :, swaps[half]],
                neighbour,
                across[half],
            )

        heads(0, 2)
        swap(0)
        for p in range(last - 2, -1, -1):
            mixture.level(1, p)
        heads(2, 3)
        weight_level(2, last - 1)
        heads(3, 4)
        swap(1)
        for p in range(last - 2, -1, -1):
            mixture.level(0, p)
        mixture.pass_on()
        for i in range(1, n_late):
            send_late(i)
        r.grads[0] = dot(r.normed[0], r.grad_q[...], TN).astype(BF16)
        weight_level(0, last)
        loads[1].wait()
        r.grad_normed[...] = dot(r.grad_q[...], r.weights[0], NT)
        weight_level(0, last - 1)
        for p in range(last - 2, -1, -1):
            weight_level(2, p)
        for half in range(2):
            copies.wait(r.swap.at[1, :, swaps[half]], me, across[half])

        def turn_back(k, carry):
            lanes = pl.ds(pl.multiple_of(k * 128, 128), 128)
            total = r.grad_kv[:, lanes] + r.swap[1, :, lanes].astype(F32)
            cosine, sine = table(r.key_table)
            total = rotate(total, cosine, -sine)
            r.grad_kv_low[:, lanes] = total.astype(BF16)
            return carry

        lax.fori_loop(0, n_heads, turn_back, 0)
        loads[2].wait()
        r.grads[1] = dot(r.normed[0], r.grad_kv_low[...], TN).astype(BF16)
        weight_level(1, last)
        grad_normed = r.grad_normed[...] + dot(r.grad_kv_low[...], r.weights[1], NT)
        residual = r.residual[...]
        inverse = lax.rsqrt(jnp.mean(residual * residual, -1, keepdims=True) + NORM_EPS)
        scaled = r.gains[0:1, :] * grad_normed
        r.input_grad[...] = (
            r.grad_hidden[...]
            + inverse * scaled
            - residual * (inverse * inverse * inverse) * jnp.mean(scaled * residual, -1, keepdims=True)
        )
        gain_one = jnp.sum(grad_normed * residual * inverse, 0, keepdims=True)
        r.small[...] = jnp.zeros_like(r.small)
        for device in range(n_devices):
            tile = device // per_tile
            owner = r.small.at[device // n_mp, device % n_mp]
            owner[0:1, :] = gain_one[:, tile * 128 : (tile + 1) * 128]
            owner[1:2, :] = gain_two[:, tile * 128 : (tile + 1) * 128]
            owner[first_row : first_row + own_router, :] = r.grad_router[
                device * own_router : (device + 1) * own_router, :
            ]

        def add_whole(here, other):
            here[...] = here[...] + other[...]

        small_tree = TreeReduce(
            copies,
            orders[0],
            n_dp,
            me,
            lambda j: r.small.at[flip_all(dp, j)],
            lambda number: r.small_rooms.at[number],
            add_whole,
        )
        for j in range(1, n_dp):
            if place_of(orders[0], j) == last:
                small_tree.send(j)
        for p in range(last - 1, -1, -1):
            if p < last - 1:
                weight_level(0, p)
            weight_level(1, p)
            for j in range(1, n_dp):
                if place_of(orders[0], j) == p:
                    small_tree.collect(j)
                    small_tree.send(j)
            if p == last - 1:
                line_out(2)
        for c in (0, 1):
            line_out(c)
        small_tree.collect(0)
        small_total = small_tree.total()
        for k in range(1, n_mp):
            device = (dp, flip_all(mp, k))
            sent[k] = copies.slot()
            copies.start(small_total.at[device[1]], r.small_line.at[k], device, sent[k])
        mixture.end(r.block_out)
        r.block_out[...] += r.hidden[...]
        for c in (2, 0, 1):
            r.shards[c] = r.line[0, c, 0].astype(F32)
            for k in range(1, n_mp):
                copies.wait(r.line.at[1, c, k], me, sent[c, k])
                r.shards[c] += r.line[1, c, k].astype(F32)
        r.small_shard[...] = small_total[mp]
        for k in range(1, n_mp):
            copies.wait(r.small_line.at[k], me, sent[k])
            r.small_shard[...] += r.small_line[k]
        for (i, k), slot in travels.items():
            copies.wait(r.arrived[k - 1].at[owned - n_late + i], me, slot)
        copies.finish()

    return launch(
        attention_back,
        identity,
        dict(
            full=(given.full, hbm()),
            late=(given.late, hbm()),
            begun=(given.arrived, hbm()),
            residual=(given.residual, vmem()),
            hidden=(given.hidden, vmem()),
            cotangent=(given.cotangent, vmem()),
            total=(given.total, vmem()),
            gate_parts=(given.gate_parts, vmem()),
            terms=(given.terms, hbm()),
            probs=(given.probs, vmem()),
            normed=(given.normed, vmem()),
            normed_two=(given.normed_two, vmem()),
            queries=(given.queries, vmem()),
            keyval=(given.keyval, vmem()),
            context=(given.context, vmem()),
            gains=(given.gains, vmem()),
            router=(given.router, vmem()),
            query_table=(given.tables[0], vmem()),
            key_table=(given.tables[1], vmem()),
        ),
        dict(
            input_grad=(single(tokens, width), vmem()),
            block_out=(single(tokens, width), vmem()),
            arrived=([low(*grad.shape) for grad in given.arrived], hbm()),
            shards=(single(3, rows, cols), vmem()),
            small_shard=(single(first_row + own_router, 128), vmem()),
        ),
        dict(
            grads=pltpu.VMEM((3, width, width), BF16),
            small=pltpu.VMEM((n_dp, n_mp, first_row + own_router, 128), F32),
            small_rooms=pltpu.VMEM((n_dp - 1, n_mp, first_row + own_router, 128), F32),
            small_line=pltpu.VMEM((n_mp, first_row + own_router, 128), F32),
            terms_even=pltpu.VMEM((groups, n_dp // 2, tokens, width), BF16),
            term_sems=pltpu.SemaphoreType.DMA((groups, n_dp // 2)),
            weight_rooms=pltpu.VMEM((3, 2, n_dp - 1, part_rows, width), BF16),
            line=pltpu.VMEM((2, 3, n_mp, rows, cols), BF16),
            rooms=rooms,
            across=across_room,
            weights=pltpu.VMEM((3, width, width), BF16),
            turned=pltpu.VMEM((128, tokens), F32),
            grad_router=pltpu.VMEM((width, 128), F32),
            grad_hidden=pltpu.VMEM((tokens, width), F32),
            grad_attn=pltpu.VMEM((tokens, width), BF16),
            grad_context=pltpu.VMEM((tokens, width), BF16),
            grad_q=pltpu.VMEM((tokens, width), BF16),
            grad_kv=pltpu.VMEM((tokens, width), F32),
            grad_kv_low=pltpu.VMEM((tokens, width), BF16),
            grad_normed=pltpu.VMEM((tokens, width), F32),
            swap=pltpu.VMEM((2, tokens, width), BF16),
            local_sems=pltpu.SemaphoreType.DMA((3,)),
        ),
        n_copies,
        62 << 20,
        dict(arrived="begun"),
    )


class TokenReduce:
    def __init__(self, copies, n_dp, me, partner, groups, block, rooms, across):
        self.copies, self.me, self.across = copies, me, across
        self.partner = partner
        self.tokens = across.shape[1]
        self.n_dp = n_dp
        self.last = n_dp.bit_length() - 2
        self.groups = groups
        self.halves = [copies.slot(), copies.slot()]

        def tree(group, part, order):
            cut = pl.ds(part * (self.tokens // 2), self.tokens // 2)
            return TreeReduce(
                copies,
                order,
                n_dp,
                me,
                lambda j: block(group, j).at[cut],
                lambda number: rooms.at[group, part, number],
                add_rows(),
            )

        self.trees = [
            [tree(group, part, order) for part, order in enumerate(orders_of(n_dp))]
            for group in range(self.groups)
        ]

    def first(self, group, j):
        for tree in self.trees[group]:
            tree.send(j)

    def level(self, group, p):
        if group == self.groups:
            return
        for j in range(1, self.n_dp):
            for tree in self.trees[group]:
                if place_of(tree.order, j) == p:
                    tree.collect(j)
                    tree.send(j)

    def pass_on(self):
        if self.groups == 1:
            return
        for part, tree in enumerate(self.trees[1]):
            tree.collect(0)
            cut = pl.ds(part * (self.tokens // 2), self.tokens // 2)
            self.copies.start(
                tree.total(), self.across.at[0, cut], self.partner, self.halves[part]
            )

    def end(self, out_ref):
        for tree in self.trees[0]:
            tree.collect(0)
        for part, tree in enumerate(self.trees[0]):
            cut = pl.ds(part * (self.tokens // 2), self.tokens // 2)
            total = tree.total()[...].astype(F32)
            if self.groups > 1:
                self.copies.wait(self.across.at[0, cut], self.me, self.halves[part])
                total = total + self.across[0, cut, :].astype(F32)
            out_ref[cut, :] = total


def reduce_rooms(groups, n_dp, tokens, width, dtype):
    return [
        pltpu.VMEM((groups, 2, n_dp - 1, tokens // 2, width), dtype),
        pltpu.VMEM((1, tokens, width), dtype),
    ]


def run_experts(n_dp, n_mp, groups, identity, rows, table, cots, packed, near):
    owned, _, hidden, width = packed.shape
    span = n_mp // groups
    units = span * hidden
    blocks = groups * n_dp
    slots = blocks * CAP
    tokens = rows.shape[0]
    per_tile = 4
    tile = per_tile * CAP
    n_tiles = blocks // per_tile
    here = [expert for experts, _ in near for expert in experts]
    coming = [expert for expert in range(owned) if expert not in here]
    n_sent = min(owned, 2)
    n_late = owned - n_sent
    n_copies = groups + 1 + 2 * (blocks - 1) + 4 * groups * (n_dp - 1)
    n_copies += (len(coming) + n_sent) * (span - 1)
    order = []
    for group in range(groups):
        for level in range(n_dp.bit_length()):
            order += [(group, j) for j in range(n_dp) if bin(j).count("1") == level]

    def experts(r):
        dp, mp = lax.axis_index("dp"), lax.axis_index("mp")
        me = (dp, mp)
        other = flip_all(mp, span)
        copies = Copies(r.send_sems, r.recv_sems)
        peers = {
            (group, j): (flip_all(dp, j), other if group else mp)
            for group in range(groups)
            for j in range(n_dp)
            if group + j
        }
        local = iter(range(n_loads))

        def load(source, target):
            copy = pltpu.make_async_copy(source, target, r.load_sems.at[next(local)])
            copy.start()
            return copy

        def units_of(k):
            return pl.ds(k * hidden, hidden)

        own_table = load(r.own_table.at[dp], r.tables.at[0])
        own_rows = load(r.rows, r.rows_all.at[0, 0])
        loads = [
            [load(r.packed.at[e], r.weights.at[e, :, units_of(0)])] for e in range(owned)
        ]
        for number, (some, _) in enumerate(near):
            for i, e in enumerate(some):
                for k in range(1, span):
                    source = r.near[number * (span - 1) + k - 1].at[i]
                    loads[e].append(load(source, r.weights.at[e, :, units_of(k)]))

        def cot_copy(number):
            group, j = order[number]
            return pltpu.make_async_copy(
                r.cots[group].at[j], r.cot.at[number % 2], r.cot_sems.at[number % 2]
            )

        cot_copy(0).start()
        greet(list(peers.values()) + [(dp, flip_all(mp, k)) for k in range(1, span)])
        if groups > 1:
            across = copies.slot()
            copies.start(r.rows, r.rows_all.at[1, 0], peers[1, 0], across)
        sent = {}
        for (group, j), device in peers.items():
            sent[group, j] = copies.slot()
            copies.start(
                r.own_table.at[device[0]],
                r.tables.at[order.index((group, j))],
                device,
                sent[group, j],
            )
        trees = [row_trees(copies, n_dp, me, r.rows_all.at[group]) for group in range(groups)]
        own_rows.wait()
        for tree in trees[0]:
            tree.send(0)
        own_table.wait()

        def hits(number, some):
            slot = lax.broadcasted_iota(jnp.int32, (CAP, tokens), 0).astype(F32)
            found = [slot == r.tables[number, pl.ds(i, 1), :] for i in some]
            return found[0] if len(found) == 1 else jnp.concatenate(found, 0)

        def fill(number):
            group, j = order[number]
            if number:
                copies.wait(r.tables.at[number], me, sent[group, j])
            if number + 1 < blocks:
                cot_copy(number + 1).start()
            pick = hits(number, range(owned)).astype(BF16)
            there = slice(number * CAP, (number + 1) * CAP)
            found = dot(pick, r.rows_all[group, j], NN).astype(BF16)
            for i in range(owned):
                r.x[i + 1, there, :] = found[i * CAP : (i + 1) * CAP]
            cot_copy(number).wait()
            found = dot(pick, r.cot[number % 2], NN).astype(BF16)
            for i in range(owned):
                r.y[i, there, :] = found[i * CAP : (i + 1) * CAP]

        def work(e, step):
            rows = pl.ds(pl.multiple_of(step * tile, 16), tile)
            x = r.x[e + 1, rows, :]
            gate = dot(x, r.weights[e, 0], NT)
            up = dot(x, r.weights[e, 1], NT)
            sigmoid = 1.0 / (1.0 + jnp.exp(-gate))
            silu = gate * sigmoid
            activation = (silu * up).astype(BF16)
            r.act[rows, :] = activation
            made = dot(activation, r.weights[e, 2], NN)
            cot = r.y[e, rows, :].astype(F32)
            chosen = []
            dots = jnp.sum(cot * made, -1, keepdims=True)
            for b in range(per_tile):
                number = step * per_tile + b
                hit = hits(number, (e,))
                chance = r.tables[number, pl.ds(4 + e, 1), :]
                chosen.append(jnp.sum(jnp.where(hit, chance, 0.0), -1, keepdims=True))
                mine = dots[b * CAP : (b + 1) * CAP]
                r.gates[number, pl.ds(e, 1), :] = jnp.sum(
                    jnp.where(hit, mine, 0.0), 0, keepdims=True
                )
            share = jnp.concatenate(chosen, 0)
            r.y[e, rows, :] = (share * made).astype(BF16)
            back = (share * cot).astype(BF16)
            r.back[rows, :] = back
            grad_act = dot(back, r.weights[e, 2], NT)
            grad_gate = grad_act * up * sigmoid * (1.0 + gate * (1.0 - sigmoid))
            grad_gate = grad_gate.astype(BF16)
            grad_up = (grad_act * silu).astype(BF16)
            r.pair[rows, pl.ds(0, units)] = grad_gate
            r.pair[rows, pl.ds(units, units)] = grad_up
            found = dot(grad_gate, r.weights[e, 0], NN) + dot(grad_up, r.weights[e, 1], NN)
            r.x[e, rows, :] = found.astype(BF16)

        def ready(e):
            for copy in loads[e]:
                copy.wait()
            if e in coming:
                for k in range(1, span):
                    copies.wait(r.weights.at[e, :, units_of(k)], me, weights_sent[e, k])

        stores = []

        def weight_grad(e):
            for c in range(3):
                source = r.act[...] if c == 2 else r.pair[:, pl.ds(c * units, units)]
                rhs = r.back[...] if c == 2 else r.x[e + 1]
                r.weights[e, c] = dot(source, rhs, TN).astype(BF16)
            stores.append(load(r.weights.at[e, :, units_of(0)], r.grad_own.at[e]))
            for k in range(1, span):
                source = r.weights.at[e, :, units_of(k)]
                if e < n_sent:
                    grads_sent[e, k] = copies.slot()
                    copies.start(
                        source, r.arrived[k - 1].at[e], (dp, flip_all(mp, k)), grads_sent[e, k]
                    )
                else:
                    stores.append(load(source, r.late[k - 1].at[e - n_sent]))

        weights_sent, grads_sent = {}, {}
        ready(0)
        done = 0
        leaving = []
        for number, (group, j) in enumerate(order):
            if j:
                for tree in sorted(trees[group], key=lambda tree: place_of(tree.order, j)):
                    tree.receive(j)
                    tree.send(j)
            elif group:
                copies.wait(r.rows_all.at[1, 0], me, across)
                for tree in trees[1]:
                    tree.send(0)
            if group == groups - 1 and j == 0:
                leaving += copies.split()
                for e in coming:
                    for k in range(1, span):
                        weights_sent[e, k] = copies.slot()
                        copies.start(
                            r.packed.at[e],
                            r.weights.at[e, :, units_of(k)],
                            (dp, flip_all(mp, k)),
                            weights_sent[e, k],
                        )
                staying = copies.split()
            fill(number)
            if number % per_tile == per_tile - 1 and number < blocks - 1:
                work(0, done)
                done += 1
        work(0, done)
        leaving += copies.split()
        copies.sent = staying
        weight_grad(0)

        def tiles(e, first, end):
            def step(at, carry):
                work(e, at)
                return carry

            lax.fori_loop(first, end, step, 0)

        for e in range(1, owned - 1):
            ready(e)
            tiles(e, 0, n_tiles)
            weight_grad(e)
        copies.finish(leaving)
        partner = (dp, other)
        reduce = TokenReduce(
            copies, n_dp, me, partner, groups, lambda g, j: r.rows_all.at[g, j], r.rooms, r.across
        )
        last = owned - 1
        if last:
            ready(last)
        scattered = []

        def sum_copy(at):
            group, j = scattered[at]
            return pltpu.make_async_copy(
                r.sums.at[at % 2], r.terms.at[group, j], r.sum_sems.at[at % 2]
            )

        own_gates = pltpu.make_async_copy(r.gates.at[0], r.gate_parts.at[dp, 0], r.gate_sem.at[0])
        gates_sent = {}

        def scatter(group, j):
            number = order.index((group, j))
            if number:
                gates_sent[group, j] = copies.slot()
                copies.start(
                    r.gates.at[number],
                    r.gate_parts.at[dp, group],
                    peers[group, j],
                    gates_sent[group, j],
                )
            else:
                own_gates.start()
            there = slice(number * CAP, (number + 1) * CAP)
            pick = hits(number, range(owned)).astype(BF16)
            found = jnp.concatenate([r.x[e, there, :] for e in range(owned)], 0)
            r.rows_all[group, j] = dot(pick, found, TN).astype(BF16)
            if j % 2:
                reduce.first(group, j)
            found = jnp.concatenate([r.y[e, there, :] for e in range(owned)], 0)
            at = len(scattered)
            scattered.append((group, j))
            if at > 1:
                sum_copy(at - 2).wait()
            r.sums[at % 2] = dot(pick, found, TN).astype(BF16)
            sum_copy(at).start()

        halves = [
            (n_tiles * group // groups, n_tiles * (group + 1) // groups) for group in range(groups)
        ]
        levels = list(range(reduce.last - 1, -1, -1))
        for group in range(groups)[::-1]:
            first, end = halves[group]
            if last == 0:
                pass
            elif group == groups - 1:
                tiles(last, first, end)
            else:
                for at in range(first, end):
                    tiles(last, at, at + 1)
                    if levels:
                        reduce.level(1, levels.pop(0))
            for j in [j for j in range(n_dp) if j % 2] + [j for j in range(n_dp) if j % 2 == 0]:
                scatter(group, j)
        if groups > 1:
            for p in levels:
                reduce.level(1, p)
        reduce.pass_on()
        for p in range(reduce.last - 1, -1, -1):
            reduce.level(0, p)
            if p == reduce.last - 1 and last:
                weight_grad(last)
        reduce.end(r.total)
        for at in (blocks - 2, blocks - 1):
            sum_copy(at).wait()
        own_gates.wait()
        for (group, j), device in peers.items():
            copies.wait(r.gate_parts.at[device[0], group], me, gates_sent[group, j])
        for (e, k), slot in grads_sent.items():
            copies.wait(r.arrived[k - 1].at[e], me, slot)
        for copy in stores:
            copy.wait()
        copies.finish()

    n_loads = 2 + owned * span + owned * span
    near_refs = [part for _, parts in near for part in parts]
    weights = packed.shape[1:]
    rooms, across_room = reduce_rooms(groups, n_dp, tokens, width, BF16)
    return launch(
        experts,
        identity,
        dict(
            rows=(rows, hbm()),
            own_table=(table, hbm()),
            cots=(cots, hbm()),
            packed=(packed, hbm()),
            near=(near_refs, hbm()),
        ),
        dict(
            terms=(low(groups, n_dp, tokens, width), hbm()),
            gate_parts=(single(n_dp, groups, 8, tokens), hbm()),
            total=(single(tokens, width), vmem()),
            grad_own=(low(owned, *weights), hbm()),
            arrived=([low(owned, *weights) for _ in range(1, span)], hbm()),
            late=([low(n_late, *weights) for _ in range(1, span) if n_late], hbm()),
        ),
        dict(
            weights=pltpu.VMEM((owned, 3, units, width), BF16),
            rows_all=pltpu.VMEM((groups, n_dp, tokens, width), BF16),
            x=pltpu.VMEM((owned + 1, slots, width), BF16),
            y=pltpu.VMEM((owned, slots, width), BF16),
            act=pltpu.VMEM((slots, units), BF16),
            pair=pltpu.VMEM((slots, 2 * units), BF16),
            back=pltpu.VMEM((slots, width), BF16),
            tables=pltpu.VMEM((blocks, 8, tokens), F32),
            gates=pltpu.VMEM((blocks, 8, tokens), F32),
            cot=pltpu.VMEM((2, tokens, width), BF16),
            sums=pltpu.VMEM((2, tokens, width), BF16),
            rooms=rooms,
            across=across_room,
            load_sems=pltpu.SemaphoreType.DMA((n_loads,)),
            cot_sems=pltpu.SemaphoreType.DMA((2,)),
            sum_sems=pltpu.SemaphoreType.DMA((2,)),
            gate_sem=pltpu.SemaphoreType.DMA((1,)),
        ),
        n_copies,
        63 << 20,
    )


def adamw(weight, gradient, moment_one, moment_two, rate_val, decay_val):
    first_new = 0.9 * moment_one + 0.1 * gradient
    second_new = 0.95 * moment_two + 0.05 * gradient * gradient
    first_hat = first_new / (1.0 - 0.9**STEP)
    second_hat = second_new / (1.0 - 0.95**STEP)
    weight_new = weight - rate_val * (
        first_hat / (jnp.sqrt(second_hat) + 1e-08) + decay_val * weight
    )
    return (gradient, weight_new, first_new, second_new)


def local(
    n_dp,
    n_mp,
    residual_in,
    cotangent,
    expert_ids,
    attn_gain,
    query_w,
    key_value_weight,
    output_w,
    moe_gain,
    router_w,
    gateup_w,
    down_w,
    attn_gain_mean,
    attn_gain_var,
    query_mean,
    query_var,
    key_value_first_moment,
    key_value_second_moment,
    output_mean,
    output_var,
    moe_gain_mean,
    moe_gain_var,
    router_mean,
    router_var,
    gateup_mean,
    gateup_var,
    down_mean,
    down_var,
):
    mp = lax.axis_index("mp")
    place_in_all = lax.axis_index("dp") * n_mp + mp
    groups = 2 if 2 * n_dp <= 16 else 1
    tokens = residual_in.shape[0]
    owned = gateup_w.shape[0]
    span = n_mp // groups
    own_gain, own_router = attn_gain.shape[0], router_w.shape[0]
    first_row, lanes = 8, 128
    per_tile = lanes // own_gain

    def spread(gain):
        return jnp.where(jnp.arange(lanes) // own_gain == place_in_all % per_tile, jnp.tile(gain, per_tile), 0.0)

    small = jnp.concatenate(
        [
            spread(attn_gain)[None],
            spread(moe_gain)[None],
            jnp.zeros((first_row - 2, lanes), F32),
            jnp.pad(router_w, ((0, 0), (0, lanes - EXPERTS))),
        ]
    )
    shards = jnp.stack([query_w, key_value_weight, output_w.T]).astype(BF16)
    cot_low = cotangent.astype(BF16)
    start = prologue(
        n_dp, n_mp, 0, first_row, small, shards, cot_low, residual_in, gateup_w, down_w
    )
    tables = [jnp.asarray(table) for table in rotary_constants()]
    early = list(range(owned))[:1]
    front = attention_forward(
        n_dp, n_mp, groups, 1, residual_in, expert_ids.T, start, cot_low, tables, early
    )

    found = run_experts(
        n_dp,
        n_mp,
        groups,
        2,
        front.normed_two,
        front.table,
        [start.cots, front.cots][:groups],
        start.packed,
        [(early, front.near)],
    )

    given = types.SimpleNamespace(
        full=front.full,
        residual=residual_in,
        hidden=front.hidden,
        cotangent=cotangent,
        total=found.total,
        late=found.late,
        arrived=found.arrived,
        gate_parts=found.gate_parts,
        terms=found.terms,
        probs=front.probs,
        normed=front.normed,
        normed_two=front.normed_two,
        queries=front.queries,
        keyval=front.keyval,
        context=front.context,
        gains=start.gains,
        router=start.router,
        tables=tables,
    )
    back = attention_backward(n_dp, n_mp, groups, 3, given, first_row)
    input_grad, block_out = back.input_grad, back.block_out
    gateup_grad, down_grad = (
        sum(part[:, cut].astype(F32) for part in [found.grad_own] + back.arrived)
        for cut in (slice(0, 2), 2)
    )
    grads, small_grads = back.shards, back.small_shard
    query_grad, keyval_grad, output_grad = grads[0], grads[1], grads[2].T
    first_lane = (place_in_all % per_tile) * own_gain
    gain_one_grad, gain_two_grad = (
        lax.dynamic_slice_in_dim(small_grads[row], first_lane, own_gain) for row in (0, 1)
    )
    router_grad = small_grads[first_row:, :EXPERTS]
    matrix_rate = 0.2 / math.sqrt(MODEL_WIDTH)
    gain_one_all = adamw(attn_gain, gain_one_grad, attn_gain_mean, attn_gain_var, 0.1, 0.0)
    query_all = adamw(query_w, query_grad, query_mean, query_var, matrix_rate, 0.1)
    keyval_all = adamw(
        key_value_weight,
        keyval_grad,
        key_value_first_moment,
        key_value_second_moment,
        matrix_rate,
        0.1,
    )
    output_all = adamw(output_w, output_grad, output_mean, output_var, 0.1, 0.1)
    gain_two_all = adamw(moe_gain, gain_two_grad, moe_gain_mean, moe_gain_var, 0.1, 0.0)
    router_all = adamw(router_w, router_grad, router_mean, router_var, matrix_rate, 0.1)
    gateup_all = adamw(gateup_w, gateup_grad, gateup_mean, gateup_var, matrix_rate, 0.1)
    down_all = adamw(down_w, down_grad, down_mean, down_var, 0.07, 0.1)
    return (
        block_out,
        input_grad,
        gain_one_all[0],
        gain_one_all[1],
        gain_one_all[2],
        gain_one_all[3],
        query_all[0],
        query_all[1],
        query_all[2],
        query_all[3],
        keyval_all[0],
        keyval_all[1],
        keyval_all[2],
        keyval_all[3],
        output_all[0],
        output_all[1],
        output_all[2],
        output_all[3],
        gain_two_all[0],
        gain_two_all[1],
        gain_two_all[2],
        gain_two_all[3],
        router_all[0],
        router_all[1],
        router_all[2],
        router_all[3],
        gateup_all[0],
        gateup_all[1],
        gateup_all[2],
        gateup_all[3],
        down_all[0],
        down_all[1],
        down_all[2],
        down_all[3],
    )


def solution(mesh):
    in_specs = (
        P(("dp", "mp"), None),
        P(("dp", "mp"), None),
        P(("dp", "mp"), None),
        P(("dp", "mp")),
        P("dp", "mp"),
        P("dp", "mp"),
        P("mp", "dp"),
        P(("dp", "mp")),
        P(("dp", "mp"), None),
        P("dp", None, "mp", None),
        P("dp", "mp", None),
        P(("dp", "mp")),
        P(("dp", "mp")),
        P("dp", "mp"),
        P("dp", "mp"),
        P("dp", "mp"),
        P("dp", "mp"),
        P("mp", "dp"),
        P("mp", "dp"),
        P(("dp", "mp")),
        P(("dp", "mp")),
        P(("dp", "mp"), None),
        P(("dp", "mp"), None),
        P("dp", None, "mp", None),
        P("dp", None, "mp", None),
        P("dp", "mp", None),
        P("dp", "mp", None),
    )
    out_specs = (
        P(("dp", "mp"), None),
        P(("dp", "mp"), None),
        P(("dp", "mp")),
        P(("dp", "mp")),
        P(("dp", "mp")),
        P(("dp", "mp")),
        P("dp", "mp"),
        P("dp", "mp"),
        P("dp", "mp"),
        P("dp", "mp"),
        P("dp", "mp"),
        P("dp", "mp"),
        P("dp", "mp"),
        P("dp", "mp"),
        P("mp", "dp"),
        P("mp", "dp"),
        P("mp", "dp"),
        P("mp", "dp"),
        P(("dp", "mp")),
        P(("dp", "mp")),
        P(("dp", "mp")),
        P(("dp", "mp")),
        P(("dp", "mp"), None),
        P(("dp", "mp"), None),
        P(("dp", "mp"), None),
        P(("dp", "mp"), None),
        P("dp", None, "mp", None),
        P("dp", None, "mp", None),
        P("dp", None, "mp", None),
        P("dp", None, "mp", None),
        P("dp", "mp", None),
        P("dp", "mp", None),
        P("dp", "mp", None),
        P("dp", "mp", None),
    )
    step = functools.partial(local, mesh.shape["dp"], mesh.shape["mp"])
    return jax.shard_map(step, mesh=mesh, in_specs=in_specs, out_specs=out_specs, check_vma=False)
```

```python
import functools
import math
import types

import jax
import jax.numpy as jnp
import numpy as np
from jax import lax
from jax.experimental import pallas as pl
from jax.experimental.pallas import tpu as pltpu
from jax.sharding import PartitionSpec as P

MODEL_WIDTH = 1024
QUERY_HEADS = 16
KEY_VALUE_HEADS = 8
HEAD_SIZE = 64
EXPERTS = 32
TOPK = 8
SEQUENCE_TOKENS = 512
STEP = 3
CAP = 80

NORM_EPS = 1e-06
MESH = pl.DeviceIdType.MESH
BF16 = jnp.bfloat16
F32 = jnp.float32


def flip(index, mask):
    return index + mask * (1 - 2 * lax.rem(lax.div(index, mask), 2))


def flip_all(index, masks):
    bit = 1
    while bit <= masks:
        if masks & bit:
            index = flip(index, bit)
        bit *= 2
    return index


def bits_of(size):
    return [1 << i for i in range(size.bit_length() - 1)]


def orders_of(n_dp):
    bits = bits_of(n_dp)
    return bits[1:] + bits[:1], bits[1:][::-1] + bits[:1]


def place_of(order, j):
    place = -1
    for at, mask in enumerate(order):
        if j & mask:
            place = at
    return place


def greet(partners):
    barrier = pltpu.get_barrier_semaphore()
    for partner in partners:
        pl.semaphore_signal(barrier, inc=1, device_id=partner, device_id_type=MESH)
    pl.semaphore_wait(barrier, len(partners))


class Copies:
    def __init__(self, send_sems, recv_sems):
        self.send_sems, self.recv_sems = send_sems, recv_sems
        self.used = 0
        self.sent = []

    def slot(self):
        self.used += 1
        return self.used - 1

    def make(self, source, target, device, slot):
        return pltpu.make_async_remote_copy(
            src_ref=source,
            dst_ref=target,
            send_sem=self.send_sems.at[slot],
            recv_sem=self.recv_sems.at[slot],
            device_id=device,
            device_id_type=MESH,
        )

    def start(self, source, target, device, slot):
        copy = self.make(source, target, device, slot)
        copy.start()
        self.sent.append(copy)

    def wait(self, target, device, slot):
        self.make(target, target, device, slot).wait_recv()

    def split(self):
        before, self.sent = self.sent, []
        return before

    def finish(self, some=None):
        for copy in self.sent if some is None else some:
            copy.wait_send()


class TreeGather:
    def __init__(self, copies, order, n_dp, me, source, target):
        self.copies, self.order, self.n_dp, self.me = copies, order, n_dp, me
        self.source, self.target = source, target
        self.slots = {j: copies.slot() for j in range(1, n_dp)}

    def level(self, j):
        return bin(j).count("1")

    def send(self, j):
        dp, mp = self.me
        for mask in self.order[place_of(self.order, j) + 1 :]:
            self.copies.start(
                self.source(j), self.target(j, mask), (flip(dp, mask), mp), self.slots[j ^ mask]
            )

    def receive(self, j):
        self.copies.wait(self.source(j), self.me, self.slots[j])

    def steps(self):
        return sorted(range(1, self.n_dp), key=lambda j: (self.level(j), place_of(self.order, j)))


def run_gathers(trees):
    n_dp = trees[0].n_dp
    for level in range(1, n_dp.bit_length()):
        for tree in trees:
            for j in tree.steps():
                if tree.level(j) == level:
                    tree.receive(j)
                    tree.send(j)


class TreeReduce:
    def __init__(self, copies, order, n_dp, me, block, room, add):
        self.copies, self.order, self.n_dp, self.me = copies, order, n_dp, me
        self.block, self.room, self.add = block, room, add
        self.keys = [
            (j, q) for j in range(n_dp) for q in range(len(order) - 1, place_of(order, j), -1)
        ]
        self.slots = {key: copies.slot() for key in self.keys}

    def number(self, key):
        return self.keys.index(key)

    def send(self, j):
        dp, mp = self.me
        p = place_of(self.order, j)
        last = len(self.order) - 1
        source = self.block(j) if p == last else self.room(self.number((j, last)))
        mask = self.order[p]
        key = (j ^ mask, p)
        self.copies.start(source, self.room(self.number(key)), (flip(dp, mask), mp), self.slots[key])

    def collect(self, j):
        last = len(self.order) - 1
        for q in range(last, place_of(self.order, j), -1):
            here = self.room(self.number((j, q)))
            self.copies.wait(here, self.me, self.slots[(j, q)])
            if q == last:
                self.add(here, self.block(j))
            else:
                self.add(self.room(self.number((j, last))), here)

    def total(self):
        return self.room(self.number((0, len(self.order) - 1)))


def add_rows(step=16):
    def add(here, other):
        def body(i, carry):
            rows = pl.ds(pl.multiple_of(i * step, step), step)
            total = here[..., rows, :].astype(F32) + other[..., rows, :].astype(F32)
            here[..., rows, :] = total.astype(here.dtype)
            return carry

        lax.fori_loop(0, here.shape[-2] // step, body, 0)

    return add


def hbm():
    return pl.BlockSpec(memory_space=pl.ANY)


def vmem():
    return pl.BlockSpec(memory_space=pltpu.VMEM)


def params(identity, limit=None):
    return pltpu.CompilerParams(
        collective_id=identity, has_side_effects=True, vmem_limit_bytes=limit
    )


def launch(kernel, identity, ins, outs, scratch, n_copies, limit=None, kept=None):
    def flat(entries):
        names, leaves, specs = [], [], []
        for name, (value, spec) in entries.items():
            several = isinstance(value, list)
            new = value if several else [value]
            names.append((name, len(new) if several else None))
            leaves += new
            specs += [spec] * len(new)
        return names, leaves, specs

    def unflat(names, leaves):
        leaves, found = list(leaves), {}
        for name, count in names:
            found[name] = leaves[0] if count is None else leaves[:count]
            leaves = leaves[1 if count is None else count :]
        return found

    scratch = scratch | dict(
        send_sems=pltpu.SemaphoreType.DMA((n_copies,)),
        recv_sems=pltpu.SemaphoreType.DMA((n_copies,)),
    )
    in_names, values, in_specs = flat(ins)
    out_names, shapes, out_specs = flat(outs)

    def numbers(names, wanted):
        at = 0
        for name, count in names:
            size = 1 if count is None else count
            if name == wanted:
                return range(at, at + size)
            at += size

    aliases = {}
    for output, source in (kept or {}).items():
        aliases |= dict(zip(numbers(in_names, source), numbers(out_names, output)))
    scratch_names = [(name, None) for name in scratch]

    def body(*refs):
        named = unflat(in_names + out_names + scratch_names, refs)
        kernel(types.SimpleNamespace(**named))

    results = pl.pallas_call(
        body,
        out_shape=tuple(shapes),
        in_specs=in_specs,
        out_specs=tuple(out_specs),
        scratch_shapes=list(scratch.values()),
        input_output_aliases=aliases,
        compiler_params=params(identity, limit),
        cost_estimate=pl.CostEstimate(flops=1, bytes_accessed=1, transcendentals=0),
        name=kernel.__name__,
    )(*values)
    return types.SimpleNamespace(**unflat(out_names, results))


def low(*shape):
    return jax.ShapeDtypeStruct(shape, BF16)


def single(*shape):
    return jax.ShapeDtypeStruct(shape, F32)


def dot(a, b, contract):
    return lax.dot_general(a, b, ((contract[:1], contract[1:]), ((), ())), preferred_element_type=F32)


NN, NT, TN = (1, 0), (1, 1), (0, 0)


def run_level(trees, level):
    for one in trees:
        for j in one.steps():
            if one.level(j) == level:
                one.receive(j)
                one.send(j)


def send_experts(copies, me, span, packed, near, experts):
    dp, mp = me
    slots = {}
    for i, expert in enumerate(experts):
        for k in range(1, span):
            slots[i, k] = copies.slot()
            copies.start(
                packed.at[expert], near[k - 1].at[i], (dp, flip_all(mp, k)), slots[i, k]
            )
    return slots


def wait_experts(copies, me, near, slots):
    for (i, k), slot in slots.items():
        copies.wait(near[k - 1].at[i], me, slot)


def row_trees(copies, n_dp, me, rows_all):
    tokens = rows_all.shape[1]

    def tree(part, order):
        cut = pl.ds(part * (tokens // 2), tokens // 2)
        return TreeGather(
            copies,
            order,
            n_dp,
            me,
            lambda j: rows_all.at[j, cut],
            lambda j, mask: rows_all.at[j ^ mask, cut],
        )

    return [tree(part, order) for part, order in enumerate(orders_of(n_dp))]


def rotary_constants():
    half_width = HEAD_SIZE // 2
    frequency = np.exp(
        np.float32(-math.log(10000.0)) * np.arange(half_width, dtype=np.float32) * np.float32(2.0)
        / np.float32(HEAD_SIZE)
    ).astype(np.float32)
    angles = np.arange(SEQUENCE_TOKENS, dtype=np.float32)[:, None] * frequency[None, :]
    cosine, sine = np.cos(angles), np.sin(angles)
    cosine = np.concatenate([cosine, cosine], 1)
    sine = np.concatenate([-sine, sine], 1)
    queries = np.stack([np.tile(cosine, (1, 2)), np.tile(sine, (1, 2))])
    keys = np.stack(
        [
            np.concatenate([cosine, np.ones_like(cosine)], 1),
            np.concatenate([sine, np.zeros_like(sine)], 1),
        ]
    )
    return queries.astype(np.float32), keys.astype(np.float32)


def rotate(value, cosine, sine):
    lane = lax.broadcasted_iota(jnp.int32, value.shape, 1)
    rolled = jnp.where(
        lane % HEAD_SIZE < HEAD_SIZE // 2,
        pltpu.roll(value, 128 - HEAD_SIZE // 2, 1),
        pltpu.roll(value, HEAD_SIZE // 2, 1),
    )
    return value * cosine + rolled * sine


def group_operands(queries, keyval):
    lane = lax.broadcasted_iota(jnp.int32, queries.shape, 1)
    both = jnp.concatenate(
        [jnp.where(lane < HEAD_SIZE, queries, 0.0), jnp.where(lane < HEAD_SIZE, 0.0, queries)], 0
    ).astype(BF16)
    lane = lax.broadcasted_iota(jnp.int32, keyval.shape, 1)
    turned = pltpu.roll(keyval, HEAD_SIZE, 1)
    keys = jnp.where(lane < HEAD_SIZE, keyval, turned).astype(BF16)
    values = jnp.where(lane < HEAD_SIZE, turned, keyval).astype(BF16)
    return both, keys, values


def merge_heads(both):
    tokens = both.shape[0] // 2
    lane = lax.broadcasted_iota(jnp.int32, (tokens, 128), 1)
    return jnp.where(lane < HEAD_SIZE, both[:tokens], both[tokens:])


def seen(tokens, mp):
    shape = (2 * tokens, 2 * tokens)
    row = lax.broadcasted_iota(jnp.int32, shape, 0) % tokens
    key = lax.broadcasted_iota(jnp.int32, shape, 1)
    shift = tokens - 2 * tokens * lax.rem(mp, 2)
    key = jnp.where(key < tokens, key, key - tokens + shift)
    return key <= row


def softmax_of(both, keys, mask):
    scores = dot(both, keys, NT) * (1.0 / math.sqrt(HEAD_SIZE))
    raised = jnp.exp(jnp.where(mask, scores, -1e30))
    return raised / jnp.sum(raised, -1, keepdims=True)


def store_blocks(trees, level, source, target, sems):
    stores = []
    for j in range(source.shape[0]) if trees else []:
        if trees[0].level(j) == level:
            stores.append(pltpu.make_async_copy(source.at[j], target.at[j], sems.at[j]))
            stores[-1].start()
    return stores


def attention_forward(
    n_dp, n_mp, groups, identity, first_row, small, shards, cot, residual, gateup, down, ids, tables, experts
):
    tokens, width = residual.shape
    half = n_mp // 2
    kinds, rows, cols = shards.shape
    part_rows = rows // 2
    half_cols = half * cols
    n_heads = width // 128
    span = n_mp // groups
    owned, _, hidden, _ = gateup.shape
    n_devices = n_dp * n_mp
    own_router = small.shape[0] - first_row
    n_experts = len(experts)
    order_a, _ = orders_of(n_dp)
    n_copies = 2 * (n_mp - 1) + 10 * (n_dp - 1) + 2 + n_experts * (span - 1)

    def attention(r):
        dp, mp = lax.axis_index("dp"), lax.axis_index("mp")
        me = (dp, mp)
        neighbour = (dp, flip(mp, 1))
        partner = (dp, flip_all(mp, span))
        copies = Copies(r.send_sems, r.recv_sems)
        loads = [
            pltpu.make_async_copy(r.gateup, r.wide.at[:, pl.ds(0, 2)], r.local_sems.at[0]),
            pltpu.make_async_copy(r.down, r.wide.at[:, 2], r.local_sems.at[1]),
        ]
        for copy in loads:
            copy.start()
        own_small = r.small_all.at[dp, mp]
        own_rows = pl.ds(pl.multiple_of(dp * rows, rows), rows)
        own_cols = pl.ds(pl.multiple_of(mp * cols, cols), cols)
        own_part = r.full.at[:, own_rows, own_cols]
        r.small_all[dp, mp] = r.small[...]
        residual = r.residual[...]
        inverse = lax.rsqrt(jnp.mean(residual * residual, -1, keepdims=True) + NORM_EPS)
        r.scaled[0] = (residual * inverse).astype(BF16)
        r.full[:, own_rows, own_cols] = r.shards[...]
        r.cots[0] = r.cot[...]
        greet(
            [(flip_all(dp, mask), mp) for mask in bits_of(n_dp)]
            + [(dp, flip_all(mp, k)) for k in range(1, n_mp)]
        )
        line = {}
        for k in range(1, n_mp):
            line[k] = (copies.slot(), copies.slot())
            copies.start(r.small, own_small, (dp, flip_all(mp, k)), line[k][0])
        for k in range(1, n_mp):
            copies.start(r.shards, own_part, (dp, flip_all(mp, k)), line[k][1])
        across = (copies.slot(), copies.slot())
        copies.start(r.scaled.at[0], r.scaled.at[1], neighbour, across[0])
        if groups > 1:
            copies.start(r.cot, r.other_cots.at[0], partner, across[1])
        near = lax.div(mp, half)
        chunks = (near, 1 - near)
        chunk_cols = [
            pl.ds(pl.multiple_of(chunk * half_cols, half_cols), half_cols) for chunk in chunks
        ]

        def small_tree(chunk):
            first = pl.multiple_of(chunk * half, half)

            def ref(j, mask=0):
                return r.small_all.at[flip_all(dp, j), pl.ds(first, half)]

            return TreeGather(copies, order_a, n_dp, me, ref, ref)

        def weight_tree(chunk, part, order):
            def ref(j, mask=0):
                start = flip_all(dp, j) * rows + part * part_rows
                there = pl.ds(pl.multiple_of(start, part_rows), part_rows)
                return r.full.at[:, there, chunk_cols[chunk]]

            return TreeGather(copies, order, n_dp, me, ref, ref)

        def wait_line(first, end, which):
            for k in range(first, end):
                other = flip_all(mp, k)
                if which:
                    there = pl.ds(pl.multiple_of(other * cols, cols), cols)
                    copies.wait(r.full.at[:, own_rows, there], me, line[k][1])
                else:
                    copies.wait(r.small_all.at[dp, other], me, line[k][0])

        small_trees = [small_tree(chunk) for chunk in chunks]
        weight_trees = [
            [weight_tree(chunk, part, order) for part, order in enumerate(orders_of(n_dp))]
            for chunk in (0, 1)
        ]
        cot_trees = row_trees(copies, n_dp, me, r.cots)
        other_trees = row_trees(copies, n_dp, me, r.other_cots) if groups > 1 else []

        def send_own(trees):
            for one in trees:
                one.send(0)

        top = n_dp.bit_length() - 1
        wait_line(1, half, 0)
        send_own(small_trees[:1])
        wait_line(half, n_mp, 0)
        send_own(small_trees[1:])
        send_own(cot_trees)
        stores = store_blocks(cot_trees, 0, r.cots, r.cots_out, r.cot_sems)
        named = lax.broadcasted_iota(jnp.int32, (EXPERTS, tokens), 0)
        chosen = jnp.zeros((EXPERTS, tokens), F32)
        for k in range(TOPK):
            chosen += jnp.where(named == r.ids[k : k + 1, :], 1.0, 0.0)
        shape = (tokens, tokens)
        earlier = lax.broadcasted_iota(jnp.int32, shape, 0) < lax.broadcasted_iota(jnp.int32, shape, 1)
        before = dot(chosen.astype(BF16), jnp.where(earlier, 1.0, 0.0).astype(BF16), NN)
        place = jnp.where(chosen > 0.0, before, -1.0)
        r.table[...] = jnp.zeros_like(r.table)
        for expert in range(EXPERTS):
            owner, which = divmod(expert, owned)
            r.table[owner, which, :] = place[expert]
        wait_line(1, half, 1)
        send_own(weight_trees[0])
        for copy in loads:
            copy.wait()
        for e in range(owned):
            r.narrow[e] = r.wide[e].astype(BF16)
        stores.append(pltpu.make_async_copy(r.narrow, r.packed, r.local_sems.at[2]))
        stores[-1].start()
        for level in range(1, top + 1):
            if level == top:
                wait_line(half, n_mp, 1)
                send_own(weight_trees[1])
            run_level(small_trees, level)
            run_level(cot_trees, level)
            stores += store_blocks(cot_trees, level, r.cots, r.cots_out, r.cot_sems)
            run_level(weight_trees[0], level)
        n_tiles = width // 128
        for row in (0, 1):
            for tile in range(n_tiles):
                total = None
                for at in range(tile * n_devices // n_tiles, (tile + 1) * n_devices // n_tiles):
                    part = r.small_all[at // n_mp, at % n_mp, row : row + 1, :]
                    total = part if total is None else total + part
                r.gains[row : row + 1, tile * 128 : (tile + 1) * 128] = total
        for at in range(n_devices):
            r.router_wide[at * own_router : (at + 1) * own_router, :] = r.small_all[
                at // n_mp, at % n_mp, first_row:, :
            ]
        r.router[...] = r.router_wide[...].astype(BF16)
        copies.wait(r.scaled.at[1], me, across[0])
        residual = r.residual[...]
        inverse = lax.rsqrt(jnp.mean(residual * residual, -1, keepdims=True) + NORM_EPS)
        gain_one = r.gains[0:1, :]
        r.normed[0] = (residual * inverse * gain_one).astype(BF16)
        r.normed[1] = (r.scaled[1].astype(F32) * gain_one).astype(BF16)
        mask = seen(tokens, mp)
        which = lax.rem(mp, 2)

        def table(ref, at):
            there = pl.ds(pl.multiple_of(at * tokens, tokens), tokens)
            return ref[0, there, :], ref[1, there, :]

        def project(chunk):
            there = chunk_cols[chunk]
            r.q[:, there] = dot(r.normed[0], r.full[0, :, there], NN)
            for part in (0, 1):
                r.kv[part, :, there] = dot(r.normed[part], r.full[1, :, there], NN)

        def heads(chunk, first, end):
            def head(k, carry):
                number = chunks[chunk] * (n_heads // 2) + k
                lanes = pl.ds(pl.multiple_of(number * 128, 128), 128)
                queries = rotate(r.q[:, lanes], *table(r.query_table, which))
                r.queries[:, lanes] = queries.astype(BF16)
                parts = []
                for part, at in enumerate((which, 1 - which)):
                    parts.append(rotate(r.kv[part, :, lanes], *table(r.key_table, at)))
                    r.keyval[part, :, lanes] = parts[part].astype(BF16)
                both, keys, values = group_operands(queries, jnp.concatenate(parts, 0))
                chance = softmax_of(both, keys, mask).astype(BF16)
                r.context[:, lanes] = merge_heads(dot(chance, values, NN)).astype(BF16)
                return carry

            lax.fori_loop(first, end, head, 0)

        run_level(weight_trees[1], 1)
        if groups > 1:
            copies.wait(r.other_cots.at[0], me, across[1])
        send_own(other_trees)
        stores += store_blocks(other_trees, 0, r.other_cots, r.other_out, r.other_sems)
        sent = send_experts(copies, me, span, r.narrow, r.near, experts)
        project(0)
        heads(0, 0, 2)
        for level in range(2, top + 1):
            run_level(weight_trees[1], level)
        stores.append(pltpu.make_async_copy(r.full, r.full_out, r.local_sems.at[3]))
        stores[-1].start()
        heads(0, 2, n_heads // 2)
        project(1)
        n_left = n_heads // 2
        for level in range(1, top + 1):
            run_level(other_trees, level)
            stores += store_blocks(other_trees, level, r.other_cots, r.other_out, r.other_sems)
            if level < top:
                first, end = [(level - 1 + i) * n_left // (top - 1) for i in (0, 1)]
                heads(1, first, end)
        hidden_rows = r.residual[...] + dot(r.context[...], r.full[2], NT)
        r.hidden[...] = hidden_rows
        inverse = lax.rsqrt(jnp.mean(hidden_rows * hidden_rows, -1, keepdims=True) + NORM_EPS)
        normed = (hidden_rows * inverse * r.gains[1:2, :]).astype(BF16)
        r.normed_two[...] = normed
        logits = dot(normed, r.router[...], NN)
        lane = lax.broadcasted_iota(jnp.int32, logits.shape, 1)
        raised = jnp.where(lane < EXPERTS, jnp.exp(logits), 0.0)
        probs = raised / jnp.sum(raised, -1, keepdims=True)
        r.probs[...] = probs
        turned = probs.T
        for expert in range(EXPERTS):
            owner, which = divmod(expert, owned)
            r.table[owner, 4 + which, :] = turned[expert]
        wait_experts(copies, me, r.near, sent)
        for copy in stores:
            copy.wait()
        copies.finish()

    return launch(
        attention,
        identity,
        dict(
            small=(small, vmem()),
            shards=(shards, vmem()),
            cot=(cot, vmem()),
            residual=(residual, vmem()),
            gateup=(gateup, hbm()),
            down=(down, hbm()),
            ids=(ids, vmem()),
            query_table=(tables[0], vmem()),
            key_table=(tables[1], vmem()),
        ),
        dict(
            gains=(single(2, width), vmem()),
            router=(low(width, 128), vmem()),
            packed=(low(owned, 3, hidden, width), hbm()),
            full_out=(low(kinds, n_dp * rows, width), hbm()),
            cots_out=(low(n_dp, tokens, width), hbm()),
            other_out=(low(n_dp, tokens, width), hbm()),
            near=([low(n_experts, 3, hidden, width) for _ in range(1, span)], hbm()),
            normed=(low(2, tokens, width), vmem()),
            queries=(low(tokens, width), vmem()),
            keyval=(low(2, tokens, width), vmem()),
            context=(low(tokens, width), vmem()),
            hidden=(single(tokens, width), vmem()),
            normed_two=(low(tokens, width), vmem()),
            probs=(single(tokens, 128), vmem()),
            table=(single(n_dp, 8, tokens), vmem()),
        ),
        dict(
            full=pltpu.VMEM((kinds, n_dp * rows, width), BF16),
            cots=pltpu.VMEM((n_dp, tokens, width), BF16),
            other_cots=pltpu.VMEM((n_dp, tokens, width), BF16),
            scaled=pltpu.VMEM((2, tokens, width), BF16),
            small_all=pltpu.VMEM((n_dp, n_mp) + small.shape, F32),
            router_wide=pltpu.VMEM((width, 128), F32),
            wide=pltpu.VMEM((owned, 3, hidden, width), F32),
            narrow=pltpu.VMEM((owned, 3, hidden, width), BF16),
            q=pltpu.VMEM((tokens, width), F32),
            kv=pltpu.VMEM((2, tokens, width), F32),
            local_sems=pltpu.SemaphoreType.DMA((4,)),
            cot_sems=pltpu.SemaphoreType.DMA((n_dp,)),
            other_sems=pltpu.SemaphoreType.DMA((n_dp,)),
        ),
        n_copies,
        60 << 20,
    )


def attention_backward(n_dp, n_mp, groups, identity, given, first_row):
    tokens, width = given.residual.shape
    n_heads = width // 128
    n_devices = n_dp * n_mp
    own_router = width // n_devices
    per_tile = n_devices // n_heads
    rows, cols = width // n_dp, width // n_mp
    part_rows = rows // 2
    orders = orders_of(n_dp)
    span = n_mp // groups
    owned = EXPERTS // n_dp
    n_late = given.late[0].shape[0] if given.late else 0
    n_copies = (2 * groups + 7) * (n_dp - 1) + 2 + 4 * (n_mp - 1) + 2 + n_late * (span - 1)

    rooms, across_room = reduce_rooms(groups, n_dp, tokens, width, BF16)

    def attention_back(r):
        dp, mp = lax.axis_index("dp"), lax.axis_index("mp")
        me = (dp, mp)
        neighbour = (dp, flip(mp, 1))
        copies = Copies(r.send_sems, r.recv_sems)
        loads = [
            pltpu.make_async_copy(r.full.at[c], r.weights.at[c], r.local_sems.at[c])
            for c in (2, 0, 1)
        ]
        for copy in loads:
            copy.start()
        even_loads = [
            pltpu.make_async_copy(
                r.terms.at[g, j], r.terms_even.at[g, j // 2], r.term_sems.at[g, j // 2]
            )
            for g in range(groups)
            for j in range(0, n_dp, 2)
        ]
        for copy in even_loads:
            copy.start()
        greet(
            [(flip_all(dp, mask), mp) for mask in bits_of(n_dp)]
            + [(dp, flip_all(mp, k)) for k in range(1, n_mp)]
        )
        partner = (dp, flip_all(mp, span))
        mixture = TokenReduce(
            copies,
            n_dp,
            me,
            partner,
            groups,
            lambda g, j: r.terms.at[g, j] if j % 2 else r.terms_even.at[g, j // 2],
            r.rooms,
            r.across,
        )
        for group in range(groups)[::-1]:
            for j in range(1, n_dp, 2):
                mixture.first(group, j)
        last = mixture.last
        for copy in even_loads:
            copy.wait()
        mixture.level(1, last - 1)
        travels = {}

        def send_late(i):
            if i < n_late:
                for k in range(1, span):
                    travels[i, k] = copies.slot()
                    copies.start(
                        r.late[k - 1].at[i],
                        r.arrived[k - 1].at[owned - n_late + i],
                        (dp, flip_all(mp, k)),
                        travels[i, k],
                    )

        send_late(0)
        r.turned[...] = jnp.zeros_like(r.turned)
        for expert in range(EXPERTS):
            owner, which = divmod(expert, owned)
            parts = r.gate_parts[owner, 0, which, :]
            for group in range(1, groups):
                parts = parts + r.gate_parts[owner, group, which, :]
            r.turned[expert, :] = parts
        grad_probs = r.turned[...].T
        probs = r.probs[...]
        grad_logits = (
            probs * (grad_probs - jnp.sum(probs * grad_probs, -1, keepdims=True))
        ).astype(BF16)
        grad_normed_two = r.total[...] + dot(grad_logits, r.router[...], NT)
        r.grad_router[...] = dot(r.normed_two[...], grad_logits, TN)
        mixture.level(0, last - 1)
        hidden = r.hidden[...]
        inverse = lax.rsqrt(jnp.mean(hidden * hidden, -1, keepdims=True) + NORM_EPS)
        scaled = r.gains[1:2, :] * grad_normed_two
        grad_hidden = (
            r.cotangent[...]
            + inverse * scaled
            - hidden * (inverse * inverse * inverse) * jnp.mean(scaled * hidden, -1, keepdims=True)
        )
        r.grad_hidden[...] = grad_hidden
        gain_two = jnp.sum(grad_normed_two * hidden * inverse, 0, keepdims=True)
        grad_attn = grad_hidden.astype(BF16)
        r.grad_attn[...] = grad_attn
        def weight_tree(c, part):
            def block(j):
                start = flip_all(dp, j) * rows + part * part_rows
                return r.grads.at[c, pl.ds(pl.multiple_of(start, part_rows), part_rows), :]

            return TreeReduce(
                copies,
                orders[part],
                n_dp,
                me,
                block,
                lambda number: r.weight_rooms.at[c, part, number],
                add_rows(),
            )

        weight_trees = [[weight_tree(c, part) for part in (0, 1)] for c in range(3)]

        def weight_level(c, p):
            for j in range(1, n_dp):
                for one in weight_trees[c]:
                    if place_of(one.order, j) == p:
                        if p < last:
                            one.collect(j)
                        one.send(j)

        r.grads[2] = dot(grad_attn, r.context[...], TN).astype(BF16)
        weight_level(2, last)
        loads[0].wait()
        r.grad_context[...] = dot(r.grad_attn[...], r.weights[2], NN).astype(BF16)
        mask = seen(tokens, mp)

        def table(ref):
            there = pl.ds(pl.multiple_of(lax.rem(mp, 2) * tokens, tokens), tokens)
            return ref[0, there, :], ref[1, there, :]

        def head(k, carry):
            lanes = pl.ds(pl.multiple_of(k * 128, 128), 128)
            keyval = jnp.concatenate([r.keyval[0, :, lanes], r.keyval[1, :, lanes]], 0)
            both, keys, values = group_operands(r.queries[:, lanes].astype(F32), keyval.astype(F32))
            grad_both = group_operands(r.grad_context[:, lanes].astype(F32), keyval.astype(F32))[0]
            chance = softmax_of(both, keys, mask)
            grad_p = dot(grad_both, values, NT)
            delta = jnp.sum(chance * grad_p, -1, keepdims=True)
            grad_s = (chance * (grad_p - delta)).astype(BF16)
            scale = 1.0 / math.sqrt(HEAD_SIZE)
            grad_q = merge_heads(dot(grad_s, keys, NN)) * scale
            cosine, sine = table(r.query_table)
            r.grad_q[:, lanes] = rotate(grad_q, cosine, -sine).astype(BF16)
            grad_k = dot(grad_s, both, TN) * scale
            grad_v = dot(chance.astype(BF16), grad_both, TN)
            lane = lax.broadcasted_iota(jnp.int32, grad_k.shape, 1)
            grad_kv = jnp.where(
                lane < HEAD_SIZE,
                grad_k + pltpu.roll(grad_k, HEAD_SIZE, 1),
                grad_v + pltpu.roll(grad_v, HEAD_SIZE, 1),
            )
            r.grad_kv[:, lanes] = grad_kv[:tokens]
            r.swap[0, :, lanes] = grad_kv[tokens:].astype(BF16)
            return carry

        sent = {}

        def line_out(c):
            for part, one in enumerate(weight_trees[c]):
                one.collect(0)
                total = one.total()
                for k in range(n_mp):
                    there = pl.ds(pl.multiple_of(flip_all(mp, k) * cols, cols), cols)
                    r.line[0, c, k, pl.ds(part * part_rows, part_rows), :] = total[:, there]
            for k in range(1, n_mp):
                sent[c, k] = copies.slot()
                copies.start(
                    r.line.at[0, c, k], r.line.at[1, c, k], (dp, flip_all(mp, k)), sent[c, k]
                )

        across = [copies.slot() for _ in range(2)]
        swaps = [pl.ds(half * (width // 2), width // 2) for half in range(2)]

        def heads(first, end):
            lax.fori_loop(first * n_heads // 4, end * n_heads // 4, head, 0)

        def swap(half):
            copies.start(
                r.swap.at[0, :, swaps[half]],
                r.swap.at[1, :, swaps[half]],
                neighbour,
                across[half],
            )

        heads(0, 2)
        swap(0)
        for p in range(last - 2, -1, -1):
            mixture.level(1, p)
        heads(2, 3)
        weight_level(2, last - 1)
        heads(3, 4)
        swap(1)
        for p in range(last - 2, -1, -1):
            mixture.level(0, p)
        mixture.pass_on()
        for i in range(1, n_late):
            send_late(i)
        r.grads[0] = dot(r.normed[0], r.grad_q[...], TN).astype(BF16)
        weight_level(0, last)
        loads[1].wait()
        r.grad_normed[...] = dot(r.grad_q[...], r.weights[0], NT)
        weight_level(0, last - 1)
        for p in range(last - 2, -1, -1):
            weight_level(2, p)
        for half in range(2):
            copies.wait(r.swap.at[1, :, swaps[half]], me, across[half])

        def turn_back(k, carry):
            lanes = pl.ds(pl.multiple_of(k * 128, 128), 128)
            total = r.grad_kv[:, lanes] + r.swap[1, :, lanes].astype(F32)
            cosine, sine = table(r.key_table)
            total = rotate(total, cosine, -sine)
            r.grad_kv_low[:, lanes] = total.astype(BF16)
            return carry

        lax.fori_loop(0, n_heads, turn_back, 0)
        loads[2].wait()
        r.grads[1] = dot(r.normed[0], r.grad_kv_low[...], TN).astype(BF16)
        weight_level(1, last)
        grad_normed = r.grad_normed[...] + dot(r.grad_kv_low[...], r.weights[1], NT)
        residual = r.residual[...]
        inverse = lax.rsqrt(jnp.mean(residual * residual, -1, keepdims=True) + NORM_EPS)
        scaled = r.gains[0:1, :] * grad_normed
        r.input_grad[...] = (
            r.grad_hidden[...]
            + inverse * scaled
            - residual * (inverse * inverse * inverse) * jnp.mean(scaled * residual, -1, keepdims=True)
        )
        gain_one = jnp.sum(grad_normed * residual * inverse, 0, keepdims=True)
        r.small[...] = jnp.zeros_like(r.small)
        for device in range(n_devices):
            tile = device // per_tile
            owner = r.small.at[device // n_mp, device % n_mp]
            owner[0:1, :] = gain_one[:, tile * 128 : (tile + 1) * 128]
            owner[1:2, :] = gain_two[:, tile * 128 : (tile + 1) * 128]
            owner[first_row : first_row + own_router, :] = r.grad_router[
                device * own_router : (device + 1) * own_router, :
            ]

        def add_whole(here, other):
            here[...] = here[...] + other[...]

        small_tree = TreeReduce(
            copies,
            orders[0],
            n_dp,
            me,
            lambda j: r.small.at[flip_all(dp, j)],
            lambda number: r.small_rooms.at[number],
            add_whole,
        )
        for j in range(1, n_dp):
            if place_of(orders[0], j) == last:
                small_tree.send(j)
        for p in range(last - 1, -1, -1):
            if p < last - 1:
                weight_level(0, p)
            weight_level(1, p)
            for j in range(1, n_dp):
                if place_of(orders[0], j) == p:
                    small_tree.collect(j)
                    small_tree.send(j)
            if p == last - 1:
                line_out(2)
        for c in (0, 1):
            line_out(c)
        small_tree.collect(0)
        small_total = small_tree.total()
        for k in range(1, n_mp):
            device = (dp, flip_all(mp, k))
            sent[k] = copies.slot()
            copies.start(small_total.at[device[1]], r.small_line.at[k], device, sent[k])
        mixture.end(r.block_out)
        r.block_out[...] += r.hidden[...]
        for c in (2, 0, 1):
            r.shards[c] = r.line[0, c, 0].astype(F32)
            for k in range(1, n_mp):
                copies.wait(r.line.at[1, c, k], me, sent[c, k])
                r.shards[c] += r.line[1, c, k].astype(F32)
        r.small_shard[...] = small_total[mp]
        for k in range(1, n_mp):
            copies.wait(r.small_line.at[k], me, sent[k])
            r.small_shard[...] += r.small_line[k]
        for (i, k), slot in travels.items():
            copies.wait(r.arrived[k - 1].at[owned - n_late + i], me, slot)
        copies.finish()

    return launch(
        attention_back,
        identity,
        dict(
            full=(given.full, hbm()),
            late=(given.late, hbm()),
            begun=(given.arrived, hbm()),
            residual=(given.residual, vmem()),
            hidden=(given.hidden, vmem()),
            cotangent=(given.cotangent, vmem()),
            total=(given.total, vmem()),
            gate_parts=(given.gate_parts, vmem()),
            terms=(given.terms, hbm()),
            probs=(given.probs, vmem()),
            normed=(given.normed, vmem()),
            normed_two=(given.normed_two, vmem()),
            queries=(given.queries, vmem()),
            keyval=(given.keyval, vmem()),
            context=(given.context, vmem()),
            gains=(given.gains, vmem()),
            router=(given.router, vmem()),
            query_table=(given.tables[0], vmem()),
            key_table=(given.tables[1], vmem()),
        ),
        dict(
            input_grad=(single(tokens, width), vmem()),
            block_out=(single(tokens, width), vmem()),
            arrived=([low(*grad.shape) for grad in given.arrived], hbm()),
            shards=(single(3, rows, cols), vmem()),
            small_shard=(single(first_row + own_router, 128), vmem()),
        ),
        dict(
            grads=pltpu.VMEM((3, width, width), BF16),
            small=pltpu.VMEM((n_dp, n_mp, first_row + own_router, 128), F32),
            small_rooms=pltpu.VMEM((n_dp - 1, n_mp, first_row + own_router, 128), F32),
            small_line=pltpu.VMEM((n_mp, first_row + own_router, 128), F32),
            terms_even=pltpu.VMEM((groups, n_dp // 2, tokens, width), BF16),
            term_sems=pltpu.SemaphoreType.DMA((groups, n_dp // 2)),
            weight_rooms=pltpu.VMEM((3, 2, n_dp - 1, part_rows, width), BF16),
            line=pltpu.VMEM((2, 3, n_mp, rows, cols), BF16),
            rooms=rooms,
            across=across_room,
            weights=pltpu.VMEM((3, width, width), BF16),
            turned=pltpu.VMEM((128, tokens), F32),
            grad_router=pltpu.VMEM((width, 128), F32),
            grad_hidden=pltpu.VMEM((tokens, width), F32),
            grad_attn=pltpu.VMEM((tokens, width), BF16),
            grad_context=pltpu.VMEM((tokens, width), BF16),
            grad_q=pltpu.VMEM((tokens, width), BF16),
            grad_kv=pltpu.VMEM((tokens, width), F32),
            grad_kv_low=pltpu.VMEM((tokens, width), BF16),
            grad_normed=pltpu.VMEM((tokens, width), F32),
            swap=pltpu.VMEM((2, tokens, width), BF16),
            local_sems=pltpu.SemaphoreType.DMA((3,)),
        ),
        n_copies,
        62 << 20,
        dict(arrived="begun"),
    )


class TokenReduce:
    def __init__(self, copies, n_dp, me, partner, groups, block, rooms, across):
        self.copies, self.me, self.across = copies, me, across
        self.partner = partner
        self.tokens = across.shape[1]
        self.n_dp = n_dp
        self.last = n_dp.bit_length() - 2
        self.groups = groups
        self.halves = [copies.slot(), copies.slot()]

        def tree(group, part, order):
            cut = pl.ds(part * (self.tokens // 2), self.tokens // 2)
            return TreeReduce(
                copies,
                order,
                n_dp,
                me,
                lambda j: block(group, j).at[cut],
                lambda number: rooms.at[group, part, number],
                add_rows(),
            )

        self.trees = [
            [tree(group, part, order) for part, order in enumerate(orders_of(n_dp))]
            for group in range(self.groups)
        ]

    def first(self, group, j):
        for tree in self.trees[group]:
            tree.send(j)

    def level(self, group, p):
        if group == self.groups:
            return
        for j in range(1, self.n_dp):
            for tree in self.trees[group]:
                if place_of(tree.order, j) == p:
                    tree.collect(j)
                    tree.send(j)

    def pass_on(self):
        if self.groups == 1:
            return
        for part, tree in enumerate(self.trees[1]):
            tree.collect(0)
            cut = pl.ds(part * (self.tokens // 2), self.tokens // 2)
            self.copies.start(
                tree.total(), self.across.at[0, cut], self.partner, self.halves[part]
            )

    def end(self, out_ref):
        for tree in self.trees[0]:
            tree.collect(0)
        for part, tree in enumerate(self.trees[0]):
            cut = pl.ds(part * (self.tokens // 2), self.tokens // 2)
            total = tree.total()[...].astype(F32)
            if self.groups > 1:
                self.copies.wait(self.across.at[0, cut], self.me, self.halves[part])
                total = total + self.across[0, cut, :].astype(F32)
            out_ref[cut, :] = total


def reduce_rooms(groups, n_dp, tokens, width, dtype):
    return [
        pltpu.VMEM((groups, 2, n_dp - 1, tokens // 2, width), dtype),
        pltpu.VMEM((1, tokens, width), dtype),
    ]


def run_experts(n_dp, n_mp, groups, identity, rows, table, cots, packed, near):
    owned, _, hidden, width = packed.shape
    span = n_mp // groups
    units = span * hidden
    blocks = groups * n_dp
    slots = blocks * CAP
    tokens = rows.shape[0]
    per_tile = 4
    tile = per_tile * CAP
    n_tiles = blocks // per_tile
    here = [expert for experts, _ in near for expert in experts]
    coming = [expert for expert in range(owned) if expert not in here]
    n_sent = min(owned, 2)
    n_late = owned - n_sent
    n_copies = groups + 1 + 2 * (blocks - 1) + 4 * groups * (n_dp - 1)
    n_copies += (len(coming) + n_sent) * (span - 1)
    order = []
    for group in range(groups):
        for level in range(n_dp.bit_length()):
            order += [(group, j) for j in range(n_dp) if bin(j).count("1") == level]

    def experts(r):
        dp, mp = lax.axis_index("dp"), lax.axis_index("mp")
        me = (dp, mp)
        other = flip_all(mp, span)
        copies = Copies(r.send_sems, r.recv_sems)
        peers = {
            (group, j): (flip_all(dp, j), other if group else mp)
            for group in range(groups)
            for j in range(n_dp)
            if group + j
        }
        local = iter(range(n_loads))

        def load(source, target):
            copy = pltpu.make_async_copy(source, target, r.load_sems.at[next(local)])
            copy.start()
            return copy

        def units_of(k):
            return pl.ds(k * hidden, hidden)

        own_table = load(r.own_table.at[dp], r.tables.at[0])
        own_rows = load(r.rows, r.rows_all.at[0, 0])
        loads = [
            [load(r.packed.at[e], r.weights.at[e, :, units_of(0)])] for e in range(owned)
        ]
        for number, (some, _) in enumerate(near):
            for i, e in enumerate(some):
                for k in range(1, span):
                    source = r.near[number * (span - 1) + k - 1].at[i]
                    loads[e].append(load(source, r.weights.at[e, :, units_of(k)]))

        def cot_copy(number):
            group, j = order[number]
            return pltpu.make_async_copy(
                r.cots[group].at[j], r.cot.at[number % 2], r.cot_sems.at[number % 2]
            )

        cot_copy(0).start()
        greet(list(peers.values()) + [(dp, flip_all(mp, k)) for k in range(1, span)])
        if groups > 1:
            across = copies.slot()
            copies.start(r.rows, r.rows_all.at[1, 0], peers[1, 0], across)
        sent = {}
        for (group, j), device in peers.items():
            sent[group, j] = copies.slot()
            copies.start(
                r.own_table.at[device[0]],
                r.tables.at[order.index((group, j))],
                device,
                sent[group, j],
            )
        trees = [row_trees(copies, n_dp, me, r.rows_all.at[group]) for group in range(groups)]
        own_rows.wait()
        for tree in trees[0]:
            tree.send(0)
        own_table.wait()

        def hits(number, some):
            slot = lax.broadcasted_iota(jnp.int32, (CAP, tokens), 0).astype(F32)
            found = [slot == r.tables[number, pl.ds(i, 1), :] for i in some]
            return found[0] if len(found) == 1 else jnp.concatenate(found, 0)

        def fill(number):
            group, j = order[number]
            if number:
                copies.wait(r.tables.at[number], me, sent[group, j])
            if number + 1 < blocks:
                cot_copy(number + 1).start()
            pick = hits(number, range(owned)).astype(BF16)
            there = slice(number * CAP, (number + 1) * CAP)
            found = dot(pick, r.rows_all[group, j], NN).astype(BF16)
            for i in range(owned):
                r.x[i + 1, there, :] = found[i * CAP : (i + 1) * CAP]
            cot_copy(number).wait()
            found = dot(pick, r.cot[number % 2], NN).astype(BF16)
            for i in range(owned):
                r.y[i, there, :] = found[i * CAP : (i + 1) * CAP]

        def work(e, step):
            rows = pl.ds(pl.multiple_of(step * tile, 16), tile)
            x = r.x[e + 1, rows, :]
            gate = dot(x, r.weights[e, 0], NT)
            up = dot(x, r.weights[e, 1], NT)
            sigmoid = 1.0 / (1.0 + jnp.exp(-gate))
            silu = gate * sigmoid
            activation = (silu * up).astype(BF16)
            r.act[rows, :] = activation
            made = dot(activation, r.weights[e, 2], NN)
            cot = r.y[e, rows, :].astype(F32)
            chosen = []
            dots = jnp.sum(cot * made, -1, keepdims=True)
            for b in range(per_tile):
                number = step * per_tile + b
                hit = hits(number, (e,))
                chance = r.tables[number, pl.ds(4 + e, 1), :]
                chosen.append(jnp.sum(jnp.where(hit, chance, 0.0), -1, keepdims=True))
                mine = dots[b * CAP : (b + 1) * CAP]
                r.gates[number, pl.ds(e, 1), :] = jnp.sum(
                    jnp.where(hit, mine, 0.0), 0, keepdims=True
                )
            share = jnp.concatenate(chosen, 0)
            r.y[e, rows, :] = (share * made).astype(BF16)
            back = (share * cot).astype(BF16)
            r.back[rows, :] = back
            grad_act = dot(back, r.weights[e, 2], NT)
            grad_gate = grad_act * up * sigmoid * (1.0 + gate * (1.0 - sigmoid))
            grad_gate = grad_gate.astype(BF16)
            grad_up = (grad_act * silu).astype(BF16)
            r.pair[rows, pl.ds(0, units)] = grad_gate
            r.pair[rows, pl.ds(units, units)] = grad_up
            found = dot(grad_gate, r.weights[e, 0], NN) + dot(grad_up, r.weights[e, 1], NN)
            r.x[e, rows, :] = found.astype(BF16)

        def ready(e):
            for copy in loads[e]:
                copy.wait()
            if e in coming:
                for k in range(1, span):
                    copies.wait(r.weights.at[e, :, units_of(k)], me, weights_sent[e, k])

        stores = []

        def weight_grad(e):
            for c in range(3):
                source = r.act[...] if c == 2 else r.pair[:, pl.ds(c * units, units)]
                rhs = r.back[...] if c == 2 else r.x[e + 1]
                r.weights[e, c] = dot(source, rhs, TN).astype(BF16)
            stores.append(load(r.weights.at[e, :, units_of(0)], r.grad_own.at[e]))
            for k in range(1, span):
                source = r.weights.at[e, :, units_of(k)]
                if e < n_sent:
                    grads_sent[e, k] = copies.slot()
                    copies.start(
                        source, r.arrived[k - 1].at[e], (dp, flip_all(mp, k)), grads_sent[e, k]
                    )
                else:
                    stores.append(load(source, r.late[k - 1].at[e - n_sent]))

        weights_sent, grads_sent = {}, {}
        ready(0)
        done = 0
        leaving = []
        for number, (group, j) in enumerate(order):
            if j:
                for tree in sorted(trees[group], key=lambda tree: place_of(tree.order, j)):
                    tree.receive(j)
                    tree.send(j)
            elif group:
                copies.wait(r.rows_all.at[1, 0], me, across)
                for tree in trees[1]:
                    tree.send(0)
            if group == groups - 1 and j == 0:
                leaving += copies.split()
                for e in coming:
                    for k in range(1, span):
                        weights_sent[e, k] = copies.slot()
                        copies.start(
                            r.packed.at[e],
                            r.weights.at[e, :, units_of(k)],
                            (dp, flip_all(mp, k)),
                            weights_sent[e, k],
                        )
                staying = copies.split()
            fill(number)
            if number % per_tile == per_tile - 1 and number < blocks - 1:
                work(0, done)
                done += 1
        work(0, done)
        leaving += copies.split()
        copies.sent = staying
        weight_grad(0)

        def tiles(e, first, end):
            def step(at, carry):
                work(e, at)
                return carry

            lax.fori_loop(first, end, step, 0)

        for e in range(1, owned - 1):
            ready(e)
            tiles(e, 0, n_tiles)
            weight_grad(e)
        copies.finish(leaving)
        partner = (dp, other)
        reduce = TokenReduce(
            copies, n_dp, me, partner, groups, lambda g, j: r.rows_all.at[g, j], r.rooms, r.across
        )
        last = owned - 1
        if last:
            ready(last)
        scattered = []

        def sum_copy(at):
            group, j = scattered[at]
            return pltpu.make_async_copy(
                r.sums.at[at % 2], r.terms.at[group, j], r.sum_sems.at[at % 2]
            )

        own_gates = pltpu.make_async_copy(r.gates.at[0], r.gate_parts.at[dp, 0], r.gate_sem.at[0])
        gates_sent = {}

        def scatter(group, j):
            number = order.index((group, j))
            if number:
                gates_sent[group, j] = copies.slot()
                copies.start(
                    r.gates.at[number],
                    r.gate_parts.at[dp, group],
                    peers[group, j],
                    gates_sent[group, j],
                )
            else:
                own_gates.start()
            there = slice(number * CAP, (number + 1) * CAP)
            pick = hits(number, range(owned)).astype(BF16)
            found = jnp.concatenate([r.x[e, there, :] for e in range(owned)], 0)
            r.rows_all[group, j] = dot(pick, found, TN).astype(BF16)
            if j % 2:
                reduce.first(group, j)
            found = jnp.concatenate([r.y[e, there, :] for e in range(owned)], 0)
            at = len(scattered)
            scattered.append((group, j))
            if at > 1:
                sum_copy(at - 2).wait()
            r.sums[at % 2] = dot(pick, found, TN).astype(BF16)
            sum_copy(at).start()

        halves = [
            (n_tiles * group // groups, n_tiles * (group + 1) // groups) for group in range(groups)
        ]
        levels = list(range(reduce.last - 1, -1, -1))
        for group in range(groups)[::-1]:
            first, end = halves[group]
            if last == 0:
                pass
            elif group == groups - 1:
                tiles(last, first, end)
            else:
                for at in range(first, end):
                    tiles(last, at, at + 1)
                    if levels:
                        reduce.level(1, levels.pop(0))
            for j in [j for j in range(n_dp) if j % 2] + [j for j in range(n_dp) if j % 2 == 0]:
                scatter(group, j)
        if groups > 1:
            for p in levels:
                reduce.level(1, p)
        reduce.pass_on()
        for p in range(reduce.last - 1, -1, -1):
            reduce.level(0, p)
            if p == reduce.last - 1 and last:
                weight_grad(last)
        reduce.end(r.total)
        for at in (blocks - 2, blocks - 1):
            sum_copy(at).wait()
        own_gates.wait()
        for (group, j), device in peers.items():
            copies.wait(r.gate_parts.at[device[0], group], me, gates_sent[group, j])
        for (e, k), slot in grads_sent.items():
            copies.wait(r.arrived[k - 1].at[e], me, slot)
        for copy in stores:
            copy.wait()
        copies.finish()

    n_loads = 2 + owned * span + owned * span
    near_refs = [part for _, parts in near for part in parts]
    weights = packed.shape[1:]
    rooms, across_room = reduce_rooms(groups, n_dp, tokens, width, BF16)
    return launch(
        experts,
        identity,
        dict(
            rows=(rows, hbm()),
            own_table=(table, hbm()),
            cots=(cots, hbm()),
            packed=(packed, hbm()),
            near=(near_refs, hbm()),
        ),
        dict(
            terms=(low(groups, n_dp, tokens, width), hbm()),
            gate_parts=(single(n_dp, groups, 8, tokens), hbm()),
            total=(single(tokens, width), vmem()),
            grad_own=(low(owned, *weights), hbm()),
            arrived=([low(owned, *weights) for _ in range(1, span)], hbm()),
            late=([low(n_late, *weights) for _ in range(1, span) if n_late], hbm()),
        ),
        dict(
            weights=pltpu.VMEM((owned, 3, units, width), BF16),
            rows_all=pltpu.VMEM((groups, n_dp, tokens, width), BF16),
            x=pltpu.VMEM((owned + 1, slots, width), BF16),
            y=pltpu.VMEM((owned, slots, width), BF16),
            act=pltpu.VMEM((slots, units), BF16),
            pair=pltpu.VMEM((slots, 2 * units), BF16),
            back=pltpu.VMEM((slots, width), BF16),
            tables=pltpu.VMEM((blocks, 8, tokens), F32),
            gates=pltpu.VMEM((blocks, 8, tokens), F32),
            cot=pltpu.VMEM((2, tokens, width), BF16),
            sums=pltpu.VMEM((2, tokens, width), BF16),
            rooms=rooms,
            across=across_room,
            load_sems=pltpu.SemaphoreType.DMA((n_loads,)),
            cot_sems=pltpu.SemaphoreType.DMA((2,)),
            sum_sems=pltpu.SemaphoreType.DMA((2,)),
            gate_sem=pltpu.SemaphoreType.DMA((1,)),
        ),
        n_copies,
        63 << 20,
    )


def adamw(weight, gradient, moment_one, moment_two, rate_val, decay_val):
    first_new = 0.9 * moment_one + 0.1 * gradient
    second_new = 0.95 * moment_two + 0.05 * gradient * gradient
    first_hat = first_new / (1.0 - 0.9**STEP)
    second_hat = second_new / (1.0 - 0.95**STEP)
    weight_new = weight - rate_val * (
        first_hat / (jnp.sqrt(second_hat) + 1e-08) + decay_val * weight
    )
    return (gradient, weight_new, first_new, second_new)


def local(
    n_dp,
    n_mp,
    residual_in,
    cotangent,
    expert_ids,
    attn_gain,
    query_w,
    key_value_weight,
    output_w,
    moe_gain,
    router_w,
    gateup_w,
    down_w,
    attn_gain_mean,
    attn_gain_var,
    query_mean,
    query_var,
    key_value_first_moment,
    key_value_second_moment,
    output_mean,
    output_var,
    moe_gain_mean,
    moe_gain_var,
    router_mean,
    router_var,
    gateup_mean,
    gateup_var,
    down_mean,
    down_var,
):
    mp = lax.axis_index("mp")
    place_in_all = lax.axis_index("dp") * n_mp + mp
    groups = 2 if 2 * n_dp <= 16 else 1
    tokens = residual_in.shape[0]
    owned = gateup_w.shape[0]
    span = n_mp // groups
    own_gain, own_router = attn_gain.shape[0], router_w.shape[0]
    first_row, lanes = 8, 128
    per_tile = lanes // own_gain

    def spread(gain):
        return jnp.where(jnp.arange(lanes) // own_gain == place_in_all % per_tile, jnp.tile(gain, per_tile), 0.0)

    small = jnp.concatenate(
        [
            spread(attn_gain)[None],
            spread(moe_gain)[None],
            jnp.zeros((first_row - 2, lanes), F32),
            jnp.pad(router_w, ((0, 0), (0, lanes - EXPERTS))),
        ]
    )
    shards = jnp.stack([query_w, key_value_weight, output_w.T]).astype(BF16)
    tables = [jnp.asarray(table) for table in rotary_constants()]
    early = list(range(owned))[:1]
    front = attention_forward(
        n_dp,
        n_mp,
        groups,
        0,
        first_row,
        small,
        shards,
        cotangent.astype(BF16),
        residual_in,
        gateup_w,
        down_w,
        expert_ids.T,
        tables,
        early,
    )

    found = run_experts(
        n_dp,
        n_mp,
        groups,
        1,
        front.normed_two,
        front.table,
        [front.cots_out, front.other_out][:groups],
        front.packed,
        [(early, front.near)],
    )

    given = types.SimpleNamespace(
        full=front.full_out,
        residual=residual_in,
        hidden=front.hidden,
        cotangent=cotangent,
        total=found.total,
        late=found.late,
        arrived=found.arrived,
        gate_parts=found.gate_parts,
        terms=found.terms,
        probs=front.probs,
        normed=front.normed,
        normed_two=front.normed_two,
        queries=front.queries,
        keyval=front.keyval,
        context=front.context,
        gains=front.gains,
        router=front.router,
        tables=tables,
    )
    back = attention_backward(n_dp, n_mp, groups, 2, given, first_row)
    input_grad, block_out = back.input_grad, back.block_out
    gateup_grad, down_grad = (
        sum(part[:, cut].astype(F32) for part in [found.grad_own] + back.arrived)
        for cut in (slice(0, 2), 2)
    )
    grads, small_grads = back.shards, back.small_shard
    query_grad, keyval_grad, output_grad = grads[0], grads[1], grads[2].T
    first_lane = (place_in_all % per_tile) * own_gain
    gain_one_grad, gain_two_grad = (
        lax.dynamic_slice_in_dim(small_grads[row], first_lane, own_gain) for row in (0, 1)
    )
    router_grad = small_grads[first_row:, :EXPERTS]
    matrix_rate = 0.2 / math.sqrt(MODEL_WIDTH)
    gain_one_all = adamw(attn_gain, gain_one_grad, attn_gain_mean, attn_gain_var, 0.1, 0.0)
    query_all = adamw(query_w, query_grad, query_mean, query_var, matrix_rate, 0.1)
    keyval_all = adamw(
        key_value_weight,
        keyval_grad,
        key_value_first_moment,
        key_value_second_moment,
        matrix_rate,
        0.1,
    )
    output_all = adamw(output_w, output_grad, output_mean, output_var, 0.1, 0.1)
    gain_two_all = adamw(moe_gain, gain_two_grad, moe_gain_mean, moe_gain_var, 0.1, 0.0)
    router_all = adamw(router_w, router_grad, router_mean, router_var, matrix_rate, 0.1)
    gateup_all = adamw(gateup_w, gateup_grad, gateup_mean, gateup_var, matrix_rate, 0.1)
    down_all = adamw(down_w, down_grad, down_mean, down_var, 0.07, 0.1)
    return (
        block_out,
        input_grad,
        gain_one_all[0],
        gain_one_all[1],
        gain_one_all[2],
        gain_one_all[3],
        query_all[0],
        query_all[1],
        query_all[2],
        query_all[3],
        keyval_all[0],
        keyval_all[1],
        keyval_all[2],
        keyval_all[3],
        output_all[0],
        output_all[1],
        output_all[2],
        output_all[3],
        gain_two_all[0],
        gain_two_all[1],
        gain_two_all[2],
        gain_two_all[3],
        router_all[0],
        router_all[1],
        router_all[2],
        router_all[3],
        gateup_all[0],
        gateup_all[1],
        gateup_all[2],
        gateup_all[3],
        down_all[0],
        down_all[1],
        down_all[2],
        down_all[3],
    )


def solution(mesh):
    in_specs = (
        P(("dp", "mp"), None),
        P(("dp", "mp"), None),
        P(("dp", "mp"), None),
        P(("dp", "mp")),
        P("dp", "mp"),
        P("dp", "mp"),
        P("mp", "dp"),
        P(("dp", "mp")),
        P(("dp", "mp"), None),
        P("dp", None, "mp", None),
        P("dp", "mp", None),
        P(("dp", "mp")),
        P(("dp", "mp")),
        P("dp", "mp"),
        P("dp", "mp"),
        P("dp", "mp"),
        P("dp", "mp"),
        P("mp", "dp"),
        P("mp", "dp"),
        P(("dp", "mp")),
        P(("dp", "mp")),
        P(("dp", "mp"), None),
        P(("dp", "mp"), None),
        P("dp", None, "mp", None),
        P("dp", None, "mp", None),
        P("dp", "mp", None),
        P("dp", "mp", None),
    )
    out_specs = (
        P(("dp", "mp"), None),
        P(("dp", "mp"), None),
        P(("dp", "mp")),
        P(("dp", "mp")),
        P(("dp", "mp")),
        P(("dp", "mp")),
        P("dp", "mp"),
        P("dp", "mp"),
        P("dp", "mp"),
        P("dp", "mp"),
        P("dp", "mp"),
        P("dp", "mp"),
        P("dp", "mp"),
        P("dp", "mp"),
        P("mp", "dp"),
        P("mp", "dp"),
        P("mp", "dp"),
        P("mp", "dp"),
        P(("dp", "mp")),
        P(("dp", "mp")),
        P(("dp", "mp")),
        P(("dp", "mp")),
        P(("dp", "mp"), None),
        P(("dp", "mp"), None),
        P(("dp", "mp"), None),
        P(("dp", "mp"), None),
        P("dp", None, "mp", None),
        P("dp", None, "mp", None),
        P("dp", None, "mp", None),
        P("dp", None, "mp", None),
        P("dp", "mp", None),
        P("dp", "mp", None),
        P("dp", "mp", None),
        P("dp", "mp", None),
    )
    step = functools.partial(local, mesh.shape["dp"], mesh.shape["mp"])
    return jax.shard_map(step, mesh=mesh, in_specs=in_specs, out_specs=out_specs, check_vma=False)
```

```python
import functools
import math
import types

import jax
import jax.numpy as jnp
import numpy as np
from jax import lax
from jax.experimental import pallas as pl
from jax.experimental.pallas import tpu as pltpu
from jax.sharding import PartitionSpec as P

MODEL_WIDTH = 1024
QUERY_HEADS = 16
KEY_VALUE_HEADS = 8
HEAD_SIZE = 64
EXPERTS = 32
TOPK = 8
SEQUENCE_TOKENS = 512
STEP = 3
CAP = 80

NORM_EPS = 1e-06
MESH = pl.DeviceIdType.MESH
BF16 = jnp.bfloat16
F32 = jnp.float32


def flip(index, mask):
    return index + mask * (1 - 2 * lax.rem(lax.div(index, mask), 2))


def flip_all(index, masks):
    bit = 1
    while bit <= masks:
        if masks & bit:
            index = flip(index, bit)
        bit *= 2
    return index


def bits_of(size):
    return [1 << i for i in range(size.bit_length() - 1)]


def orders_of(n_dp):
    bits = bits_of(n_dp)
    return bits[1:] + bits[:1], bits[1:][::-1] + bits[:1]


def place_of(order, j):
    place = -1
    for at, mask in enumerate(order):
        if j & mask:
            place = at
    return place


def greet(partners):
    barrier = pltpu.get_barrier_semaphore()
    for partner in partners:
        pl.semaphore_signal(barrier, inc=1, device_id=partner, device_id_type=MESH)
    pl.semaphore_wait(barrier, len(partners))


class Copies:
    def __init__(self, send_sems, recv_sems):
        self.send_sems, self.recv_sems = send_sems, recv_sems
        self.used = 0
        self.sent = []

    def slot(self):
        self.used += 1
        return self.used - 1

    def make(self, source, target, device, slot):
        return pltpu.make_async_remote_copy(
            src_ref=source,
            dst_ref=target,
            send_sem=self.send_sems.at[slot],
            recv_sem=self.recv_sems.at[slot],
            device_id=device,
            device_id_type=MESH,
        )

    def start(self, source, target, device, slot):
        copy = self.make(source, target, device, slot)
        copy.start()
        self.sent.append(copy)

    def wait(self, target, device, slot):
        self.make(target, target, device, slot).wait_recv()

    def split(self):
        before, self.sent = self.sent, []
        return before

    def finish(self, some=None):
        for copy in self.sent if some is None else some:
            copy.wait_send()


class TreeGather:
    def __init__(self, copies, order, n_dp, me, source, target):
        self.copies, self.order, self.n_dp, self.me = copies, order, n_dp, me
        self.source, self.target = source, target
        self.slots = {j: copies.slot() for j in range(1, n_dp)}

    def level(self, j):
        return bin(j).count("1")

    def send(self, j):
        dp, mp = self.me
        for mask in self.order[place_of(self.order, j) + 1 :]:
            self.copies.start(
                self.source(j), self.target(j, mask), (flip(dp, mask), mp), self.slots[j ^ mask]
            )

    def receive(self, j):
        self.copies.wait(self.source(j), self.me, self.slots[j])

    def steps(self):
        return sorted(range(1, self.n_dp), key=lambda j: (self.level(j), place_of(self.order, j)))


def run_gathers(trees):
    n_dp = trees[0].n_dp
    for level in range(1, n_dp.bit_length()):
        for tree in trees:
            for j in tree.steps():
                if tree.level(j) == level:
                    tree.receive(j)
                    tree.send(j)


class TreeReduce:
    def __init__(self, copies, order, n_dp, me, block, room, add):
        self.copies, self.order, self.n_dp, self.me = copies, order, n_dp, me
        self.block, self.room, self.add = block, room, add
        self.keys = [
            (j, q) for j in range(n_dp) for q in range(len(order) - 1, place_of(order, j), -1)
        ]
        self.slots = {key: copies.slot() for key in self.keys}

    def number(self, key):
        return self.keys.index(key)

    def send(self, j):
        dp, mp = self.me
        p = place_of(self.order, j)
        last = len(self.order) - 1
        source = self.block(j) if p == last else self.room(self.number((j, last)))
        mask = self.order[p]
        key = (j ^ mask, p)
        self.copies.start(source, self.room(self.number(key)), (flip(dp, mask), mp), self.slots[key])

    def collect(self, j):
        last = len(self.order) - 1
        for q in range(last, place_of(self.order, j), -1):
            here = self.room(self.number((j, q)))
            self.copies.wait(here, self.me, self.slots[(j, q)])
            if q == last:
                self.add(here, self.block(j))
            else:
                self.add(self.room(self.number((j, last))), here)

    def total(self):
        return self.room(self.number((0, len(self.order) - 1)))


def add_rows(step=16):
    def add(here, other):
        def body(i, carry):
            rows = pl.ds(pl.multiple_of(i * step, step), step)
            total = here[..., rows, :].astype(F32) + other[..., rows, :].astype(F32)
            here[..., rows, :] = total.astype(here.dtype)
            return carry

        lax.fori_loop(0, here.shape[-2] // step, body, 0)

    return add


def hbm():
    return pl.BlockSpec(memory_space=pl.ANY)


def vmem():
    return pl.BlockSpec(memory_space=pltpu.VMEM)


def params(identity, limit=None):
    return pltpu.CompilerParams(
        collective_id=identity, has_side_effects=True, vmem_limit_bytes=limit
    )


def launch(kernel, identity, ins, outs, scratch, n_copies, limit=None, kept=None):
    def flat(entries):
        names, leaves, specs = [], [], []
        for name, (value, spec) in entries.items():
            several = isinstance(value, list)
            new = value if several else [value]
            names.append((name, len(new) if several else None))
            leaves += new
            specs += [spec] * len(new)
        return names, leaves, specs

    def unflat(names, leaves):
        leaves, found = list(leaves), {}
        for name, count in names:
            found[name] = leaves[0] if count is None else leaves[:count]
            leaves = leaves[1 if count is None else count :]
        return found

    scratch = scratch | dict(
        send_sems=pltpu.SemaphoreType.DMA((n_copies,)),
        recv_sems=pltpu.SemaphoreType.DMA((n_copies,)),
    )
    in_names, values, in_specs = flat(ins)
    out_names, shapes, out_specs = flat(outs)

    def numbers(names, wanted):
        at = 0
        for name, count in names:
            size = 1 if count is None else count
            if name == wanted:
                return range(at, at + size)
            at += size

    aliases = {}
    for output, source in (kept or {}).items():
        aliases |= dict(zip(numbers(in_names, source), numbers(out_names, output)))
    scratch_names = [(name, None) for name in scratch]

    def body(*refs):
        named = unflat(in_names + out_names + scratch_names, refs)
        kernel(types.SimpleNamespace(**named))

    results = pl.pallas_call(
        body,
        out_shape=tuple(shapes),
        in_specs=in_specs,
        out_specs=tuple(out_specs),
        scratch_shapes=list(scratch.values()),
        input_output_aliases=aliases,
        compiler_params=params(identity, limit),
        cost_estimate=pl.CostEstimate(flops=1, bytes_accessed=1, transcendentals=0),
        name=kernel.__name__,
    )(*values)
    return types.SimpleNamespace(**unflat(out_names, results))


def low(*shape):
    return jax.ShapeDtypeStruct(shape, BF16)


def single(*shape):
    return jax.ShapeDtypeStruct(shape, F32)


def dot(a, b, contract):
    return lax.dot_general(a, b, ((contract[:1], contract[1:]), ((), ())), preferred_element_type=F32)


NN, NT, TN = (1, 0), (1, 1), (0, 0)


def run_level(trees, level):
    for one in trees:
        for j in one.steps():
            if one.level(j) == level:
                one.receive(j)
                one.send(j)


def send_experts(copies, me, span, packed, near, experts):
    dp, mp = me
    slots = {}
    for i, expert in enumerate(experts):
        for k in range(1, span):
            slots[i, k] = copies.slot()
            copies.start(
                packed.at[expert], near[k - 1].at[i], (dp, flip_all(mp, k)), slots[i, k]
            )
    return slots


def wait_experts(copies, me, near, slots):
    for (i, k), slot in slots.items():
        copies.wait(near[k - 1].at[i], me, slot)


def row_trees(copies, n_dp, me, rows_all):
    tokens = rows_all.shape[1]

    def tree(part, order):
        cut = pl.ds(part * (tokens // 2), tokens // 2)
        return TreeGather(
            copies,
            order,
            n_dp,
            me,
            lambda j: rows_all.at[j, cut],
            lambda j, mask: rows_all.at[j ^ mask, cut],
        )

    return [tree(part, order) for part, order in enumerate(orders_of(n_dp))]


def rotary_constants():
    half_width = HEAD_SIZE // 2
    frequency = np.exp(
        np.float32(-math.log(10000.0)) * np.arange(half_width, dtype=np.float32) * np.float32(2.0)
        / np.float32(HEAD_SIZE)
    ).astype(np.float32)
    angles = np.arange(SEQUENCE_TOKENS, dtype=np.float32)[:, None] * frequency[None, :]
    cosine, sine = np.cos(angles), np.sin(angles)
    cosine = np.concatenate([cosine, cosine], 1)
    sine = np.concatenate([-sine, sine], 1)
    queries = np.stack([np.tile(cosine, (1, 2)), np.tile(sine, (1, 2))])
    keys = np.stack(
        [
            np.concatenate([cosine, np.ones_like(cosine)], 1),
            np.concatenate([sine, np.zeros_like(sine)], 1),
        ]
    )
    return queries.astype(np.float32), keys.astype(np.float32)


def rotate(value, cosine, sine):
    lane = lax.broadcasted_iota(jnp.int32, value.shape, 1)
    rolled = jnp.where(
        lane % HEAD_SIZE < HEAD_SIZE // 2,
        pltpu.roll(value, 128 - HEAD_SIZE // 2, 1),
        pltpu.roll(value, HEAD_SIZE // 2, 1),
    )
    return value * cosine + rolled * sine


def group_operands(queries, keyval):
    lane = lax.broadcasted_iota(jnp.int32, queries.shape, 1)
    both = jnp.concatenate(
        [jnp.where(lane < HEAD_SIZE, queries, 0.0), jnp.where(lane < HEAD_SIZE, 0.0, queries)], 0
    ).astype(BF16)
    lane = lax.broadcasted_iota(jnp.int32, keyval.shape, 1)
    turned = pltpu.roll(keyval, HEAD_SIZE, 1)
    keys = jnp.where(lane < HEAD_SIZE, keyval, turned).astype(BF16)
    values = jnp.where(lane < HEAD_SIZE, turned, keyval).astype(BF16)
    return both, keys, values


def merge_heads(both):
    tokens = both.shape[0] // 2
    lane = lax.broadcasted_iota(jnp.int32, (tokens, 128), 1)
    return jnp.where(lane < HEAD_SIZE, both[:tokens], both[tokens:])


def seen(tokens, mp):
    shape = (2 * tokens, 2 * tokens)
    row = lax.broadcasted_iota(jnp.int32, shape, 0) % tokens
    key = lax.broadcasted_iota(jnp.int32, shape, 1)
    shift = tokens - 2 * tokens * lax.rem(mp, 2)
    key = jnp.where(key < tokens, key, key - tokens + shift)
    return key <= row


def softmax_of(both, keys, mask):
    scores = dot(both, keys, NT) * (1.0 / math.sqrt(HEAD_SIZE))
    raised = jnp.exp(jnp.where(mask, scores, -1e30))
    return raised / jnp.sum(raised, -1, keepdims=True)


def store_blocks(trees, level, source, target, sems):
    stores = []
    for j in range(source.shape[0]) if trees else []:
        if trees[0].level(j) == level:
            stores.append(pltpu.make_async_copy(source.at[j], target.at[j], sems.at[j]))
            stores[-1].start()
    return stores


def attention_forward(
    n_dp, n_mp, groups, identity, first_row, small, shards, cot, residual, gateup, down, ids, tables, experts
):
    tokens, width = residual.shape
    half = n_mp // 2
    kinds, rows, cols = shards.shape
    part_rows = rows // 2
    half_cols = half * cols
    n_heads = width // 128
    span = n_mp // groups
    owned, _, hidden, _ = gateup.shape
    n_devices = n_dp * n_mp
    own_router = small.shape[0] - first_row
    n_experts = len(experts)
    order_a, _ = orders_of(n_dp)
    n_copies = 2 * (n_mp - 1) + 10 * (n_dp - 1) + 2 + n_experts * (span - 1)

    def attention(r):
        dp, mp = lax.axis_index("dp"), lax.axis_index("mp")
        me = (dp, mp)
        neighbour = (dp, flip(mp, 1))
        partner = (dp, flip_all(mp, span))
        copies = Copies(r.send_sems, r.recv_sems)
        loads = [
            pltpu.make_async_copy(r.gateup, r.wide.at[:, pl.ds(0, 2)], r.local_sems.at[0]),
            pltpu.make_async_copy(r.down, r.wide.at[:, 2], r.local_sems.at[1]),
        ]
        for copy in loads:
            copy.start()
        own_small = r.small_all.at[dp, mp]
        own_rows = pl.ds(pl.multiple_of(dp * rows, rows), rows)
        own_cols = pl.ds(pl.multiple_of(mp * cols, cols), cols)
        own_part = r.full.at[:, own_rows, own_cols]
        r.small_all[dp, mp] = r.small[...]
        residual = r.residual[...]
        inverse = lax.rsqrt(jnp.mean(residual * residual, -1, keepdims=True) + NORM_EPS)
        r.scaled[0] = (residual * inverse).astype(BF16)
        r.full[:, own_rows, own_cols] = r.shards[...]
        r.cots[0] = r.cot[...]
        greet(
            [(flip_all(dp, mask), mp) for mask in bits_of(n_dp)]
            + [(dp, flip_all(mp, k)) for k in range(1, n_mp)]
        )
        line = {}
        for k in range(1, n_mp):
            line[k] = (copies.slot(), copies.slot())
            copies.start(r.small, own_small, (dp, flip_all(mp, k)), line[k][0])
        for k in range(1, n_mp):
            copies.start(r.shards, own_part, (dp, flip_all(mp, k)), line[k][1])
        across = (copies.slot(), copies.slot())
        copies.start(r.scaled.at[0], r.scaled.at[1], neighbour, across[0])
        if groups > 1:
            copies.start(r.cot, r.other_cots.at[0], partner, across[1])
        near = lax.div(mp, half)
        chunks = (near, 1 - near)
        chunk_cols = [
            pl.ds(pl.multiple_of(chunk * half_cols, half_cols), half_cols) for chunk in chunks
        ]

        def small_tree(chunk):
            first = pl.multiple_of(chunk * half, half)

            def ref(j, mask=0):
                return r.small_all.at[flip_all(dp, j), pl.ds(first, half)]

            return TreeGather(copies, order_a, n_dp, me, ref, ref)

        def weight_tree(chunk, part, order):
            def ref(j, mask=0):
                start = flip_all(dp, j) * rows + part * part_rows
                there = pl.ds(pl.multiple_of(start, part_rows), part_rows)
                return r.full.at[:, there, chunk_cols[chunk]]

            return TreeGather(copies, order, n_dp, me, ref, ref)

        def wait_line(first, end, which):
            for k in range(first, end):
                other = flip_all(mp, k)
                if which:
                    there = pl.ds(pl.multiple_of(other * cols, cols), cols)
                    copies.wait(r.full.at[:, own_rows, there], me, line[k][1])
                else:
                    copies.wait(r.small_all.at[dp, other], me, line[k][0])

        small_trees = [small_tree(chunk) for chunk in chunks]
        weight_trees = [
            [weight_tree(chunk, part, order) for part, order in enumerate(orders_of(n_dp))]
            for chunk in (0, 1)
        ]
        cot_trees = row_trees(copies, n_dp, me, r.cots)
        other_trees = row_trees(copies, n_dp, me, r.other_cots) if groups > 1 else []

        def send_own(trees):
            for one in trees:
                one.send(0)

        top = n_dp.bit_length() - 1
        wait_line(1, half, 0)
        send_own(small_trees[:1])
        wait_line(half, n_mp, 0)
        send_own(small_trees[1:])
        send_own(cot_trees)
        stores = store_blocks(cot_trees, 0, r.cots, r.cots_out, r.cot_sems)
        named = lax.broadcasted_iota(jnp.int32, (EXPERTS, tokens), 0)
        chosen = jnp.zeros((EXPERTS, tokens), F32)
        for k in range(TOPK):
            chosen += jnp.where(named == r.ids[k : k + 1, :], 1.0, 0.0)
        shape = (tokens, tokens)
        earlier = lax.broadcasted_iota(jnp.int32, shape, 0) < lax.broadcasted_iota(jnp.int32, shape, 1)
        before = dot(chosen.astype(BF16), jnp.where(earlier, 1.0, 0.0).astype(BF16), NN)
        place = jnp.where(chosen > 0.0, before, -1.0)
        r.table[...] = jnp.zeros_like(r.table)
        for expert in range(EXPERTS):
            owner, which = divmod(expert, owned)
            r.table[owner, which, :] = place[expert]
        wait_line(1, half, 1)
        send_own(weight_trees[0])
        for copy in loads:
            copy.wait()
        for e in range(owned):
            r.narrow[e] = r.wide[e].astype(BF16)
        stores.append(pltpu.make_async_copy(r.narrow, r.packed, r.local_sems.at[2]))
        stores[-1].start()
        for level in range(1, top + 1):
            if level == top:
                wait_line(half, n_mp, 1)
                send_own(weight_trees[1])
            run_level(small_trees, level)
            run_level(cot_trees, level)
            stores += store_blocks(cot_trees, level, r.cots, r.cots_out, r.cot_sems)
            run_level(weight_trees[0], level)
        n_tiles = width // 128
        for row in (0, 1):
            for tile in range(n_tiles):
                total = None
                for at in range(tile * n_devices // n_tiles, (tile + 1) * n_devices // n_tiles):
                    part = r.small_all[at // n_mp, at % n_mp, row : row + 1, :]
                    total = part if total is None else total + part
                r.gains[row : row + 1, tile * 128 : (tile + 1) * 128] = total
        for at in range(n_devices):
            r.router_wide[at * own_router : (at + 1) * own_router, :] = r.small_all[
                at // n_mp, at % n_mp, first_row:, :
            ]
        r.router[...] = r.router_wide[...].astype(BF16)
        copies.wait(r.scaled.at[1], me, across[0])
        residual = r.residual[...]
        inverse = lax.rsqrt(jnp.mean(residual * residual, -1, keepdims=True) + NORM_EPS)
        gain_one = r.gains[0:1, :]
        r.normed[0] = (residual * inverse * gain_one).astype(BF16)
        r.normed[1] = (r.scaled[1].astype(F32) * gain_one).astype(BF16)
        mask = seen(tokens, mp)
        which = lax.rem(mp, 2)

        def table(ref, at):
            there = pl.ds(pl.multiple_of(at * tokens, tokens), tokens)
            return ref[0, there, :], ref[1, there, :]

        def project(chunk):
            there = chunk_cols[chunk]
            r.q[:, there] = dot(r.normed[0], r.full[0, :, there], NN)
            for part in (0, 1):
                r.kv[part, :, there] = dot(r.normed[part], r.full[1, :, there], NN)

        def heads(chunk, first, end):
            def head(k, carry):
                number = chunks[chunk] * (n_heads // 2) + k
                lanes = pl.ds(pl.multiple_of(number * 128, 128), 128)
                queries = rotate(r.q[:, lanes], *table(r.query_table, which))
                r.queries[:, lanes] = queries.astype(BF16)
                parts = []
                for part, at in enumerate((which, 1 - which)):
                    parts.append(rotate(r.kv[part, :, lanes], *table(r.key_table, at)))
                    r.keyval[part, :, lanes] = parts[part].astype(BF16)
                both, keys, values = group_operands(queries, jnp.concatenate(parts, 0))
                chance = softmax_of(both, keys, mask).astype(BF16)
                r.context[:, lanes] = merge_heads(dot(chance, values, NN)).astype(BF16)
                return carry

            lax.fori_loop(first, end, head, 0)

        run_level(weight_trees[1], 1)
        if groups > 1:
            copies.wait(r.other_cots.at[0], me, across[1])
        send_own(other_trees)
        stores += store_blocks(other_trees, 0, r.other_cots, r.other_out, r.other_sems)
        sent = send_experts(copies, me, span, r.narrow, r.near, experts)
        project(0)
        heads(0, 0, 2)
        for level in range(2, top + 1):
            run_level(weight_trees[1], level)
        stores.append(pltpu.make_async_copy(r.full, r.full_out, r.local_sems.at[3]))
        stores[-1].start()
        heads(0, 2, n_heads // 2)
        project(1)
        n_left = n_heads // 2
        for level in range(1, top + 1):
            run_level(other_trees, level)
            stores += store_blocks(other_trees, level, r.other_cots, r.other_out, r.other_sems)
            if level < top:
                first, end = [(level - 1 + i) * n_left // (top - 1) for i in (0, 1)]
                heads(1, first, end)
        hidden_rows = r.residual[...] + dot(r.context[...], r.full[2], NT)
        r.hidden[...] = hidden_rows
        inverse = lax.rsqrt(jnp.mean(hidden_rows * hidden_rows, -1, keepdims=True) + NORM_EPS)
        normed = (hidden_rows * inverse * r.gains[1:2, :]).astype(BF16)
        r.normed_two[...] = normed
        logits = dot(normed, r.router[...], NN)
        lane = lax.broadcasted_iota(jnp.int32, logits.shape, 1)
        raised = jnp.where(lane < EXPERTS, jnp.exp(logits), 0.0)
        probs = raised / jnp.sum(raised, -1, keepdims=True)
        r.probs[...] = probs
        turned = probs.T
        for expert in range(EXPERTS):
            owner, which = divmod(expert, owned)
            r.table[owner, 4 + which, :] = turned[expert]
        wait_experts(copies, me, r.near, sent)
        for copy in stores:
            copy.wait()
        copies.finish()

    return launch(
        attention,
        identity,
        dict(
            small=(small, vmem()),
            shards=(shards, vmem()),
            cot=(cot, vmem()),
            residual=(residual, vmem()),
            gateup=(gateup, hbm()),
            down=(down, hbm()),
            ids=(ids, vmem()),
            query_table=(tables[0], vmem()),
            key_table=(tables[1], vmem()),
        ),
        dict(
            gains=(single(2, width), vmem()),
            router=(low(width, 128), vmem()),
            packed=(low(owned, 3, hidden, width), hbm()),
            full_out=(low(kinds, n_dp * rows, width), hbm()),
            cots_out=(low(n_dp, tokens, width), hbm()),
            other_out=(low(n_dp, tokens, width), hbm()),
            near=([low(n_experts, 3, hidden, width) for _ in range(1, span)], hbm()),
            normed=(low(2, tokens, width), vmem()),
            queries=(low(tokens, width), vmem()),
            keyval=(low(2, tokens, width), vmem()),
            context=(low(tokens, width), vmem()),
            hidden=(single(tokens, width), vmem()),
            normed_two=(low(tokens, width), vmem()),
            probs=(single(tokens, 128), vmem()),
            table=(single(n_dp, 8, tokens), vmem()),
        ),
        dict(
            full=pltpu.VMEM((kinds, n_dp * rows, width), BF16),
            cots=pltpu.VMEM((n_dp, tokens, width), BF16),
            other_cots=pltpu.VMEM((n_dp, tokens, width), BF16),
            scaled=pltpu.VMEM((2, tokens, width), BF16),
            small_all=pltpu.VMEM((n_dp, n_mp) + small.shape, F32),
            router_wide=pltpu.VMEM((width, 128), F32),
            wide=pltpu.VMEM((owned, 3, hidden, width), F32),
            narrow=pltpu.VMEM((owned, 3, hidden, width), BF16),
            q=pltpu.VMEM((tokens, width), F32),
            kv=pltpu.VMEM((2, tokens, width), F32),
            local_sems=pltpu.SemaphoreType.DMA((4,)),
            cot_sems=pltpu.SemaphoreType.DMA((n_dp,)),
            other_sems=pltpu.SemaphoreType.DMA((n_dp,)),
        ),
        n_copies,
        60 << 20,
    )


def attention_backward(n_dp, n_mp, groups, identity, given, first_row):
    tokens, width = given.residual.shape
    n_heads = width // 128
    n_devices = n_dp * n_mp
    own_router = width // n_devices
    per_tile = n_devices // n_heads
    rows, cols = width // n_dp, width // n_mp
    part_rows = rows // 2
    orders = orders_of(n_dp)
    span = n_mp // groups
    owned = EXPERTS // n_dp
    n_late = given.late[0].shape[0] if given.late else 0
    n_copies = (2 * groups + 7) * (n_dp - 1) + 2 + 4 * (n_mp - 1) + 2 + n_late * (span - 1)

    rooms, across_room = reduce_rooms(groups, n_dp, tokens, width, BF16)

    def attention_back(r):
        dp, mp = lax.axis_index("dp"), lax.axis_index("mp")
        me = (dp, mp)
        neighbour = (dp, flip(mp, 1))
        copies = Copies(r.send_sems, r.recv_sems)
        loads = [
            pltpu.make_async_copy(r.full.at[c], r.weights.at[c], r.local_sems.at[c])
            for c in (2, 0, 1)
        ]
        for copy in loads:
            copy.start()
        even_loads = [
            pltpu.make_async_copy(
                r.terms.at[g, j], r.terms_even.at[g, j // 2], r.term_sems.at[g, j // 2]
            )
            for g in range(groups)
            for j in range(0, n_dp, 2)
        ]
        for copy in even_loads:
            copy.start()
        greet(
            [(flip_all(dp, mask), mp) for mask in bits_of(n_dp)]
            + [(dp, flip_all(mp, k)) for k in range(1, n_mp)]
        )
        partner = (dp, flip_all(mp, span))
        mixture = TokenReduce(
            copies,
            n_dp,
            me,
            partner,
            groups,
            lambda g, j: r.terms.at[g, j] if j % 2 else r.terms_even.at[g, j // 2],
            r.rooms,
            r.across,
        )
        for group in range(groups)[::-1]:
            for j in range(1, n_dp, 2):
                mixture.first(group, j)
        last = mixture.last
        for copy in even_loads:
            copy.wait()
        mixture.level(1, last - 1)
        travels = {}

        def send_late(i):
            if i < n_late:
                for k in range(1, span):
                    travels[i, k] = copies.slot()
                    copies.start(
                        r.late[k - 1].at[i],
                        r.arrived[k - 1].at[owned - n_late + i],
                        (dp, flip_all(mp, k)),
                        travels[i, k],
                    )

        send_late(0)
        r.turned[...] = jnp.zeros_like(r.turned)
        for expert in range(EXPERTS):
            owner, which = divmod(expert, owned)
            parts = r.gate_parts[owner, 0, which, :]
            for group in range(1, groups):
                parts = parts + r.gate_parts[owner, group, which, :]
            r.turned[expert, :] = parts
        grad_probs = r.turned[...].T
        probs = r.probs[...]
        grad_logits = (
            probs * (grad_probs - jnp.sum(probs * grad_probs, -1, keepdims=True))
        ).astype(BF16)
        grad_normed_two = r.total[...] + dot(grad_logits, r.router[...], NT)
        r.grad_router[...] = dot(r.normed_two[...], grad_logits, TN)
        mixture.level(0, last - 1)
        hidden = r.hidden[...]
        inverse = lax.rsqrt(jnp.mean(hidden * hidden, -1, keepdims=True) + NORM_EPS)
        scaled = r.gains[1:2, :] * grad_normed_two
        grad_hidden = (
            r.cotangent[...]
            + inverse * scaled
            - hidden * (inverse * inverse * inverse) * jnp.mean(scaled * hidden, -1, keepdims=True)
        )
        r.grad_hidden[...] = grad_hidden
        gain_two = jnp.sum(grad_normed_two * hidden * inverse, 0, keepdims=True)
        grad_attn = grad_hidden.astype(BF16)
        r.grad_attn[...] = grad_attn
        def weight_tree(c, part):
            def block(j):
                start = flip_all(dp, j) * rows + part * part_rows
                return r.grads.at[c, pl.ds(pl.multiple_of(start, part_rows), part_rows), :]

            return TreeReduce(
                copies,
                orders[part],
                n_dp,
                me,
                block,
                lambda number: r.weight_rooms.at[c, part, number],
                add_rows(),
            )

        weight_trees = [[weight_tree(c, part) for part in (0, 1)] for c in range(3)]

        def weight_level(c, p):
            for j in range(1, n_dp):
                for one in weight_trees[c]:
                    if place_of(one.order, j) == p:
                        if p < last:
                            one.collect(j)
                        one.send(j)

        r.grads[2] = dot(grad_attn, r.context[...], TN).astype(BF16)
        weight_level(2, last)
        loads[0].wait()
        r.grad_context[...] = dot(r.grad_attn[...], r.weights[2], NN).astype(BF16)
        mask = seen(tokens, mp)

        def table(ref):
            there = pl.ds(pl.multiple_of(lax.rem(mp, 2) * tokens, tokens), tokens)
            return ref[0, there, :], ref[1, there, :]

        def head(k, carry):
            lanes = pl.ds(pl.multiple_of(k * 128, 128), 128)
            keyval = jnp.concatenate([r.keyval[0, :, lanes], r.keyval[1, :, lanes]], 0)
            both, keys, values = group_operands(r.queries[:, lanes].astype(F32), keyval.astype(F32))
            grad_both = group_operands(r.grad_context[:, lanes].astype(F32), keyval.astype(F32))[0]
            chance = softmax_of(both, keys, mask)
            grad_p = dot(grad_both, values, NT)
            delta = jnp.sum(chance * grad_p, -1, keepdims=True)
            grad_s = (chance * (grad_p - delta)).astype(BF16)
            scale = 1.0 / math.sqrt(HEAD_SIZE)
            grad_q = merge_heads(dot(grad_s, keys, NN)) * scale
            cosine, sine = table(r.query_table)
            r.grad_q[:, lanes] = rotate(grad_q, cosine, -sine).astype(BF16)
            grad_k = dot(grad_s, both, TN) * scale
            grad_v = dot(chance.astype(BF16), grad_both, TN)
            lane = lax.broadcasted_iota(jnp.int32, grad_k.shape, 1)
            grad_kv = jnp.where(
                lane < HEAD_SIZE,
                grad_k + pltpu.roll(grad_k, HEAD_SIZE, 1),
                grad_v + pltpu.roll(grad_v, HEAD_SIZE, 1),
            )
            r.grad_kv[:, lanes] = grad_kv[:tokens]
            r.swap[0, :, lanes] = grad_kv[tokens:].astype(BF16)
            return carry

        sent = {}

        def line_out(c):
            for part, one in enumerate(weight_trees[c]):
                one.collect(0)
                total = one.total()
                for k in range(n_mp):
                    there = pl.ds(pl.multiple_of(flip_all(mp, k) * cols, cols), cols)
                    r.line[0, c, k, pl.ds(part * part_rows, part_rows), :] = total[:, there]
            for k in range(1, n_mp):
                sent[c, k] = copies.slot()
                copies.start(
                    r.line.at[0, c, k], r.line.at[1, c, k], (dp, flip_all(mp, k)), sent[c, k]
                )

        across = [copies.slot() for _ in range(2)]
        swaps = [pl.ds(half * (width // 2), width // 2) for half in range(2)]

        def heads(first, end):
            lax.fori_loop(first * n_heads // 4, end * n_heads // 4, head, 0)

        def swap(half):
            copies.start(
                r.swap.at[0, :, swaps[half]],
                r.swap.at[1, :, swaps[half]],
                neighbour,
                across[half],
            )

        heads(0, 2)
        swap(0)
        for p in range(last - 2, -1, -1):
            mixture.level(1, p)
        heads(2, 3)
        weight_level(2, last - 1)
        heads(3, 4)
        swap(1)
        for p in range(last - 2, -1, -1):
            mixture.level(0, p)
        mixture.pass_on()
        for i in range(1, n_late):
            send_late(i)
        r.grads[0] = dot(r.normed[0], r.grad_q[...], TN).astype(BF16)
        weight_level(0, last)
        loads[1].wait()
        r.grad_normed[...] = dot(r.grad_q[...], r.weights[0], NT)
        weight_level(0, last - 1)
        for p in range(last - 2, -1, -1):
            weight_level(2, p)
        for half in range(2):
            copies.wait(r.swap.at[1, :, swaps[half]], me, across[half])

        def turn_back(k, carry):
            lanes = pl.ds(pl.multiple_of(k * 128, 128), 128)
            total = r.grad_kv[:, lanes] + r.swap[1, :, lanes].astype(F32)
            cosine, sine = table(r.key_table)
            total = rotate(total, cosine, -sine)
            r.grad_kv_low[:, lanes] = total.astype(BF16)
            return carry

        lax.fori_loop(0, n_heads, turn_back, 0)
        loads[2].wait()
        r.grads[1] = dot(r.normed[0], r.grad_kv_low[...], TN).astype(BF16)
        weight_level(1, last)
        grad_normed = r.grad_normed[...] + dot(r.grad_kv_low[...], r.weights[1], NT)
        residual = r.residual[...]
        inverse = lax.rsqrt(jnp.mean(residual * residual, -1, keepdims=True) + NORM_EPS)
        scaled = r.gains[0:1, :] * grad_normed
        r.input_grad[...] = (
            r.grad_hidden[...]
            + inverse * scaled
            - residual * (inverse * inverse * inverse) * jnp.mean(scaled * residual, -1, keepdims=True)
        )
        gain_one = jnp.sum(grad_normed * residual * inverse, 0, keepdims=True)
        r.small[...] = jnp.zeros_like(r.small)
        for device in range(n_devices):
            tile = device // per_tile
            owner = r.small.at[device // n_mp, device % n_mp]
            owner[0:1, :] = gain_one[:, tile * 128 : (tile + 1) * 128]
            owner[1:2, :] = gain_two[:, tile * 128 : (tile + 1) * 128]
            owner[first_row : first_row + own_router, :] = r.grad_router[
                device * own_router : (device + 1) * own_router, :
            ]

        def add_whole(here, other):
            here[...] = here[...] + other[...]

        small_tree = TreeReduce(
            copies,
            orders[0],
            n_dp,
            me,
            lambda j: r.small.at[flip_all(dp, j)],
            lambda number: r.small_rooms.at[number],
            add_whole,
        )
        for j in range(1, n_dp):
            if place_of(orders[0], j) == last:
                small_tree.send(j)
        for p in range(last - 1, -1, -1):
            if p < last - 1:
                weight_level(0, p)
            weight_level(1, p)
            for j in range(1, n_dp):
                if place_of(orders[0], j) == p:
                    small_tree.collect(j)
                    small_tree.send(j)
            if p == last - 1:
                line_out(2)
        for c in (0, 1):
            line_out(c)
        small_tree.collect(0)
        small_total = small_tree.total()
        for k in range(1, n_mp):
            device = (dp, flip_all(mp, k))
            sent[k] = copies.slot()
            copies.start(small_total.at[device[1]], r.small_line.at[k], device, sent[k])
        mixture.end(r.block_out)
        r.block_out[...] += r.hidden[...]
        for c in (2, 0, 1):
            r.shards[c] = r.line[0, c, 0].astype(F32)
            for k in range(1, n_mp):
                copies.wait(r.line.at[1, c, k], me, sent[c, k])
                r.shards[c] += r.line[1, c, k].astype(F32)
        r.small_shard[...] = small_total[mp]
        for k in range(1, n_mp):
            copies.wait(r.small_line.at[k], me, sent[k])
            r.small_shard[...] += r.small_line[k]
        for (i, k), slot in travels.items():
            copies.wait(r.arrived[k - 1].at[owned - n_late + i], me, slot)
        copies.finish()

    return launch(
        attention_back,
        identity,
        dict(
            full=(given.full, hbm()),
            late=(given.late, hbm()),
            begun=(given.arrived, hbm()),
            residual=(given.residual, vmem()),
            hidden=(given.hidden, vmem()),
            cotangent=(given.cotangent, vmem()),
            total=(given.total, vmem()),
            gate_parts=(given.gate_parts, vmem()),
            terms=(given.terms, hbm()),
            probs=(given.probs, vmem()),
            normed=(given.normed, vmem()),
            normed_two=(given.normed_two, vmem()),
            queries=(given.queries, vmem()),
            keyval=(given.keyval, vmem()),
            context=(given.context, vmem()),
            gains=(given.gains, vmem()),
            router=(given.router, vmem()),
            query_table=(given.tables[0], vmem()),
            key_table=(given.tables[1], vmem()),
        ),
        dict(
            input_grad=(single(tokens, width), vmem()),
            block_out=(single(tokens, width), vmem()),
            arrived=([low(*grad.shape) for grad in given.arrived], hbm()),
            shards=(single(3, rows, cols), vmem()),
            small_shard=(single(first_row + own_router, 128), vmem()),
        ),
        dict(
            grads=pltpu.VMEM((3, width, width), BF16),
            small=pltpu.VMEM((n_dp, n_mp, first_row + own_router, 128), F32),
            small_rooms=pltpu.VMEM((n_dp - 1, n_mp, first_row + own_router, 128), F32),
            small_line=pltpu.VMEM((n_mp, first_row + own_router, 128), F32),
            terms_even=pltpu.VMEM((groups, n_dp // 2, tokens, width), BF16),
            term_sems=pltpu.SemaphoreType.DMA((groups, n_dp // 2)),
            weight_rooms=pltpu.VMEM((3, 2, n_dp - 1, part_rows, width), BF16),
            line=pltpu.VMEM((2, 3, n_mp, rows, cols), BF16),
            rooms=rooms,
            across=across_room,
            weights=pltpu.VMEM((3, width, width), BF16),
            turned=pltpu.VMEM((128, tokens), F32),
            grad_router=pltpu.VMEM((width, 128), F32),
            grad_hidden=pltpu.VMEM((tokens, width), F32),
            grad_attn=pltpu.VMEM((tokens, width), BF16),
            grad_context=pltpu.VMEM((tokens, width), BF16),
            grad_q=pltpu.VMEM((tokens, width), BF16),
            grad_kv=pltpu.VMEM((tokens, width), F32),
            grad_kv_low=pltpu.VMEM((tokens, width), BF16),
            grad_normed=pltpu.VMEM((tokens, width), F32),
            swap=pltpu.VMEM((2, tokens, width), BF16),
            local_sems=pltpu.SemaphoreType.DMA((3,)),
        ),
        n_copies,
        62 << 20,
        dict(arrived="begun"),
    )


class TokenReduce:
    def __init__(self, copies, n_dp, me, partner, groups, block, rooms, across):
        self.copies, self.me, self.across = copies, me, across
        self.partner = partner
        self.tokens = across.shape[1]
        self.n_dp = n_dp
        self.last = n_dp.bit_length() - 2
        self.groups = groups
        self.halves = [copies.slot(), copies.slot()]

        def tree(group, part, order):
            cut = pl.ds(part * (self.tokens // 2), self.tokens // 2)
            return TreeReduce(
                copies,
                order,
                n_dp,
                me,
                lambda j: block(group, j).at[cut],
                lambda number: rooms.at[group, part, number],
                add_rows(),
            )

        self.trees = [
            [tree(group, part, order) for part, order in enumerate(orders_of(n_dp))]
            for group in range(self.groups)
        ]

    def first(self, group, j):
        for tree in self.trees[group]:
            tree.send(j)

    def level(self, group, p):
        if group == self.groups:
            return
        for j in range(1, self.n_dp):
            for tree in self.trees[group]:
                if place_of(tree.order, j) == p:
                    tree.collect(j)
                    tree.send(j)

    def pass_on(self):
        if self.groups == 1:
            return
        for part, tree in enumerate(self.trees[1]):
            tree.collect(0)
            cut = pl.ds(part * (self.tokens // 2), self.tokens // 2)
            self.copies.start(
                tree.total(), self.across.at[0, cut], self.partner, self.halves[part]
            )

    def end(self, out_ref):
        for tree in self.trees[0]:
            tree.collect(0)
        for part, tree in enumerate(self.trees[0]):
            cut = pl.ds(part * (self.tokens // 2), self.tokens // 2)
            total = tree.total()[...].astype(F32)
            if self.groups > 1:
                self.copies.wait(self.across.at[0, cut], self.me, self.halves[part])
                total = total + self.across[0, cut, :].astype(F32)
            out_ref[cut, :] = total


def reduce_rooms(groups, n_dp, tokens, width, dtype):
    return [
        pltpu.VMEM((groups, 2, n_dp - 1, tokens // 2, width), dtype),
        pltpu.VMEM((1, tokens, width), dtype),
    ]


def run_experts(n_dp, n_mp, groups, identity, rows, table, cots, packed, near):
    owned, _, hidden, width = packed.shape
    span = n_mp // groups
    units = span * hidden
    blocks = groups * n_dp
    slots = blocks * CAP
    tokens = rows.shape[0]
    per_tile = 4
    tile = per_tile * CAP
    n_tiles = blocks // per_tile
    here = [expert for experts, _ in near for expert in experts]
    coming = [expert for expert in range(owned) if expert not in here]
    n_sent = min(owned, 2)
    n_late = owned - n_sent
    n_copies = groups + 1 + 2 * (blocks - 1) + 4 * groups * (n_dp - 1)
    n_copies += (len(coming) + n_sent) * (span - 1)
    order = []
    for group in range(groups):
        for level in range(n_dp.bit_length()):
            order += [(group, j) for j in range(n_dp) if bin(j).count("1") == level]

    def experts(r):
        dp, mp = lax.axis_index("dp"), lax.axis_index("mp")
        me = (dp, mp)
        other = flip_all(mp, span)
        copies = Copies(r.send_sems, r.recv_sems)
        peers = {
            (group, j): (flip_all(dp, j), other if group else mp)
            for group in range(groups)
            for j in range(n_dp)
            if group + j
        }
        local = iter(range(n_loads))

        def load(source, target):
            copy = pltpu.make_async_copy(source, target, r.load_sems.at[next(local)])
            copy.start()
            return copy

        def units_of(k):
            return pl.ds(k * hidden, hidden)

        own_table = load(r.own_table.at[dp], r.tables.at[0])
        own_rows = load(r.rows, r.rows_all.at[0, 0])
        loads = [
            [load(r.packed.at[e], r.weights.at[e, :, units_of(0)])] for e in range(owned)
        ]
        for number, (some, _) in enumerate(near):
            for i, e in enumerate(some):
                for k in range(1, span):
                    source = r.near[number * (span - 1) + k - 1].at[i]
                    loads[e].append(load(source, r.weights.at[e, :, units_of(k)]))

        def cot_copy(number):
            group, j = order[number]
            return pltpu.make_async_copy(
                r.cots[group].at[j], r.cot.at[number % 2], r.cot_sems.at[number % 2]
            )

        cot_copy(0).start()
        greet(list(peers.values()) + [(dp, flip_all(mp, k)) for k in range(1, span)])
        if groups > 1:
            across = copies.slot()
            copies.start(r.rows, r.rows_all.at[1, 0], peers[1, 0], across)
        weights_sent, grads_sent = {}, {}

        def send_weights(e):
            for k in range(1, span):
                weights_sent[e, k] = copies.slot()
                copies.start(
                    r.packed.at[e],
                    r.weights.at[e, :, units_of(k)],
                    (dp, flip_all(mp, k)),
                    weights_sent[e, k],
                )

        for e in coming[:1]:
            send_weights(e)
        sent = {}
        for (group, j), device in peers.items():
            sent[group, j] = copies.slot()
            copies.start(
                r.own_table.at[device[0]],
                r.tables.at[order.index((group, j))],
                device,
                sent[group, j],
            )
        trees = [row_trees(copies, n_dp, me, r.rows_all.at[group]) for group in range(groups)]
        own_rows.wait()
        for tree in trees[0]:
            tree.send(0)
        own_table.wait()

        def hits(number, some):
            slot = lax.broadcasted_iota(jnp.int32, (CAP, tokens), 0).astype(F32)
            found = [slot == r.tables[number, pl.ds(i, 1), :] for i in some]
            return found[0] if len(found) == 1 else jnp.concatenate(found, 0)

        def fill(number):
            group, j = order[number]
            if number:
                copies.wait(r.tables.at[number], me, sent[group, j])
            if number + 1 < blocks:
                cot_copy(number + 1).start()
            pick = hits(number, range(owned)).astype(BF16)
            there = slice(number * CAP, (number + 1) * CAP)
            found = dot(pick, r.rows_all[group, j], NN).astype(BF16)
            for i in range(owned):
                r.x[i + 1, there, :] = found[i * CAP : (i + 1) * CAP]
            cot_copy(number).wait()
            found = dot(pick, r.cot[number % 2], NN).astype(BF16)
            for i in range(owned):
                r.y[i, there, :] = found[i * CAP : (i + 1) * CAP]

        def work(e, step):
            rows = pl.ds(pl.multiple_of(step * tile, 16), tile)
            x = r.x[e + 1, rows, :]
            gate = dot(x, r.weights[e, 0], NT)
            up = dot(x, r.weights[e, 1], NT)
            sigmoid = 1.0 / (1.0 + jnp.exp(-gate))
            silu = gate * sigmoid
            activation = (silu * up).astype(BF16)
            r.act[rows, :] = activation
            made = dot(activation, r.weights[e, 2], NN)
            cot = r.y[e, rows, :].astype(F32)
            chosen = []
            dots = jnp.sum(cot * made, -1, keepdims=True)
            for b in range(per_tile):
                number = step * per_tile + b
                hit = hits(number, (e,))
                chance = r.tables[number, pl.ds(4 + e, 1), :]
                chosen.append(jnp.sum(jnp.where(hit, chance, 0.0), -1, keepdims=True))
                mine = dots[b * CAP : (b + 1) * CAP]
                r.gates[number, pl.ds(e, 1), :] = jnp.sum(
                    jnp.where(hit, mine, 0.0), 0, keepdims=True
                )
            share = jnp.concatenate(chosen, 0)
            r.y[e, rows, :] = (share * made).astype(BF16)
            back = (share * cot).astype(BF16)
            r.back[rows, :] = back
            grad_act = dot(back, r.weights[e, 2], NT)
            grad_gate = grad_act * up * sigmoid * (1.0 + gate * (1.0 - sigmoid))
            grad_gate = grad_gate.astype(BF16)
            grad_up = (grad_act * silu).astype(BF16)
            r.pair[rows, pl.ds(0, units)] = grad_gate
            r.pair[rows, pl.ds(units, units)] = grad_up
            found = dot(grad_gate, r.weights[e, 0], NN) + dot(grad_up, r.weights[e, 1], NN)
            r.x[e, rows, :] = found.astype(BF16)

        def ready(e):
            for copy in loads[e]:
                copy.wait()
            if e in coming:
                for k in range(1, span):
                    copies.wait(r.weights.at[e, :, units_of(k)], me, weights_sent[e, k])

        stores = []

        def weight_grad(e):
            for c in range(3):
                source = r.act[...] if c == 2 else r.pair[:, pl.ds(c * units, units)]
                rhs = r.back[...] if c == 2 else r.x[e + 1]
                r.weights[e, c] = dot(source, rhs, TN).astype(BF16)
            stores.append(load(r.weights.at[e, :, units_of(0)], r.grad_own.at[e]))
            for k in range(1, span):
                source = r.weights.at[e, :, units_of(k)]
                if e < n_sent:
                    grads_sent[e, k] = copies.slot()
                    copies.start(
                        source, r.arrived[k - 1].at[e], (dp, flip_all(mp, k)), grads_sent[e, k]
                    )
                else:
                    stores.append(load(source, r.late[k - 1].at[e - n_sent]))

        ready(0)
        done = 0
        leaving = []
        for number, (group, j) in enumerate(order):
            if j:
                for tree in sorted(trees[group], key=lambda tree: place_of(tree.order, j)):
                    tree.receive(j)
                    tree.send(j)
            elif group:
                copies.wait(r.rows_all.at[1, 0], me, across)
                for tree in trees[1]:
                    tree.send(0)
            if group == groups - 1 and j == 0:
                leaving += copies.split()
                for e in coming[1:]:
                    send_weights(e)
                staying = copies.split()
            fill(number)
            if number % per_tile == per_tile - 1 and number < blocks - 1:
                work(0, done)
                done += 1
        work(0, done)
        leaving += copies.split()
        copies.sent = staying
        weight_grad(0)

        def tiles(e, first, end):
            def step(at, carry):
                work(e, at)
                return carry

            lax.fori_loop(first, end, step, 0)

        for e in range(1, owned - 1):
            ready(e)
            tiles(e, 0, n_tiles)
            weight_grad(e)
        copies.finish(leaving)
        partner = (dp, other)
        reduce = TokenReduce(
            copies, n_dp, me, partner, groups, lambda g, j: r.rows_all.at[g, j], r.rooms, r.across
        )
        last = owned - 1
        if last:
            ready(last)
        scattered = []

        def sum_copy(at):
            group, j = scattered[at]
            return pltpu.make_async_copy(
                r.sums.at[at % 2], r.terms.at[group, j], r.sum_sems.at[at % 2]
            )

        own_gates = pltpu.make_async_copy(r.gates.at[0], r.gate_parts.at[dp, 0], r.gate_sem.at[0])
        gates_sent = {}

        def scatter(group, j):
            number = order.index((group, j))
            if number:
                gates_sent[group, j] = copies.slot()
                copies.start(
                    r.gates.at[number],
                    r.gate_parts.at[dp, group],
                    peers[group, j],
                    gates_sent[group, j],
                )
            else:
                own_gates.start()
            there = slice(number * CAP, (number + 1) * CAP)
            pick = hits(number, range(owned)).astype(BF16)
            found = jnp.concatenate([r.x[e, there, :] for e in range(owned)], 0)
            r.rows_all[group, j] = dot(pick, found, TN).astype(BF16)
            if j % 2:
                reduce.first(group, j)
            found = jnp.concatenate([r.y[e, there, :] for e in range(owned)], 0)
            at = len(scattered)
            scattered.append((group, j))
            if at > 1:
                sum_copy(at - 2).wait()
            r.sums[at % 2] = dot(pick, found, TN).astype(BF16)
            sum_copy(at).start()

        halves = [
            (n_tiles * group // groups, n_tiles * (group + 1) // groups) for group in range(groups)
        ]
        levels = list(range(reduce.last - 1, -1, -1))
        for group in range(groups)[::-1]:
            first, end = halves[group]
            if last == 0:
                pass
            elif group == groups - 1:
                tiles(last, first, end)
            else:
                for at in range(first, end):
                    tiles(last, at, at + 1)
                    if levels:
                        reduce.level(1, levels.pop(0))
            for j in [j for j in range(n_dp) if j % 2] + [j for j in range(n_dp) if j % 2 == 0]:
                scatter(group, j)
        if groups > 1:
            for p in levels:
                reduce.level(1, p)
        reduce.pass_on()
        for p in range(reduce.last - 1, -1, -1):
            reduce.level(0, p)
            if p == reduce.last - 1 and last:
                weight_grad(last)
        reduce.end(r.total)
        for at in (blocks - 2, blocks - 1):
            sum_copy(at).wait()
        own_gates.wait()
        for (group, j), device in peers.items():
            copies.wait(r.gate_parts.at[device[0], group], me, gates_sent[group, j])
        for (e, k), slot in grads_sent.items():
            copies.wait(r.arrived[k - 1].at[e], me, slot)
        for copy in stores:
            copy.wait()
        copies.finish()

    n_loads = 2 + owned * span + owned * span
    near_refs = [part for _, parts in near for part in parts]
    weights = packed.shape[1:]
    rooms, across_room = reduce_rooms(groups, n_dp, tokens, width, BF16)
    return launch(
        experts,
        identity,
        dict(
            rows=(rows, hbm()),
            own_table=(table, hbm()),
            cots=(cots, hbm()),
            packed=(packed, hbm()),
            near=(near_refs, hbm()),
        ),
        dict(
            terms=(low(groups, n_dp, tokens, width), hbm()),
            gate_parts=(single(n_dp, groups, 8, tokens), hbm()),
            total=(single(tokens, width), vmem()),
            grad_own=(low(owned, *weights), hbm()),
            arrived=([low(owned, *weights) for _ in range(1, span)], hbm()),
            late=([low(n_late, *weights) for _ in range(1, span) if n_late], hbm()),
        ),
        dict(
            weights=pltpu.VMEM((owned, 3, units, width), BF16),
            rows_all=pltpu.VMEM((groups, n_dp, tokens, width), BF16),
            x=pltpu.VMEM((owned + 1, slots, width), BF16),
            y=pltpu.VMEM((owned, slots, width), BF16),
            act=pltpu.VMEM((slots, units), BF16),
            pair=pltpu.VMEM((slots, 2 * units), BF16),
            back=pltpu.VMEM((slots, width), BF16),
            tables=pltpu.VMEM((blocks, 8, tokens), F32),
            gates=pltpu.VMEM((blocks, 8, tokens), F32),
            cot=pltpu.VMEM((2, tokens, width), BF16),
            sums=pltpu.VMEM((2, tokens, width), BF16),
            rooms=rooms,
            across=across_room,
            load_sems=pltpu.SemaphoreType.DMA((n_loads,)),
            cot_sems=pltpu.SemaphoreType.DMA((2,)),
            sum_sems=pltpu.SemaphoreType.DMA((2,)),
            gate_sem=pltpu.SemaphoreType.DMA((1,)),
        ),
        n_copies,
        63 << 20,
    )


def adamw(weight, gradient, moment_one, moment_two, rate_val, decay_val):
    first_new = 0.9 * moment_one + 0.1 * gradient
    second_new = 0.95 * moment_two + 0.05 * gradient * gradient
    first_hat = first_new / (1.0 - 0.9**STEP)
    second_hat = second_new / (1.0 - 0.95**STEP)
    weight_new = weight - rate_val * (
        first_hat / (jnp.sqrt(second_hat) + 1e-08) + decay_val * weight
    )
    return (gradient, weight_new, first_new, second_new)


def local(
    n_dp,
    n_mp,
    residual_in,
    cotangent,
    expert_ids,
    attn_gain,
    query_w,
    key_value_weight,
    output_w,
    moe_gain,
    router_w,
    gateup_w,
    down_w,
    attn_gain_mean,
    attn_gain_var,
    query_mean,
    query_var,
    key_value_first_moment,
    key_value_second_moment,
    output_mean,
    output_var,
    moe_gain_mean,
    moe_gain_var,
    router_mean,
    router_var,
    gateup_mean,
    gateup_var,
    down_mean,
    down_var,
):
    mp = lax.axis_index("mp")
    place_in_all = lax.axis_index("dp") * n_mp + mp
    groups = 2 if 2 * n_dp <= 16 else 1
    tokens = residual_in.shape[0]
    owned = gateup_w.shape[0]
    span = n_mp // groups
    own_gain, own_router = attn_gain.shape[0], router_w.shape[0]
    first_row, lanes = 8, 128
    per_tile = lanes // own_gain

    def spread(gain):
        return jnp.where(jnp.arange(lanes) // own_gain == place_in_all % per_tile, jnp.tile(gain, per_tile), 0.0)

    small = jnp.concatenate(
        [
            spread(attn_gain)[None],
            spread(moe_gain)[None],
            jnp.zeros((first_row - 2, lanes), F32),
            jnp.pad(router_w, ((0, 0), (0, lanes - EXPERTS))),
        ]
    )
    shards = jnp.stack([query_w, key_value_weight, output_w.T]).astype(BF16)
    tables = [jnp.asarray(table) for table in rotary_constants()]
    early = list(range(owned))[:1]
    front = attention_forward(
        n_dp,
        n_mp,
        groups,
        0,
        first_row,
        small,
        shards,
        cotangent.astype(BF16),
        residual_in,
        gateup_w,
        down_w,
        expert_ids.T,
        tables,
        early,
    )

    found = run_experts(
        n_dp,
        n_mp,
        groups,
        1,
        front.normed_two,
        front.table,
        [front.cots_out, front.other_out][:groups],
        front.packed,
        [(early, front.near)],
    )

    given = types.SimpleNamespace(
        full=front.full_out,
        residual=residual_in,
        hidden=front.hidden,
        cotangent=cotangent,
        total=found.total,
        late=found.late,
        arrived=found.arrived,
        gate_parts=found.gate_parts,
        terms=found.terms,
        probs=front.probs,
        normed=front.normed,
        normed_two=front.normed_two,
        queries=front.queries,
        keyval=front.keyval,
        context=front.context,
        gains=front.gains,
        router=front.router,
        tables=tables,
    )
    back = attention_backward(n_dp, n_mp, groups, 2, given, first_row)
    input_grad, block_out = back.input_grad, back.block_out
    gateup_grad, down_grad = (
        sum(part[:, cut].astype(F32) for part in [found.grad_own] + back.arrived)
        for cut in (slice(0, 2), 2)
    )
    grads, small_grads = back.shards, back.small_shard
    query_grad, keyval_grad, output_grad = grads[0], grads[1], grads[2].T
    first_lane = (place_in_all % per_tile) * own_gain
    gain_one_grad, gain_two_grad = (
        lax.dynamic_slice_in_dim(small_grads[row], first_lane, own_gain) for row in (0, 1)
    )
    router_grad = small_grads[first_row:, :EXPERTS]
    matrix_rate = 0.2 / math.sqrt(MODEL_WIDTH)
    gain_one_all = adamw(attn_gain, gain_one_grad, attn_gain_mean, attn_gain_var, 0.1, 0.0)
    query_all = adamw(query_w, query_grad, query_mean, query_var, matrix_rate, 0.1)
    keyval_all = adamw(
        key_value_weight,
        keyval_grad,
        key_value_first_moment,
        key_value_second_moment,
        matrix_rate,
        0.1,
    )
    output_all = adamw(output_w, output_grad, output_mean, output_var, 0.1, 0.1)
    gain_two_all = adamw(moe_gain, gain_two_grad, moe_gain_mean, moe_gain_var, 0.1, 0.0)
    router_all = adamw(router_w, router_grad, router_mean, router_var, matrix_rate, 0.1)
    gateup_all = adamw(gateup_w, gateup_grad, gateup_mean, gateup_var, matrix_rate, 0.1)
    down_all = adamw(down_w, down_grad, down_mean, down_var, 0.07, 0.1)
    return (
        block_out,
        input_grad,
        gain_one_all[0],
        gain_one_all[1],
        gain_one_all[2],
        gain_one_all[3],
        query_all[0],
        query_all[1],
        query_all[2],
        query_all[3],
        keyval_all[0],
        keyval_all[1],
        keyval_all[2],
        keyval_all[3],
        output_all[0],
        output_all[1],
        output_all[2],
        output_all[3],
        gain_two_all[0],
        gain_two_all[1],
        gain_two_all[2],
        gain_two_all[3],
        router_all[0],
        router_all[1],
        router_all[2],
        router_all[3],
        gateup_all[0],
        gateup_all[1],
        gateup_all[2],
        gateup_all[3],
        down_all[0],
        down_all[1],
        down_all[2],
        down_all[3],
    )


def solution(mesh):
    in_specs = (
        P(("dp", "mp"), None),
        P(("dp", "mp"), None),
        P(("dp", "mp"), None),
        P(("dp", "mp")),
        P("dp", "mp"),
        P("dp", "mp"),
        P("mp", "dp"),
        P(("dp", "mp")),
        P(("dp", "mp"), None),
        P("dp", None, "mp", None),
        P("dp", "mp", None),
        P(("dp", "mp")),
        P(("dp", "mp")),
        P("dp", "mp"),
        P("dp", "mp"),
        P("dp", "mp"),
        P("dp", "mp"),
        P("mp", "dp"),
        P("mp", "dp"),
        P(("dp", "mp")),
        P(("dp", "mp")),
        P(("dp", "mp"), None),
        P(("dp", "mp"), None),
        P("dp", None, "mp", None),
        P("dp", None, "mp", None),
        P("dp", "mp", None),
        P("dp", "mp", None),
    )
    out_specs = (
        P(("dp", "mp"), None),
        P(("dp", "mp"), None),
        P(("dp", "mp")),
        P(("dp", "mp")),
        P(("dp", "mp")),
        P(("dp", "mp")),
        P("dp", "mp"),
        P("dp", "mp"),
        P("dp", "mp"),
        P("dp", "mp"),
        P("dp", "mp"),
        P("dp", "mp"),
        P("dp", "mp"),
        P("dp", "mp"),
        P("mp", "dp"),
        P("mp", "dp"),
        P("mp", "dp"),
        P("mp", "dp"),
        P(("dp", "mp")),
        P(("dp", "mp")),
        P(("dp", "mp")),
        P(("dp", "mp")),
        P(("dp", "mp"), None),
        P(("dp", "mp"), None),
        P(("dp", "mp"), None),
        P(("dp", "mp"), None),
        P("dp", None, "mp", None),
        P("dp", None, "mp", None),
        P("dp", None, "mp", None),
        P("dp", None, "mp", None),
        P("dp", "mp", None),
        P("dp", "mp", None),
        P("dp", "mp", None),
        P("dp", "mp", None),
    )
    step = functools.partial(local, mesh.shape["dp"], mesh.shape["mp"])
    return jax.shard_map(step, mesh=mesh, in_specs=in_specs, out_specs=out_specs, check_vma=False)
```
